32 devices in a mesh: fsdp: 8 (over z, x), rep: 4 (over y, core).
Axes of the slice: x: 2, y: 2, z: 4, core: 2. Of those that a mesh axis runs over, the one named last changes fastest.
Arguments:
- patches: bfloat16 [37632, 768], P(('fsdp', 'rep')), may hold values from -6 to 6
- slot_clip: int32 [768], P(('fsdp', 'rep')), may hold values from -1 to 767, as said below
- out_grad: bfloat16 [37632, 768], P(('fsdp', 'rep')), may hold values from -6 to 6
- project_in_weight: float32 [768, 2304], P('fsdp'), may hold values from -0.21875 to 0.21875
- project_in_moment: float32 [768, 2304], P('fsdp'), may hold values from -320 to 320
- project_in_average: float32 [768, 2304], P('fsdp'), may hold values from -0.21875 to 0.21875
- project_out_weight: float32 [768, 768], P('fsdp'), may hold values from -0.625 to 0.625
- project_out_moment: float32 [768, 768], P('fsdp'), may hold values from -320 to 320
- project_out_average: float32 [768, 768], P('fsdp'), may hold values from -0.625 to 0.625
- expand_weight: float32 [768, 3072], P('fsdp'), may hold values from -0.21875 to 0.21875
- expand_moment: float32 [768, 3072], P('fsdp'), may hold values from -320 to 320
- expand_average: float32 [768, 3072], P('fsdp'), may hold values from -0.21875 to 0.21875
- contract_weight: float32 [3072, 768], P('fsdp'), may hold values from -0.109375 to 0.109375
- contract_moment: float32 [3072, 768], P('fsdp'), may hold values from -320 to 320
- contract_average: float32 [3072, 768], P('fsdp'), may hold values from -0.109375 to 0.109375
- vector_weight: float32 [10, 768], P(None, 'fsdp'), may hold values from -1.2 to 1.6, as said below
- vector_moment: float32 [10, 768], P(None, 'fsdp'), may hold values from -512 to 512
- vector_average: float32 [10, 768], P(None, 'fsdp'), may hold values from -1.2 to 1.6, as said below
Outputs:
- block_out: bfloat16 [37632, 768], P(('fsdp', 'rep'))
- patch_grad: float32 [37632, 768], P(('fsdp', 'rep'))
- project_in_grad: float32 [768, 2304], P('fsdp')
- project_in_moment_new: float32 [768, 2304], P('fsdp')
- project_in_weight_new: float32 [768, 2304], P('fsdp')
- project_in_average_new: float32 [768, 2304], P('fsdp')
- project_in_weight_low: bfloat16 [768, 2304], P('fsdp')
- project_out_grad: float32 [768, 768], P('fsdp')
- project_out_moment_new: float32 [768, 768], P('fsdp')
- project_out_weight_new: float32 [768, 768], P('fsdp')
- project_out_average_new: float32 [768, 768], P('fsdp')
- project_out_weight_low: bfloat16 [768, 768], P('fsdp')
- expand_grad: float32 [768, 3072], P('fsdp')
- expand_moment_new: float32 [768, 3072], P('fsdp')
- expand_weight_new: float32 [768, 3072], P('fsdp')
- expand_average_new: float32 [768, 3072], P('fsdp')
- expand_weight_low: bfloat16 [768, 3072], P('fsdp')
- contract_grad: float32 [3072, 768], P('fsdp')
- contract_moment_new: float32 [3072, 768], P('fsdp')
- contract_weight_new: float32 [3072, 768], P('fsdp')
- contract_average_new: float32 [3072, 768], P('fsdp')
- contract_weight_low: bfloat16 [3072, 768], P('fsdp')
- vector_grad: float32 [10, 768], P(None, 'fsdp')
- vector_moment_new: float32 [10, 768], P(None, 'fsdp')
- vector_weight_new: float32 [10, 768], P(None, 'fsdp')
- vector_average_new: float32 [10, 768], P(None, 'fsdp')
- vector_weight_low: bfloat16 [10, 768], P(None, 'fsdp')
The draws below stay inside these ranges and needn't reach their ends.
Inputs may be any that keep to these rules, and one draw needn't show every extreme that they name: `slot_clip`: slots of one device hold whole clips one after another, then its empty slots (-1); equal numbers stand only on one device; a clip has at most 8 frames, and some clip has exactly 8; each device has 12 or more live slots, and some device has no empty one. `vector_weight`: rows 0 and 3 lie within 0.4 to 1.6, the others within -1.2 to 1.2. `vector_average`: rows 0 and 3 lie within 0.4 to 1.6, the others within -1.2 to 1.2.
All inputs are finite; a program needn't handle non-finite values.
Results may differ from the reference program's by a relative error of at most 0.015.
Values may be sent and summed in bfloat16 or wider, within the bound.
A program may use at most 192 MiB of HBM per device.

```python
import math
import jax
import jax.numpy as jnp
from jax import lax

D = 768
HEADS = 12
HEAD_DIM = 64
FF = 3072
PATCH = 49
MAXCLIP = 8
SLOTS = 24
FRAMES = 768
TOKENS = 37632
N_FSDP = 8
N_REP = 4


def vector_rows(key, spread_bias):
    drawn = jnp.clip(jax.random.normal(key, (10, D), jnp.float32), -4.0, 4.0)
    row_number = jnp.arange(10)[:, None]
    is_gain = (row_number == 0) | (row_number == 3)
    return jnp.where(is_gain, 1.0 + 0.15 * drawn, spread_bias * drawn)


def draw_vector_weight(key, part):
    key = jax.random.fold_in(key, 21)
    return vector_rows(key, 0.3)


def draw_vector_average(key, part):
    key = jax.random.fold_in(key, 22)
    return vector_rows(key, 0.3)


def draw_slot_clip(key, part):
    key = jax.random.fold_in(key, 11)
    device_total = FRAMES // SLOTS
    keys_all = jax.random.split(key, 3)
    opening = jax.random.randint(keys_all[0], (device_total, SLOTS), 0, 4) == 0
    slot_number = jnp.arange(SLOTS, dtype=jnp.int32)[None, :]
    device_number = jnp.arange(device_total, dtype=jnp.int32)[:, None]
    forced = slot_number % MAXCLIP == 0
    chosen = jax.random.randint(keys_all[1], (), 0, device_total)
    opening = jnp.where(device_number == chosen, forced, opening | forced)
    local_clip = jnp.cumsum(opening.astype(jnp.int32), axis=1) - 1
    clip_ids = device_number * SLOTS + local_clip
    filled = jax.random.randint(keys_all[2], (device_total, 1), SLOTS // 2, SLOTS + 1)
    filled = jnp.where(device_number == chosen, SLOTS, filled)
    return jnp.where(slot_number < filled, clip_ids, -1).reshape(FRAMES).astype(jnp.int32)


def raised(values, own_key, source, target, parts, factor):
    owner, partner = [(jnp.arange(values.shape[dim]) // (values.shape[dim] // parts)).reshape([-1 if axis == dim else 1 for axis in range(values.ndim)]) for dim in (source, target)]
    chosen = jax.random.permutation(own_key, parts)[partner]
    strong = (owner == chosen) | (owner == (partner + parts // 2) % parts)
    return jnp.where(strong, factor * values, values)


def block_levels(own_key, shape, cuts, smallest, high):
    def one(dim, blocks):
        draws = jax.random.uniform(jax.random.fold_in(jax.random.fold_in(own_key, 6), dim), (blocks,), jnp.float32, smallest / len(cuts), high / len(cuts))
        return jnp.repeat(jnp.exp(draws), shape[dim] // blocks).reshape((-1,) + (1,) * (len(shape) - dim - 1))

    level = one(*cuts[0])
    for cut in cuts[1:]:
        level = level * one(*cut)
    return level


def normal_values(stream_key, extent, deviation, most, cuts=(), kind=jnp.bfloat16):
    entries = jax.random.normal(stream_key, extent, jnp.float32) * deviation
    if len(cuts) > 0:
        entries = block_levels(stream_key, extent, cuts, -0.22, 0.18) * entries
    return jnp.clip(entries, min=-most, max=most).astype(kind)


def heavy_noise(rng, dims, deviation, bound, cuts, heavy, held_as=jnp.bfloat16):
    entries = deviation * jax.random.normal(rng, dims, jnp.float32)
    if cuts:
        entries = entries * block_levels(rng, dims, cuts, -0.22, 0.18)
    return jnp.clip(raised(entries, jax.random.fold_in(rng, 3), *heavy), -bound, bound).astype(held_as)


def setup_inputs(seed: int = 0) -> dict:
    splits = jax.random.split(jax.random.key(seed), 19)
    return {
        "patches": heavy_noise(splits[0], (TOKENS, D), 1.0, 6.0, ((0, 32),), (0, 1, 32, 2.75)),
        "slot_clip": draw_slot_clip(jax.random.fold_in(splits[18], 71), 0),
        "out_grad": normal_values(splits[2], (TOKENS, D), 1.0, 6.0, ((0, 32),)),
        "project_in_weight": normal_values(splits[3], (D, 3 * D), D ** -0.5, 0.21875, ((0, 8),), jnp.float32),
        "project_in_moment": normal_values(splits[4], (D, 3 * D), (0.3 * TOKENS ** 0.5), 320.0, ((0, 8),), jnp.float32),
        "project_in_average": normal_values(splits[5], (D, 3 * D), D ** -0.5, 0.21875, ((0, 8),), jnp.float32),
        "project_out_weight": normal_values(splits[6], (D, D), (D // 8) ** -0.5, 0.625, ((0, 8),), jnp.float32),
        "project_out_moment": normal_values(splits[7], (D, D), (0.3 * TOKENS ** 0.5), 320.0, ((0, 8),), jnp.float32),
        "project_out_average": normal_values(splits[8], (D, D), (D // 8) ** -0.5, 0.625, ((0, 8),), jnp.float32),
        "expand_weight": normal_values(splits[9], (D, FF), D ** -0.5, 0.21875, ((0, 8),), jnp.float32),
        "expand_moment": normal_values(splits[10], (D, FF), (0.3 * TOKENS ** 0.5), 320.0, ((0, 8),), jnp.float32),
        "expand_average": normal_values(splits[11], (D, FF), D ** -0.5, 0.21875, ((0, 8),), jnp.float32),
        "contract_weight": normal_values(splits[12], (FF, D), FF ** -0.5, 0.109375, ((0, 8),), jnp.float32),
        "contract_moment": normal_values(splits[13], (FF, D), (0.3 * TOKENS ** 0.5), 320.0, ((0, 8),), jnp.float32),
        "contract_average": normal_values(splits[14], (FF, D), FF ** -0.5, 0.109375, ((0, 8),), jnp.float32),
        "vector_weight": draw_vector_weight(jax.random.fold_in(splits[18], 71), 0),
        "vector_moment": normal_values(splits[16], (10, D), (0.5 * TOKENS ** 0.5), 512.0, ((1, 8),), jnp.float32),
        "vector_average": draw_vector_average(jax.random.fold_in(splits[18], 71), 0),
    }


@jax.custom_vjp
def low(v):
    return lax.optimization_barrier(v.astype(jnp.bfloat16)).astype(jnp.float32)

@jax.custom_vjp
def low_back(v):
    return v

def low_keep(v):
    return (low(v), None)

def low_pass(kept, grad):
    return (grad,)

def back_keep(v):
    return (v, None)

def back_low(kept, grad):
    return (low(grad),)
low.defvjp(low_keep, low_pass)
low_back.defvjp(back_keep, back_low)
EPSILON = 1e-06
MOMENTUM = 0.5
AVERAGE = 0.5
RATES = (0.3, 0.3, 0.1, 0.03, 0.5)
NEGATIVE = -1e+30

def matmul_high(left, right):
    return jnp.dot(left, right, precision=lax.Precision.HIGHEST, preferred_element_type=jnp.float32)

def norm_apply(values, gain, shift):
    row_mean = lax.optimization_barrier(jnp.mean(values, axis=-1, keepdims=True))
    centred = values - row_mean
    spread = lax.optimization_barrier(jnp.mean(centred * centred, axis=-1, keepdims=True))
    return centred * lax.rsqrt(spread + EPSILON) * gain + shift

def layer(inputs, clips, inward, outward, expand, contract, vectors):
    gain_one, shift_one, bias_out = (vectors[0], vectors[1], vectors[2])
    gain_two, shift_two, bias_last = (vectors[3], vectors[4], vectors[5])
    bias_expand = vectors[6:10].reshape(FF)
    row_total = inputs.shape[0]
    normed = low(norm_apply(inputs, gain_one, shift_one))
    triple = matmul_high(normed, inward)
    scale = HEAD_DIM ** (-0.5)
    query = low(low_back(triple[:, :D] * scale)).reshape(row_total, HEADS, HEAD_DIM)
    keys = low(low_back(triple[:, D:2 * D])).reshape(row_total, HEADS, HEAD_DIM)
    values = low(low_back(triple[:, 2 * D:])).reshape(row_total, HEADS, HEAD_DIM)
    scores = low_back(jnp.einsum('qhd,khd->hqk', query, keys, precision=lax.Precision.HIGHEST))
    positions = jnp.arange(row_total)
    allowed = (clips[:, None] == clips[None, :]) & (clips[None, :] >= 0) | (positions[:, None] == positions[None, :])
    masked = jnp.where(allowed[None], scores, NEGATIVE)
    probs = low(jax.nn.softmax(masked, axis=-1))
    attended = jnp.einsum('hqk,khd->qhd', probs, values, precision=lax.Precision.HIGHEST).reshape(row_total, D)
    mixed = low(low_back(attended))
    branch = low_back(matmul_high(mixed, outward) + bias_out)
    middle = inputs + branch
    normed_two = low(norm_apply(middle, gain_two, shift_two))
    before = low_back(matmul_high(normed_two, expand) + bias_expand)
    hidden = low(jax.nn.gelu(before, approximate=False))
    return middle + low_back(matmul_high(hidden, contract) + bias_last)

def reference(patches, slot_clip, out_grad, project_in_weight, project_in_moment, project_in_average, project_out_weight, project_out_moment, project_out_average, expand_weight, expand_moment, expand_average, contract_weight, contract_moment, contract_average, vector_weight, vector_moment, vector_average):
    masters = (project_in_weight, project_out_weight, expand_weight, contract_weight, vector_weight)
    moments = (project_in_moment, project_out_moment, expand_moment, contract_moment, vector_moment)
    averages = (project_in_average, project_out_average, expand_average, contract_average, vector_average)
    token_clip = jnp.repeat(slot_clip, PATCH)
    live_rows = (token_clip >= 0).astype(jnp.float32)[:, None]
    rows_device = SLOTS * PATCH
    device_total = N_FSDP * N_REP
    clip_blocks = token_clip.reshape(device_total, rows_device)
    checked = jax.checkpoint(layer)

    def whole(inputs, inward, outward, expand, contract, vectors):
        lowered = (low(inward), low(outward), low(expand), low(contract), low(vectors))
        blocks = inputs.reshape(device_total, rows_device, D)

        def visit(carry, item):
            return (carry, checked(item[0], item[1], *lowered))
        carry_out, results = lax.scan(visit, jnp.zeros((), jnp.float32), (blocks, clip_blocks))
        return results.reshape(TOKENS, D)
    result, pull_back = jax.vjp(whole, patches.astype(jnp.float32), *masters)
    grads = pull_back(out_grad.astype(jnp.float32) * live_rows)
    outputs = [result.astype(jnp.bfloat16), grads[0]]
    for member in range(5):
        grad_sum = grads[member + 1]
        rate = RATES[member] / math.sqrt(TOKENS)
        moment_new = MOMENTUM * moments[member] + grad_sum
        weight_new = masters[member] - rate * (grad_sum + MOMENTUM * moment_new)
        average_new = AVERAGE * averages[member] + (1.0 - AVERAGE) * weight_new
        outputs.extend([grad_sum, moment_new, weight_new, average_new, weight_new.astype(jnp.bfloat16)])
    return tuple(outputs)
```

```python
import functools
import math

import jax
import jax.numpy as jnp
from jax import lax
from jax.sharding import PartitionSpec as P
import jax.experimental.pallas as pl
import jax.experimental.pallas.tpu as pltpu

BF, F32 = jnp.bfloat16, jnp.float32
HEAD_DIM = 64
SLOT = 49
LIVE_MAX = 8
WIN = 416
EPSILON = 1e-06
MOMENTUM = 0.5
AVERAGE = 0.5
RATES = (0.3, 0.3, 0.1, 0.03, 0.5)
NEG = -1e30

def dg(a,b,ca,cb):
    return lax.dot_general(a,b,(((ca,),(cb,)),((),())),preferred_element_type=F32)

def group_end(clips, start, slots):
    end = start+1
    for e in range(2, LIVE_MAX+1):
        cand = start+e
        safe = jnp.minimum(cand, slots-1)
        edge = (cand == slots) | ((cand < slots) & ((clips[safe] != clips[jnp.maximum(safe-1,0)]) | (clips[safe] < 0)))
        end = jnp.where(edge, cand, end)
    return end

def fill_bias(clips, w0, slots, bias):
    def keys(shape, dim):
        row = lax.broadcasted_iota(jnp.int32, shape, dim) + w0
        slot = (row*1338) >> 16
        def one(s, key):
            return jnp.where((slot == s) & (clips[s] >= 0), clips[s], key)
        return lax.fori_loop(0, slots, one, -1-row, unroll=True)
    bias[...] = jnp.where(keys((WIN,1),0) == keys((1,WIN),1), 0.0, NEG)

def clear_tail(ref, slots):
    tail = slots*SLOT//16*16
    ref[pl.ds(tail, ref.shape[0]-tail), :] = jnp.zeros((ref.shape[0]-tail, ref.shape[1]), BF)

def fwd_kernel(clips, t_ref, o_ref, bias):
    slots = clips.shape[0]
    rows = t_ref.shape[0]; D = o_ref.shape[1]
    clear_tail(o_ref, slots)
    def group(g, start):
        @pl.when(start < slots)
        def _():
            end = group_end(clips, start, slots)
            r0 = start*SLOT; r1 = end*SLOT
            w0 = pl.multiple_of(jnp.minimum((r0>>4)<<4, rows-WIN), 16)
            fill_bias(clips, w0, slots, bias)
            rowi = lax.broadcasted_iota(jnp.int32,(WIN,128),0)+w0
            mine = (rowi >= r0) & (rowi < r1)
            lane = lax.broadcasted_iota(jnp.int32,(1,128),1)
            win = pl.ds(w0, WIN)
            for p in range(D//128):
                q = t_ref[win, pl.ds(p*128,128)]
                k = t_ref[win, pl.ds(D+p*128,128)]
                v = t_ref[win, pl.ds(2*D+p*128,128)]
                outs=[]
                for h in range(2):
                    keep = (lane//64 == h).astype(BF)
                    s = dg(q*keep, k, 1, 1) + bias[...]
                    top = jnp.max(s, axis=1, keepdims=True)
                    e = jnp.exp(s-top)
                    inv = 1.0/jnp.sum(e, axis=1, keepdims=True)
                    pl_ = (e*inv).astype(BF)
                    outs.append(jnp.dot(pl_, v, preferred_element_type=F32))
                o = jnp.where(lane < 64, outs[0], outs[1])
                old = o_ref[win, pl.ds(p*128,128)]
                o_ref[win, pl.ds(p*128,128)] = jnp.where(mine, o, old.astype(F32)).astype(BF)
        return jnp.where(start < slots, group_end(clips, start, slots), start)
    lax.fori_loop(0, (2*slots)//(LIVE_MAX+1)+1, group, 0)

def bwd_kernel(clips, t_ref, do_ref, dt_ref, bias):
    slots = clips.shape[0]
    rows = t_ref.shape[0]; D = do_ref.shape[1]
    clear_tail(dt_ref, slots)
    def group(g, start):
        @pl.when(start < slots)
        def _():
            end = group_end(clips, start, slots)
            r0 = start*SLOT; r1 = end*SLOT
            w0 = pl.multiple_of(jnp.minimum((r0>>4)<<4, rows-WIN), 16)
            fill_bias(clips, w0, slots, bias)
            rowi = lax.broadcasted_iota(jnp.int32,(WIN,128),0)+w0
            mine = (rowi >= r0) & (rowi < r1)
            lane = lax.broadcasted_iota(jnp.int32,(1,128),1)
            win = pl.ds(w0, WIN)
            for p in range(D//128):
                q = t_ref[win, pl.ds(p*128,128)]
                k = t_ref[win, pl.ds(D+p*128,128)]
                v = t_ref[win, pl.ds(2*D+p*128,128)]
                do = do_ref[win, pl.ds(p*128,128)]
                dqs=[];dks=[];dvs=[]
                for h in range(2):
                    keep = (lane//64 == h).astype(BF)
                    s = dg(k, q*keep, 1, 1) + bias[...]
                    top = jnp.max(s, axis=0, keepdims=True)
                    e = jnp.exp(s-top)
                    inv = 1.0/jnp.sum(e, axis=0, keepdims=True)
                    pt = e*inv
                    dp = dg(v, do*keep, 1, 1)
                    dvs.append(jnp.dot(pt.astype(BF), do, preferred_element_type=F32))
                    inner = jnp.sum(dp*pt, axis=0, keepdims=True)
                    ds = (pt*(dp-inner)).astype(BF)
                    dks.append(jnp.dot(ds, q, preferred_element_type=F32))
                    dqs.append(dg(ds, k, 0, 0))
                for i,x in enumerate((dqs,dks,dvs)):
                    new = jnp.where(lane < 64, x[0], x[1]).astype(BF).astype(F32)
                    if i==0: new = new*(64**-0.5)
                    c = pl.ds(i*D+p*128,128)
                    old = dt_ref[win, c].astype(F32)
                    dt_ref[win, c] = jnp.where(mine, new, old).astype(BF)
        return jnp.where(start < slots, group_end(clips, start, slots), start)
    lax.fori_loop(0, (2*slots)//(LIVE_MAX+1)+1, group, 0)

def attend(clips, t):
    D=t.shape[1]//3
    return pl.pallas_call(fwd_kernel, out_shape=jax.ShapeDtypeStruct((t.shape[0],D),BF),
      in_specs=[pl.BlockSpec(memory_space=pltpu.SMEM), pl.BlockSpec(memory_space=pltpu.VMEM)],
      out_specs=pl.BlockSpec(memory_space=pltpu.VMEM),
      scratch_shapes=[pltpu.VMEM((WIN,WIN),F32)],
      compiler_params=pltpu.CompilerParams(vmem_limit_bytes=48*2**20),name="attention_forward")(clips,t)
def attend_back(clips, t, do):
    return pl.pallas_call(bwd_kernel, out_shape=jax.ShapeDtypeStruct(t.shape,BF),
      in_specs=[pl.BlockSpec(memory_space=pltpu.SMEM)]+[pl.BlockSpec(memory_space=pltpu.VMEM)]*2,
      out_specs=pl.BlockSpec(memory_space=pltpu.VMEM),
      scratch_shapes=[pltpu.VMEM((WIN,WIN),F32)],
      compiler_params=pltpu.CompilerParams(vmem_limit_bytes=48*2**20),name="attention_backward")(clips,t,do)


RT = 400


def dot_nt(left, right):
    return lax.dot_general(left, right, (((1,), (1,)), ((), ())), preferred_element_type=F32)


def dot_tn(left, right):
    return lax.dot_general(left, right, (((0,), (0,)), ((), ())), preferred_element_type=F32)


def dot_nn(left, right):
    return jnp.dot(left, right, preferred_element_type=F32)


def norm_parts(values):
    centred = values - jnp.mean(values, axis=-1, keepdims=True)
    scale = lax.rsqrt(jnp.mean(centred * centred, axis=-1, keepdims=True) + EPSILON)
    return centred * scale, scale


def norm_back(grad, gain, unit, scale):
    inner = grad * gain
    return scale * (
        inner
        - jnp.mean(inner, axis=-1, keepdims=True)
        - unit * jnp.mean(inner * unit, axis=-1, keepdims=True)
    )


def gelu_pair(u):
    bell = jnp.exp(-0.5 * u * u)
    t = 1.0 / (1.0 + (0.3275911 * 0.5**0.5) * jnp.abs(u))
    poly = t * (
        0.5 * 0.254829592
        + t * (-0.5 * 0.284496736 + t * (0.5 * 1.421413741 + t * (-0.5 * 1.453152027 + t * (0.5 * 1.061405429))))
    )
    tail = poly * bell
    phi = jnp.where(u < 0, tail, 1.0 - tail)
    return u * phi, phi + u * (bell * (2.0 * math.pi) ** -0.5)


def column_sum(values):
    return jnp.sum(values, axis=0, keepdims=True)


def tiles(rows, body):
    @pl.loop(0, rows // RT)
    def _(i):
        body(pl.ds(pl.multiple_of(i * RT, 16), RT))


def qkv_norm(x_ref, vec, a1_ref):
    def one(win):
        unit, _ = norm_parts(x_ref[win, :].astype(F32))
        a1_ref[win, :] = (unit * vec[0:1, :] + vec[1:2, :]).astype(BF)

    tiles(x_ref.shape[0], one)


def qkv_block(a1_ref, w_ref, t_ref, part):
    width = a1_ref.shape[1]

    def one(win):
        out = dot_nn(a1_ref[win, :], w_ref[...])
        if part == 0:
            out = out * HEAD_DIM**-0.5
        t_ref[win, pl.ds(part * width, width)] = out.astype(BF)

    tiles(a1_ref.shape[0], one)


def qkv_kernel(x_ref, vec, w_ref, t_ref, a1_ref):
    qkv_norm(x_ref, vec, a1_ref)
    for part in range(3):
        qkv_block(a1_ref, w_ref.at[part], t_ref, part)


def middle_step(x_ref, o_ref, vec, wo_ref, m_ref, a2_ref):
    def one(win):
        middle = x_ref[win, :].astype(F32) + (dot_nn(o_ref[win, :], wo_ref[...]) + vec[2:3, :])
        m_ref[win, :] = middle
        unit, _ = norm_parts(middle)
        a2_ref[win, :] = (unit * vec[3:4, :] + vec[4:5, :]).astype(BF)

    tiles(x_ref.shape[0], one)


def chunk_step(first, bias, a2_ref, dy_ref, we_ref, wc_ref, h_ref, du_ref, y_ref, da2_ref, be_ref):
    be_ref[...] = jnp.zeros_like(be_ref)

    def one(win):
        hidden, slope = gelu_pair(dot_nn(a2_ref[win, :], we_ref[...]) + bias)
        hidden = hidden.astype(BF)
        h_ref[win, :] = hidden
        du = (dot_nt(dy_ref[win, :], wc_ref[...]) * slope).astype(BF)
        du_ref[win, :] = du
        be_ref[...] += column_sum(du.astype(F32))
        y = dot_nn(hidden, wc_ref[...])
        da2 = dot_nt(du, we_ref[...])
        if first is True:
            y_ref[win, :] = y
            da2_ref[win, :] = da2
        else:
            y_ref[win, :] += y
            da2_ref[win, :] += da2

    tiles(a2_ref.shape[0], one)


def middle_back(live_rows, m_ref, y_ref, dy_ref, da2_ref, vec, wo_ref, out_ref, dm_ref, dz_ref, do_ref, sums):
    sums[...] = jnp.zeros_like(sums)

    def one(win):
        middle = m_ref[win, :]
        out_ref[win, :] = (middle + (y_ref[win, :] + vec[5:6, :])).astype(BF)
        unit, scale = norm_parts(middle)
        da2 = da2_ref[win, :]
        dy = dy_ref[win, :].astype(F32)
        dm = dy + norm_back(da2, vec[3:4, :], unit, scale)
        dm_ref[win, :] = dm
        dz = dm.astype(BF)
        dz_ref[win, :] = dz
        do_ref[win, :] = dot_nt(dz, wo_ref[...]).astype(BF)
        sums[0:1, :] += column_sum(da2 * unit)
        sums[1:2, :] += column_sum(da2)
        sums[2:3, :] += column_sum(dz.astype(F32))
        sums[3:4, :] += column_sum(dy)

    tiles(m_ref.shape[0], one)


def feed_kernel(
    x_ref, o_ref, dy_ref, vec, wo_ref, we_ref, wc_ref,
    out_ref, dm_ref, do_ref, gwo_ref, gwe_ref, gwc_ref, sums, be_ref,
    m_ref, a2_ref, h_ref, du_ref, y_ref, da2_ref, dz_ref,
):
    middle_step(x_ref, o_ref, vec, wo_ref, m_ref, a2_ref)
    for j in range(4):
        chunk_step(
            j == 0, vec[6 + j : 7 + j, :], a2_ref, dy_ref, we_ref.at[j], wc_ref.at[j],
            h_ref, du_ref, y_ref, da2_ref, be_ref.at[pl.ds(8 * j, 1)],
        )
        gwc_ref[j] = dot_tn(h_ref[...], dy_ref[...]).astype(BF)
        gwe_ref[j] = dot_tn(a2_ref[...], du_ref[...]).astype(BF)
    middle_back(None, m_ref, y_ref, dy_ref, da2_ref, vec, wo_ref, out_ref, dm_ref, dz_ref, do_ref, sums)
    gwo_ref[...] = dot_tn(o_ref[...], dz_ref[...]).astype(BF)


def first_back(x_ref, dt_ref, dm_ref, vec, w_refs, pg_ref, sums):
    sums[...] = jnp.zeros_like(sums)
    width = x_ref.shape[1]

    def one(win):
        da1 = dot_nt(dt_ref[win, pl.ds(0, width)], w_refs[0][...])
        da1 += dot_nt(dt_ref[win, pl.ds(width, width)], w_refs[1][...])
        da1 += dot_nt(dt_ref[win, pl.ds(2 * width, width)], w_refs[2][...])
        unit, scale = norm_parts(x_ref[win, :].astype(F32))
        pg_ref[win, :] = dm_ref[win, :] + norm_back(da1, vec[0:1, :], unit, scale)
        sums[0:1, :] += column_sum(da1 * unit)
        sums[1:2, :] += column_sum(da1)

    tiles(x_ref.shape[0], one)


def first_kernel(x_ref, a1_ref, dt_ref, dm_ref, vec, w_ref, pg_ref, gwi_ref, sums):
    width = x_ref.shape[1]
    for part in range(3):
        gwi_ref[part] = dot_tn(a1_ref[...], dt_ref[:, pl.ds(part * width, width)]).astype(BF)
    first_back(x_ref, dt_ref, dm_ref, vec, [w_ref.at[p] for p in range(3)], pg_ref, sums)


VM = pl.BlockSpec(memory_space=pltpu.VMEM)
SM = pl.BlockSpec(memory_space=pltpu.SMEM)


def vmem_call(kernel, name, ins, outs, scratch=(), smem=0):
    return pl.pallas_call(
        kernel,
        out_shape=[jax.ShapeDtypeStruct(s, d) for s, d in outs],
        in_specs=[SM] * smem + [VM] * (len(ins) - smem),
        out_specs=[VM] * len(outs),
        scratch_shapes=[pltpu.VMEM(s, d) for s, d in scratch],
        compiler_params=pltpu.CompilerParams(vmem_limit_bytes=60 * 2**20),
        name=name,
    )(*ins)


def run_qkv(x, vec, wi):
    rows, width = x.shape
    return vmem_call(
        qkv_kernel, "project_in", (x, vec, wi), [((rows, 3 * width), BF), ((rows, width), BF)]
    )


def run_feed(x, o, dy, vec, wo, we, wc):
    rows, width = x.shape
    wide, low = ((rows, width), F32), ((rows, width), BF)
    return vmem_call(
        feed_kernel, "feed_forward", (x, o, dy, vec, wo, we, wc),
        [low, wide, low, ((width, width), BF), ((4, width, width), BF), ((4, width, width), BF),
         ((8, width), F32), ((32, width), F32)],
        [wide, low, low, low, wide, wide, low],
    )


def run_first(x, a1, dt, dm, vec, wi):
    rows, width = x.shape
    return vmem_call(
        first_kernel, "project_in_back", (x, a1, dt, dm, vec, wi),
        [((rows, width), F32), ((3, width, width), BF), ((8, width), F32)],
    )


def pack_shards(wi, wo, we, wc, parts):
    rows, width = wo.shape
    wi = wi.reshape(rows, 3, width).swapaxes(0, 1)
    we = we.reshape(rows, parts, 4, rows).transpose(2, 0, 1, 3).reshape(4, rows, width)
    wc = wc.reshape(4, rows, width)
    return jnp.concatenate([wi, wo[None], we, wc], axis=0)


def unpack_shards(blocks, parts):
    rows, width = blocks.shape[1:]
    wi = blocks[0:3].swapaxes(0, 1).reshape(rows, 3 * width)
    we = blocks[4:8].reshape(4, rows, parts, rows).transpose(1, 2, 0, 3).reshape(rows, 4 * width)
    return wi, blocks[3], we, blocks[8:12].reshape(4 * rows, width)


def on_device(
    patches, slot_clip, out_grad,
    project_in_weight, project_in_moment, project_in_average,
    project_out_weight, project_out_moment, project_out_average,
    expand_weight, expand_moment, expand_average,
    contract_weight, contract_moment, contract_average,
    vector_weight, vector_moment, vector_average,
):
    masters = (project_in_weight, project_out_weight, expand_weight, contract_weight, vector_weight)
    moments = (project_in_moment, project_out_moment, expand_moment, contract_moment, vector_moment)
    averages = (project_in_average, project_out_average, expand_average, contract_average, vector_average)
    parts, copies = lax.axis_size("fsdp"), lax.axis_size("rep")
    mine, copy = lax.axis_index("fsdp"), lax.axis_index("rep")
    count, width = patches.shape
    rows = (count + RT - 1) // RT * RT
    sh = width // parts

    packed = pack_shards(*(m.astype(BF) for m in masters[:4]), parts).reshape(12 * sh, width)
    piece = 12 * sh // copies
    quarter = lax.dynamic_slice_in_dim(packed, copy * piece, piece, 0)
    full = lax.all_gather(quarter, ("fsdp", "rep"), axis=0, tiled=True)
    full = full.reshape(parts, 12, sh, width).swapaxes(0, 1).reshape(12, width, width)
    vec = lax.all_gather(vector_weight.astype(BF), "fsdp", axis=1, tiled=True).astype(F32)
    be = vec[6:].reshape(parts, 4, sh).swapaxes(0, 1).reshape(4, width)
    vec = jnp.concatenate([vec[:6], be, jnp.zeros((6, width), F32)], axis=0)

    pad = ((0, rows - count), (0, 0))
    live = jnp.repeat(slot_clip >= 0, SLOT)[:, None]
    x = jnp.pad(patches, pad)
    dy = jnp.pad(jnp.where(live, out_grad, 0), pad)
    t, a1 = run_qkv(x, vec, full[0:3])
    o = attend(slot_clip, t)
    out, dm, do, gwo, gwe, gwc, sums_two, sums_be = run_feed(x, o, dy, vec, full[3], full[4:8], full[8:12])
    dt = attend_back(slot_clip, t, do)
    pg, gwi, sums_one = run_first(x, a1, dt, dm, vec, full[0:3])

    grads = jnp.concatenate([gwi, gwo[None], gwe, gwc], axis=0)
    grads = grads.reshape(12, parts, sh, width).swapaxes(0, 1).reshape(parts * 12 * sh, width)
    grads = lax.psum_scatter(grads, ("fsdp", "rep"), scatter_dimension=0, tiled=True)
    grads = lax.all_gather(grads, "rep", axis=0, tiled=True).reshape(12, sh, width)
    be_grad = sums_be[::8].reshape(4, parts, sh).swapaxes(0, 1).reshape(4, width)
    vector = jnp.concatenate(
        [sums_one[0:2], sums_two[2:3], sums_two[0:2], sums_two[3:4], be_grad], axis=0
    )
    vector = lax.dynamic_slice_in_dim(lax.psum(vector, ("fsdp", "rep")), mine * sh, sh, 1)
    total_grads = tuple(g.astype(F32) for g in unpack_shards(grads, parts)) + (vector,)

    tokens_all = count * parts * copies
    outputs = [out[:count], pg[:count]]
    for member in range(5):
        grad_sum = total_grads[member]
        rate = RATES[member] / tokens_all**0.5
        moment_new = MOMENTUM * moments[member] + grad_sum
        weight_new = masters[member] - rate * (grad_sum + MOMENTUM * moment_new)
        average_new = AVERAGE * averages[member] + (1.0 - AVERAGE) * weight_new
        outputs.extend([grad_sum, moment_new, weight_new, average_new, weight_new.astype(BF)])
    return tuple(outputs)


def solution(mesh):
    tokens = P(("fsdp", "rep"), None)
    split, split_vector = P("fsdp", None), P(None, "fsdp")
    in_specs = (tokens, P(("fsdp", "rep")), tokens) + (split,) * 12 + (split_vector,) * 3
    out_specs = (tokens,) * 2 + (split,) * 20 + (split_vector,) * 5
    return jax.shard_map(on_device, mesh=mesh, in_specs=in_specs, out_specs=out_specs, check_vma=False)
```

```python
import functools
import math

import jax
import jax.numpy as jnp
from jax import lax
from jax.sharding import PartitionSpec as P
import jax.experimental.pallas as pl
import jax.experimental.pallas.tpu as pltpu

BF, F32 = jnp.bfloat16, jnp.float32
HEAD_DIM = 64
SLOT = 49
LIVE_MAX = 8
WIN = 416
EPSILON = 1e-06
MOMENTUM = 0.5
AVERAGE = 0.5
RATES = (0.3, 0.3, 0.1, 0.03, 0.5)
NEG = -1e30

def dg(a,b,ca,cb):
    return lax.dot_general(a,b,(((ca,),(cb,)),((),())),preferred_element_type=F32)

def group_end(clips, start, slots):
    end = start+1
    for e in range(2, LIVE_MAX+1):
        cand = start+e
        safe = jnp.minimum(cand, slots-1)
        edge = (cand == slots) | ((cand < slots) & ((clips[safe] != clips[jnp.maximum(safe-1,0)]) | (clips[safe] < 0)))
        end = jnp.where(edge, cand, end)
    return end

def fill_bias(clips, w0, slots, bias):
    def keys(shape, dim):
        row = lax.broadcasted_iota(jnp.int32, shape, dim) + w0
        slot = (row*1338) >> 16
        def one(s, key):
            return jnp.where((slot == s) & (clips[s] >= 0), clips[s], key)
        return lax.fori_loop(0, slots, one, -1-row, unroll=True)
    bias[...] = jnp.where(keys((WIN,1),0) == keys((1,WIN),1), 0.0, NEG)

def clear_tail(ref, slots):
    tail = slots*SLOT//16*16
    ref[pl.ds(tail, ref.shape[0]-tail), :] = jnp.zeros((ref.shape[0]-tail, ref.shape[1]), BF)

def fwd_kernel(clips, t_ref, g_ref, o_ref, dy_ref, bias):
    slots = clips.shape[0]
    rows = t_ref.shape[0]; D = o_ref.shape[1]
    clear_tail(o_ref, slots)
    clear_tail(dy_ref, slots)
    slot = (lax.broadcasted_iota(jnp.int32,(slots*SLOT,1),0)*1338) >> 16
    live = lax.fori_loop(0, slots, lambda s, was: jnp.where((slot == s) & (clips[s] >= 0), 1.0, was), jnp.zeros((slots*SLOT,1),F32), unroll=True)
    dy_ref[pl.ds(0,slots*SLOT), :] = jnp.where(live > 0, g_ref[...].astype(F32), 0.0).astype(BF)
    def group(g, start):
        @pl.when(start < slots)
        def _():
            end = group_end(clips, start, slots)
            r0 = start*SLOT; r1 = end*SLOT
            w0 = pl.multiple_of(jnp.minimum((r0>>4)<<4, rows-WIN), 16)
            fill_bias(clips, w0, slots, bias)
            rowi = lax.broadcasted_iota(jnp.int32,(WIN,128),0)+w0
            mine = (rowi >= r0) & (rowi < r1)
            lane = lax.broadcasted_iota(jnp.int32,(1,128),1)
            win = pl.ds(w0, WIN)
            for p in range(D//128):
                q = t_ref[win, pl.ds(p*128,128)]
                k = t_ref[win, pl.ds(D+p*128,128)]
                v = t_ref[win, pl.ds(2*D+p*128,128)]
                outs=[]
                for h in range(2):
                    keep = (lane//64 == h).astype(BF)
                    s = dg(q*keep, k, 1, 1) + bias[...]
                    top = jnp.max(s, axis=1, keepdims=True)
                    e = jnp.exp(s-top)
                    inv = 1.0/jnp.sum(e, axis=1, keepdims=True)
                    pl_ = (e*inv).astype(BF)
                    outs.append(jnp.dot(pl_, v, preferred_element_type=F32))
                o = jnp.where(lane < 64, outs[0], outs[1])
                old = o_ref[win, pl.ds(p*128,128)]
                o_ref[win, pl.ds(p*128,128)] = jnp.where(mine, o, old.astype(F32)).astype(BF)
        return jnp.where(start < slots, group_end(clips, start, slots), start)
    lax.fori_loop(0, (2*slots)//(LIVE_MAX+1)+1, group, 0)

def bwd_kernel(clips, t_ref, do_ref, dt_ref, bias):
    slots = clips.shape[0]
    rows = t_ref.shape[0]; D = do_ref.shape[1]
    clear_tail(dt_ref, slots)
    def group(g, start):
        @pl.when(start < slots)
        def _():
            end = group_end(clips, start, slots)
            r0 = start*SLOT; r1 = end*SLOT
            w0 = pl.multiple_of(jnp.minimum((r0>>4)<<4, rows-WIN), 16)
            fill_bias(clips, w0, slots, bias)
            rowi = lax.broadcasted_iota(jnp.int32,(WIN,128),0)+w0
            mine = (rowi >= r0) & (rowi < r1)
            lane = lax.broadcasted_iota(jnp.int32,(1,128),1)
            win = pl.ds(w0, WIN)
            for p in range(D//128):
                q = t_ref[win, pl.ds(p*128,128)]
                k = t_ref[win, pl.ds(D+p*128,128)]
                v = t_ref[win, pl.ds(2*D+p*128,128)]
                do = do_ref[win, pl.ds(p*128,128)]
                dqs=[];dks=[];dvs=[]
                for h in range(2):
                    keep = (lane//64 == h).astype(BF)
                    s = dg(k, q*keep, 1, 1) + bias[...]
                    top = jnp.max(s, axis=0, keepdims=True)
                    e = jnp.exp(s-top)
                    inv = 1.0/jnp.sum(e, axis=0, keepdims=True)
                    pt = e*inv
                    dp = dg(v, do*keep, 1, 1)
                    dvs.append(jnp.dot(pt.astype(BF), do, preferred_element_type=F32))
                    inner = jnp.sum(dp*pt, axis=0, keepdims=True)
                    ds = (pt*(dp-inner)).astype(BF)
                    dks.append(jnp.dot(ds, q, preferred_element_type=F32))
                    dqs.append(dg(ds, k, 0, 0))
                for i,x in enumerate((dqs,dks,dvs)):
                    new = jnp.where(lane < 64, x[0], x[1]).astype(BF).astype(F32)
                    if i==0: new = new*(64**-0.5)
                    c = pl.ds(i*D+p*128,128)
                    old = dt_ref[win, c].astype(F32)
                    dt_ref[win, c] = jnp.where(mine, new, old).astype(BF)
        return jnp.where(start < slots, group_end(clips, start, slots), start)
    lax.fori_loop(0, (2*slots)//(LIVE_MAX+1)+1, group, 0)

def attend(clips, t, g):
    D=t.shape[1]//3
    return pl.pallas_call(fwd_kernel, out_shape=[jax.ShapeDtypeStruct((t.shape[0],D),BF)]*2,
      in_specs=[pl.BlockSpec(memory_space=pltpu.SMEM)]+[pl.BlockSpec(memory_space=pltpu.VMEM)]*2,
      out_specs=[pl.BlockSpec(memory_space=pltpu.VMEM)]*2,
      scratch_shapes=[pltpu.VMEM((WIN,WIN),F32)],
      compiler_params=pltpu.CompilerParams(vmem_limit_bytes=48*2**20),name="attention_forward")(clips,t,g)
def attend_back(clips, t, do):
    return pl.pallas_call(bwd_kernel, out_shape=jax.ShapeDtypeStruct(t.shape,BF),
      in_specs=[pl.BlockSpec(memory_space=pltpu.SMEM)]+[pl.BlockSpec(memory_space=pltpu.VMEM)]*2,
      out_specs=pl.BlockSpec(memory_space=pltpu.VMEM),
      scratch_shapes=[pltpu.VMEM((WIN,WIN),F32)],
      compiler_params=pltpu.CompilerParams(vmem_limit_bytes=48*2**20),name="attention_backward")(clips,t,do)


RT = 400


def dot_nt(left, right):
    return lax.dot_general(left, right, (((1,), (1,)), ((), ())), preferred_element_type=F32)


def dot_tn(left, right):
    return lax.dot_general(left, right, (((0,), (0,)), ((), ())), preferred_element_type=F32)


def dot_nn(left, right):
    return jnp.dot(left, right, preferred_element_type=F32)


def norm_parts(values):
    centred = values - jnp.mean(values, axis=-1, keepdims=True)
    scale = lax.rsqrt(jnp.mean(centred * centred, axis=-1, keepdims=True) + EPSILON)
    return centred * scale, scale


def norm_back(grad, gain, unit, scale):
    inner = grad * gain
    return scale * (
        inner
        - jnp.mean(inner, axis=-1, keepdims=True)
        - unit * jnp.mean(inner * unit, axis=-1, keepdims=True)
    )


def gelu_pair(u):
    bell = jnp.exp(-0.5 * u * u)
    t = 1.0 / (1.0 + (0.3275911 * 0.5**0.5) * jnp.abs(u))
    poly = t * (
        0.5 * 0.254829592
        + t * (-0.5 * 0.284496736 + t * (0.5 * 1.421413741 + t * (-0.5 * 1.453152027 + t * (0.5 * 1.061405429))))
    )
    tail = poly * bell
    phi = jnp.where(u < 0, tail, 1.0 - tail)
    return u * phi, phi + u * (bell * (2.0 * math.pi) ** -0.5)


def column_sum(values):
    return jnp.sum(values, axis=0, keepdims=True)


def tiles(rows, body):
    @pl.loop(0, rows // RT)
    def _(i):
        body(pl.ds(pl.multiple_of(i * RT, 16), RT))


def qkv_norm(x_ref, vec, a1_ref):
    def one(win):
        unit, _ = norm_parts(x_ref[win, :].astype(F32))
        a1_ref[win, :] = (unit * vec[0:1, :] + vec[1:2, :]).astype(BF)

    tiles(x_ref.shape[0], one)


def qkv_block(a1_ref, w_ref, t_ref, part):
    width = a1_ref.shape[1]
    weight = w_ref[part].reshape(width, width)

    def one(win):
        out = dot_nn(a1_ref[win, :], weight)
        if part == 0:
            out = out * HEAD_DIM**-0.5
        t_ref[win, pl.ds(part * width, width)] = out.astype(BF)

    tiles(a1_ref.shape[0], one)


def qkv_kernel(x_ref, vec, w_ref, t_ref, a1_ref):
    qkv_norm(x_ref, vec, a1_ref)
    for part in range(3):
        qkv_block(a1_ref, w_ref, t_ref, part)


def middle_step(x_ref, o_ref, vec, wo_ref, m_ref, a2_ref):
    def one(win):
        middle = x_ref[win, :].astype(F32) + (dot_nn(o_ref[win, :], wo_ref[...]) + vec[2:3, :])
        m_ref[win, :] = middle
        unit, _ = norm_parts(middle)
        a2_ref[win, :] = (unit * vec[3:4, :] + vec[4:5, :]).astype(BF)

    tiles(x_ref.shape[0], one)


def chunk_step(first, bias, a2_ref, dy_ref, we_ref, wc_ref, h_ref, du_ref, y_ref, da2_ref, be_ref):
    be_ref[...] = jnp.zeros_like(be_ref)

    def one(win):
        hidden, slope = gelu_pair(dot_nn(a2_ref[win, :], we_ref[...]) + bias)
        hidden = hidden.astype(BF)
        h_ref[win, :] = hidden
        du = (dot_nt(dy_ref[win, :], wc_ref[...]) * slope).astype(BF)
        du_ref[win, :] = du
        be_ref[...] += column_sum(du.astype(F32))
        y = dot_nn(hidden, wc_ref[...])
        da2 = dot_nt(du, we_ref[...])
        if first is True:
            y_ref[win, :] = y
            da2_ref[win, :] = da2
        else:
            y_ref[win, :] += y
            da2_ref[win, :] += da2

    tiles(a2_ref.shape[0], one)


def middle_back(live_rows, m_ref, y_ref, dy_ref, da2_ref, vec, wo_ref, out_ref, dm_ref, dz_ref, do_ref, sums):
    sums[...] = jnp.zeros_like(sums)

    def one(win):
        middle = m_ref[win, :]
        out_ref[win, :] = (middle + (y_ref[win, :] + vec[5:6, :])).astype(BF)
        unit, scale = norm_parts(middle)
        da2 = da2_ref[win, :]
        dy = dy_ref[win, :].astype(F32)
        dm = dy + norm_back(da2, vec[3:4, :], unit, scale)
        dm_ref[win, :] = dm
        dz = dm.astype(BF)
        dz_ref[win, :] = dz
        do_ref[win, :] = dot_nt(dz, wo_ref[...]).astype(BF)
        sums[0:1, :] += column_sum(da2 * unit)
        sums[1:2, :] += column_sum(da2)
        sums[2:3, :] += column_sum(dz.astype(F32))
        sums[3:4, :] += column_sum(dy)

    tiles(m_ref.shape[0], one)


def feed_kernel(
    x_ref, o_ref, dy_ref, vec, wo_ref, we_ref, wc_ref,
    out_ref, dm_ref, do_ref, gwo_ref, gwe_ref, gwc_ref, sums, be_ref,
    m_ref, a2_ref, h_ref, du_ref, y_ref, da2_ref, dz_ref,
):
    middle_step(x_ref, o_ref, vec, wo_ref, m_ref, a2_ref)
    for j in range(4):
        chunk_step(
            j == 0, vec[6 + j : 7 + j, :], a2_ref, dy_ref, we_ref.at[j], wc_ref.at[j],
            h_ref, du_ref, y_ref, da2_ref, be_ref.at[pl.ds(8 * j, 1)],
        )
        gwc_ref[j] = dot_tn(h_ref[...], dy_ref[...]).astype(BF)
        gwe_ref[j] = dot_tn(a2_ref[...], du_ref[...]).astype(BF)
    middle_back(None, m_ref, y_ref, dy_ref, da2_ref, vec, wo_ref, out_ref, dm_ref, dz_ref, do_ref, sums)
    gwo_ref[...] = dot_tn(o_ref[...], dz_ref[...]).astype(BF)


def first_back(x_ref, dt_ref, dm_ref, vec, w_refs, pg_ref, sums):
    sums[...] = jnp.zeros_like(sums)
    width = x_ref.shape[1]

    def one(win):
        da1 = dot_nt(dt_ref[win, pl.ds(0, width)], w_refs[0][...])
        da1 += dot_nt(dt_ref[win, pl.ds(width, width)], w_refs[1][...])
        da1 += dot_nt(dt_ref[win, pl.ds(2 * width, width)], w_refs[2][...])
        unit, scale = norm_parts(x_ref[win, :].astype(F32))
        pg_ref[win, :] = dm_ref[win, :] + norm_back(da1, vec[0:1, :], unit, scale)
        sums[0:1, :] += column_sum(da1 * unit)
        sums[1:2, :] += column_sum(da1)

    tiles(x_ref.shape[0], one)


def first_kernel(x_ref, a1_ref, dt_ref, dm_ref, vec, w_ref, pg_ref, gwi_ref, sums):
    width = x_ref.shape[1]
    for part in range(3):
        gwi_ref[part] = dot_tn(a1_ref[...], dt_ref[:, pl.ds(part * width, width)]).astype(BF)
    first_back(x_ref, dt_ref, dm_ref, vec, [w_ref.at[p] for p in range(3)], pg_ref, sums)


VM = pl.BlockSpec(memory_space=pltpu.VMEM)
SM = pl.BlockSpec(memory_space=pltpu.SMEM)


def vmem_call(kernel, name, ins, outs, scratch=(), smem=0):
    return pl.pallas_call(
        kernel,
        out_shape=[jax.ShapeDtypeStruct(s, d) for s, d in outs],
        in_specs=[SM] * smem + [VM] * (len(ins) - smem),
        out_specs=[VM] * len(outs),
        scratch_shapes=[pltpu.VMEM(s, d) for s, d in scratch],
        compiler_params=pltpu.CompilerParams(vmem_limit_bytes=60 * 2**20),
        name=name,
    )(*ins)


MESH = pl.DeviceIdType.MESH


class Place:
    def __init__(self, parts, sh, width):
        mine, copy = lax.axis_index("fsdp"), lax.axis_index("rep")
        self.outer_count = parts // 2
        self.outer, self.inner = mine // 2, mine % 2
        self.plane, self.core = copy // 2, copy % 2
        self.third = sh // 3
        self.half = width // 2

    def device(self, outer=None, inner=None, plane=None, core=None):
        outer = self.outer if outer is None else outer
        inner = self.inner if inner is None else inner
        plane = self.plane if plane is None else plane
        core = self.core if core is None else core
        return (outer * 2 + inner, plane * 2 + core)

    def far(self, k):
        return (self.outer + k) % self.outer_count

    def ranks(self):
        return range(1, self.outer_count)

    def columns(self, core=None):
        core = self.core if core is None else core
        return pl.ds(pl.multiple_of(core * self.half, 128), self.half)

    def held(self):
        return pl.ds(pl.multiple_of(self.plane * self.third, 16), 2 * self.third)

    def own(self, plane=None):
        plane = self.plane if plane is None else plane
        return pl.ds(pl.multiple_of(plane * (2 * self.third), 16), self.third)

    def peers(self):
        return [self.device(outer=self.far(k)) for k in self.ranks()] + [
            self.device(inner=1 - self.inner),
            self.device(plane=1 - self.plane),
            self.device(core=1 - self.core),
        ]

    def greet(self):
        barrier = pltpu.get_barrier_semaphore()
        peers = self.peers()
        for peer in peers:
            pl.semaphore_signal(barrier, inc=1, device_id=peer, device_id_type=MESH)
        pl.semaphore_wait(barrier, len(peers))


def remote(src, dst, sems, index, device):
    return pltpu.make_async_remote_copy(
        src_ref=src, dst_ref=dst, send_sem=sems[0].at[index], recv_sem=sems[1].at[index],
        device_id=device, device_id_type=MESH,
    )


def start(copies):
    for copy in copies:
        copy.start()


def landed(copies):
    for copy in copies:
        copy.wait_recv()


def sent(copies):
    for copy in copies:
        copy.wait_send()


class Gather:
    def __init__(self, place, shard, full, sems):
        self.p, self.shard, self.full, self.sems = place, shard, full, sems

    def far(self, b):
        p = self.p
        return [
            remote(
                self.shard.at[b, p.held(), p.columns()],
                self.full.at[b, p.outer, p.inner, p.held(), p.columns()],
                self.sems, (b, k - 1), p.device(outer=p.far(k)),
            )
            for k in p.ranks()
        ]

    def pair(self, b, which):
        p = self.p
        if which == 0:
            ref = self.full.at[b, :, p.inner, p.held(), p.columns()]
            device = p.device(inner=1 - p.inner)
        elif which == 1:
            ref = self.full.at[b, :, :, p.own(), p.columns()]
            device = p.device(plane=1 - p.plane)
        else:
            ref = self.full.at[b, :, :, :, p.columns()]
            device = p.device(core=1 - p.core)
        return [remote(ref, ref, self.sems, (b, p.outer_count - 1 + which), device)]

    def put_own(self, b):
        p = self.p
        self.full[b, p.outer, p.inner, p.held(), p.columns()] = self.shard[b, p.held(), p.columns()]

    def step(self, s, count, lag):
        for stage in range(5):
            @pl.when((s >= stage * lag) & (s < count + stage * lag))
            def _():
                b = s - stage * lag
                if stage == 0:
                    start(self.far(b))
                    self.put_own(b)
                else:
                    landed(self.far(b) if stage == 1 else self.pair(b, stage - 2))
                    if stage < 4:
                        start(self.pair(b, stage - 1))

    def finish(self, count):
        @pl.loop(0, count)
        def _(b):
            sent(self.far(b))
            for which in range(3):
                sent(self.pair(b, which))


def gather_sems(blocks, parts):
    shape = (blocks, parts // 2 - 1 + 3)
    return [pltpu.SemaphoreType.DMA(shape), pltpu.SemaphoreType.DMA(shape)]


class Reduce:
    def __init__(self, place, grad, out, bufs, sems):
        self.p, self.grad, self.out, self.sems = place, grad, out, sems
        self.from_core, self.from_plane, self.from_inner, self.from_far, self.part, self.from_part = bufs

    @staticmethod
    def scratch(blocks, parts, sh, width):
        outer, third, half = parts // 2, sh // 3, width // 2
        shape = (blocks, outer - 1 + 5)
        return [
            pltpu.VMEM((blocks, outer, 2, sh, half), BF),
            pltpu.VMEM((blocks, outer, 2, third, half), BF),
            pltpu.VMEM((blocks, outer, 2 * third, half), BF),
            pltpu.VMEM((blocks, outer - 1, 2 * third, half), BF),
            pltpu.VMEM((blocks, 2 * third, half), BF),
            pltpu.VMEM((blocks, 2 * third, half), BF),
            pltpu.SemaphoreType.DMA(shape),
            pltpu.SemaphoreType.DMA(shape),
        ]

    def copies(self, b, stage):
        p = self.p
        base = p.outer_count - 1
        if stage == 0:
            src, dst = self.grad.at[b, :, :, :, p.columns(1 - p.core)], self.from_core.at[b]
            device = p.device(core=1 - p.core)
        elif stage == 1:
            src, dst = self.grad.at[b, :, :, p.own(1 - p.plane), p.columns()], self.from_plane.at[b]
            device = p.device(plane=1 - p.plane)
        elif stage == 2:
            src, dst = self.grad.at[b, :, 1 - p.inner, p.held(), p.columns()], self.from_inner.at[b]
            device = p.device(inner=1 - p.inner)
        elif stage == 3:
            return [
                remote(
                    self.grad.at[b, p.far(k), p.inner, p.held(), p.columns()],
                    self.from_far.at[b, k - 1], self.sems, (b, k - 1), p.device(outer=p.far(k)),
                )
                for k in p.ranks()
            ]
        elif stage == 4:
            src, dst = self.part.at[b], self.from_part.at[b]
            device = p.device(plane=1 - p.plane)
        else:
            src = dst = self.out.at[b, :, p.columns()]
            device = p.device(core=1 - p.core)
        return [remote(src, dst, self.sems, (b, base + (stage if stage < 3 else stage - 1)), device)]

    def add(self, b, stage):
        p = self.p
        if stage == 0:
            @pl.loop(0, p.outer_count)
            def _(o):
                for i in range(2):
                    index = (b, o, i, slice(None), p.columns())
                    self.grad[index] = (self.grad[index].astype(F32) + self.from_core[b, o, i].astype(F32)).astype(BF)
        elif stage == 1:
            for i in range(2):
                @pl.loop(0, p.outer_count)
                def _(o):
                    index = (b, o, i, p.own(), p.columns())
                    self.grad[index] = (self.grad[index].astype(F32) + self.from_plane[b, o, i].astype(F32)).astype(BF)
        elif stage == 2:
            @pl.loop(0, p.outer_count)
            def _(o):
                index = (b, o, p.inner, p.held(), p.columns())
                self.grad[index] = (self.grad[index].astype(F32) + self.from_inner[b, o].astype(F32)).astype(BF)
        elif stage == 3:
            total = self.grad[b, p.outer, p.inner, p.held(), p.columns()].astype(F32)
            for k in p.ranks():
                total += self.from_far[b, k - 1].astype(F32)
            self.part[b] = total.astype(BF)
        elif stage == 4:
            third = p.third
            for plane in range(2):
                @pl.when(p.plane == plane)
                def _():
                    mine, other = self.part, self.from_part
                    first, last = (mine, other) if plane == 0 else (other, mine)
                    self.out[b, pl.ds(0, third), p.columns()] = first[b, pl.ds(0, third), :]
                    middle = first[b, pl.ds(third, third), :].astype(F32) + last[b, pl.ds(0, third), :].astype(F32)
                    self.out[b, pl.ds(third, third), p.columns()] = middle.astype(BF)
                    self.out[b, pl.ds(2 * third, third), p.columns()] = last[b, pl.ds(third, third), :]

    def stage(self, b, stage):
        if stage > 0:
            landed(self.copies(b, stage - 1))
            self.add(b, stage - 1)
        if stage < 6:
            start(self.copies(b, stage))

    def step(self, s, count, lag):
        for stage in range(7):
            @pl.when((s >= stage * lag) & (s < count + stage * lag))
            def _():
                self.stage(s - stage * lag, stage)

    def finish(self, count):
        @pl.loop(0, count)
        def _(b):
            for stage in range(6):
                sent(self.copies(b, stage))


class Vector:
    def __init__(self, place, total, bufs, sems, everywhere):
        self.p, self.total, self.sems = place, total, sems
        self.pairs, self.fars = bufs
        self.order = (0, 1, 2) if everywhere else (2,)

    @staticmethod
    def scratch(parts, shape, dtype):
        sems = (parts // 2 - 1 + 3,)
        return [
            pltpu.VMEM((6,) + shape, dtype), pltpu.VMEM((parts // 2,) + shape, dtype),
            pltpu.SemaphoreType.DMA(sems), pltpu.SemaphoreType.DMA(sems),
        ]

    def pair(self, which):
        p = self.p
        device = (
            p.device(core=1 - p.core), p.device(plane=1 - p.plane), p.device(inner=1 - p.inner)
        )[which]
        return [remote(self.pairs.at[2 * which], self.pairs.at[2 * which + 1], self.sems, p.outer_count - 1 + which, device)]

    def far(self):
        p = self.p
        mine = self.fars.at[p.outer]
        return [remote(mine, mine, self.sems, k - 1, p.device(outer=p.far(k))) for k in p.ranks()]

    def far_landed(self):
        p = self.p
        for k in p.ranks():
            theirs = self.fars.at[(p.outer + p.outer_count - k) % p.outer_count]
            remote(theirs, theirs, self.sems, k - 1, p.device(outer=p.far(k))).wait_recv()

    def stage(self, number):
        order = self.order
        if number > 0 and number <= len(order):
            which = order[number - 1]
            landed(self.pair(which))
            self.total[...] = self.total[...] + self.pairs[2 * which + 1]
        if number < len(order):
            which = order[number]
            self.pairs[2 * which] = self.total[...]
            start(self.pair(which))
        elif number == len(order):
            self.fars[self.p.outer] = self.total[...]
            start(self.far())
        else:
            self.far_landed()
            total = self.fars[0]
            for o in range(1, self.p.outer_count):
                total = total + self.fars[o]
            self.total[...] = total

    def stages(self):
        return len(self.order) + 2

    def finish(self):
        for which in self.order:
            sent(self.pair(which))
        sent(self.far())


FIRST_BLOCKS = 6
TILES = 3


def flat(ref, b):
    block = ref[b]
    return block.reshape(block.shape[0] * block.shape[1] * block.shape[2], block.shape[3])


def gather_kernel(parts, x_ref, vec_in, shard, t_ref, a1_ref, xp_ref, full, vec, *scratch):
    count, width = x_ref.shape
    rows = xp_ref.shape[0]
    place = Place(parts, shard.shape[1], width)
    weights = Gather(place, shard, full, scratch[0:2])
    vectors = Vector(place, vec, scratch[2:4], scratch[4:6], False)
    place.greet()
    weights.step(0, FIRST_BLOCKS, 1)
    vec[...] = vec_in[...]
    vectors.stage(0)
    tail = count // 16 * 16
    xp_ref[pl.ds(tail, rows - tail), :] = jnp.zeros((rows - tail, width), BF)
    xp_ref[pl.ds(0, count), :] = x_ref[...]
    vectors.stage(1)
    weights.step(1, FIRST_BLOCKS, 1)
    vectors.stage(2)
    weights.step(2, FIRST_BLOCKS, 1)
    qkv_norm(xp_ref, vec, a1_ref)
    weights.step(3, FIRST_BLOCKS, 1)
    for s in range(4, FIRST_BLOCKS + 4):
        weights.step(s, FIRST_BLOCKS, 1)
        if s - 4 < 3:
            qkv_block(a1_ref, full, t_ref, s - 4)
    weights.finish(FIRST_BLOCKS)
    vectors.finish()


def feed_comm_kernel(
    parts, x_ref, o_ref, dy_ref, vec, wo_ref, we0_ref, wc0_ref, shard,
    out_ref, dm_ref, do_ref, dz_ref, grad_out, sums, be_ref,
    a2_ref, y_ref, da2_ref, full, grad, local, *scratch,
):
    rows, width = x_ref.shape
    sh = shard.shape[1]
    place = Place(parts, sh, width)
    later = shard.shape[0]
    weights = Gather(place, shard, full.at[pl.ds(2, later)], scratch[0:2])
    grads = Reduce(place, grad, grad_out, scratch[2:8], scratch[8:10])
    place.greet()
    du_ref, h_ref = do_ref, dz_ref
    ready = [
        pltpu.make_async_copy(ref.at[0], full.at[b], local.at[b]) for b, ref in enumerate((we0_ref, wc0_ref))
    ]
    start(ready)

    def win(i):
        return pl.ds(i * RT, RT)

    wo = flat(wo_ref, 0)
    weights.step(0, later, 1)
    for i in range(TILES):
        middle = x_ref[win(i), :].astype(F32) + (dot_nn(o_ref[win(i), :], wo) + vec[2:3, :])
        dm_ref[win(i), :] = middle
        unit, _ = norm_parts(middle)
        a2_ref[win(i), :] = (unit * vec[3:4, :] + vec[4:5, :]).astype(BF)
        y_ref[win(i), :] = jnp.zeros((RT, width), F32)
        da2_ref[win(i), :] = jnp.zeros((RT, width), F32)
        weights.step(i + 1, later, 1)
    for copy in ready:
        copy.wait()

    def passing(j, i):
        for parity in range(2):
            for back in range(3):
                stage = i - 3 - parity + 5 * back
                if 0 <= stage <= 6:
                    if back == 0:
                        grads.stage(2 * j + parity, stage)
                    else:
                        @pl.when(j >= back)
                        def _():
                            grads.stage(2 * (j - back) + parity, stage)

    @pl.loop(0, 4)
    def _(j):
        bias = vec[pl.ds(6 + j, 1), :]
        be_sum = jnp.zeros((1, width), F32)
        for i in range(TILES):
            hidden, slope = gelu_pair(dot_nn(a2_ref[win(i), :], flat(full, 2 * j)) + bias)
            hidden = hidden.astype(BF)
            h_ref[win(i), :] = hidden
            du = (dot_nt(dy_ref[win(i), :], flat(full, 2 * j + 1)) * slope).astype(BF)
            du_ref[win(i), :] = du
            be_sum += column_sum(du.astype(F32))
            y_ref[win(i), :] += dot_nn(hidden, flat(full, 2 * j + 1))
            da2_ref[win(i), :] += dot_nt(du, flat(full, 2 * j))
            weights.step(4 + 5 * j + i, later, 1)
            passing(j, i)
        be_ref[pl.ds(j, 1), :] = be_sum
        grad[2 * j] = dot_tn(h_ref[...], dy_ref[...]).astype(BF).reshape(grad.shape[1:])
        weights.step(4 + 5 * j + 3, later, 1)
        passing(j, 3)
        grad[2 * j + 1] = dot_tn(a2_ref[...], du_ref[...]).astype(BF).reshape(grad.shape[1:])
        weights.step(4 + 5 * j + 4, later, 1)
        passing(j, 4)

    sums[...] = jnp.zeros_like(sums)
    for slot in range(5, 12):
        i = slot - 5
        if i < TILES:
            middle = dm_ref[win(i), :]
            out_ref[win(i), :] = (middle + (y_ref[win(i), :] + vec[5:6, :])).astype(BF)
            unit, scale = norm_parts(middle)
            da2 = da2_ref[win(i), :]
            dy = dy_ref[win(i), :].astype(F32)
            dm = dy + norm_back(da2, vec[3:4, :], unit, scale)
            dm_ref[win(i), :] = dm
            dz = dm.astype(BF)
            dz_ref[win(i), :] = dz
            do_ref[win(i), :] = dot_nt(dz, wo).astype(BF)
            sums[0:1, :] += column_sum(da2 * unit)
            sums[1:2, :] += column_sum(da2)
            sums[2:3, :] += column_sum(dz.astype(F32))
            sums[3:4, :] += column_sum(dy)
        for j in range(2, 4):
            for parity in range(2):
                stage = slot - 3 - parity + 5 * (3 - j)
                if 0 <= stage <= 6:
                    grads.stage(2 * j + parity, stage)
    weights.finish(later)
    grads.finish(8)


def first_comm_kernel(
    parts, x_ref, a1_ref, o_ref, dz_ref, dt_ref, dm_ref, vec, wi_ref, sums_two, be_ref,
    pg_ref, grad_out, total, grad, *scratch,
):
    rows, width = x_ref.shape
    place = Place(parts, width // parts, width)
    grads = Reduce(place, grad, grad_out, scratch[0:6], scratch[6:8])
    vectors = Vector(place, total, scratch[8:10], scratch[10:12], True)
    place.greet()
    total[...] = jnp.zeros_like(total)
    total[2:3, :] = sums_two[2:3, :]
    total[3:5, :] = sums_two[0:2, :]
    total[5:6, :] = sums_two[3:4, :]
    total[6:10, :] = be_ref[0:4, :]
    grad[0] = dot_tn(o_ref[...], dz_ref[...]).astype(BF).reshape(grad.shape[1:])
    grads.step(0, 4, 1)
    for part in range(3):
        block = dot_tn(a1_ref[...], dt_ref[:, pl.ds(part * width, width)]).astype(BF)
        grad[part + 1] = block.reshape(grad.shape[1:])
        grads.step(part + 1, 4, 1)
    for i in range(TILES):
        win = pl.ds(i * RT, RT)
        da1 = dot_nt(dt_ref[win, pl.ds(0, width)], flat(wi_ref, 0))
        da1 += dot_nt(dt_ref[win, pl.ds(width, width)], flat(wi_ref, 1))
        da1 += dot_nt(dt_ref[win, pl.ds(2 * width, width)], flat(wi_ref, 2))
        unit, scale = norm_parts(x_ref[win, :].astype(F32))
        pg_ref[win, :] = dm_ref[win, :] + norm_back(da1, vec[0:1, :], unit, scale)
        total[0:1, :] += column_sum(da1 * unit)
        total[1:2, :] += column_sum(da1)
        grads.step(4 + i, 4, 1)
    for s in range(7, 10):
        vectors.stage(s - 7)
        grads.step(s, 4, 1)
    for number in range(3, vectors.stages()):
        vectors.stage(number)
    grads.finish(4)
    vectors.finish()


def comm_call(kernel, name, which, ins, outs, scratch, far=()):
    return pl.pallas_call(
        kernel,
        out_shape=[jax.ShapeDtypeStruct(s, d) for s, d in outs],
        in_specs=[pl.BlockSpec(memory_space=pl.ANY) if i in far else VM for i in range(len(ins))],
        out_specs=[VM] * len(outs),
        scratch_shapes=scratch,
        compiler_params=pltpu.CompilerParams(
            vmem_limit_bytes=62 * 2**20, collective_id=which, has_side_effects=True
        ),
        name=name,
    )(*ins)


def run_qkv(x, vec, wi):
    rows, width = x.shape
    return vmem_call(
        qkv_kernel, "project_in", (x, vec, wi), [((rows, 3 * width), BF), ((rows, width), BF)]
    )


def run_feed(x, o, dy, vec, wo, we, wc):
    rows, width = x.shape
    wide, low = ((rows, width), F32), ((rows, width), BF)
    return vmem_call(
        feed_kernel, "feed_forward", (x, o, dy, vec, wo, we, wc),
        [low, wide, low, ((width, width), BF), ((4, width, width), BF), ((4, width, width), BF),
         ((8, width), F32), ((32, width), F32)],
        [wide, low, low, low, wide, wide, low],
    )


def run_first(x, a1, dt, dm, vec, wi):
    rows, width = x.shape
    return vmem_call(
        first_kernel, "project_in_back", (x, a1, dt, dm, vec, wi),
        [((rows, width), F32), ((3, width, width), BF), ((8, width), F32)],
    )


def pack_shards(wi, wo, we, wc, parts):
    rows, width = wo.shape
    wi = wi.reshape(rows, 3, width).swapaxes(0, 1)
    we = we.reshape(rows, parts, 4, rows).transpose(2, 0, 1, 3).reshape(4, rows, width)
    wc = wc.reshape(4, rows, width)
    return jnp.concatenate([wi, wo[None], we, wc], axis=0)


def unpack_shards(blocks, parts):
    rows, width = blocks.shape[1:]
    wi = blocks[0:3].swapaxes(0, 1).reshape(rows, 3 * width)
    we = blocks[4:8].reshape(4, rows, parts, rows).transpose(1, 2, 0, 3).reshape(rows, 4 * width)
    return wi, blocks[3], we, blocks[8:12].reshape(4 * rows, width)


def plain_path(patches, slot_clip, out_grad, masters, vector_weight):
    parts, copies = lax.axis_size("fsdp"), lax.axis_size("rep")
    mine, copy = lax.axis_index("fsdp"), lax.axis_index("rep")
    count, width = patches.shape
    rows = (count + RT - 1) // RT * RT
    sh = width // parts
    packed = pack_shards(*(m.astype(BF) for m in masters), parts).reshape(12 * sh, width)
    piece = 12 * sh // copies
    quarter = lax.dynamic_slice_in_dim(packed, copy * piece, piece, 0)
    full = lax.all_gather(quarter, ("fsdp", "rep"), axis=0, tiled=True)
    full = full.reshape(parts, 12, sh, width).swapaxes(0, 1).reshape(12, width, width)
    vec = lax.all_gather(vector_weight.astype(BF), "fsdp", axis=1, tiled=True).astype(F32)
    be = vec[6:].reshape(parts, 4, sh).swapaxes(0, 1).reshape(4, width)
    vec = jnp.concatenate([vec[:6], be, jnp.zeros((6, width), F32)], axis=0)

    pad = ((0, rows - count), (0, 0))
    x = jnp.pad(patches, pad)
    t, a1 = run_qkv(x, vec, full[0:3])
    o, dy = attend(slot_clip, t, out_grad)
    out, dm, do, gwo, gwe, gwc, sums_two, sums_be = run_feed(x, o, dy, vec, full[3], full[4:8], full[8:12])
    dt = attend_back(slot_clip, t, do)
    pg, gwi, sums_one = run_first(x, a1, dt, dm, vec, full[0:3])

    grads = jnp.concatenate([gwi, gwo[None], gwe, gwc], axis=0)
    grads = grads.reshape(12, parts, sh, width).swapaxes(0, 1).reshape(parts * 12 * sh, width)
    grads = lax.psum_scatter(grads, ("fsdp", "rep"), scatter_dimension=0, tiled=True)
    grads = lax.all_gather(grads, "rep", axis=0, tiled=True).reshape(12, sh, width)
    be_grad = sums_be[::8].reshape(4, parts, sh).swapaxes(0, 1).reshape(4, width)
    vector = jnp.concatenate(
        [sums_one[0:2], sums_two[2:3], sums_two[0:2], sums_two[3:4], be_grad], axis=0
    )
    vector = lax.dynamic_slice_in_dim(lax.psum(vector, ("fsdp", "rep")), mine * sh, sh, 1)
    return out[:count], pg[:count], tuple(g.astype(F32) for g in unpack_shards(grads, parts)) + (vector,)


def direct_path(patches, slot_clip, out_grad, masters, vector_weight):
    parts = lax.axis_size("fsdp")
    mine = lax.axis_index("fsdp")
    count, width = patches.shape
    rows = (count + RT - 1) // RT * RT
    sh = width // parts
    block = (parts // 2, 2, sh, width)
    wide, low = ((rows, width), F32), ((rows, width), BF)

    packed = pack_shards(*(m.astype(BF) for m in masters), parts)
    first = jnp.concatenate([packed[0:5], packed[8:9]], axis=0)
    later = packed[5:8], packed[9:12]
    later = jnp.stack(later, axis=1).reshape(6, sh, width)
    vector_low = vector_weight.astype(BF).astype(F32)
    place = jnp.arange(parts)[None, :, None]
    row = jnp.arange(4)[:, None, None]
    apart = parts // 4
    top = jnp.where(place == mine, vector_low[:6, None, :], 0.0)
    be = jnp.repeat(vector_low[6:], apart, axis=0)[None]
    be = jnp.where((row == mine % 4) & (place % apart == mine // 4), be, 0.0)
    placed = jnp.concatenate([top, be, jnp.zeros((6, parts, sh), F32)], axis=0).reshape(16, width)

    t, a1, x, full, vec = comm_call(
        functools.partial(gather_kernel, parts), "gather_project_in", 0, (patches, placed, first),
        [((rows, 3 * width), BF), low, low, ((FIRST_BLOCKS,) + block, BF), ((16, width), F32)],
        gather_sems(FIRST_BLOCKS, parts) + Vector.scratch(parts, (16, width), F32),
    )
    o, dy = attend(slot_clip, t, out_grad)
    out, dm, do, dz, grads_two, sums_two, sums_be = comm_call(
        functools.partial(feed_comm_kernel, parts), "feed_forward_reduce", 1,
        (x, o, dy, vec, full[3:4], full[4:5], full[5:6], later),
        [low, wide, low, low, ((8, sh, width), BF), ((8, width), F32), ((8, width), F32)],
        [pltpu.VMEM(*low), pltpu.VMEM(*wide), pltpu.VMEM(*wide),
         pltpu.VMEM((8,) + block, BF), pltpu.VMEM((8,) + block, BF), pltpu.SemaphoreType.DMA((2,))]
        + gather_sems(6, parts) + Reduce.scratch(8, parts, sh, width), far=(5, 6),
    )
    dt = attend_back(slot_clip, t, do)
    pg, grads_one, vector = comm_call(
        functools.partial(first_comm_kernel, parts), "project_in_back_reduce", 2,
        (x, a1, o, dz, dt, dm, vec, full[0:3], sums_two, sums_be),
        [wide, ((4, sh, width), BF), ((16, width), F32)],
        [pltpu.VMEM((4,) + block, BF)] + Reduce.scratch(4, parts, sh, width)
        + Vector.scratch(parts, (16, width), F32),
    )
    blocks = jnp.concatenate([grads_one[1:4], grads_one[0:1], grads_two[1::2], grads_two[0::2]], axis=0)
    top = lax.dynamic_slice_in_dim(vector[:6], mine * sh, sh, 1)
    be = lax.dynamic_slice_in_dim(vector, 6 + mine % 4, 1, 0).reshape(4, apart, sh)
    be = lax.dynamic_index_in_dim(be, mine // 4, 1, keepdims=False)
    vector = jnp.concatenate([top, be], axis=0)
    grads = tuple(g.astype(F32) for g in unpack_shards(blocks, parts)) + (vector,)
    return out[:count], pg[:count], grads


def on_device(
    patches, slot_clip, out_grad,
    project_in_weight, project_in_moment, project_in_average,
    project_out_weight, project_out_moment, project_out_average,
    expand_weight, expand_moment, expand_average,
    contract_weight, contract_moment, contract_average,
    vector_weight, vector_moment, vector_average,
):
    masters = (project_in_weight, project_out_weight, expand_weight, contract_weight, vector_weight)
    moments = (project_in_moment, project_out_moment, expand_moment, contract_moment, vector_moment)
    averages = (project_in_average, project_out_average, expand_average, contract_average, vector_average)
    parts, copies = lax.axis_size("fsdp"), lax.axis_size("rep")
    count, width = patches.shape
    direct = copies == 4 and parts % 4 == 0 and width // parts % 48 == 0
    path = direct_path if direct else plain_path
    out, pg, total_grads = path(patches, slot_clip, out_grad, masters[:4], vector_weight)

    tokens_all = count * parts * copies
    outputs = [out, pg]
    for member in range(5):
        grad_sum = total_grads[member]
        rate = RATES[member] / tokens_all**0.5
        moment_new = MOMENTUM * moments[member] + grad_sum
        weight_new = masters[member] - rate * (grad_sum + MOMENTUM * moment_new)
        average_new = AVERAGE * averages[member] + (1.0 - AVERAGE) * weight_new
        outputs.extend([grad_sum, moment_new, weight_new, average_new, weight_new.astype(BF)])
    return tuple(outputs)


def solution(mesh):
    tokens = P(("fsdp", "rep"), None)
    split, split_vector = P("fsdp", None), P(None, "fsdp")
    in_specs = (tokens, P(("fsdp", "rep")), tokens) + (split,) * 12 + (split_vector,) * 3
    out_specs = (tokens,) * 2 + (split,) * 20 + (split_vector,) * 5
    return jax.shard_map(on_device, mesh=mesh, in_specs=in_specs, out_specs=out_specs, check_vma=False)
```

```python
import functools
import math

import jax
import jax.numpy as jnp
from jax import lax
from jax.sharding import PartitionSpec as P
import jax.experimental.pallas as pl
import jax.experimental.pallas.tpu as pltpu

BF, F32 = jnp.bfloat16, jnp.float32
HEAD_DIM = 64
SLOT = 49
LIVE_MAX = 8
WIN = 416
EPSILON = 1e-06
MOMENTUM = 0.5
AVERAGE = 0.5
RATES = (0.3, 0.3, 0.1, 0.03, 0.5)
NEG = -1e30

def dg(a,b,ca,cb):
    return lax.dot_general(a,b,(((ca,),(cb,)),((),())),preferred_element_type=F32)

def group_end(clips, start, slots):
    end = start+1
    for e in range(2, LIVE_MAX+1):
        cand = start+e
        safe = jnp.minimum(cand, slots-1)
        edge = (cand == slots) | ((cand < slots) & ((clips[safe] != clips[jnp.maximum(safe-1,0)]) | (clips[safe] < 0)))
        end = jnp.where(edge, cand, end)
    return end

def fill_bias(clips, w0, slots, bias):
    def keys(shape, dim):
        row = lax.broadcasted_iota(jnp.int32, shape, dim) + w0
        slot = (row*1338) >> 16
        def one(s, key):
            return jnp.where((slot == s) & (clips[s] >= 0), clips[s], key)
        return lax.fori_loop(0, slots, one, -1-row, unroll=True)
    bias[...] = jnp.where(keys((WIN,1),0) == keys((1,WIN),1), 0.0, NEG)

def clear_tail(ref, slots):
    tail = slots*SLOT//16*16
    ref[pl.ds(tail, ref.shape[0]-tail), :] = jnp.zeros((ref.shape[0]-tail, ref.shape[1]), BF)

def fwd_kernel(clips, t_ref, g_ref, o_ref, dy_ref, bias):
    slots = clips.shape[0]
    rows = t_ref.shape[0]; D = o_ref.shape[1]
    clear_tail(o_ref, slots)
    clear_tail(dy_ref, slots)
    slot = (lax.broadcasted_iota(jnp.int32,(slots*SLOT,1),0)*1338) >> 16
    live = lax.fori_loop(0, slots, lambda s, was: jnp.where((slot == s) & (clips[s] >= 0), 1.0, was), jnp.zeros((slots*SLOT,1),F32), unroll=True)
    dy_ref[pl.ds(0,slots*SLOT), :] = jnp.where(live > 0, g_ref[...].astype(F32), 0.0).astype(BF)
    def group(g, start):
        @pl.when(start < slots)
        def _():
            end = group_end(clips, start, slots)
            r0 = start*SLOT; r1 = end*SLOT
            w0 = pl.multiple_of(jnp.minimum((r0>>4)<<4, rows-WIN), 16)
            fill_bias(clips, w0, slots, bias)
            rowi = lax.broadcasted_iota(jnp.int32,(WIN,128),0)+w0
            mine = (rowi >= r0) & (rowi < r1)
            lane = lax.broadcasted_iota(jnp.int32,(1,128),1)
            win = pl.ds(w0, WIN)
            for p in range(D//128):
                q = t_ref[win, pl.ds(p*128,128)]
                k = t_ref[win, pl.ds(D+p*128,128)]
                v = t_ref[win, pl.ds(2*D+p*128,128)]
                outs=[]
                for h in range(2):
                    keep = (lane//64 == h).astype(BF)
                    s = dg(q*keep, k, 1, 1) + bias[...]
                    top = jnp.max(s, axis=1, keepdims=True)
                    e = jnp.exp(s-top)
                    inv = 1.0/jnp.sum(e, axis=1, keepdims=True)
                    pl_ = (e*inv).astype(BF)
                    outs.append(jnp.dot(pl_, v, preferred_element_type=F32))
                o = jnp.where(lane < 64, outs[0], outs[1])
                old = o_ref[win, pl.ds(p*128,128)]
                o_ref[win, pl.ds(p*128,128)] = jnp.where(mine, o, old.astype(F32)).astype(BF)
        return jnp.where(start < slots, group_end(clips, start, slots), start)
    lax.fori_loop(0, (2*slots)//(LIVE_MAX+1)+1, group, 0)

def bwd_kernel(clips, t_ref, do_ref, dt_ref, bias):
    slots = clips.shape[0]
    rows = t_ref.shape[0]; D = do_ref.shape[1]
    clear_tail(dt_ref, slots)
    def group(g, start):
        @pl.when(start < slots)
        def _():
            end = group_end(clips, start, slots)
            r0 = start*SLOT; r1 = end*SLOT
            w0 = pl.multiple_of(jnp.minimum((r0>>4)<<4, rows-WIN), 16)
            fill_bias(clips, w0, slots, bias)
            rowi = lax.broadcasted_iota(jnp.int32,(WIN,128),0)+w0
            mine = (rowi >= r0) & (rowi < r1)
            lane = lax.broadcasted_iota(jnp.int32,(1,128),1)
            win = pl.ds(w0, WIN)
            for p in range(D//128):
                q = t_ref[win, pl.ds(p*128,128)]
                k = t_ref[win, pl.ds(D+p*128,128)]
                v = t_ref[win, pl.ds(2*D+p*128,128)]
                do = do_ref[win, pl.ds(p*128,128)]
                dqs=[];dks=[];dvs=[]
                for h in range(2):
                    keep = (lane//64 == h).astype(BF)
                    s = dg(k, q*keep, 1, 1) + bias[...]
                    top = jnp.max(s, axis=0, keepdims=True)
                    e = jnp.exp(s-top)
                    inv = 1.0/jnp.sum(e, axis=0, keepdims=True)
                    pt = e*inv
                    dp = dg(v, do*keep, 1, 1)
                    dvs.append(jnp.dot(pt.astype(BF), do, preferred_element_type=F32))
                    inner = jnp.sum(dp*pt, axis=0, keepdims=True)
                    ds = (pt*(dp-inner)).astype(BF)
                    dks.append(jnp.dot(ds, q, preferred_element_type=F32))
                    dqs.append(dg(ds, k, 0, 0))
                for i,x in enumerate((dqs,dks,dvs)):
                    new = jnp.where(lane < 64, x[0], x[1]).astype(BF).astype(F32)
                    if i==0: new = new*(64**-0.5)
                    c = pl.ds(i*D+p*128,128)
                    old = dt_ref[win, c].astype(F32)
                    dt_ref[win, c] = jnp.where(mine, new, old).astype(BF)
        return jnp.where(start < slots, group_end(clips, start, slots), start)
    lax.fori_loop(0, (2*slots)//(LIVE_MAX+1)+1, group, 0)

def attend(clips, t, g):
    D=t.shape[1]//3
    return pl.pallas_call(fwd_kernel, out_shape=[jax.ShapeDtypeStruct((t.shape[0],D),BF)]*2,
      in_specs=[pl.BlockSpec(memory_space=pltpu.SMEM)]+[pl.BlockSpec(memory_space=pltpu.VMEM)]*2,
      out_specs=[pl.BlockSpec(memory_space=pltpu.VMEM)]*2,
      scratch_shapes=[pltpu.VMEM((WIN,WIN),F32)],
      compiler_params=pltpu.CompilerParams(vmem_limit_bytes=48*2**20),name="attention_forward")(clips,t,g)
def attend_back(clips, t, do):
    return pl.pallas_call(bwd_kernel, out_shape=jax.ShapeDtypeStruct(t.shape,BF),
      in_specs=[pl.BlockSpec(memory_space=pltpu.SMEM)]+[pl.BlockSpec(memory_space=pltpu.VMEM)]*2,
      out_specs=pl.BlockSpec(memory_space=pltpu.VMEM),
      scratch_shapes=[pltpu.VMEM((WIN,WIN),F32)],
      compiler_params=pltpu.CompilerParams(vmem_limit_bytes=48*2**20),name="attention_backward")(clips,t,do)


RT = 400


def dot_nt(left, right):
    return lax.dot_general(left, right, (((1,), (1,)), ((), ())), preferred_element_type=F32)


def dot_tn(left, right):
    return lax.dot_general(left, right, (((0,), (0,)), ((), ())), preferred_element_type=F32)


def dot_nn(left, right):
    return jnp.dot(left, right, preferred_element_type=F32)


def norm_parts(values):
    centred = values - jnp.mean(values, axis=-1, keepdims=True)
    scale = lax.rsqrt(jnp.mean(centred * centred, axis=-1, keepdims=True) + EPSILON)
    return centred * scale, scale


def norm_back(grad, gain, unit, scale):
    inner = grad * gain
    return scale * (
        inner
        - jnp.mean(inner, axis=-1, keepdims=True)
        - unit * jnp.mean(inner * unit, axis=-1, keepdims=True)
    )


def gelu_pair(u):
    bell = jnp.exp(-0.5 * u * u)
    t = 1.0 / (1.0 + (0.3275911 * 0.5**0.5) * jnp.abs(u))
    poly = t * (
        0.5 * 0.254829592
        + t * (-0.5 * 0.284496736 + t * (0.5 * 1.421413741 + t * (-0.5 * 1.453152027 + t * (0.5 * 1.061405429))))
    )
    tail = poly * bell
    phi = jnp.where(u < 0, tail, 1.0 - tail)
    return u * phi, phi + u * (bell * (2.0 * math.pi) ** -0.5)


def column_sum(values):
    return jnp.sum(values, axis=0, keepdims=True)


def tiles(rows, body):
    @pl.loop(0, rows // RT)
    def _(i):
        body(pl.ds(pl.multiple_of(i * RT, 16), RT))


def qkv_norm(x_ref, vec, a1_ref):
    def one(win):
        unit, _ = norm_parts(x_ref[win, :].astype(F32))
        a1_ref[win, :] = (unit * vec[0:1, :] + vec[1:2, :]).astype(BF)

    tiles(x_ref.shape[0], one)


def qkv_block(a1_ref, w_ref, t_ref, part):
    width = a1_ref.shape[1]
    weight = w_ref[part].reshape(width, width)

    def one(win):
        out = dot_nn(a1_ref[win, :], weight)
        if part == 0:
            out = out * HEAD_DIM**-0.5
        t_ref[win, pl.ds(part * width, width)] = out.astype(BF)

    tiles(a1_ref.shape[0], one)


def qkv_kernel(x_ref, vec, w_ref, t_ref, a1_ref):
    qkv_norm(x_ref, vec, a1_ref)
    for part in range(3):
        qkv_block(a1_ref, w_ref, t_ref, part)


def middle_step(x_ref, o_ref, vec, wo_ref, m_ref, a2_ref):
    def one(win):
        middle = x_ref[win, :].astype(F32) + (dot_nn(o_ref[win, :], wo_ref[...]) + vec[2:3, :])
        m_ref[win, :] = middle
        unit, _ = norm_parts(middle)
        a2_ref[win, :] = (unit * vec[3:4, :] + vec[4:5, :]).astype(BF)

    tiles(x_ref.shape[0], one)


def chunk_step(first, bias, a2_ref, dy_ref, we_ref, wc_ref, h_ref, du_ref, y_ref, da2_ref, be_ref):
    be_ref[...] = jnp.zeros_like(be_ref)

    def one(win):
        hidden, slope = gelu_pair(dot_nn(a2_ref[win, :], we_ref[...]) + bias)
        hidden = hidden.astype(BF)
        h_ref[win, :] = hidden
        du = (dot_nt(dy_ref[win, :], wc_ref[...]) * slope).astype(BF)
        du_ref[win, :] = du
        be_ref[...] += column_sum(du.astype(F32))
        y = dot_nn(hidden, wc_ref[...])
        da2 = dot_nt(du, we_ref[...])
        if first is True:
            y_ref[win, :] = y
            da2_ref[win, :] = da2
        else:
            y_ref[win, :] += y
            da2_ref[win, :] += da2

    tiles(a2_ref.shape[0], one)


def middle_back(live_rows, m_ref, y_ref, dy_ref, da2_ref, vec, wo_ref, out_ref, dm_ref, dz_ref, do_ref, sums):
    sums[...] = jnp.zeros_like(sums)

    def one(win):
        middle = m_ref[win, :]
        out_ref[win, :] = (middle + (y_ref[win, :] + vec[5:6, :])).astype(BF)
        unit, scale = norm_parts(middle)
        da2 = da2_ref[win, :]
        dy = dy_ref[win, :].astype(F32)
        dm = dy + norm_back(da2, vec[3:4, :], unit, scale)
        dm_ref[win, :] = dm
        dz = dm.astype(BF)
        dz_ref[win, :] = dz
        do_ref[win, :] = dot_nt(dz, wo_ref[...]).astype(BF)
        sums[0:1, :] += column_sum(da2 * unit)
        sums[1:2, :] += column_sum(da2)
        sums[2:3, :] += column_sum(dz.astype(F32))
        sums[3:4, :] += column_sum(dy)

    tiles(m_ref.shape[0], one)


def feed_kernel(
    x_ref, o_ref, dy_ref, vec, wo_ref, we_ref, wc_ref,
    out_ref, dm_ref, do_ref, gwo_ref, gwe_ref, gwc_ref, sums, be_ref,
    m_ref, a2_ref, h_ref, du_ref, y_ref, da2_ref, dz_ref,
):
    middle_step(x_ref, o_ref, vec, wo_ref, m_ref, a2_ref)
    for j in range(4):
        chunk_step(
            j == 0, vec[6 + j : 7 + j, :], a2_ref, dy_ref, we_ref.at[j], wc_ref.at[j],
            h_ref, du_ref, y_ref, da2_ref, be_ref.at[pl.ds(8 * j, 1)],
        )
        gwc_ref[j] = dot_tn(h_ref[...], dy_ref[...]).astype(BF)
        gwe_ref[j] = dot_tn(a2_ref[...], du_ref[...]).astype(BF)
    middle_back(None, m_ref, y_ref, dy_ref, da2_ref, vec, wo_ref, out_ref, dm_ref, dz_ref, do_ref, sums)
    gwo_ref[...] = dot_tn(o_ref[...], dz_ref[...]).astype(BF)


def first_back(x_ref, dt_ref, dm_ref, vec, w_refs, pg_ref, sums):
    sums[...] = jnp.zeros_like(sums)
    width = x_ref.shape[1]

    def one(win):
        da1 = dot_nt(dt_ref[win, pl.ds(0, width)], w_refs[0][...])
        da1 += dot_nt(dt_ref[win, pl.ds(width, width)], w_refs[1][...])
        da1 += dot_nt(dt_ref[win, pl.ds(2 * width, width)], w_refs[2][...])
        unit, scale = norm_parts(x_ref[win, :].astype(F32))
        pg_ref[win, :] = dm_ref[win, :] + norm_back(da1, vec[0:1, :], unit, scale)
        sums[0:1, :] += column_sum(da1 * unit)
        sums[1:2, :] += column_sum(da1)

    tiles(x_ref.shape[0], one)


def first_kernel(x_ref, a1_ref, dt_ref, dm_ref, vec, w_ref, pg_ref, gwi_ref, sums):
    width = x_ref.shape[1]
    for part in range(3):
        gwi_ref[part] = dot_tn(a1_ref[...], dt_ref[:, pl.ds(part * width, width)]).astype(BF)
    first_back(x_ref, dt_ref, dm_ref, vec, [w_ref.at[p] for p in range(3)], pg_ref, sums)


VM = pl.BlockSpec(memory_space=pltpu.VMEM)
SM = pl.BlockSpec(memory_space=pltpu.SMEM)


def vmem_call(kernel, name, ins, outs, scratch=(), smem=0):
    return pl.pallas_call(
        kernel,
        out_shape=[jax.ShapeDtypeStruct(s, d) for s, d in outs],
        in_specs=[SM] * smem + [VM] * (len(ins) - smem),
        out_specs=[VM] * len(outs),
        scratch_shapes=[pltpu.VMEM(s, d) for s, d in scratch],
        compiler_params=pltpu.CompilerParams(vmem_limit_bytes=60 * 2**20),
        name=name,
    )(*ins)


MESH = pl.DeviceIdType.MESH


class Place:
    def __init__(self, parts, sh, width):
        mine, copy = lax.axis_index("fsdp"), lax.axis_index("rep")
        self.outer_count = parts // 2
        self.outer, self.inner = mine // 2, mine % 2
        self.plane, self.core = copy // 2, copy % 2
        self.third = sh // 3
        self.half = width // 2

    def device(self, outer=None, inner=None, plane=None, core=None):
        outer = self.outer if outer is None else outer
        inner = self.inner if inner is None else inner
        plane = self.plane if plane is None else plane
        core = self.core if core is None else core
        return (outer * 2 + inner, plane * 2 + core)

    def far(self, k):
        return (self.outer + k) % self.outer_count

    def ranks(self):
        return range(1, self.outer_count)

    def columns(self, core=None):
        core = self.core if core is None else core
        return pl.ds(pl.multiple_of(core * self.half, 128), self.half)

    def held(self):
        return pl.ds(pl.multiple_of(self.plane * self.third, 16), 2 * self.third)

    def own(self, plane=None):
        plane = self.plane if plane is None else plane
        return pl.ds(pl.multiple_of(plane * (2 * self.third), 16), self.third)

    def peers(self):
        return [self.device(outer=self.far(k)) for k in self.ranks()] + [
            self.device(inner=1 - self.inner),
            self.device(plane=1 - self.plane),
            self.device(core=1 - self.core),
        ]

    def greet(self):
        barrier = pltpu.get_barrier_semaphore()
        peers = self.peers()
        for peer in peers:
            pl.semaphore_signal(barrier, inc=1, device_id=peer, device_id_type=MESH)
        pl.semaphore_wait(barrier, len(peers))


def remote(src, dst, sems, index, device):
    return pltpu.make_async_remote_copy(
        src_ref=src, dst_ref=dst, send_sem=sems[0].at[index], recv_sem=sems[1].at[index],
        device_id=device, device_id_type=MESH,
    )


def start(copies):
    for copy in copies:
        copy.start()


def landed(copies):
    for copy in copies:
        copy.wait_recv()


def sent(copies):
    for copy in copies:
        copy.wait_send()


class Gather:
    def __init__(self, place, shard, full, sems):
        self.p, self.shard, self.full, self.sems = place, shard, full, sems

    def far(self, b):
        p = self.p
        return [
            remote(
                self.shard.at[b, p.held(), p.columns()],
                self.full.at[b, p.outer, p.inner, p.held(), p.columns()],
                self.sems, (b, k - 1), p.device(outer=p.far(k)),
            )
            for k in p.ranks()
        ]

    def pair(self, b, which):
        p = self.p
        if which == 0:
            ref = self.full.at[b, :, p.inner, p.held(), p.columns()]
            device = p.device(inner=1 - p.inner)
        elif which == 1:
            ref = self.full.at[b, :, :, p.own(), p.columns()]
            device = p.device(plane=1 - p.plane)
        else:
            ref = self.full.at[b, :, :, :, p.columns()]
            device = p.device(core=1 - p.core)
        return [remote(ref, ref, self.sems, (b, p.outer_count - 1 + which), device)]

    def put_own(self, b):
        p = self.p
        self.full[b, p.outer, p.inner, p.held(), p.columns()] = self.shard[b, p.held(), p.columns()]

    def step(self, s, count, lag):
        for stage in range(5):
            @pl.when((s >= stage * lag) & (s < count + stage * lag))
            def _():
                b = s - stage * lag
                if stage == 0:
                    start(self.far(b))
                    self.put_own(b)
                else:
                    landed(self.far(b) if stage == 1 else self.pair(b, stage - 2))
                    if stage < 4:
                        start(self.pair(b, stage - 1))

    def finish(self, count):
        @pl.loop(0, count)
        def _(b):
            sent(self.far(b))
            for which in range(3):
                sent(self.pair(b, which))


def gather_sems(blocks, parts):
    shape = (blocks, parts // 2 - 1 + 3)
    return [pltpu.SemaphoreType.DMA(shape), pltpu.SemaphoreType.DMA(shape)]


class Reduce:
    def __init__(self, place, grad, out, bufs, sems):
        self.p, self.grad, self.out, self.sems = place, grad, out, sems
        self.from_core, self.from_plane, self.from_inner, self.from_far, self.part, self.from_part = bufs

    @staticmethod
    def scratch(blocks, parts, sh, width):
        outer, third, half = parts // 2, sh // 3, width // 2
        shape = (blocks, outer - 1 + 5)
        return [
            pltpu.VMEM((blocks, outer, 2, sh, half), BF),
            pltpu.VMEM((blocks, outer, 2, third, half), BF),
            pltpu.VMEM((blocks, outer, 2 * third, half), BF),
            pltpu.VMEM((blocks, outer - 1, 2 * third, half), BF),
            pltpu.VMEM((blocks, 2 * third, half), BF),
            pltpu.VMEM((blocks, 2 * third, half), BF),
            pltpu.SemaphoreType.DMA(shape),
            pltpu.SemaphoreType.DMA(shape),
        ]

    def copies(self, b, stage):
        p = self.p
        base = p.outer_count - 1
        if stage == 0:
            src, dst = self.grad.at[b, :, :, :, p.columns(1 - p.core)], self.from_core.at[b]
            device = p.device(core=1 - p.core)
        elif stage == 1:
            src, dst = self.grad.at[b, :, :, p.own(1 - p.plane), p.columns()], self.from_plane.at[b]
            device = p.device(plane=1 - p.plane)
        elif stage == 2:
            src, dst = self.grad.at[b, :, 1 - p.inner, p.held(), p.columns()], self.from_inner.at[b]
            device = p.device(inner=1 - p.inner)
        elif stage == 3:
            return [
                remote(
                    self.grad.at[b, p.far(k), p.inner, p.held(), p.columns()],
                    self.from_far.at[b, k - 1], self.sems, (b, k - 1), p.device(outer=p.far(k)),
                )
                for k in p.ranks()
            ]
        elif stage == 4:
            src, dst = self.part.at[b], self.from_part.at[b]
            device = p.device(plane=1 - p.plane)
        else:
            src = dst = self.out.at[b, :, p.columns()]
            device = p.device(core=1 - p.core)
        return [remote(src, dst, self.sems, (b, base + (stage if stage < 3 else stage - 1)), device)]

    def add(self, b, stage):
        p = self.p
        if stage == 0:
            @pl.loop(0, p.outer_count)
            def _(o):
                for i in range(2):
                    index = (b, o, i, slice(None), p.columns())
                    self.grad[index] = (self.grad[index].astype(F32) + self.from_core[b, o, i].astype(F32)).astype(BF)
        elif stage == 1:
            for i in range(2):
                @pl.loop(0, p.outer_count)
                def _(o):
                    index = (b, o, i, p.own(), p.columns())
                    self.grad[index] = (self.grad[index].astype(F32) + self.from_plane[b, o, i].astype(F32)).astype(BF)
        elif stage == 2:
            @pl.loop(0, p.outer_count)
            def _(o):
                index = (b, o, p.inner, p.held(), p.columns())
                self.grad[index] = (self.grad[index].astype(F32) + self.from_inner[b, o].astype(F32)).astype(BF)
        elif stage == 3:
            total = self.grad[b, p.outer, p.inner, p.held(), p.columns()].astype(F32)
            for k in p.ranks():
                total += self.from_far[b, k - 1].astype(F32)
            self.part[b] = total.astype(BF)
        elif stage == 4:
            third = p.third
            for plane in range(2):
                @pl.when(p.plane == plane)
                def _():
                    mine, other = self.part, self.from_part
                    first, last = (mine, other) if plane == 0 else (other, mine)
                    self.out[b, pl.ds(0, third), p.columns()] = first[b, pl.ds(0, third), :]
                    middle = first[b, pl.ds(third, third), :].astype(F32) + last[b, pl.ds(0, third), :].astype(F32)
                    self.out[b, pl.ds(third, third), p.columns()] = middle.astype(BF)
                    self.out[b, pl.ds(2 * third, third), p.columns()] = last[b, pl.ds(third, third), :]

    def stage(self, b, stage):
        if stage > 0:
            landed(self.copies(b, stage - 1))
            self.add(b, stage - 1)
        if stage < 6:
            start(self.copies(b, stage))

    def step(self, s, count, lag):
        for stage in range(7):
            @pl.when((s >= stage * lag) & (s < count + stage * lag))
            def _():
                self.stage(s - stage * lag, stage)

    def finish(self, count):
        @pl.loop(0, count)
        def _(b):
            for stage in range(6):
                sent(self.copies(b, stage))


class Vector:
    def __init__(self, place, total, bufs, sems, everywhere):
        self.p, self.total, self.sems = place, total, sems
        self.pairs, self.fars = bufs
        self.order = (0, 1, 2) if everywhere else (2,)

    @staticmethod
    def scratch(parts, shape, dtype):
        sems = (parts // 2 - 1 + 3,)
        return [
            pltpu.VMEM((6,) + shape, dtype), pltpu.VMEM((parts // 2,) + shape, dtype),
            pltpu.SemaphoreType.DMA(sems), pltpu.SemaphoreType.DMA(sems),
        ]

    def pair(self, which):
        p = self.p
        device = (
            p.device(core=1 - p.core), p.device(plane=1 - p.plane), p.device(inner=1 - p.inner)
        )[which]
        return [remote(self.pairs.at[2 * which], self.pairs.at[2 * which + 1], self.sems, p.outer_count - 1 + which, device)]

    def far(self):
        p = self.p
        mine = self.fars.at[p.outer]
        return [remote(mine, mine, self.sems, k - 1, p.device(outer=p.far(k))) for k in p.ranks()]

    def far_landed(self):
        p = self.p
        for k in p.ranks():
            theirs = self.fars.at[(p.outer + p.outer_count - k) % p.outer_count]
            remote(theirs, theirs, self.sems, k - 1, p.device(outer=p.far(k))).wait_recv()

    def stage(self, number):
        order = self.order
        if number > 0 and number <= len(order):
            which = order[number - 1]
            landed(self.pair(which))
            self.total[...] = self.total[...] + self.pairs[2 * which + 1]
        if number < len(order):
            which = order[number]
            self.pairs[2 * which] = self.total[...]
            start(self.pair(which))
        elif number == len(order):
            self.fars[self.p.outer] = self.total[...]
            start(self.far())
        else:
            self.far_landed()
            total = self.fars[0]
            for o in range(1, self.p.outer_count):
                total = total + self.fars[o]
            self.total[...] = total

    def stages(self):
        return len(self.order) + 2

    def finish(self):
        for which in self.order:
            sent(self.pair(which))
        sent(self.far())


FIRST_BLOCKS = 8
TILES = 3


def flat(ref, b):
    block = ref[b]
    return block.reshape(block.shape[0] * block.shape[1] * block.shape[2], block.shape[3])


def gather_kernel(
    parts, x_ref, vec_in, shard, t_out, a1_ref, xp_ref, wi_out, wo_out, ff_out, vec, t_ref, full, local, *scratch
):
    count, width = x_ref.shape
    rows = xp_ref.shape[0]
    place = Place(parts, shard.shape[1], width)
    weights = Gather(place, shard, full, scratch[0:2])
    vectors = Vector(place, vec, scratch[2:4], scratch[4:6], False)
    place.greet()
    weights.step(0, FIRST_BLOCKS, 1)
    vec[...] = vec_in[...]
    vectors.stage(0)
    tail = count // 16 * 16
    xp_ref[pl.ds(tail, rows - tail), :] = jnp.zeros((rows - tail, width), BF)
    xp_ref[pl.ds(0, count), :] = x_ref[...]
    vectors.stage(1)
    weights.step(1, FIRST_BLOCKS, 1)
    vectors.stage(2)
    weights.step(2, FIRST_BLOCKS, 1)
    qkv_norm(xp_ref, vec, a1_ref)
    weights.step(3, FIRST_BLOCKS, 1)
    leaving = []
    for s in range(4, FIRST_BLOCKS + 4):
        b = s - 4
        weights.step(s, FIRST_BLOCKS, 1)
        out = wi_out.at[b] if b < 3 else wo_out.at[0] if b == 3 else ff_out.at[b - 4]
        leaving.append(pltpu.make_async_copy(full.at[b], out, local.at[b]))
        leaving[-1].start()
        if b < 3:
            qkv_block(a1_ref, full, t_ref, b)
            part = pl.ds(b * width, width)
            leaving.append(pltpu.make_async_copy(t_ref.at[:, part], t_out.at[:, part], local.at[FIRST_BLOCKS + b]))
            leaving[-1].start()
    for copy in leaving:
        copy.wait()
    weights.finish(FIRST_BLOCKS)
    vectors.finish()


def feed_comm_kernel(
    parts, x_ref, o_ref, dy_ref, vec, wo_ref, early, shard,
    out_ref, dm_ref, do_ref, dz_ref, grad_out, sums, be_ref,
    a2_ref, y_ref, da2_ref, full, grad, local, *scratch,
):
    rows, width = x_ref.shape
    sh = shard.shape[1]
    place = Place(parts, sh, width)
    later, have = shard.shape[0], early.shape[0]
    weights = Gather(place, shard, full.at[pl.ds(have, later)], scratch[0:2])
    grads = Reduce(place, grad, grad_out, scratch[2:8], scratch[8:10])
    du_ref, h_ref = do_ref, dz_ref
    ready = pltpu.make_async_copy(early, full.at[pl.ds(0, have)], local)
    ready.start()
    place.greet()

    def win(i):
        return pl.ds(i * RT, RT)

    def slot(number):
        weights.step(number, later, 3)

    wo = flat(wo_ref, 0)
    slot(0)
    for i in range(TILES):
        middle = x_ref[win(i), :].astype(F32) + (dot_nn(o_ref[win(i), :], wo) + vec[2:3, :])
        dm_ref[win(i), :] = middle
        unit, _ = norm_parts(middle)
        a2_ref[win(i), :] = (unit * vec[3:4, :] + vec[4:5, :]).astype(BF)
        y_ref[win(i), :] = jnp.zeros((RT, width), F32)
        da2_ref[win(i), :] = jnp.zeros((RT, width), F32)
        slot(i + 1)
    ready.wait()

    def due(position, back, parity):
        steps = position - 3 - parity + 5 * back
        return steps // 2 if steps % 2 == 0 and 0 <= steps <= 12 else None

    def passing(j, position):
        for back in range(3, -1, -1):
            for parity in range(2):
                stage = due(position, back, parity)
                if stage is None:
                    continue
                if back == 0:
                    grads.stage(2 * j + parity, stage)
                else:
                    @pl.when(j >= back)
                    def _():
                        grads.stage(2 * (j - back) + parity, stage)

    @pl.loop(0, 4)
    def _(j):
        bias = vec[pl.ds(6 + j, 1), :]
        be_sum = jnp.zeros((1, width), F32)
        for i in range(TILES):
            hidden, slope = gelu_pair(dot_nn(a2_ref[win(i), :], flat(full, 2 * j)) + bias)
            hidden = hidden.astype(BF)
            h_ref[win(i), :] = hidden
            du = (dot_nt(dy_ref[win(i), :], flat(full, 2 * j + 1)) * slope).astype(BF)
            du_ref[win(i), :] = du
            be_sum += column_sum(du.astype(F32))
            y_ref[win(i), :] += dot_nn(hidden, flat(full, 2 * j + 1))
            da2_ref[win(i), :] += dot_nt(du, flat(full, 2 * j))
            slot(4 + 5 * j + i)
            passing(j, i)
        be_ref[pl.ds(j, 1), :] = be_sum
        grad[2 * j] = dot_tn(h_ref[...], dy_ref[...]).astype(BF).reshape(grad.shape[1:])
        slot(4 + 5 * j + 3)
        passing(j, 3)
        grad[2 * j + 1] = dot_tn(a2_ref[...], du_ref[...]).astype(BF).reshape(grad.shape[1:])
        slot(4 + 5 * j + 4)
        passing(j, 4)

    sums[...] = jnp.zeros_like(sums)
    for position in range(5, 17):
        i = position - 5
        if i < TILES:
            middle = dm_ref[win(i), :]
            out_ref[win(i), :] = (middle + (y_ref[win(i), :] + vec[5:6, :])).astype(BF)
            unit, scale = norm_parts(middle)
            da2 = da2_ref[win(i), :]
            dy = dy_ref[win(i), :].astype(F32)
            dm = dy + norm_back(da2, vec[3:4, :], unit, scale)
            dm_ref[win(i), :] = dm
            dz = dm.astype(BF)
            dz_ref[win(i), :] = dz
            do_ref[win(i), :] = dot_nt(dz, wo).astype(BF)
            sums[0:1, :] += column_sum(da2 * unit)
            sums[1:2, :] += column_sum(da2)
            sums[2:3, :] += column_sum(dz.astype(F32))
            sums[3:4, :] += column_sum(dy)
        for j in range(1, 4):
            for parity in range(2):
                stage = due(position + 5 * (3 - j), 0, parity)
                if stage is not None:
                    grads.stage(2 * j + parity, stage)
    weights.finish(later)
    grads.finish(8)


def first_comm_kernel(
    parts, x_ref, a1_ref, o_ref, dz_ref, dt_ref, dm_ref, vec, wi_ref, sums_two, be_ref,
    pg_ref, grad_out, total, grad, *scratch,
):
    rows, width = x_ref.shape
    place = Place(parts, width // parts, width)
    grads = Reduce(place, grad, grad_out, scratch[0:6], scratch[6:8])
    vectors = Vector(place, total, scratch[8:10], scratch[10:12], True)
    place.greet()
    total[...] = jnp.zeros_like(total)
    total[2:3, :] = sums_two[2:3, :]
    total[3:5, :] = sums_two[0:2, :]
    total[5:6, :] = sums_two[3:4, :]
    total[6:10, :] = be_ref[0:4, :]
    grad[0] = dot_tn(o_ref[...], dz_ref[...]).astype(BF).reshape(grad.shape[1:])
    grads.step(0, 4, 1)
    for part in range(3):
        block = dot_tn(a1_ref[...], dt_ref[:, pl.ds(part * width, width)]).astype(BF)
        grad[part + 1] = block.reshape(grad.shape[1:])
        grads.step(part + 1, 4, 1)
    for i in range(TILES):
        win = pl.ds(i * RT, RT)
        da1 = dot_nt(dt_ref[win, pl.ds(0, width)], flat(wi_ref, 0))
        da1 += dot_nt(dt_ref[win, pl.ds(width, width)], flat(wi_ref, 1))
        da1 += dot_nt(dt_ref[win, pl.ds(2 * width, width)], flat(wi_ref, 2))
        unit, scale = norm_parts(x_ref[win, :].astype(F32))
        pg_ref[win, :] = dm_ref[win, :] + norm_back(da1, vec[0:1, :], unit, scale)
        total[0:1, :] += column_sum(da1 * unit)
        total[1:2, :] += column_sum(da1)
        grads.step(4 + i, 4, 1)
    for s in range(7, 10):
        vectors.stage(s - 7)
        grads.step(s, 4, 1)
    for number in range(3, vectors.stages()):
        vectors.stage(number)
    grads.finish(4)
    vectors.finish()


def comm_call(kernel, name, which, ins, outs, scratch, far=(), far_out=()):
    return pl.pallas_call(
        kernel,
        out_shape=[jax.ShapeDtypeStruct(s, d) for s, d in outs],
        in_specs=[pl.BlockSpec(memory_space=pl.ANY) if i in far else VM for i in range(len(ins))],
        out_specs=[pl.BlockSpec(memory_space=pl.ANY) if i in far_out else VM for i in range(len(outs))],
        scratch_shapes=scratch,
        compiler_params=pltpu.CompilerParams(
            vmem_limit_bytes=62 * 2**20, collective_id=which, has_side_effects=True
        ),
        name=name,
    )(*ins)


STEPS = 6


def update_kernel(rates, g_one, g_two, *refs):
    state, outs, flat_we = refs[:12], refs[12:32], refs[32]
    i = pl.program_id(0)
    sh, width = g_two.shape[1:]
    parts = width // sh

    @pl.when(i == 0)
    def _():
        for j in range(4):
            for p in range(parts):
                flat_we[:, pl.ds((4 * p + j) * sh, sh)] = g_two[2 * j + 1, :, pl.ds(p * sh, sh)].astype(F32)

    half, sixth = width // 2, width // STEPS
    odd = pl.ds(pl.multiple_of(i % 2 * half, 128), half)
    third = sh // 3
    pieces = [g_two[2 * (k // 3), pl.ds(pl.multiple_of(k % 3 * third, 16), third), :] for k in (2 * i, 2 * i + 1)]
    sums = (
        g_one[1 + i // 2, :, odd].astype(F32),
        g_one[0, :, pl.ds(pl.multiple_of(i * sixth, 128), sixth)].astype(F32),
        flat_we[:, pl.ds(pl.multiple_of(i * 4 * sixth, 128), 4 * sixth)],
        jnp.concatenate(pieces, axis=0).astype(F32),
    )
    for member in range(4):
        weight, moment, average = (ref[...] for ref in state[3 * member : 3 * member + 3])
        grad, moment_out, weight_out, average_out, low_out = outs[5 * member : 5 * member + 5]
        total = sums[member]
        grad[...] = total
        moment_new = MOMENTUM * moment + total
        weight_new = weight - rates[member] * (total + MOMENTUM * moment_new)
        moment_out[...] = moment_new
        weight_out[...] = weight_new
        average_out[...] = AVERAGE * average + (1.0 - AVERAGE) * weight_new
        low_out[...] = weight_new.astype(BF)


def update(rates, g_one, g_two, masters, moments, averages):
    sh, width = g_two.shape[1:]
    across = [
        pl.BlockSpec((sh, width // 2), lambda i: (0, i)),
        pl.BlockSpec((sh, width // STEPS), lambda i: (0, i)),
        pl.BlockSpec((sh, 4 * width // STEPS), lambda i: (0, i)),
        pl.BlockSpec((4 * sh // STEPS, width), lambda i: (i, 0)),
    ]
    ins, specs, outs, out_specs = [], [], [], []
    for member in range(4):
        ins += [masters[member], moments[member], averages[member]]
        specs += [across[member]] * 3
        shape = masters[member].shape
        outs += [jax.ShapeDtypeStruct(shape, F32)] * 4 + [jax.ShapeDtypeStruct(shape, BF)]
        out_specs += [across[member]] * 5
    return pl.pallas_call(
        functools.partial(update_kernel, rates),
        grid=(STEPS,),
        out_shape=outs,
        in_specs=[pl.BlockSpec(g.shape, lambda i: (0, 0, 0)) for g in (g_one, g_two)] + specs,
        out_specs=out_specs,
        scratch_shapes=[pltpu.VMEM((sh, 4 * width), F32)],
        compiler_params=pltpu.CompilerParams(vmem_limit_bytes=48 * 2**20),
        name="momentum_step",
    )(g_one, g_two, *ins)


def run_qkv(x, vec, wi):
    rows, width = x.shape
    return vmem_call(
        qkv_kernel, "project_in", (x, vec, wi), [((rows, 3 * width), BF), ((rows, width), BF)]
    )


def run_feed(x, o, dy, vec, wo, we, wc):
    rows, width = x.shape
    wide, low = ((rows, width), F32), ((rows, width), BF)
    return vmem_call(
        feed_kernel, "feed_forward", (x, o, dy, vec, wo, we, wc),
        [low, wide, low, ((width, width), BF), ((4, width, width), BF), ((4, width, width), BF),
         ((8, width), F32), ((32, width), F32)],
        [wide, low, low, low, wide, wide, low],
    )


def run_first(x, a1, dt, dm, vec, wi):
    rows, width = x.shape
    return vmem_call(
        first_kernel, "project_in_back", (x, a1, dt, dm, vec, wi),
        [((rows, width), F32), ((3, width, width), BF), ((8, width), F32)],
    )


def pack_shards(wi, wo, we, wc, parts):
    rows, width = wo.shape
    wi = wi.reshape(rows, 3, width).swapaxes(0, 1)
    we = we.reshape(rows, parts, 4, rows).transpose(2, 0, 1, 3).reshape(4, rows, width)
    wc = wc.reshape(4, rows, width)
    return jnp.concatenate([wi, wo[None], we, wc], axis=0)


def unpack_shards(blocks, parts):
    rows, width = blocks.shape[1:]
    wi = blocks[0:3].swapaxes(0, 1).reshape(rows, 3 * width)
    we = blocks[4:8].reshape(4, rows, parts, rows).transpose(1, 2, 0, 3).reshape(rows, 4 * width)
    return wi, blocks[3], we, blocks[8:12].reshape(4 * rows, width)


def step(grad_sum, rate, weight, moment, average):
    moment_new = MOMENTUM * moment + grad_sum
    weight_new = weight - rate * (grad_sum + MOMENTUM * moment_new)
    average_new = AVERAGE * average + (1.0 - AVERAGE) * weight_new
    return [grad_sum, moment_new, weight_new, average_new, weight_new.astype(BF)]


def plain_path(patches, slot_clip, out_grad, masters, moments, averages, rates, vector_weight):
    parts, copies = lax.axis_size("fsdp"), lax.axis_size("rep")
    mine, copy = lax.axis_index("fsdp"), lax.axis_index("rep")
    count, width = patches.shape
    rows = (count + RT - 1) // RT * RT
    sh = width // parts
    packed = pack_shards(*(m.astype(BF) for m in masters), parts).reshape(12 * sh, width)
    piece = 12 * sh // copies
    quarter = lax.dynamic_slice_in_dim(packed, copy * piece, piece, 0)
    full = lax.all_gather(quarter, ("fsdp", "rep"), axis=0, tiled=True)
    full = full.reshape(parts, 12, sh, width).swapaxes(0, 1).reshape(12, width, width)
    vec = lax.all_gather(vector_weight.astype(BF), "fsdp", axis=1, tiled=True).astype(F32)
    be = vec[6:].reshape(parts, 4, sh).swapaxes(0, 1).reshape(4, width)
    vec = jnp.concatenate([vec[:6], be, jnp.zeros((6, width), F32)], axis=0)

    pad = ((0, rows - count), (0, 0))
    x = jnp.pad(patches, pad)
    t, a1 = run_qkv(x, vec, full[0:3])
    o, dy = attend(slot_clip, t, out_grad)
    out, dm, do, gwo, gwe, gwc, sums_two, sums_be = run_feed(x, o, dy, vec, full[3], full[4:8], full[8:12])
    dt = attend_back(slot_clip, t, do)
    pg, gwi, sums_one = run_first(x, a1, dt, dm, vec, full[0:3])

    grads = jnp.concatenate([gwi, gwo[None], gwe, gwc], axis=0)
    grads = grads.reshape(12, parts, sh, width).swapaxes(0, 1).reshape(parts * 12 * sh, width)
    grads = lax.psum_scatter(grads, ("fsdp", "rep"), scatter_dimension=0, tiled=True)
    grads = lax.all_gather(grads, "rep", axis=0, tiled=True).reshape(12, sh, width)
    be_grad = sums_be[::8].reshape(4, parts, sh).swapaxes(0, 1).reshape(4, width)
    vector = jnp.concatenate(
        [sums_one[0:2], sums_two[2:3], sums_two[0:2], sums_two[3:4], be_grad], axis=0
    )
    vector = lax.dynamic_slice_in_dim(lax.psum(vector, ("fsdp", "rep")), mine * sh, sh, 1)
    outputs = []
    for member, grad in enumerate(unpack_shards(grads, parts)):
        outputs += step(grad.astype(F32), rates[member], masters[member], moments[member], averages[member])
    return out[:count], pg[:count], vector, outputs


def direct_path(patches, slot_clip, out_grad, masters, moments, averages, rates, vector_weight):
    parts = lax.axis_size("fsdp")
    mine = lax.axis_index("fsdp")
    count, width = patches.shape
    rows = (count + RT - 1) // RT * RT
    sh = width // parts
    block = (parts // 2, 2, sh, width)
    wide, low = ((rows, width), F32), ((rows, width), BF)

    packed = pack_shards(*(m.astype(BF) for m in masters), parts)
    first = jnp.concatenate([packed[0:5], packed[8:9], packed[5:6], packed[9:10]], axis=0)
    later = jnp.stack((packed[6:8], packed[10:12]), axis=1).reshape(4, sh, width)
    vector_low = vector_weight.astype(BF).astype(F32)
    place = jnp.arange(parts)[None, :, None]
    row = jnp.arange(4)[:, None, None]
    apart = parts // 4
    top = jnp.where(place == mine, vector_low[:6, None, :], 0.0)
    be = jnp.repeat(vector_low[6:], apart, axis=0)[None]
    be = jnp.where((row == mine % 4) & (place % apart == mine // 4), be, 0.0)
    placed = jnp.concatenate([top, be, jnp.zeros((6, parts, sh), F32)], axis=0).reshape(16, width)

    t, a1, x, wi, wo, early, vec = comm_call(
        functools.partial(gather_kernel, parts), "gather_project_in", 0, (patches, placed, first),
        [((rows, 3 * width), BF), low, low, ((3,) + block, BF), ((1,) + block, BF),
         ((FIRST_BLOCKS - 4,) + block, BF), ((16, width), F32)],
        [pltpu.VMEM((rows, 3 * width), BF), pltpu.VMEM((FIRST_BLOCKS,) + block, BF),
         pltpu.SemaphoreType.DMA((FIRST_BLOCKS + 3,))]
        + gather_sems(FIRST_BLOCKS, parts) + Vector.scratch(parts, (16, width), F32),
        far_out=(0, 3, 4, 5),
    )
    o, dy = attend(slot_clip, t, out_grad)
    out, dm, do, dz, grads_two, sums_two, sums_be = comm_call(
        functools.partial(feed_comm_kernel, parts), "feed_forward_reduce", 1,
        (x, o, dy, vec, wo, early, later),
        [low, wide, low, low, ((8, sh, width), BF), ((8, width), F32), ((8, width), F32)],
        [pltpu.VMEM(*low), pltpu.VMEM(*wide), pltpu.VMEM(*wide),
         pltpu.VMEM((8,) + block, BF), pltpu.VMEM((8,) + block, BF), pltpu.SemaphoreType.DMA]
        + gather_sems(4, parts) + Reduce.scratch(8, parts, sh, width), far=(5,),
    )
    dt = attend_back(slot_clip, t, do)
    pg, grads_one, vector = comm_call(
        functools.partial(first_comm_kernel, parts), "project_in_back_reduce", 2,
        (x, a1, o, dz, dt, dm, vec, wi, sums_two, sums_be),
        [wide, ((4, sh, width), BF), ((16, width), F32)],
        [pltpu.VMEM((4,) + block, BF)] + Reduce.scratch(4, parts, sh, width)
        + Vector.scratch(parts, (16, width), F32),
    )
    top = lax.dynamic_slice_in_dim(vector[:6], mine * sh, sh, 1)
    be = lax.dynamic_slice_in_dim(vector, 6 + mine % 4, 1, 0).reshape(4, apart, sh)
    be = lax.dynamic_index_in_dim(be, mine // 4, 1, keepdims=False)
    vector = jnp.concatenate([top, be], axis=0)
    return out[:count], pg[:count], vector, update(rates, grads_one, grads_two, masters, moments, averages)


def on_device(
    patches, slot_clip, out_grad,
    project_in_weight, project_in_moment, project_in_average,
    project_out_weight, project_out_moment, project_out_average,
    expand_weight, expand_moment, expand_average,
    contract_weight, contract_moment, contract_average,
    vector_weight, vector_moment, vector_average,
):
    masters = (project_in_weight, project_out_weight, expand_weight, contract_weight, vector_weight)
    moments = (project_in_moment, project_out_moment, expand_moment, contract_moment, vector_moment)
    averages = (project_in_average, project_out_average, expand_average, contract_average, vector_average)
    parts, copies = lax.axis_size("fsdp"), lax.axis_size("rep")
    count, width = patches.shape
    direct = copies == 4 and parts % 4 == 0 and width // parts % 48 == 0
    path = direct_path if direct else plain_path
    tokens_all = count * parts * copies
    rates = [rate / tokens_all**0.5 for rate in RATES]
    out, pg, vector, outputs = path(
        patches, slot_clip, out_grad, masters[:4], moments[:4], averages[:4], rates, vector_weight
    )
    return (out, pg, *outputs, *step(vector, rates[4], masters[4], moments[4], averages[4]))


def solution(mesh):
    tokens = P(("fsdp", "rep"), None)
    split, split_vector = P("fsdp", None), P(None, "fsdp")
    in_specs = (tokens, P(("fsdp", "rep")), tokens) + (split,) * 12 + (split_vector,) * 3
    out_specs = (tokens,) * 2 + (split,) * 20 + (split_vector,) * 5
    return jax.shard_map(on_device, mesh=mesh, in_specs=in_specs, out_specs=out_specs, check_vma=False)
```

```python
import functools
import math

import jax
import jax.numpy as jnp
from jax import lax
from jax.sharding import PartitionSpec as P
import jax.experimental.pallas as pl
import jax.experimental.pallas.tpu as pltpu

BF, F32 = jnp.bfloat16, jnp.float32
HEAD_DIM = 64
SLOT = 49
LIVE_MAX = 8
WIN = 416
EPSILON = 1e-06
MOMENTUM = 0.5
AVERAGE = 0.5
RATES = (0.3, 0.3, 0.1, 0.03, 0.5)
NEG = -1e30

def dg(a,b,ca,cb):
    return lax.dot_general(a,b,(((ca,),(cb,)),((),())),preferred_element_type=F32)

def group_end(clips, start, slots):
    end = start+1
    for e in range(2, LIVE_MAX+1):
        cand = start+e
        safe = jnp.minimum(cand, slots-1)
        edge = (cand == slots) | ((cand < slots) & ((clips[safe] != clips[jnp.maximum(safe-1,0)]) | (clips[safe] < 0)))
        end = jnp.where(edge, cand, end)
    return end

def fill_bias(clips, w0, slots, bias):
    def keys(shape, dim):
        row = lax.broadcasted_iota(jnp.int32, shape, dim) + w0
        slot = (row*1338) >> 16
        def one(s, key):
            return jnp.where((slot == s) & (clips[s] >= 0), clips[s], key)
        return lax.fori_loop(0, slots, one, -1-row, unroll=True)
    bias[...] = jnp.where(keys((WIN,1),0) == keys((1,WIN),1), 0.0, NEG)

def clear_tail(ref, slots):
    tail = slots*SLOT//16*16
    ref[pl.ds(tail, ref.shape[0]-tail), :] = jnp.zeros((ref.shape[0]-tail, ref.shape[1]), BF)

def fwd_kernel(clips, t_ref, g_ref, o_ref, dy_ref, bias):
    slots = clips.shape[0]
    rows = t_ref.shape[0]; D = o_ref.shape[1]
    clear_tail(o_ref, slots)
    clear_tail(dy_ref, slots)
    slot = (lax.broadcasted_iota(jnp.int32,(slots*SLOT,1),0)*1338) >> 16
    live = lax.fori_loop(0, slots, lambda s, was: jnp.where((slot == s) & (clips[s] >= 0), 1.0, was), jnp.zeros((slots*SLOT,1),F32), unroll=True)
    dy_ref[pl.ds(0,slots*SLOT), :] = jnp.where(live > 0, g_ref[...].astype(F32), 0.0).astype(BF)
    def group(g, start):
        @pl.when(start < slots)
        def _():
            end = group_end(clips, start, slots)
            r0 = start*SLOT; r1 = end*SLOT
            w0 = pl.multiple_of(jnp.minimum((r0>>4)<<4, rows-WIN), 16)
            fill_bias(clips, w0, slots, bias)
            rowi = lax.broadcasted_iota(jnp.int32,(WIN,128),0)+w0
            mine = (rowi >= r0) & (rowi < r1)
            lane = lax.broadcasted_iota(jnp.int32,(1,128),1)
            win = pl.ds(w0, WIN)
            for p in range(D//128):
                q = t_ref[win, pl.ds(p*128,128)]
                k = t_ref[win, pl.ds(D+p*128,128)]
                v = t_ref[win, pl.ds(2*D+p*128,128)]
                outs=[]
                for h in range(2):
                    keep = (lane//64 == h).astype(BF)
                    s = dg(q*keep, k, 1, 1) + bias[...]
                    top = jnp.max(s, axis=1, keepdims=True)
                    e = jnp.exp(s-top)
                    inv = 1.0/jnp.sum(e, axis=1, keepdims=True)
                    pl_ = (e*inv).astype(BF)
                    outs.append(jnp.dot(pl_, v, preferred_element_type=F32))
                o = jnp.where(lane < 64, outs[0], outs[1])
                old = o_ref[win, pl.ds(p*128,128)]
                o_ref[win, pl.ds(p*128,128)] = jnp.where(mine, o, old.astype(F32)).astype(BF)
        return jnp.where(start < slots, group_end(clips, start, slots), start)
    lax.fori_loop(0, (2*slots)//(LIVE_MAX+1)+1, group, 0)

def bwd_kernel(clips, t_ref, do_ref, dt_ref, bias):
    slots = clips.shape[0]
    rows = t_ref.shape[0]; D = do_ref.shape[1]
    clear_tail(dt_ref, slots)
    def group(g, start):
        @pl.when(start < slots)
        def _():
            end = group_end(clips, start, slots)
            r0 = start*SLOT; r1 = end*SLOT
            w0 = pl.multiple_of(jnp.minimum((r0>>4)<<4, rows-WIN), 16)
            fill_bias(clips, w0, slots, bias)
            rowi = lax.broadcasted_iota(jnp.int32,(WIN,128),0)+w0
            mine = (rowi >= r0) & (rowi < r1)
            lane = lax.broadcasted_iota(jnp.int32,(1,128),1)
            win = pl.ds(w0, WIN)
            for p in range(D//128):
                q = t_ref[win, pl.ds(p*128,128)]
                k = t_ref[win, pl.ds(D+p*128,128)]
                v = t_ref[win, pl.ds(2*D+p*128,128)]
                do = do_ref[win, pl.ds(p*128,128)]
                dqs=[];dks=[];dvs=[]
                for h in range(2):
                    keep = (lane//64 == h).astype(BF)
                    s = dg(k, q*keep, 1, 1) + bias[...]
                    top = jnp.max(s, axis=0, keepdims=True)
                    e = jnp.exp(s-top)
                    inv = 1.0/jnp.sum(e, axis=0, keepdims=True)
                    pt = e*inv
                    dp = dg(v, do*keep, 1, 1)
                    dvs.append(jnp.dot(pt.astype(BF), do, preferred_element_type=F32))
                    inner = jnp.sum(dp*pt, axis=0, keepdims=True)
                    ds = (pt*(dp-inner)).astype(BF)
                    dks.append(jnp.dot(ds, q, preferred_element_type=F32))
                    dqs.append(dg(ds, k, 0, 0))
                for i,x in enumerate((dqs,dks,dvs)):
                    new = jnp.where(lane < 64, x[0], x[1]).astype(BF).astype(F32)
                    if i==0: new = new*(64**-0.5)
                    c = pl.ds(i*D+p*128,128)
                    old = dt_ref[win, c].astype(F32)
                    dt_ref[win, c] = jnp.where(mine, new, old).astype(BF)
        return jnp.where(start < slots, group_end(clips, start, slots), start)
    lax.fori_loop(0, (2*slots)//(LIVE_MAX+1)+1, group, 0)

def attend(clips, t, g):
    D=t.shape[1]//3
    return pl.pallas_call(fwd_kernel, out_shape=[jax.ShapeDtypeStruct((t.shape[0],D),BF)]*2,
      in_specs=[pl.BlockSpec(memory_space=pltpu.SMEM)]+[pl.BlockSpec(memory_space=pltpu.VMEM)]*2,
      out_specs=[pl.BlockSpec(memory_space=pltpu.VMEM)]*2,
      scratch_shapes=[pltpu.VMEM((WIN,WIN),F32)],
      compiler_params=pltpu.CompilerParams(vmem_limit_bytes=48*2**20),name="attention_forward")(clips,t,g)
def attend_back(clips, t, do):
    return pl.pallas_call(bwd_kernel, out_shape=jax.ShapeDtypeStruct(t.shape,BF),
      in_specs=[pl.BlockSpec(memory_space=pltpu.SMEM)]+[pl.BlockSpec(memory_space=pltpu.VMEM)]*2,
      out_specs=pl.BlockSpec(memory_space=pltpu.VMEM),
      scratch_shapes=[pltpu.VMEM((WIN,WIN),F32)],
      compiler_params=pltpu.CompilerParams(vmem_limit_bytes=48*2**20),name="attention_backward")(clips,t,do)


RT = 400


def dot_nt(left, right):
    return lax.dot_general(left, right, (((1,), (1,)), ((), ())), preferred_element_type=F32)


def dot_tn(left, right):
    return lax.dot_general(left, right, (((0,), (0,)), ((), ())), preferred_element_type=F32)


def dot_nn(left, right):
    return jnp.dot(left, right, preferred_element_type=F32)


def norm_parts(values):
    centred = values - jnp.mean(values, axis=-1, keepdims=True)
    scale = lax.rsqrt(jnp.mean(centred * centred, axis=-1, keepdims=True) + EPSILON)
    return centred * scale, scale


def norm_back(grad, gain, unit, scale):
    inner = grad * gain
    return scale * (
        inner
        - jnp.mean(inner, axis=-1, keepdims=True)
        - unit * jnp.mean(inner * unit, axis=-1, keepdims=True)
    )


def gelu_pair(u):
    bell = jnp.exp(-0.5 * u * u)
    t = 1.0 / (1.0 + (0.3275911 * 0.5**0.5) * jnp.abs(u))
    poly = t * (
        0.5 * 0.254829592
        + t * (-0.5 * 0.284496736 + t * (0.5 * 1.421413741 + t * (-0.5 * 1.453152027 + t * (0.5 * 1.061405429))))
    )
    tail = poly * bell
    phi = jnp.where(u < 0, tail, 1.0 - tail)
    return u * phi, phi + u * (bell * (2.0 * math.pi) ** -0.5)


def column_sum(values):
    return jnp.sum(values, axis=0, keepdims=True)


def tiles(rows, body):
    @pl.loop(0, rows // RT)
    def _(i):
        body(pl.ds(pl.multiple_of(i * RT, 16), RT))


def qkv_norm(x_ref, vec, a1_ref):
    def one(win):
        unit, _ = norm_parts(x_ref[win, :].astype(F32))
        a1_ref[win, :] = (unit * vec[0:1, :] + vec[1:2, :]).astype(BF)

    tiles(x_ref.shape[0], one)


def qkv_block(a1_ref, w_ref, t_ref, part):
    width = a1_ref.shape[1]
    weight = w_ref[part].reshape(width, width)

    def one(win):
        out = dot_nn(a1_ref[win, :], weight)
        if part == 0:
            out = out * HEAD_DIM**-0.5
        t_ref[win, pl.ds(part * width, width)] = out.astype(BF)

    tiles(a1_ref.shape[0], one)


def qkv_kernel(x_ref, vec, w_ref, t_ref, a1_ref):
    qkv_norm(x_ref, vec, a1_ref)
    for part in range(3):
        qkv_block(a1_ref, w_ref, t_ref, part)


def middle_step(x_ref, o_ref, vec, wo_ref, m_ref, a2_ref):
    def one(win):
        middle = x_ref[win, :].astype(F32) + (dot_nn(o_ref[win, :], wo_ref[...]) + vec[2:3, :])
        m_ref[win, :] = middle
        unit, _ = norm_parts(middle)
        a2_ref[win, :] = (unit * vec[3:4, :] + vec[4:5, :]).astype(BF)

    tiles(x_ref.shape[0], one)


def chunk_step(first, bias, a2_ref, dy_ref, we_ref, wc_ref, h_ref, du_ref, y_ref, da2_ref, be_ref):
    be_ref[...] = jnp.zeros_like(be_ref)

    def one(win):
        hidden, slope = gelu_pair(dot_nn(a2_ref[win, :], we_ref[...]) + bias)
        hidden = hidden.astype(BF)
        h_ref[win, :] = hidden
        du = (dot_nt(dy_ref[win, :], wc_ref[...]) * slope).astype(BF)
        du_ref[win, :] = du
        be_ref[...] += column_sum(du.astype(F32))
        y = dot_nn(hidden, wc_ref[...])
        da2 = dot_nt(du, we_ref[...])
        if first is True:
            y_ref[win, :] = y
            da2_ref[win, :] = da2
        else:
            y_ref[win, :] += y
            da2_ref[win, :] += da2

    tiles(a2_ref.shape[0], one)


def middle_back(live_rows, m_ref, y_ref, dy_ref, da2_ref, vec, wo_ref, out_ref, dm_ref, dz_ref, do_ref, sums):
    sums[...] = jnp.zeros_like(sums)

    def one(win):
        middle = m_ref[win, :]
        out_ref[win, :] = (middle + (y_ref[win, :] + vec[5:6, :])).astype(BF)
        unit, scale = norm_parts(middle)
        da2 = da2_ref[win, :]
        dy = dy_ref[win, :].astype(F32)
        dm = dy + norm_back(da2, vec[3:4, :], unit, scale)
        dm_ref[win, :] = dm
        dz = dm.astype(BF)
        dz_ref[win, :] = dz
        do_ref[win, :] = dot_nt(dz, wo_ref[...]).astype(BF)
        sums[0:1, :] += column_sum(da2 * unit)
        sums[1:2, :] += column_sum(da2)
        sums[2:3, :] += column_sum(dz.astype(F32))
        sums[3:4, :] += column_sum(dy)

    tiles(m_ref.shape[0], one)


def feed_kernel(
    x_ref, o_ref, dy_ref, vec, wo_ref, we_ref, wc_ref,
    out_ref, dm_ref, do_ref, gwo_ref, gwe_ref, gwc_ref, sums, be_ref,
    m_ref, a2_ref, h_ref, du_ref, y_ref, da2_ref, dz_ref,
):
    middle_step(x_ref, o_ref, vec, wo_ref, m_ref, a2_ref)
    for j in range(4):
        chunk_step(
            j == 0, vec[6 + j : 7 + j, :], a2_ref, dy_ref, we_ref.at[j], wc_ref.at[j],
            h_ref, du_ref, y_ref, da2_ref, be_ref.at[pl.ds(8 * j, 1)],
        )
        gwc_ref[j] = dot_tn(h_ref[...], dy_ref[...]).astype(BF)
        gwe_ref[j] = dot_tn(a2_ref[...], du_ref[...]).astype(BF)
    middle_back(None, m_ref, y_ref, dy_ref, da2_ref, vec, wo_ref, out_ref, dm_ref, dz_ref, do_ref, sums)
    gwo_ref[...] = dot_tn(o_ref[...], dz_ref[...]).astype(BF)


def first_back(x_ref, dt_ref, dm_ref, vec, w_refs, pg_ref, sums):
    sums[...] = jnp.zeros_like(sums)
    width = x_ref.shape[1]

    def one(win):
        da1 = dot_nt(dt_ref[win, pl.ds(0, width)], w_refs[0][...])
        da1 += dot_nt(dt_ref[win, pl.ds(width, width)], w_refs[1][...])
        da1 += dot_nt(dt_ref[win, pl.ds(2 * width, width)], w_refs[2][...])
        unit, scale = norm_parts(x_ref[win, :].astype(F32))
        pg_ref[win, :] = dm_ref[win, :] + norm_back(da1, vec[0:1, :], unit, scale)
        sums[0:1, :] += column_sum(da1 * unit)
        sums[1:2, :] += column_sum(da1)

    tiles(x_ref.shape[0], one)


def first_kernel(x_ref, a1_ref, dt_ref, dm_ref, vec, w_ref, pg_ref, gwi_ref, sums):
    width = x_ref.shape[1]
    for part in range(3):
        gwi_ref[part] = dot_tn(a1_ref[...], dt_ref[:, pl.ds(part * width, width)]).astype(BF)
    first_back(x_ref, dt_ref, dm_ref, vec, [w_ref.at[p] for p in range(3)], pg_ref, sums)


VM = pl.BlockSpec(memory_space=pltpu.VMEM)
SM = pl.BlockSpec(memory_space=pltpu.SMEM)


def vmem_call(kernel, name, ins, outs, scratch=(), smem=0):
    return pl.pallas_call(
        kernel,
        out_shape=[jax.ShapeDtypeStruct(s, d) for s, d in outs],
        in_specs=[SM] * smem + [VM] * (len(ins) - smem),
        out_specs=[VM] * len(outs),
        scratch_shapes=[pltpu.VMEM(s, d) for s, d in scratch],
        compiler_params=pltpu.CompilerParams(vmem_limit_bytes=60 * 2**20),
        name=name,
    )(*ins)


MESH = pl.DeviceIdType.MESH


class Place:
    def __init__(self, parts, sh, width):
        mine, copy = lax.axis_index("fsdp"), lax.axis_index("rep")
        self.outer_count = parts // 2
        self.outer, self.inner = mine // 2, mine % 2
        self.plane, self.core = copy // 2, copy % 2
        self.third = sh // 3
        self.half = width // 2

    def device(self, outer=None, inner=None, plane=None, core=None):
        outer = self.outer if outer is None else outer
        inner = self.inner if inner is None else inner
        plane = self.plane if plane is None else plane
        core = self.core if core is None else core
        return (outer * 2 + inner, plane * 2 + core)

    def far(self, k):
        return (self.outer + k) % self.outer_count

    def ranks(self):
        return range(1, self.outer_count)

    def columns(self, core=None):
        core = self.core if core is None else core
        return pl.ds(pl.multiple_of(core * self.half, 128), self.half)

    def held(self):
        return pl.ds(pl.multiple_of(self.plane * self.third, 16), 2 * self.third)

    def own(self, plane=None):
        plane = self.plane if plane is None else plane
        return pl.ds(pl.multiple_of(plane * (2 * self.third), 16), self.third)

    def peers(self):
        return [self.device(outer=self.far(k)) for k in self.ranks()] + [
            self.device(inner=1 - self.inner),
            self.device(plane=1 - self.plane),
            self.device(core=1 - self.core),
        ]

    def greet(self):
        barrier = pltpu.get_barrier_semaphore()
        peers = self.peers()
        for peer in peers:
            pl.semaphore_signal(barrier, inc=1, device_id=peer, device_id_type=MESH)
        pl.semaphore_wait(barrier, len(peers))


def remote(src, dst, sems, index, device):
    return pltpu.make_async_remote_copy(
        src_ref=src, dst_ref=dst, send_sem=sems[0].at[index], recv_sem=sems[1].at[index],
        device_id=device, device_id_type=MESH,
    )


def start(copies):
    for copy in copies:
        copy.start()


def landed(copies):
    for copy in copies:
        copy.wait_recv()


def sent(copies):
    for copy in copies:
        copy.wait_send()


class Gather:
    def __init__(self, place, shard, full, sems):
        self.p, self.shard, self.full, self.sems = place, shard, full, sems

    def far(self, b):
        p = self.p
        return [
            remote(
                self.shard.at[b, p.held(), p.columns()],
                self.full.at[b, p.outer, p.inner, p.held(), p.columns()],
                self.sems, (b, k - 1), p.device(outer=p.far(k)),
            )
            for k in p.ranks()
        ]

    def pair(self, b, which):
        p = self.p
        if which == 0:
            ref = self.full.at[b, :, p.inner, p.held(), p.columns()]
            device = p.device(inner=1 - p.inner)
        elif which == 1:
            ref = self.full.at[b, :, :, p.own(), p.columns()]
            device = p.device(plane=1 - p.plane)
        else:
            ref = self.full.at[b, :, :, :, p.columns()]
            device = p.device(core=1 - p.core)
        return [remote(ref, ref, self.sems, (b, p.outer_count - 1 + which), device)]

    def put_own(self, b):
        p = self.p
        self.full[b, p.outer, p.inner, p.held(), p.columns()] = self.shard[b, p.held(), p.columns()]

    def step(self, s, count, lag):
        for stage in range(5):
            @pl.when((s >= stage * lag) & (s < count + stage * lag))
            def _():
                self.stage(s - stage * lag, stage)

    def stage(self, b, stage):
        if stage == 0:
            start(self.far(b))
            self.put_own(b)
        else:
            landed(self.far(b) if stage == 1 else self.pair(b, stage - 2))
            if stage < 4:
                start(self.pair(b, stage - 1))

    def finish(self, count):
        @pl.loop(0, count)
        def _(b):
            sent(self.far(b))
            for which in range(3):
                sent(self.pair(b, which))


def gather_sems(blocks, parts):
    shape = (blocks, parts // 2 - 1 + 3)
    return [pltpu.SemaphoreType.DMA(shape), pltpu.SemaphoreType.DMA(shape)]


class Reduce:
    def __init__(self, place, grad, out, bufs, sems):
        self.p, self.grad, self.out, self.sems = place, grad, out, sems
        self.from_core, self.from_plane, self.from_inner, self.from_far, self.part, self.from_part = bufs

    @staticmethod
    def scratch(blocks, parts, sh, width):
        outer, third, half = parts // 2, sh // 3, width // 2
        shape = (blocks, outer - 1 + 5)
        return [
            pltpu.VMEM((blocks, outer, 2, sh, half), BF),
            pltpu.VMEM((blocks, outer, 2, third, half), BF),
            pltpu.VMEM((blocks, outer, 2 * third, half), BF),
            pltpu.VMEM((blocks, outer - 1, 2 * third, half), BF),
            pltpu.VMEM((blocks, 2 * third, half), BF),
            pltpu.VMEM((blocks, 2 * third, half), BF),
            pltpu.SemaphoreType.DMA(shape),
            pltpu.SemaphoreType.DMA(shape),
        ]

    def copies(self, b, stage):
        p = self.p
        base = p.outer_count - 1
        if stage == 0:
            src, dst = self.grad.at[b, :, :, :, p.columns(1 - p.core)], self.from_core.at[b]
            device = p.device(core=1 - p.core)
        elif stage == 1:
            src, dst = self.grad.at[b, :, :, p.own(1 - p.plane), p.columns()], self.from_plane.at[b]
            device = p.device(plane=1 - p.plane)
        elif stage == 2:
            src, dst = self.grad.at[b, :, 1 - p.inner, p.held(), p.columns()], self.from_inner.at[b]
            device = p.device(inner=1 - p.inner)
        elif stage == 3:
            return [
                remote(
                    self.grad.at[b, p.far(k), p.inner, p.held(), p.columns()],
                    self.from_far.at[b, k - 1], self.sems, (b, k - 1), p.device(outer=p.far(k)),
                )
                for k in p.ranks()
            ]
        elif stage == 4:
            src, dst = self.part.at[b], self.from_part.at[b]
            device = p.device(plane=1 - p.plane)
        else:
            src = dst = self.out.at[b, :, p.columns()]
            device = p.device(core=1 - p.core)
        return [remote(src, dst, self.sems, (b, base + (stage if stage < 3 else stage - 1)), device)]

    def add(self, b, stage):
        p = self.p
        if stage == 0:
            @pl.loop(0, p.outer_count)
            def _(o):
                for i in range(2):
                    index = (b, o, i, slice(None), p.columns())
                    self.grad[index] = (self.grad[index].astype(F32) + self.from_core[b, o, i].astype(F32)).astype(BF)
        elif stage == 1:
            for i in range(2):
                @pl.loop(0, p.outer_count)
                def _(o):
                    index = (b, o, i, p.own(), p.columns())
                    self.grad[index] = (self.grad[index].astype(F32) + self.from_plane[b, o, i].astype(F32)).astype(BF)
        elif stage == 2:
            @pl.loop(0, p.outer_count)
            def _(o):
                index = (b, o, p.inner, p.held(), p.columns())
                self.grad[index] = (self.grad[index].astype(F32) + self.from_inner[b, o].astype(F32)).astype(BF)
        elif stage == 3:
            total = self.grad[b, p.outer, p.inner, p.held(), p.columns()].astype(F32)
            for k in p.ranks():
                total += self.from_far[b, k - 1].astype(F32)
            self.part[b] = total.astype(BF)
        elif stage == 4:
            third = p.third
            for plane in range(2):
                @pl.when(p.plane == plane)
                def _():
                    mine, other = self.part, self.from_part
                    first, last = (mine, other) if plane == 0 else (other, mine)
                    self.out[b, pl.ds(0, third), p.columns()] = first[b, pl.ds(0, third), :]
                    middle = first[b, pl.ds(third, third), :].astype(F32) + last[b, pl.ds(0, third), :].astype(F32)
                    self.out[b, pl.ds(third, third), p.columns()] = middle.astype(BF)
                    self.out[b, pl.ds(2 * third, third), p.columns()] = last[b, pl.ds(third, third), :]

    def stage(self, b, stage):
        if stage > 0:
            landed(self.copies(b, stage - 1))
            self.add(b, stage - 1)
        if stage < 6:
            start(self.copies(b, stage))

    def step(self, s, count, lag):
        for stage in range(7):
            @pl.when((s >= stage * lag) & (s < count + stage * lag))
            def _():
                self.stage(s - stage * lag, stage)

    def finish(self, count):
        @pl.loop(0, count)
        def _(b):
            for stage in range(6):
                sent(self.copies(b, stage))


class Vector:
    def __init__(self, place, total, bufs, sems, everywhere):
        self.p, self.total, self.sems = place, total, sems
        self.pairs, self.fars = bufs
        self.order = (0, 1, 2) if everywhere else (2,)

    @staticmethod
    def scratch(parts, shape, dtype):
        sems = (parts // 2 - 1 + 3,)
        return [
            pltpu.VMEM((6,) + shape, dtype), pltpu.VMEM((parts // 2,) + shape, dtype),
            pltpu.SemaphoreType.DMA(sems), pltpu.SemaphoreType.DMA(sems),
        ]

    def pair(self, which):
        p = self.p
        device = (
            p.device(core=1 - p.core), p.device(plane=1 - p.plane), p.device(inner=1 - p.inner)
        )[which]
        return [remote(self.pairs.at[2 * which], self.pairs.at[2 * which + 1], self.sems, p.outer_count - 1 + which, device)]

    def far(self):
        p = self.p
        mine = self.fars.at[p.outer]
        return [remote(mine, mine, self.sems, k - 1, p.device(outer=p.far(k))) for k in p.ranks()]

    def far_landed(self):
        p = self.p
        for k in p.ranks():
            theirs = self.fars.at[(p.outer + p.outer_count - k) % p.outer_count]
            remote(theirs, theirs, self.sems, k - 1, p.device(outer=p.far(k))).wait_recv()

    def stage(self, number):
        order = self.order
        if number > 0 and number <= len(order):
            which = order[number - 1]
            landed(self.pair(which))
            self.total[...] = self.total[...] + self.pairs[2 * which + 1]
        if number < len(order):
            which = order[number]
            self.pairs[2 * which] = self.total[...]
            start(self.pair(which))
        elif number == len(order):
            self.fars[self.p.outer] = self.total[...]
            start(self.far())
        else:
            self.far_landed()
            total = self.fars[0]
            for o in range(1, self.p.outer_count):
                total = total + self.fars[o]
            self.total[...] = total

    def stages(self):
        return len(self.order) + 2

    def finish(self):
        for which in self.order:
            sent(self.pair(which))
        sent(self.far())


FIRST_BLOCKS = 8
TILES = 3


def flat(ref, b):
    block = ref[b]
    return block.reshape(block.shape[0] * block.shape[1] * block.shape[2], block.shape[3])


def gather_kernel(
    parts, x_ref, vec_in, shard, t_out, a1_ref, xp_ref, wi_out, wo_out, ff_out, vec, t_ref, full, local, *scratch
):
    count, width = x_ref.shape
    rows = xp_ref.shape[0]
    place = Place(parts, shard.shape[1], width)
    weights = Gather(place, shard, full, scratch[0:2])
    vectors = Vector(place, vec, scratch[2:4], scratch[4:6], False)
    place.greet()
    weights.step(0, FIRST_BLOCKS, 1)
    vec[...] = vec_in[...]
    vectors.stage(0)
    tail = count // 16 * 16
    xp_ref[pl.ds(tail, rows - tail), :] = jnp.zeros((rows - tail, width), BF)
    xp_ref[pl.ds(0, count), :] = x_ref[...]
    vectors.stage(1)
    weights.step(1, FIRST_BLOCKS, 1)
    vectors.stage(2)
    weights.step(2, FIRST_BLOCKS, 1)
    qkv_norm(xp_ref, vec, a1_ref)
    weights.step(3, FIRST_BLOCKS, 1)
    leaving = []
    for s in range(4, FIRST_BLOCKS + 4):
        b = s - 4
        weights.step(s, FIRST_BLOCKS, 1)
        out = wi_out.at[b] if b < 3 else wo_out.at[0] if b == 3 else ff_out.at[b - 4]
        leaving.append(pltpu.make_async_copy(full.at[b], out, local.at[b]))
        leaving[-1].start()
        if b < 3:
            qkv_block(a1_ref, full, t_ref, b)
            part = pl.ds(b * width, width)
            leaving.append(pltpu.make_async_copy(t_ref.at[:, part], t_out.at[:, part], local.at[FIRST_BLOCKS + b]))
            leaving[-1].start()
    for copy in leaving:
        copy.wait()
    weights.finish(FIRST_BLOCKS)
    vectors.finish()


def feed_comm_kernel(
    parts, x_ref, o_ref, dy_ref, vec, wo_ref, early, last, shard,
    out_ref, dm_ref, do_ref, dz_ref, grad_out, grad_rest, sums, be_ref,
    a2_ref, y_ref, da2_ref, full, grad, local, *scratch,
):
    rows, width = x_ref.shape
    sh = shard.shape[1]
    place = Place(parts, sh, width)
    later, have = shard.shape[0], early.shape[0]
    weights = Gather(place, shard, full.at[pl.ds(have, later)], scratch[0:2])
    grads = Reduce(place, grad.at[pl.ds(0, have)], grad_out, scratch[2:8], scratch[8:10])
    du_ref, h_ref = do_ref, dz_ref
    ready = [pltpu.make_async_copy(early, full.at[pl.ds(0, have)], local.at[0])] + [
        pltpu.make_async_copy(last.at[:, :, b], full.at[have + later + b], local.at[1 + b]) for b in range(2)
    ]
    start(ready)
    place.greet()

    def win(i):
        return pl.ds(i * RT, RT)

    def slot(number):
        for b in range(2):
            for stage, at in enumerate((0, 4, 7, 10, 12)):
                due = at + b
                if isinstance(number, int):
                    if due == number:
                        weights.stage(b, stage)
                elif due >= 4:
                    @pl.when(number == due)
                    def _():
                        weights.stage(b, stage)

    wo = flat(wo_ref, 0)
    slot(0)
    for i in range(TILES):
        middle = x_ref[win(i), :].astype(F32) + (dot_nn(o_ref[win(i), :], wo) + vec[2:3, :])
        dm_ref[win(i), :] = middle
        unit, _ = norm_parts(middle)
        a2_ref[win(i), :] = (unit * vec[3:4, :] + vec[4:5, :]).astype(BF)
        y_ref[win(i), :] = jnp.zeros((RT, width), F32)
        da2_ref[win(i), :] = jnp.zeros((RT, width), F32)
        slot(i + 1)
    for copy in ready:
        copy.wait()

    def leave(b):
        return pltpu.make_async_copy(grad.at[b], grad_rest.at[:, :, b - 4], local.at[b - 1])

    def due(position, back, parity):
        steps = position - 3 - parity + 5 * back
        return steps // 2 if steps % 2 == 0 and 0 <= steps <= 12 else None

    def passing(j, position):
        for back in range(3, -1, -1):
            for parity in range(2):
                stage = due(position, back, parity)
                if stage is None:
                    continue

                @pl.when((j >= back) & (j < back + 2))
                def _():
                    grads.stage(2 * (j - back) + parity, stage)

    @pl.loop(0, 4)
    def _(j):
        bias = vec[pl.ds(6 + j, 1), :]
        be_sum = jnp.zeros((1, width), F32)
        for i in range(TILES):
            hidden, slope = gelu_pair(dot_nn(a2_ref[win(i), :], flat(full, 2 * j)) + bias)
            hidden = hidden.astype(BF)
            h_ref[win(i), :] = hidden
            du = (dot_nt(dy_ref[win(i), :], flat(full, 2 * j + 1)) * slope).astype(BF)
            du_ref[win(i), :] = du
            be_sum += column_sum(du.astype(F32))
            y_ref[win(i), :] += dot_nn(hidden, flat(full, 2 * j + 1))
            da2_ref[win(i), :] += dot_nt(du, flat(full, 2 * j))
            slot(4 + 5 * j + i)
            passing(j, i)
        be_ref[pl.ds(j, 1), :] = be_sum
        grad[2 * j] = dot_tn(h_ref[...], dy_ref[...]).astype(BF).reshape(grad.shape[1:])
        slot(4 + 5 * j + 3)
        passing(j, 3)
        grad[2 * j + 1] = dot_tn(a2_ref[...], du_ref[...]).astype(BF).reshape(grad.shape[1:])
        slot(4 + 5 * j + 4)
        passing(j, 4)

        @pl.when(j >= 2)
        def _():
            for parity in range(2):
                leave(2 * j + parity).start()

    sums[...] = jnp.zeros_like(sums)
    for position in range(5, 8):
        i = position - 5
        if i < TILES:
            middle = dm_ref[win(i), :]
            out_ref[win(i), :] = (middle + (y_ref[win(i), :] + vec[5:6, :])).astype(BF)
            unit, scale = norm_parts(middle)
            da2 = da2_ref[win(i), :]
            dy = dy_ref[win(i), :].astype(F32)
            dm = dy + norm_back(da2, vec[3:4, :], unit, scale)
            dm_ref[win(i), :] = dm
            dz = dm.astype(BF)
            dz_ref[win(i), :] = dz
            do_ref[win(i), :] = dot_nt(dz, wo).astype(BF)
            sums[0:1, :] += column_sum(da2 * unit)
            sums[1:2, :] += column_sum(da2)
            sums[2:3, :] += column_sum(dz.astype(F32))
            sums[3:4, :] += column_sum(dy)
        for j in range(0, 2):
            for parity in range(2):
                stage = due(position + 5 * (3 - j), 0, parity)
                if stage is not None:
                    grads.stage(2 * j + parity, stage)
    weights.finish(later)
    grads.finish(have)
    for b in range(4, 8):
        leave(b).wait()


def first_comm_kernel(
    parts, x_ref, a1_ref, o_ref, dz_ref, dt_ref, dm_ref, vec, wi_ref, sums_two, be_ref,
    pg_ref, grad_out, total, grad, *scratch,
):
    rows, width = x_ref.shape
    place = Place(parts, width // parts, width)
    grads = Reduce(place, grad, grad_out, scratch[0:6], scratch[6:8])
    vectors = Vector(place, total, scratch[8:10], scratch[10:12], True)
    place.greet()
    total[...] = jnp.zeros_like(total)
    total[2:3, :] = sums_two[2:3, :]
    total[3:5, :] = sums_two[0:2, :]
    total[5:6, :] = sums_two[3:4, :]
    total[6:10, :] = be_ref[0:4, :]
    grad[0] = dot_tn(o_ref[...], dz_ref[...]).astype(BF).reshape(grad.shape[1:])
    grads.step(0, 4, 1)
    for part in range(3):
        block = dot_tn(a1_ref[...], dt_ref[:, pl.ds(part * width, width)]).astype(BF)
        grad[part + 1] = block.reshape(grad.shape[1:])
        grads.step(part + 1, 4, 1)
    for i in range(TILES):
        win = pl.ds(i * RT, RT)
        da1 = dot_nt(dt_ref[win, pl.ds(0, width)], flat(wi_ref, 0))
        da1 += dot_nt(dt_ref[win, pl.ds(width, width)], flat(wi_ref, 1))
        da1 += dot_nt(dt_ref[win, pl.ds(2 * width, width)], flat(wi_ref, 2))
        unit, scale = norm_parts(x_ref[win, :].astype(F32))
        pg_ref[win, :] = dm_ref[win, :] + norm_back(da1, vec[0:1, :], unit, scale)
        total[0:1, :] += column_sum(da1 * unit)
        total[1:2, :] += column_sum(da1)
        grads.step(4 + i, 4, 1)
    for s in range(7, 10):
        vectors.stage(s - 7)
        grads.step(s, 4, 1)
    for number in range(3, vectors.stages()):
        vectors.stage(number)
    grads.finish(4)
    vectors.finish()


def comm_call(kernel, name, which, ins, outs, scratch, far=(), far_out=()):
    return pl.pallas_call(
        kernel,
        out_shape=[jax.ShapeDtypeStruct(s, d) for s, d in outs],
        in_specs=[pl.BlockSpec(memory_space=pl.ANY) if i in far else VM for i in range(len(ins))],
        out_specs=[pl.BlockSpec(memory_space=pl.ANY) if i in far_out else VM for i in range(len(outs))],
        scratch_shapes=scratch,
        compiler_params=pltpu.CompilerParams(
            vmem_limit_bytes=62 * 2**20, collective_id=which, has_side_effects=True
        ),
        name=name,
    )(*ins)


STEPS = 6


def update_kernel(rates, g_one, g_two, *refs):
    state, outs, flat_we = refs[:12], refs[12:32], refs[32]
    i = pl.program_id(0)
    sh, width = g_two.shape[1:]
    parts = width // sh

    @pl.when(i == 0)
    def _():
        for j in range(4):
            for p in range(parts):
                flat_we[:, pl.ds((4 * p + j) * sh, sh)] = g_two[2 * j + 1, :, pl.ds(p * sh, sh)].astype(F32)

    half, sixth = width // 2, width // STEPS
    odd = pl.ds(pl.multiple_of(i % 2 * half, 128), half)
    third = sh // 3
    pieces = [g_two[2 * (k // 3), pl.ds(pl.multiple_of(k % 3 * third, 16), third), :] for k in (2 * i, 2 * i + 1)]
    sums = (
        g_one[1 + i // 2, :, odd].astype(F32),
        g_one[0, :, pl.ds(pl.multiple_of(i * sixth, 128), sixth)].astype(F32),
        flat_we[:, pl.ds(pl.multiple_of(i * 4 * sixth, 128), 4 * sixth)],
        jnp.concatenate(pieces, axis=0).astype(F32),
    )
    for member in range(4):
        weight, moment, average = (ref[...] for ref in state[3 * member : 3 * member + 3])
        grad, moment_out, weight_out, average_out, low_out = outs[5 * member : 5 * member + 5]
        total = sums[member]
        grad[...] = total
        moment_new = MOMENTUM * moment + total
        weight_new = weight - rates[member] * (total + MOMENTUM * moment_new)
        moment_out[...] = moment_new
        weight_out[...] = weight_new
        average_out[...] = AVERAGE * average + (1.0 - AVERAGE) * weight_new
        low_out[...] = weight_new.astype(BF)


def update(rates, g_one, g_two, masters, moments, averages):
    sh, width = g_two.shape[1:]
    across = [
        pl.BlockSpec((sh, width // 2), lambda i: (0, i)),
        pl.BlockSpec((sh, width // STEPS), lambda i: (0, i)),
        pl.BlockSpec((sh, 4 * width // STEPS), lambda i: (0, i)),
        pl.BlockSpec((4 * sh // STEPS, width), lambda i: (i, 0)),
    ]
    ins, specs, outs, out_specs = [], [], [], []
    for member in range(4):
        ins += [masters[member], moments[member], averages[member]]
        specs += [across[member]] * 3
        shape = masters[member].shape
        outs += [jax.ShapeDtypeStruct(shape, F32)] * 4 + [jax.ShapeDtypeStruct(shape, BF)]
        out_specs += [across[member]] * 5
    return pl.pallas_call(
        functools.partial(update_kernel, rates),
        grid=(STEPS,),
        out_shape=outs,
        in_specs=[pl.BlockSpec(g.shape, lambda i: (0, 0, 0)) for g in (g_one, g_two)] + specs,
        out_specs=out_specs,
        scratch_shapes=[pltpu.VMEM((sh, 4 * width), F32)],
        compiler_params=pltpu.CompilerParams(vmem_limit_bytes=48 * 2**20),
        name="momentum_step",
    )(g_one, g_two, *ins)


def run_qkv(x, vec, wi):
    rows, width = x.shape
    return vmem_call(
        qkv_kernel, "project_in", (x, vec, wi), [((rows, 3 * width), BF), ((rows, width), BF)]
    )


def run_feed(x, o, dy, vec, wo, we, wc):
    rows, width = x.shape
    wide, low = ((rows, width), F32), ((rows, width), BF)
    return vmem_call(
        feed_kernel, "feed_forward", (x, o, dy, vec, wo, we, wc),
        [low, wide, low, ((width, width), BF), ((4, width, width), BF), ((4, width, width), BF),
         ((8, width), F32), ((32, width), F32)],
        [wide, low, low, low, wide, wide, low],
    )


def run_first(x, a1, dt, dm, vec, wi):
    rows, width = x.shape
    return vmem_call(
        first_kernel, "project_in_back", (x, a1, dt, dm, vec, wi),
        [((rows, width), F32), ((3, width, width), BF), ((8, width), F32)],
    )


def pack_shards(wi, wo, we, wc, parts):
    rows, width = wo.shape
    wi = wi.reshape(rows, 3, width).swapaxes(0, 1)
    we = we.reshape(rows, parts, 4, rows).transpose(2, 0, 1, 3).reshape(4, rows, width)
    wc = wc.reshape(4, rows, width)
    return jnp.concatenate([wi, wo[None], we, wc], axis=0)


def unpack_shards(blocks, parts):
    rows, width = blocks.shape[1:]
    wi = blocks[0:3].swapaxes(0, 1).reshape(rows, 3 * width)
    we = blocks[4:8].reshape(4, rows, parts, rows).transpose(1, 2, 0, 3).reshape(rows, 4 * width)
    return wi, blocks[3], we, blocks[8:12].reshape(4 * rows, width)


def step(grad_sum, rate, weight, moment, average):
    moment_new = MOMENTUM * moment + grad_sum
    weight_new = weight - rate * (grad_sum + MOMENTUM * moment_new)
    average_new = AVERAGE * average + (1.0 - AVERAGE) * weight_new
    return [grad_sum, moment_new, weight_new, average_new, weight_new.astype(BF)]


def plain_path(patches, slot_clip, out_grad, masters, moments, averages, rates, vector_weight):
    parts, copies = lax.axis_size("fsdp"), lax.axis_size("rep")
    mine, copy = lax.axis_index("fsdp"), lax.axis_index("rep")
    count, width = patches.shape
    rows = (count + RT - 1) // RT * RT
    sh = width // parts
    packed = pack_shards(*(m.astype(BF) for m in masters), parts).reshape(12 * sh, width)
    piece = 12 * sh // copies
    quarter = lax.dynamic_slice_in_dim(packed, copy * piece, piece, 0)
    full = lax.all_gather(quarter, ("fsdp", "rep"), axis=0, tiled=True)
    full = full.reshape(parts, 12, sh, width).swapaxes(0, 1).reshape(12, width, width)
    vec = lax.all_gather(vector_weight.astype(BF), "fsdp", axis=1, tiled=True).astype(F32)
    be = vec[6:].reshape(parts, 4, sh).swapaxes(0, 1).reshape(4, width)
    vec = jnp.concatenate([vec[:6], be, jnp.zeros((6, width), F32)], axis=0)

    pad = ((0, rows - count), (0, 0))
    x = jnp.pad(patches, pad)
    t, a1 = run_qkv(x, vec, full[0:3])
    o, dy = attend(slot_clip, t, out_grad)
    out, dm, do, gwo, gwe, gwc, sums_two, sums_be = run_feed(x, o, dy, vec, full[3], full[4:8], full[8:12])
    dt = attend_back(slot_clip, t, do)
    pg, gwi, sums_one = run_first(x, a1, dt, dm, vec, full[0:3])

    grads = jnp.concatenate([gwi, gwo[None], gwe, gwc], axis=0)
    grads = grads.reshape(12, parts, sh, width).swapaxes(0, 1).reshape(parts * 12 * sh, width)
    grads = lax.psum_scatter(grads, ("fsdp", "rep"), scatter_dimension=0, tiled=True)
    grads = lax.all_gather(grads, "rep", axis=0, tiled=True).reshape(12, sh, width)
    be_grad = sums_be[::8].reshape(4, parts, sh).swapaxes(0, 1).reshape(4, width)
    vector = jnp.concatenate(
        [sums_one[0:2], sums_two[2:3], sums_two[0:2], sums_two[3:4], be_grad], axis=0
    )
    vector = lax.dynamic_slice_in_dim(lax.psum(vector, ("fsdp", "rep")), mine * sh, sh, 1)
    outputs = []
    for member, grad in enumerate(unpack_shards(grads, parts)):
        outputs += step(grad.astype(F32), rates[member], masters[member], moments[member], averages[member])
    return out[:count], pg[:count], vector, outputs


def direct_path(patches, slot_clip, out_grad, masters, moments, averages, rates, vector_weight):
    parts = lax.axis_size("fsdp")
    mine = lax.axis_index("fsdp")
    count, width = patches.shape
    rows = (count + RT - 1) // RT * RT
    sh = width // parts
    block = (parts // 2, 2, sh, width)
    wide, low = ((rows, width), F32), ((rows, width), BF)

    packed = pack_shards(*(m.astype(BF) for m in masters), parts)
    first = jnp.concatenate([packed[0:5], packed[8:9], packed[5:6], packed[9:10]], axis=0)
    later = jnp.concatenate([packed[6:7], packed[10:11]], axis=0)
    last = jnp.concatenate([packed[7:8], packed[11:12]], axis=0).reshape(2 * sh, width)
    piece = 2 * sh // lax.axis_size("rep")
    last = lax.dynamic_slice_in_dim(last, lax.axis_index("rep") * piece, piece, 0)
    vector_low = vector_weight.astype(BF).astype(F32)
    place = jnp.arange(parts)[None, :, None]
    row = jnp.arange(4)[:, None, None]
    apart = parts // 4
    top = jnp.where(place == mine, vector_low[:6, None, :], 0.0)
    be = jnp.repeat(vector_low[6:], apart, axis=0)[None]
    be = jnp.where((row == mine % 4) & (place % apart == mine // 4), be, 0.0)
    placed = jnp.concatenate([top, be, jnp.zeros((6, parts, sh), F32)], axis=0).reshape(16, width)

    t, a1, x, wi, wo, early, vec = comm_call(
        functools.partial(gather_kernel, parts), "gather_project_in", 0, (patches, placed, first),
        [((rows, 3 * width), BF), low, low, ((3,) + block, BF), ((1,) + block, BF),
         ((FIRST_BLOCKS - 4,) + block, BF), ((16, width), F32)],
        [pltpu.VMEM((rows, 3 * width), BF), pltpu.VMEM((FIRST_BLOCKS,) + block, BF),
         pltpu.SemaphoreType.DMA((FIRST_BLOCKS + 3,))]
        + gather_sems(FIRST_BLOCKS, parts) + Vector.scratch(parts, (16, width), F32),
        far_out=(0, 3, 4, 5),
    )
    last, vec = lax.optimization_barrier((last, vec))
    last = lax.all_gather(last, ("fsdp", "rep"), axis=0, tiled=True).reshape(parts // 2, 2, 2, sh, width)
    o, dy = attend(slot_clip, t, out_grad)
    out, dm, do, dz, grads_two, rest, sums_two, sums_be = comm_call(
        functools.partial(feed_comm_kernel, parts), "feed_forward_reduce", 1,
        (x, o, dy, vec, wo, early, last, later),
        [low, wide, low, low, ((4, sh, width), BF), ((parts // 2, 2, 4, sh, width), BF), ((8, width), F32), ((8, width), F32)],
        [pltpu.VMEM(*low), pltpu.VMEM(*wide), pltpu.VMEM(*wide),
         pltpu.VMEM((8,) + block, BF), pltpu.VMEM((8,) + block, BF), pltpu.SemaphoreType.DMA((7,))]
        + gather_sems(2, parts) + Reduce.scratch(4, parts, sh, width), far=(5, 6), far_out=(5,),
    )
    rest = lax.psum_scatter(rest.reshape(parts * 4 * sh, width), ("fsdp", "rep"), scatter_dimension=0, tiled=True)
    rest = lax.all_gather(rest, "rep", axis=0, tiled=True).reshape(4, sh, width)
    grads_two = jnp.concatenate([grads_two, rest], axis=0)
    dt = attend_back(slot_clip, t, do)
    pg, grads_one, vector = comm_call(
        functools.partial(first_comm_kernel, parts), "project_in_back_reduce", 2,
        (x, a1, o, dz, dt, dm, vec, wi, sums_two, sums_be),
        [wide, ((4, sh, width), BF), ((16, width), F32)],
        [pltpu.VMEM((4,) + block, BF)] + Reduce.scratch(4, parts, sh, width)
        + Vector.scratch(parts, (16, width), F32),
    )
    top = lax.dynamic_slice_in_dim(vector[:6], mine * sh, sh, 1)
    be = lax.dynamic_slice_in_dim(vector, 6 + mine % 4, 1, 0).reshape(4, apart, sh)
    be = lax.dynamic_index_in_dim(be, mine // 4, 1, keepdims=False)
    vector = jnp.concatenate([top, be], axis=0)
    return out[:count], pg[:count], vector, update(rates, grads_one, grads_two, masters, moments, averages)


def on_device(
    patches, slot_clip, out_grad,
    project_in_weight, project_in_moment, project_in_average,
    project_out_weight, project_out_moment, project_out_average,
    expand_weight, expand_moment, expand_average,
    contract_weight, contract_moment, contract_average,
    vector_weight, vector_moment, vector_average,
):
    masters = (project_in_weight, project_out_weight, expand_weight, contract_weight, vector_weight)
    moments = (project_in_moment, project_out_moment, expand_moment, contract_moment, vector_moment)
    averages = (project_in_average, project_out_average, expand_average, contract_average, vector_average)
    parts, copies = lax.axis_size("fsdp"), lax.axis_size("rep")
    count, width = patches.shape
    direct = copies == 4 and parts % 4 == 0 and width // parts % 48 == 0
    path = direct_path if direct else plain_path
    tokens_all = count * parts * copies
    rates = [rate / tokens_all**0.5 for rate in RATES]
    out, pg, vector, outputs = path(
        patches, slot_clip, out_grad, masters[:4], moments[:4], averages[:4], rates, vector_weight
    )
    return (out, pg, *outputs, *step(vector, rates[4], masters[4], moments[4], averages[4]))


def solution(mesh):
    tokens = P(("fsdp", "rep"), None)
    split, split_vector = P("fsdp", None), P(None, "fsdp")
    in_specs = (tokens, P(("fsdp", "rep")), tokens) + (split,) * 12 + (split_vector,) * 3
    out_specs = (tokens,) * 2 + (split,) * 20 + (split_vector,) * 5
    return jax.shard_map(on_device, mesh=mesh, in_specs=in_specs, out_specs=out_specs, check_vma=False)
```

```python
import functools
import math

import jax
import jax.numpy as jnp
from jax import lax
from jax.sharding import PartitionSpec as P
import jax.experimental.pallas as pl
import jax.experimental.pallas.tpu as pltpu

BF, F32 = jnp.bfloat16, jnp.float32
HEAD_DIM = 64
SLOT = 49
LIVE_MAX = 8
WIN = 416
EPSILON = 1e-06
MOMENTUM = 0.5
AVERAGE = 0.5
RATES = (0.3, 0.3, 0.1, 0.03, 0.5)
NEG = -1e30

def dg(a,b,ca,cb):
    return lax.dot_general(a,b,(((ca,),(cb,)),((),())),preferred_element_type=F32)

def group_end(clips, start, slots):
    end = start+1
    for e in range(2, LIVE_MAX+1):
        cand = start+e
        safe = jnp.minimum(cand, slots-1)
        edge = (cand == slots) | ((cand < slots) & ((clips[safe] != clips[jnp.maximum(safe-1,0)]) | (clips[safe] < 0)))
        end = jnp.where(edge, cand, end)
    return end

def fill_bias(clips, w0, slots, bias):
    def keys(shape, dim):
        row = lax.broadcasted_iota(jnp.int32, shape, dim) + w0
        slot = (row*1338) >> 16
        def one(s, key):
            return jnp.where((slot == s) & (clips[s] >= 0), clips[s], key)
        return lax.fori_loop(0, slots, one, -1-row, unroll=True)
    bias[...] = jnp.where(keys((WIN,1),0) == keys((1,WIN),1), 0.0, NEG)

def clear_tail(ref, slots):
    tail = slots*SLOT//16*16
    ref[pl.ds(tail, ref.shape[0]-tail), :] = jnp.zeros((ref.shape[0]-tail, ref.shape[1]), BF)

def fwd_kernel(clips, t_ref, g_ref, o_ref, dy_ref, bias):
    slots = clips.shape[0]
    rows = t_ref.shape[0]; D = o_ref.shape[1]
    clear_tail(o_ref, slots)
    clear_tail(dy_ref, slots)
    slot = (lax.broadcasted_iota(jnp.int32,(slots*SLOT,1),0)*1338) >> 16
    live = lax.fori_loop(0, slots, lambda s, was: jnp.where((slot == s) & (clips[s] >= 0), 1.0, was), jnp.zeros((slots*SLOT,1),F32), unroll=True)
    dy_ref[pl.ds(0,slots*SLOT), :] = jnp.where(live > 0, g_ref[...].astype(F32), 0.0).astype(BF)
    def group(g, start):
        @pl.when(start < slots)
        def _():
            end = group_end(clips, start, slots)
            r0 = start*SLOT; r1 = end*SLOT
            w0 = pl.multiple_of(jnp.minimum((r0>>4)<<4, rows-WIN), 16)
            fill_bias(clips, w0, slots, bias)
            rowi = lax.broadcasted_iota(jnp.int32,(WIN,128),0)+w0
            mine = (rowi >= r0) & (rowi < r1)
            lane = lax.broadcasted_iota(jnp.int32,(1,128),1)
            win = pl.ds(w0, WIN)
            for p in range(D//128):
                q = t_ref[win, pl.ds(p*128,128)]
                k = t_ref[win, pl.ds(D+p*128,128)]
                v = t_ref[win, pl.ds(2*D+p*128,128)]
                outs=[]
                for h in range(2):
                    keep = (lane//64 == h).astype(BF)
                    s = dg(q*keep, k, 1, 1) + bias[...]
                    top = jnp.max(s, axis=1, keepdims=True)
                    e = jnp.exp(s-top)
                    inv = 1.0/jnp.sum(e, axis=1, keepdims=True)
                    pl_ = (e*inv).astype(BF)
                    outs.append(jnp.dot(pl_, v, preferred_element_type=F32))
                o = jnp.where(lane < 64, outs[0], outs[1])
                old = o_ref[win, pl.ds(p*128,128)]
                o_ref[win, pl.ds(p*128,128)] = jnp.where(mine, o, old.astype(F32)).astype(BF)
        return jnp.where(start < slots, group_end(clips, start, slots), start)
    lax.fori_loop(0, (2*slots)//(LIVE_MAX+1)+1, group, 0)

def bwd_kernel(clips, t_ref, do_ref, dt_ref, bias):
    slots = clips.shape[0]
    rows = t_ref.shape[0]; D = do_ref.shape[1]
    clear_tail(dt_ref, slots)
    def group(g, start):
        @pl.when(start < slots)
        def _():
            end = group_end(clips, start, slots)
            r0 = start*SLOT; r1 = end*SLOT
            w0 = pl.multiple_of(jnp.minimum((r0>>4)<<4, rows-WIN), 16)
            fill_bias(clips, w0, slots, bias)
            rowi = lax.broadcasted_iota(jnp.int32,(WIN,128),0)+w0
            mine = (rowi >= r0) & (rowi < r1)
            lane = lax.broadcasted_iota(jnp.int32,(1,128),1)
            win = pl.ds(w0, WIN)
            for p in range(D//128):
                q = t_ref[win, pl.ds(p*128,128)]
                k = t_ref[win, pl.ds(D+p*128,128)]
                v = t_ref[win, pl.ds(2*D+p*128,128)]
                do = do_ref[win, pl.ds(p*128,128)]
                dqs=[];dks=[];dvs=[]
                for h in range(2):
                    keep = (lane//64 == h).astype(BF)
                    s = dg(k, q*keep, 1, 1) + bias[...]
                    top = jnp.max(s, axis=0, keepdims=True)
                    e = jnp.exp(s-top)
                    inv = 1.0/jnp.sum(e, axis=0, keepdims=True)
                    pt = e*inv
                    dp = dg(v, do*keep, 1, 1)
                    dvs.append(jnp.dot(pt.astype(BF), do, preferred_element_type=F32))
                    inner = jnp.sum(dp*pt, axis=0, keepdims=True)
                    ds = (pt*(dp-inner)).astype(BF)
                    dks.append(jnp.dot(ds, q, preferred_element_type=F32))
                    dqs.append(dg(ds, k, 0, 0))
                for i,x in enumerate((dqs,dks,dvs)):
                    new = jnp.where(lane < 64, x[0], x[1]).astype(BF).astype(F32)
                    if i==0: new = new*(64**-0.5)
                    c = pl.ds(i*D+p*128,128)
                    old = dt_ref[win, c].astype(F32)
                    dt_ref[win, c] = jnp.where(mine, new, old).astype(BF)
        return jnp.where(start < slots, group_end(clips, start, slots), start)
    lax.fori_loop(0, (2*slots)//(LIVE_MAX+1)+1, group, 0)

def attend(clips, t, g):
    D=t.shape[1]//3
    return pl.pallas_call(fwd_kernel, out_shape=[jax.ShapeDtypeStruct((t.shape[0],D),BF)]*2,
      in_specs=[pl.BlockSpec(memory_space=pltpu.SMEM)]+[pl.BlockSpec(memory_space=pltpu.VMEM)]*2,
      out_specs=[pl.BlockSpec(memory_space=pltpu.VMEM)]*2,
      scratch_shapes=[pltpu.VMEM((WIN,WIN),F32)],
      compiler_params=pltpu.CompilerParams(vmem_limit_bytes=48*2**20),name="attention_forward")(clips,t,g)
def attend_back(clips, t, do):
    return pl.pallas_call(bwd_kernel, out_shape=jax.ShapeDtypeStruct(t.shape,BF),
      in_specs=[pl.BlockSpec(memory_space=pltpu.SMEM)]+[pl.BlockSpec(memory_space=pltpu.VMEM)]*2,
      out_specs=pl.BlockSpec(memory_space=pltpu.VMEM),
      scratch_shapes=[pltpu.VMEM((WIN,WIN),F32)],
      compiler_params=pltpu.CompilerParams(vmem_limit_bytes=48*2**20),name="attention_backward")(clips,t,do)


RT = 400


def dot_nt(left, right):
    return lax.dot_general(left, right, (((1,), (1,)), ((), ())), preferred_element_type=F32)


def dot_tn(left, right):
    return lax.dot_general(left, right, (((0,), (0,)), ((), ())), preferred_element_type=F32)


def dot_nn(left, right):
    return jnp.dot(left, right, preferred_element_type=F32)


def norm_parts(values):
    centred = values - jnp.mean(values, axis=-1, keepdims=True)
    scale = lax.rsqrt(jnp.mean(centred * centred, axis=-1, keepdims=True) + EPSILON)
    return centred * scale, scale


def norm_back(grad, gain, unit, scale):
    inner = grad * gain
    return scale * (
        inner
        - jnp.mean(inner, axis=-1, keepdims=True)
        - unit * jnp.mean(inner * unit, axis=-1, keepdims=True)
    )


def gelu_pair(u):
    bell = jnp.exp(-0.5 * u * u)
    t = 1.0 / (1.0 + (0.3275911 * 0.5**0.5) * jnp.abs(u))
    poly = t * (
        0.5 * 0.254829592
        + t * (-0.5 * 0.284496736 + t * (0.5 * 1.421413741 + t * (-0.5 * 1.453152027 + t * (0.5 * 1.061405429))))
    )
    tail = poly * bell
    phi = jnp.where(u < 0, tail, 1.0 - tail)
    return u * phi, phi + u * (bell * (2.0 * math.pi) ** -0.5)


def column_sum(values):
    return jnp.sum(values, axis=0, keepdims=True)


def tiles(rows, body):
    @pl.loop(0, rows // RT)
    def _(i):
        body(pl.ds(pl.multiple_of(i * RT, 16), RT))


def qkv_norm(x_ref, vec, a1_ref):
    def one(win):
        unit, _ = norm_parts(x_ref[win, :].astype(F32))
        a1_ref[win, :] = (unit * vec[0:1, :] + vec[1:2, :]).astype(BF)

    tiles(x_ref.shape[0], one)


def qkv_block(a1_ref, w_ref, t_ref, part):
    width = a1_ref.shape[1]
    weight = w_ref[part].reshape(width, width)

    def one(win):
        out = dot_nn(a1_ref[win, :], weight)
        if part == 0:
            out = out * HEAD_DIM**-0.5
        t_ref[win, pl.ds(part * width, width)] = out.astype(BF)

    tiles(a1_ref.shape[0], one)


def qkv_kernel(x_ref, vec, w_ref, t_ref, a1_ref):
    qkv_norm(x_ref, vec, a1_ref)
    for part in range(3):
        qkv_block(a1_ref, w_ref, t_ref, part)


def middle_step(x_ref, o_ref, vec, wo_ref, m_ref, a2_ref):
    def one(win):
        middle = x_ref[win, :].astype(F32) + (dot_nn(o_ref[win, :], wo_ref[...]) + vec[2:3, :])
        m_ref[win, :] = middle
        unit, _ = norm_parts(middle)
        a2_ref[win, :] = (unit * vec[3:4, :] + vec[4:5, :]).astype(BF)

    tiles(x_ref.shape[0], one)


def chunk_step(first, bias, a2_ref, dy_ref, we_ref, wc_ref, h_ref, du_ref, y_ref, da2_ref, be_ref):
    be_ref[...] = jnp.zeros_like(be_ref)

    def one(win):
        hidden, slope = gelu_pair(dot_nn(a2_ref[win, :], we_ref[...]) + bias)
        hidden = hidden.astype(BF)
        h_ref[win, :] = hidden
        du = (dot_nt(dy_ref[win, :], wc_ref[...]) * slope).astype(BF)
        du_ref[win, :] = du
        be_ref[...] += column_sum(du.astype(F32))
        y = dot_nn(hidden, wc_ref[...])
        da2 = dot_nt(du, we_ref[...])
        if first is True:
            y_ref[win, :] = y
            da2_ref[win, :] = da2
        else:
            y_ref[win, :] += y
            da2_ref[win, :] += da2

    tiles(a2_ref.shape[0], one)


def middle_back(live_rows, m_ref, y_ref, dy_ref, da2_ref, vec, wo_ref, out_ref, dm_ref, dz_ref, do_ref, sums):
    sums[...] = jnp.zeros_like(sums)

    def one(win):
        middle = m_ref[win, :]
        out_ref[win, :] = (middle + (y_ref[win, :] + vec[5:6, :])).astype(BF)
        unit, scale = norm_parts(middle)
        da2 = da2_ref[win, :]
        dy = dy_ref[win, :].astype(F32)
        dm = dy + norm_back(da2, vec[3:4, :], unit, scale)
        dm_ref[win, :] = dm
        dz = dm.astype(BF)
        dz_ref[win, :] = dz
        do_ref[win, :] = dot_nt(dz, wo_ref[...]).astype(BF)
        sums[0:1, :] += column_sum(da2 * unit)
        sums[1:2, :] += column_sum(da2)
        sums[2:3, :] += column_sum(dz.astype(F32))
        sums[3:4, :] += column_sum(dy)

    tiles(m_ref.shape[0], one)


def feed_kernel(
    x_ref, o_ref, dy_ref, vec, wo_ref, we_ref, wc_ref,
    out_ref, dm_ref, do_ref, gwo_ref, gwe_ref, gwc_ref, sums, be_ref,
    m_ref, a2_ref, h_ref, du_ref, y_ref, da2_ref, dz_ref,
):
    middle_step(x_ref, o_ref, vec, wo_ref, m_ref, a2_ref)
    for j in range(4):
        chunk_step(
            j == 0, vec[6 + j : 7 + j, :], a2_ref, dy_ref, we_ref.at[j], wc_ref.at[j],
            h_ref, du_ref, y_ref, da2_ref, be_ref.at[pl.ds(8 * j, 1)],
        )
        gwc_ref[j] = dot_tn(h_ref[...], dy_ref[...]).astype(BF)
        gwe_ref[j] = dot_tn(a2_ref[...], du_ref[...]).astype(BF)
    middle_back(None, m_ref, y_ref, dy_ref, da2_ref, vec, wo_ref, out_ref, dm_ref, dz_ref, do_ref, sums)
    gwo_ref[...] = dot_tn(o_ref[...], dz_ref[...]).astype(BF)


def first_back(x_ref, dt_ref, dm_ref, vec, w_refs, pg_ref, sums):
    sums[...] = jnp.zeros_like(sums)
    width = x_ref.shape[1]

    def one(win):
        da1 = dot_nt(dt_ref[win, pl.ds(0, width)], w_refs[0][...])
        da1 += dot_nt(dt_ref[win, pl.ds(width, width)], w_refs[1][...])
        da1 += dot_nt(dt_ref[win, pl.ds(2 * width, width)], w_refs[2][...])
        unit, scale = norm_parts(x_ref[win, :].astype(F32))
        pg_ref[win, :] = dm_ref[win, :] + norm_back(da1, vec[0:1, :], unit, scale)
        sums[0:1, :] += column_sum(da1 * unit)
        sums[1:2, :] += column_sum(da1)

    tiles(x_ref.shape[0], one)


def first_kernel(x_ref, a1_ref, dt_ref, dm_ref, vec, w_ref, pg_ref, gwi_ref, sums):
    width = x_ref.shape[1]
    for part in range(3):
        gwi_ref[part] = dot_tn(a1_ref[...], dt_ref[:, pl.ds(part * width, width)]).astype(BF)
    first_back(x_ref, dt_ref, dm_ref, vec, [w_ref.at[p] for p in range(3)], pg_ref, sums)


VM = pl.BlockSpec(memory_space=pltpu.VMEM)
SM = pl.BlockSpec(memory_space=pltpu.SMEM)


def vmem_call(kernel, name, ins, outs, scratch=(), smem=0):
    return pl.pallas_call(
        kernel,
        out_shape=[jax.ShapeDtypeStruct(s, d) for s, d in outs],
        in_specs=[SM] * smem + [VM] * (len(ins) - smem),
        out_specs=[VM] * len(outs),
        scratch_shapes=[pltpu.VMEM(s, d) for s, d in scratch],
        compiler_params=pltpu.CompilerParams(vmem_limit_bytes=60 * 2**20),
        name=name,
    )(*ins)


MESH = pl.DeviceIdType.MESH


class Place:
    def __init__(self, parts, sh, width):
        mine, copy = lax.axis_index("fsdp"), lax.axis_index("rep")
        self.outer_count = parts // 2
        self.outer, self.inner = mine // 2, mine % 2
        self.plane, self.core = copy // 2, copy % 2
        self.third = sh // 3
        self.half = width // 2

    def device(self, outer=None, inner=None, plane=None, core=None):
        outer = self.outer if outer is None else outer
        inner = self.inner if inner is None else inner
        plane = self.plane if plane is None else plane
        core = self.core if core is None else core
        return (outer * 2 + inner, plane * 2 + core)

    def far(self, k):
        return (self.outer + k) % self.outer_count

    def ranks(self):
        return range(1, self.outer_count)

    def columns(self, core=None):
        core = self.core if core is None else core
        return pl.ds(pl.multiple_of(core * self.half, 128), self.half)

    def held(self):
        return pl.ds(pl.multiple_of(self.plane * self.third, 16), 2 * self.third)

    def own(self, plane=None):
        plane = self.plane if plane is None else plane
        return pl.ds(pl.multiple_of(plane * (2 * self.third), 16), self.third)

    def peers(self):
        return [self.device(outer=self.far(k)) for k in self.ranks()] + [
            self.device(inner=1 - self.inner),
            self.device(plane=1 - self.plane),
            self.device(core=1 - self.core),
        ]

    def greet(self):
        barrier = pltpu.get_barrier_semaphore()
        peers = self.peers()
        for peer in peers:
            pl.semaphore_signal(barrier, inc=1, device_id=peer, device_id_type=MESH)
        pl.semaphore_wait(barrier, len(peers))


def remote(src, dst, sems, index, device):
    return pltpu.make_async_remote_copy(
        src_ref=src, dst_ref=dst, send_sem=sems[0].at[index], recv_sem=sems[1].at[index],
        device_id=device, device_id_type=MESH,
    )


def start(copies):
    for copy in copies:
        copy.start()


def landed(copies):
    for copy in copies:
        copy.wait_recv()


def sent(copies):
    for copy in copies:
        copy.wait_send()


class Gather:
    def __init__(self, place, shard, full, sems):
        self.p, self.shard, self.full, self.sems = place, shard, full, sems

    def far(self, b):
        p = self.p
        return [
            remote(
                self.shard.at[b, p.held(), p.columns()],
                self.full.at[b, p.outer, p.inner, p.held(), p.columns()],
                self.sems, (b, k - 1), p.device(outer=p.far(k)),
            )
            for k in p.ranks()
        ]

    def pair(self, b, which):
        p = self.p
        if which == 0:
            ref = self.full.at[b, :, p.inner, p.held(), p.columns()]
            device = p.device(inner=1 - p.inner)
        elif which == 1:
            ref = self.full.at[b, :, :, p.own(), p.columns()]
            device = p.device(plane=1 - p.plane)
        else:
            ref = self.full.at[b, :, :, :, p.columns()]
            device = p.device(core=1 - p.core)
        return [remote(ref, ref, self.sems, (b, p.outer_count - 1 + which), device)]

    def put_own(self, b):
        p = self.p
        self.full[b, p.outer, p.inner, p.held(), p.columns()] = self.shard[b, p.held(), p.columns()]

    def step(self, s, count, lag):
        for stage in range(5):
            @pl.when((s >= stage * lag) & (s < count + stage * lag))
            def _():
                self.stage(s - stage * lag, stage)

    def stage(self, b, stage):
        if stage == 0:
            start(self.far(b))
            self.put_own(b)
        else:
            landed(self.far(b) if stage == 1 else self.pair(b, stage - 2))
            if stage < 4:
                start(self.pair(b, stage - 1))

    def finish(self, count):
        @pl.loop(0, count)
        def _(b):
            sent(self.far(b))
            for which in range(3):
                sent(self.pair(b, which))


def gather_sems(blocks, parts):
    shape = (blocks, parts // 2 - 1 + 3)
    return [pltpu.SemaphoreType.DMA(shape), pltpu.SemaphoreType.DMA(shape)]


class Reduce:
    def __init__(self, place, grad, out, bufs, sems):
        self.p, self.grad, self.out, self.sems = place, grad, out, sems
        self.from_core, self.from_plane, self.from_inner, self.from_far, self.part, self.from_part = bufs

    @staticmethod
    def scratch(blocks, parts, sh, width):
        outer, third, half = parts // 2, sh // 3, width // 2
        shape = (blocks, outer - 1 + 5)
        return [
            pltpu.VMEM((blocks, outer, 2, sh, half), BF),
            pltpu.VMEM((blocks, outer, 2, third, half), BF),
            pltpu.VMEM((blocks, outer, 2 * third, half), BF),
            pltpu.VMEM((blocks, outer - 1, 2 * third, half), BF),
            pltpu.VMEM((blocks, 2 * third, half), BF),
            pltpu.VMEM((blocks, 2 * third, half), BF),
            pltpu.SemaphoreType.DMA(shape),
            pltpu.SemaphoreType.DMA(shape),
        ]

    def copies(self, b, stage):
        p = self.p
        base = p.outer_count - 1
        if stage == 0:
            src, dst = self.grad.at[b, :, :, :, p.columns(1 - p.core)], self.from_core.at[b]
            device = p.device(core=1 - p.core)
        elif stage == 1:
            src, dst = self.grad.at[b, :, :, p.own(1 - p.plane), p.columns()], self.from_plane.at[b]
            device = p.device(plane=1 - p.plane)
        elif stage == 2:
            src, dst = self.grad.at[b, :, 1 - p.inner, p.held(), p.columns()], self.from_inner.at[b]
            device = p.device(inner=1 - p.inner)
        elif stage == 3:
            return [
                remote(
                    self.grad.at[b, p.far(k), p.inner, p.held(), p.columns()],
                    self.from_far.at[b, k - 1], self.sems, (b, k - 1), p.device(outer=p.far(k)),
                )
                for k in p.ranks()
            ]
        elif stage == 4:
            src, dst = self.part.at[b], self.from_part.at[b]
            device = p.device(plane=1 - p.plane)
        else:
            src = dst = self.out.at[b, :, p.columns()]
            device = p.device(core=1 - p.core)
        return [remote(src, dst, self.sems, (b, base + (stage if stage < 3 else stage - 1)), device)]

    def add(self, b, stage):
        p = self.p
        if stage == 0:
            @pl.loop(0, p.outer_count)
            def _(o):
                for i in range(2):
                    index = (b, o, i, slice(None), p.columns())
                    self.grad[index] = (self.grad[index].astype(F32) + self.from_core[b, o, i].astype(F32)).astype(BF)
        elif stage == 1:
            for i in range(2):
                @pl.loop(0, p.outer_count)
                def _(o):
                    index = (b, o, i, p.own(), p.columns())
                    self.grad[index] = (self.grad[index].astype(F32) + self.from_plane[b, o, i].astype(F32)).astype(BF)
        elif stage == 2:
            @pl.loop(0, p.outer_count)
            def _(o):
                index = (b, o, p.inner, p.held(), p.columns())
                self.grad[index] = (self.grad[index].astype(F32) + self.from_inner[b, o].astype(F32)).astype(BF)
        elif stage == 3:
            total = self.grad[b, p.outer, p.inner, p.held(), p.columns()].astype(F32)
            for k in p.ranks():
                total += self.from_far[b, k - 1].astype(F32)
            self.part[b] = total.astype(BF)
        elif stage == 4:
            third = p.third
            for plane in range(2):
                @pl.when(p.plane == plane)
                def _():
                    mine, other = self.part, self.from_part
                    first, last = (mine, other) if plane == 0 else (other, mine)
                    self.out[b, pl.ds(0, third), p.columns()] = first[b, pl.ds(0, third), :]
                    middle = first[b, pl.ds(third, third), :].astype(F32) + last[b, pl.ds(0, third), :].astype(F32)
                    self.out[b, pl.ds(third, third), p.columns()] = middle.astype(BF)
                    self.out[b, pl.ds(2 * third, third), p.columns()] = last[b, pl.ds(third, third), :]

    def stage(self, b, stage):
        if stage > 0:
            landed(self.copies(b, stage - 1))
            self.add(b, stage - 1)
        if stage < 6:
            start(self.copies(b, stage))

    def step(self, s, count, lag):
        for stage in range(7):
            @pl.when((s >= stage * lag) & (s < count + stage * lag))
            def _():
                self.stage(s - stage * lag, stage)

    def finish(self, count):
        @pl.loop(0, count)
        def _(b):
            for stage in range(6):
                sent(self.copies(b, stage))


class Vector:
    def __init__(self, place, total, bufs, sems, everywhere):
        self.p, self.total, self.sems = place, total, sems
        self.pairs, self.fars = bufs
        self.order = (0, 1, 2) if everywhere else (2,)

    @staticmethod
    def scratch(parts, shape, dtype):
        sems = (parts // 2 - 1 + 3,)
        return [
            pltpu.VMEM((6,) + shape, dtype), pltpu.VMEM((parts // 2,) + shape, dtype),
            pltpu.SemaphoreType.DMA(sems), pltpu.SemaphoreType.DMA(sems),
        ]

    def pair(self, which):
        p = self.p
        device = (
            p.device(core=1 - p.core), p.device(plane=1 - p.plane), p.device(inner=1 - p.inner)
        )[which]
        return [remote(self.pairs.at[2 * which], self.pairs.at[2 * which + 1], self.sems, p.outer_count - 1 + which, device)]

    def far(self):
        p = self.p
        mine = self.fars.at[p.outer]
        return [remote(mine, mine, self.sems, k - 1, p.device(outer=p.far(k))) for k in p.ranks()]

    def far_landed(self):
        p = self.p
        for k in p.ranks():
            theirs = self.fars.at[(p.outer + p.outer_count - k) % p.outer_count]
            remote(theirs, theirs, self.sems, k - 1, p.device(outer=p.far(k))).wait_recv()

    def stage(self, number):
        order = self.order
        if number > 0 and number <= len(order):
            which = order[number - 1]
            landed(self.pair(which))
            self.total[...] = self.total[...] + self.pairs[2 * which + 1]
        if number < len(order):
            which = order[number]
            self.pairs[2 * which] = self.total[...]
            start(self.pair(which))
        elif number == len(order):
            self.fars[self.p.outer] = self.total[...]
            start(self.far())
        else:
            self.far_landed()
            total = self.fars[0]
            for o in range(1, self.p.outer_count):
                total = total + self.fars[o]
            self.total[...] = total

    def stages(self):
        return len(self.order) + 2

    def finish(self):
        for which in self.order:
            sent(self.pair(which))
        sent(self.far())


FIRST_BLOCKS = 10


TILES = 3


def flat(ref, b):
    block = ref[b]
    return block.reshape(block.shape[0] * block.shape[1] * block.shape[2], block.shape[3])


def one_hot(shape, shift, along):
    row = lax.broadcasted_iota(jnp.int32, shape, 0)
    column = lax.broadcasted_iota(jnp.int32, shape, 1)
    return jnp.where((column - row if along else row - column) == shift, 1.0, 0.0)


def place_vectors(parts, vector, vec):
    sh, width = vector.shape[1], vec.shape[1]
    mine, apart = lax.axis_index("fsdp"), parts // 4
    low = vector[...].astype(BF)
    vec[...] = jnp.zeros_like(vec)
    vec[0:6, :] = dot_nn(low, one_hot((sh, width), mine * sh, True).astype(BF))[0:6, :]
    row = lax.broadcasted_iota(jnp.int32, (4, width), 0)
    for i in range(4):
        spot = one_hot((sh, width), (apart * i + mine // 4) * sh, True).astype(BF)
        vec[6:10, :] += jnp.where(row == mine % 4, dot_nn(low, spot)[6 + i : 7 + i, :], 0.0)


def gather_kernel(
    parts, x_ref, vector, wi_ref, wo_ref, we_ref, wc_ref,
    t_out, a1_ref, xp_ref, wi_out, wo_out, ff_out, rest_out, vec, t_ref, full, shard, local, *scratch
):
    count, width = x_ref.shape
    rows = xp_ref.shape[0]
    sh = wo_ref.shape[0]
    place = Place(parts, sh, width)
    weights = Gather(place, shard, full, scratch[0:2])
    vectors = Vector(place, vec, scratch[2:4], scratch[4:6], False)

    def pack_chunk(j, we_to, wc_to):
        for p in range(parts):
            we_to[:, pl.ds(p * sh, sh)] = we_ref[:, pl.ds((4 * p + j) * sh, sh)].astype(BF)
        wc_to[...] = wc_ref[pl.ds(j * sh, sh), :].astype(BF)

    shard[0] = wi_ref[:, pl.ds(0, width)].astype(BF)
    place.greet()
    weights.step(0, FIRST_BLOCKS, 1)
    place_vectors(parts, vector, vec)
    vectors.stage(0)
    for part in range(1, 3):
        shard[part] = wi_ref[:, pl.ds(part * width, width)].astype(BF)
    shard[3] = wo_ref[...].astype(BF)
    weights.step(1, FIRST_BLOCKS, 1)
    vectors.stage(1)
    tail = count // 16 * 16
    xp_ref[pl.ds(tail, rows - tail), :] = jnp.zeros((rows - tail, width), BF)
    xp_ref[pl.ds(0, count), :] = x_ref[...]
    weights.step(2, FIRST_BLOCKS, 1)
    vectors.stage(2)
    pack_chunk(0, shard.at[4], shard.at[5])
    weights.step(3, FIRST_BLOCKS, 1)
    qkv_norm(xp_ref, vec, a1_ref)
    leaving = []
    for s in range(4, FIRST_BLOCKS + 4):
        b = s - 4
        weights.step(s, FIRST_BLOCKS, 1)
        out = wi_out.at[b] if b < 3 else wo_out.at[0] if b == 3 else ff_out.at[b - 4]
        leaving.append(pltpu.make_async_copy(full.at[b], out, local.at[b]))
        leaving[-1].start()
        if b < 2:
            pack_chunk(b + 1, shard.at[2 * b + 6], shard.at[2 * b + 7])
        if b == 3:
            pack_chunk(3, rest_out.at[0], rest_out.at[1])
        if b < 3:
            qkv_block(a1_ref, full, t_ref, b)
            part = pl.ds(b * width, width)
            leaving.append(pltpu.make_async_copy(t_ref.at[:, part], t_out.at[:, part], local.at[FIRST_BLOCKS + b]))
            leaving[-1].start()
    for copy in leaving:
        copy.wait()
    weights.finish(FIRST_BLOCKS)
    vectors.finish()


def feed_comm_kernel(
    parts, x_ref, o_ref, dy_ref, vec, wo_ref, early, shard,
    out_ref, dm_ref, do_ref, dz_ref, grad_out, grad_rest, sums, be_ref,
    a2_ref, y_ref, da2_ref, full, grad, local, *scratch,
):
    rows, width = x_ref.shape
    sh = shard.shape[1]
    place = Place(parts, sh, width)
    later, have = shard.shape[0], early.shape[0]
    weights = Gather(place, shard, full.at[pl.ds(have, later)], scratch[0:2])
    grads = Reduce(place, grad.at[pl.ds(0, 4)], grad_out, scratch[2:8], scratch[8:10])
    du_ref, h_ref = do_ref, dz_ref
    ready = [pltpu.make_async_copy(early, full.at[pl.ds(0, have)], local.at[0])]
    start(ready)
    place.greet()

    def win(i):
        return pl.ds(i * RT, RT)

    def slot(number):
        for b in range(2):
            for stage, at in enumerate((0, 4, 8, 12, 16)):
                due = at + 2 * b
                if isinstance(number, int):
                    if due == number:
                        weights.stage(b, stage)
                elif due >= 4:
                    @pl.when(number == due)
                    def _():
                        weights.stage(b, stage)

    wo = flat(wo_ref, 0)
    slot(0)
    for i in range(TILES):
        middle = x_ref[win(i), :].astype(F32) + (dot_nn(o_ref[win(i), :], wo) + vec[2:3, :])
        dm_ref[win(i), :] = middle
        unit, _ = norm_parts(middle)
        a2_ref[win(i), :] = (unit * vec[3:4, :] + vec[4:5, :]).astype(BF)
        y_ref[win(i), :] = jnp.zeros((RT, width), F32)
        da2_ref[win(i), :] = jnp.zeros((RT, width), F32)
        slot(i + 1)
    for copy in ready:
        copy.wait()

    def leave(b):
        return pltpu.make_async_copy(grad.at[b], grad_rest.at[b - 4], local.at[b - 3])

    def due(position, back, parity):
        steps = position - 3 - parity + 5 * back
        return steps // 3 if steps % 3 == 0 and 0 <= steps <= 18 else None

    def passing(j, position):
        for back in range(4, -1, -1):
            for parity in range(2):
                stage = due(position, back, parity)
                if stage is None or back == 4:
                    continue

                @pl.when((j >= back) & (j < back + 2))
                def _():
                    grads.stage(2 * (j - back) + parity, stage)

    @pl.loop(0, 4)
    def _(j):
        bias = vec[pl.ds(6 + j, 1), :]
        be_sum = jnp.zeros((1, width), F32)
        for i in range(TILES):
            hidden, slope = gelu_pair(dot_nn(a2_ref[win(i), :], flat(full, 2 * j)) + bias)
            hidden = hidden.astype(BF)
            h_ref[win(i), :] = hidden
            du = (dot_nt(dy_ref[win(i), :], flat(full, 2 * j + 1)) * slope).astype(BF)
            du_ref[win(i), :] = du
            be_sum += column_sum(du.astype(F32))
            y_ref[win(i), :] += dot_nn(hidden, flat(full, 2 * j + 1))
            da2_ref[win(i), :] += dot_nt(du, flat(full, 2 * j))
            slot(4 + 5 * j + i)
            passing(j, i)
        be_ref[pl.ds(j, 1), :] = be_sum
        grad[2 * j] = dot_tn(h_ref[...], dy_ref[...]).astype(BF).reshape(grad.shape[1:])
        slot(4 + 5 * j + 3)
        passing(j, 3)
        grad[2 * j + 1] = dot_tn(a2_ref[...], du_ref[...]).astype(BF).reshape(grad.shape[1:])
        slot(4 + 5 * j + 4)
        passing(j, 4)

        @pl.when(j >= 2)
        def _():
            for parity in range(2):
                leave(2 * j + parity).start()

    sums[...] = jnp.zeros_like(sums)
    for position in range(5, 13):
        i = position - 5
        if i < TILES:
            middle = dm_ref[win(i), :]
            out_ref[win(i), :] = (middle + (y_ref[win(i), :] + vec[5:6, :])).astype(BF)
            unit, scale = norm_parts(middle)
            da2 = da2_ref[win(i), :]
            dy = dy_ref[win(i), :].astype(F32)
            dm = dy + norm_back(da2, vec[3:4, :], unit, scale)
            dm_ref[win(i), :] = dm
            dz = dm.astype(BF)
            dz_ref[win(i), :] = dz
            do_ref[win(i), :] = dot_nt(dz, wo).astype(BF)
            sums[0:1, :] += column_sum(da2 * unit)
            sums[1:2, :] += column_sum(da2)
            sums[2:3, :] += column_sum(dz.astype(F32))
            sums[3:4, :] += column_sum(dy)
        for j in range(0, 2):
            for parity in range(2):
                stage = due(position + 5 * (3 - j), 0, parity)
                if stage is not None:
                    grads.stage(2 * j + parity, stage)
    weights.finish(later)
    grads.finish(4)
    for b in range(4, 8):
        leave(b).wait()


LAST_BLOCKS = 8


def first_comm_kernel(
    parts, x_in, a1_in, o_in, dz_in, dt_in, dm_in, vec, wi_in, sums_two, be_ref, rest_in,
    pg_ref, grad_out, total, grad, x_ref, a1_ref, o_ref, dz_ref, dt_ref, dm_ref, wi_ref, local, *scratch,
):
    rows, width = x_ref.shape
    place = Place(parts, width // parts, width)
    grads = Reduce(place, grad, grad_out, scratch[0:6], scratch[6:8])
    vectors = Vector(place, total, scratch[8:10], scratch[10:12], True)
    arriving = [
        pltpu.make_async_copy(rest_in.at[pl.ds(0, 2)], grad.at[pl.ds(0, 2)], local.at[0]),
        pltpu.make_async_copy(rest_in.at[pl.ds(2, 2)], grad.at[pl.ds(2, 2)], local.at[1]),
    ] + [
        pltpu.make_async_copy(source, ref, local.at[2 + i])
        for i, (source, ref) in enumerate(
            ((o_in, o_ref), (dz_in, dz_ref), (a1_in, a1_ref), (dt_in, dt_ref), (wi_in, wi_ref), (x_in, x_ref), (dm_in, dm_ref))
        )
    ]
    start(arriving)
    place.greet()
    total[...] = jnp.zeros_like(total)
    total[2:3, :] = sums_two[2:3, :]
    total[3:5, :] = sums_two[0:2, :]
    total[5:6, :] = sums_two[3:4, :]
    total[6:10, :] = be_ref[0:4, :]

    def step(s):
        grads.step(s, LAST_BLOCKS, 1)

    arriving[0].wait()
    step(0)
    arriving[1].wait()
    for i in (2, 3):
        arriving[i].wait()
    grad[4] = dot_tn(o_ref[...], dz_ref[...]).astype(BF).reshape(grad.shape[1:])
    step(1)
    for i in (4, 5):
        arriving[i].wait()
    for part in range(3):
        block = dot_tn(a1_ref[...], dt_ref[:, pl.ds(part * width, width)]).astype(BF)
        grad[part + 5] = block.reshape(grad.shape[1:])
        step(part + 2)
    for i in (6, 7, 8):
        arriving[i].wait()
    for i in range(TILES):
        win = pl.ds(i * RT, RT)
        da1 = dot_nt(dt_ref[win, pl.ds(0, width)], flat(wi_ref, 0))
        da1 += dot_nt(dt_ref[win, pl.ds(width, width)], flat(wi_ref, 1))
        da1 += dot_nt(dt_ref[win, pl.ds(2 * width, width)], flat(wi_ref, 2))
        unit, scale = norm_parts(x_ref[win, :].astype(F32))
        pg_ref[win, :] = dm_ref[win, :] + norm_back(da1, vec[0:1, :], unit, scale)
        total[0:1, :] += column_sum(da1 * unit)
        total[1:2, :] += column_sum(da1)
        step(5 + i)
    for s in range(8, LAST_BLOCKS + 6):
        if s - 8 < vectors.stages():
            vectors.stage(s - 8)
        step(s)
    grads.finish(LAST_BLOCKS)
    vectors.finish()


def comm_call(kernel, name, which, ins, outs, scratch, far=(), far_out=()):
    return pl.pallas_call(
        kernel,
        out_shape=[jax.ShapeDtypeStruct(s, d) for s, d in outs],
        in_specs=[pl.BlockSpec(memory_space=pl.ANY) if i in far else VM for i in range(len(ins))],
        out_specs=[pl.BlockSpec(memory_space=pl.ANY) if i in far_out else VM for i in range(len(outs))],
        scratch_shapes=scratch,
        compiler_params=pltpu.CompilerParams(
            vmem_limit_bytes=62 * 2**20, collective_id=which, has_side_effects=True
        ),
        name=name,
    )(*ins)


STEPS = 6


def extract_vectors(parts, total, picked):
    sh, width = picked.shape[1], total.shape[1]
    mine, apart = lax.axis_index("fsdp"), parts // 4

    def pick(rows, shift):
        return jnp.dot(
            rows, one_hot((width, sh), shift, False), precision=lax.Precision.HIGHEST, preferred_element_type=F32
        )

    picked[0:8, :] = pick(total[0:8, :], mine * sh)
    held = total[6:10, :]
    row = lax.broadcasted_iota(jnp.int32, held.shape, 0)
    held = jnp.sum(jnp.where(row == mine % 4, held, 0.0), axis=0, keepdims=True)
    held = jnp.broadcast_to(held, (8, width))
    for i in range(4):
        picked[6 + i : 7 + i, :] = pick(held, (apart * i + mine // 4) * sh)[0:1, :]


def update_kernel(rates, g_two, g_one, total, out_in, pg_in, *refs):
    state, outs, picked, flat_we = refs[:15], refs[15:42], refs[42], refs[43]
    i = pl.program_id(0)
    sh, width = g_one.shape[1:]
    parts = width // sh

    @pl.when(i == 0)
    def _():
        extract_vectors(parts, total, picked)
        for j in range(4):
            for p in range(parts):
                block = g_two[2 * j + 1] if j < 2 else g_one[2 * j - 3]
                flat_we[:, pl.ds((4 * p + j) * sh, sh)] = block[:, p * sh : (p + 1) * sh].astype(F32)

    outs[0][...] = out_in[...]
    outs[1][...] = pg_in[...]
    half, sixth = width // 2, width // STEPS
    odd = pl.ds(pl.multiple_of(i % 2 * half, 128), half)
    third = sh // 3

    def contract_rows(k):
        rows = pl.ds(pl.multiple_of(k % 3 * third, 16), third)
        j = k // 3
        low, high = g_two[2 * jnp.minimum(j, 1), rows, :], g_one[2 * jnp.maximum(j, 2) - 4, rows, :]
        return jnp.where(j < 2, low.astype(F32), high.astype(F32))

    sums = (
        g_one[5 + i // 2, :, odd].astype(F32),
        g_one[4, :, pl.ds(pl.multiple_of(i * sixth, 128), sixth)].astype(F32),
        flat_we[:, pl.ds(pl.multiple_of(i * 4 * sixth, 128), 4 * sixth)],
        jnp.concatenate([contract_rows(2 * i), contract_rows(2 * i + 1)], axis=0),
        picked[0:10, :],
    )
    for member in range(5):
        weight, moment, average = (ref[...] for ref in state[3 * member : 3 * member + 3])
        for ref, value in zip(
            outs[2 + 5 * member : 7 + 5 * member], step(sums[member], rates[member], weight, moment, average)
        ):
            ref[...] = value


def update(rates, count, g_two, g_one, total, out, pg, masters, moments, averages):
    sh, width = g_one.shape[1:]
    across = [
        pl.BlockSpec((sh, width // 2), lambda i: (0, i)),
        pl.BlockSpec((sh, width // STEPS), lambda i: (0, i)),
        pl.BlockSpec((sh, 4 * width // STEPS), lambda i: (0, i)),
        pl.BlockSpec((4 * sh // STEPS, width), lambda i: (i, 0)),
        pl.BlockSpec(masters[4].shape, lambda i: (0, 0)),
    ]
    rows = (count + STEPS - 1) // STEPS
    by_row = pl.BlockSpec(((rows + 15) // 16 * 16, width), lambda i: (i, 0))
    ins, specs = [], []
    outs = [jax.ShapeDtypeStruct((count, width), BF), jax.ShapeDtypeStruct((count, width), F32)]
    out_specs = [by_row] * 2
    for member in range(5):
        ins += [masters[member], moments[member], averages[member]]
        specs += [across[member]] * 3
        shape = masters[member].shape
        outs += [jax.ShapeDtypeStruct(shape, F32)] * 4 + [jax.ShapeDtypeStruct(shape, BF)]
        out_specs += [across[member]] * 5
    return pl.pallas_call(
        functools.partial(update_kernel, rates),
        grid=(STEPS,),
        out_shape=outs,
        in_specs=[pl.BlockSpec(g.shape, lambda i: (0, 0, 0)) for g in (g_two, g_one)]
        + [pl.BlockSpec(total.shape, lambda i: (0, 0))] + [by_row] * 2 + specs,
        out_specs=out_specs,
        scratch_shapes=[pltpu.VMEM((16, sh), F32), pltpu.VMEM((sh, 4 * width), F32)],
        compiler_params=pltpu.CompilerParams(vmem_limit_bytes=48 * 2**20),
        name="momentum_step",
    )(g_two, g_one, total, out, pg, *ins)


def run_qkv(x, vec, wi):
    rows, width = x.shape
    return vmem_call(
        qkv_kernel, "project_in", (x, vec, wi), [((rows, 3 * width), BF), ((rows, width), BF)]
    )


def run_feed(x, o, dy, vec, wo, we, wc):
    rows, width = x.shape
    wide, low = ((rows, width), F32), ((rows, width), BF)
    return vmem_call(
        feed_kernel, "feed_forward", (x, o, dy, vec, wo, we, wc),
        [low, wide, low, ((width, width), BF), ((4, width, width), BF), ((4, width, width), BF),
         ((8, width), F32), ((32, width), F32)],
        [wide, low, low, low, wide, wide, low],
    )


def run_first(x, a1, dt, dm, vec, wi):
    rows, width = x.shape
    return vmem_call(
        first_kernel, "project_in_back", (x, a1, dt, dm, vec, wi),
        [((rows, width), F32), ((3, width, width), BF), ((8, width), F32)],
    )


def pack_shards(wi, wo, we, wc, parts):
    rows, width = wo.shape
    wi = wi.reshape(rows, 3, width).swapaxes(0, 1)
    we = we.reshape(rows, parts, 4, rows).transpose(2, 0, 1, 3).reshape(4, rows, width)
    wc = wc.reshape(4, rows, width)
    return jnp.concatenate([wi, wo[None], we, wc], axis=0)


def unpack_shards(blocks, parts):
    rows, width = blocks.shape[1:]
    wi = blocks[0:3].swapaxes(0, 1).reshape(rows, 3 * width)
    we = blocks[4:8].reshape(4, rows, parts, rows).transpose(1, 2, 0, 3).reshape(rows, 4 * width)
    return wi, blocks[3], we, blocks[8:12].reshape(4 * rows, width)


def step(grad_sum, rate, weight, moment, average):
    moment_new = MOMENTUM * moment + grad_sum
    weight_new = weight - rate * (grad_sum + MOMENTUM * moment_new)
    average_new = AVERAGE * average + (1.0 - AVERAGE) * weight_new
    return [grad_sum, moment_new, weight_new, average_new, weight_new.astype(BF)]


def plain_path(patches, slot_clip, out_grad, masters, moments, averages, rates):
    parts, copies = lax.axis_size("fsdp"), lax.axis_size("rep")
    mine, copy = lax.axis_index("fsdp"), lax.axis_index("rep")
    count, width = patches.shape
    rows = (count + RT - 1) // RT * RT
    sh = width // parts
    packed = pack_shards(*(m.astype(BF) for m in masters[:4]), parts).reshape(12 * sh, width)
    piece = 12 * sh // copies
    quarter = lax.dynamic_slice_in_dim(packed, copy * piece, piece, 0)
    full = lax.all_gather(quarter, ("fsdp", "rep"), axis=0, tiled=True)
    full = full.reshape(parts, 12, sh, width).swapaxes(0, 1).reshape(12, width, width)
    vec = lax.all_gather(masters[4].astype(BF), "fsdp", axis=1, tiled=True).astype(F32)
    be = vec[6:].reshape(parts, 4, sh).swapaxes(0, 1).reshape(4, width)
    vec = jnp.concatenate([vec[:6], be, jnp.zeros((6, width), F32)], axis=0)

    pad = ((0, rows - count), (0, 0))
    x = jnp.pad(patches, pad)
    t, a1 = run_qkv(x, vec, full[0:3])
    o, dy = attend(slot_clip, t, out_grad)
    out, dm, do, gwo, gwe, gwc, sums_two, sums_be = run_feed(x, o, dy, vec, full[3], full[4:8], full[8:12])
    dt = attend_back(slot_clip, t, do)
    pg, gwi, sums_one = run_first(x, a1, dt, dm, vec, full[0:3])

    grads = jnp.concatenate([gwi, gwo[None], gwe, gwc], axis=0)
    grads = grads.reshape(12, parts, sh, width).swapaxes(0, 1).reshape(parts * 12 * sh, width)
    grads = lax.psum_scatter(grads, ("fsdp", "rep"), scatter_dimension=0, tiled=True)
    grads = lax.all_gather(grads, "rep", axis=0, tiled=True).reshape(12, sh, width)
    be_grad = sums_be[::8].reshape(4, parts, sh).swapaxes(0, 1).reshape(4, width)
    vector = jnp.concatenate(
        [sums_one[0:2], sums_two[2:3], sums_two[0:2], sums_two[3:4], be_grad], axis=0
    )
    vector = lax.dynamic_slice_in_dim(lax.psum(vector, ("fsdp", "rep")), mine * sh, sh, 1)
    outputs = []
    for member, grad in enumerate((*unpack_shards(grads, parts), vector)):
        outputs += step(grad.astype(F32), rates[member], masters[member], moments[member], averages[member])
    return (out[:count], pg[:count], *outputs)


def direct_path(patches, slot_clip, out_grad, masters, moments, averages, rates):
    parts = lax.axis_size("fsdp")
    count, width = patches.shape
    rows = (count + RT - 1) // RT * RT
    sh = width // parts
    block = (parts // 2, 2, sh, width)
    wide, low = ((rows, width), F32), ((rows, width), BF)
    t, a1, x, wi, wo, early, later, vec = comm_call(
        functools.partial(gather_kernel, parts), "gather_project_in", 0, (patches, masters[4], *masters[:4]),
        [((rows, 3 * width), BF), low, low, ((3,) + block, BF), ((1,) + block, BF),
         ((FIRST_BLOCKS - 4,) + block, BF), ((2, sh, width), BF), ((16, width), F32)],
        [pltpu.VMEM((rows, 3 * width), BF), pltpu.VMEM((FIRST_BLOCKS,) + block, BF),
         pltpu.VMEM((FIRST_BLOCKS, sh, width), BF), pltpu.SemaphoreType.DMA((FIRST_BLOCKS + 3,))]
        + gather_sems(FIRST_BLOCKS, parts) + Vector.scratch(parts, (16, width), F32),
        far_out=(0, 3, 4, 5),
    )
    o, dy = attend(slot_clip, t, out_grad)
    out, dm, do, dz, grads_two, rest, sums_two, sums_be = comm_call(
        functools.partial(feed_comm_kernel, parts), "feed_forward_reduce", 1,
        (x, o, dy, vec, wo, early, later),
        [low, wide, low, low, ((4, sh, width), BF), ((4,) + block, BF), ((8, width), F32), ((8, width), F32)],
        [pltpu.VMEM(*low), pltpu.VMEM(*wide), pltpu.VMEM(*wide),
         pltpu.VMEM((8,) + block, BF), pltpu.VMEM((8,) + block, BF), pltpu.SemaphoreType.DMA((5,))]
        + gather_sems(2, parts) + Reduce.scratch(4, parts, sh, width), far=(5,), far_out=(5,),
    )
    dt = attend_back(slot_clip, t, do)
    pg, grads_one, total = comm_call(
        functools.partial(first_comm_kernel, parts), "project_in_back_reduce", 2,
        (x, a1, o, dz, dt, dm, vec, wi, sums_two, sums_be, rest),
        [wide, ((LAST_BLOCKS, sh, width), BF), ((16, width), F32)],
        [pltpu.VMEM((LAST_BLOCKS,) + block, BF), pltpu.VMEM(*low), pltpu.VMEM(*low), pltpu.VMEM(*low),
         pltpu.VMEM(*low), pltpu.VMEM((rows, 3 * width), BF), pltpu.VMEM(*wide), pltpu.VMEM((3,) + block, BF),
         pltpu.SemaphoreType.DMA((9,))]
        + Reduce.scratch(LAST_BLOCKS, parts, sh, width) + Vector.scratch(parts, (16, width), F32),
        far=(0, 1, 2, 3, 4, 5, 7, 10),
    )
    return update(rates, count, grads_two, grads_one, total, out, pg, masters, moments, averages)


def on_device(
    patches, slot_clip, out_grad,
    project_in_weight, project_in_moment, project_in_average,
    project_out_weight, project_out_moment, project_out_average,
    expand_weight, expand_moment, expand_average,
    contract_weight, contract_moment, contract_average,
    vector_weight, vector_moment, vector_average,
):
    masters = (project_in_weight, project_out_weight, expand_weight, contract_weight, vector_weight)
    moments = (project_in_moment, project_out_moment, expand_moment, contract_moment, vector_moment)
    averages = (project_in_average, project_out_average, expand_average, contract_average, vector_average)
    parts, copies = lax.axis_size("fsdp"), lax.axis_size("rep")
    count, width = patches.shape
    direct = copies == 4 and parts % 4 == 0 and width // parts % 48 == 0
    path = direct_path if direct else plain_path
    tokens_all = count * parts * copies
    rates = [rate / tokens_all**0.5 for rate in RATES]
    return tuple(path(patches, slot_clip, out_grad, masters, moments, averages, rates))


def solution(mesh):
    tokens = P(("fsdp", "rep"), None)
    split, split_vector = P("fsdp", None), P(None, "fsdp")
    in_specs = (tokens, P(("fsdp", "rep")), tokens) + (split,) * 12 + (split_vector,) * 3
    out_specs = (tokens,) * 2 + (split,) * 20 + (split_vector,) * 5
    return jax.shard_map(on_device, mesh=mesh, in_specs=in_specs, out_specs=out_specs, check_vma=False)
```

```python
import functools
import math

import jax
import jax.numpy as jnp
from jax import lax
from jax.sharding import PartitionSpec as P
import jax.experimental.pallas as pl
import jax.experimental.pallas.tpu as pltpu

BF, F32 = jnp.bfloat16, jnp.float32
HEAD_DIM = 64
SLOT = 49
LIVE_MAX = 8
WIN = 416
EPSILON = 1e-06
MOMENTUM = 0.5
AVERAGE = 0.5
RATES = (0.3, 0.3, 0.1, 0.03, 0.5)
NEG = -1e30

def dg(a,b,ca,cb):
    return lax.dot_general(a,b,(((ca,),(cb,)),((),())),preferred_element_type=F32)

def both(x, lane):
    keep = (lane < 64).astype(BF)
    return jnp.concatenate([x*keep, x*(1-keep)], axis=0)

def group_end(clips, start, slots):
    end = start+1
    for e in range(2, LIVE_MAX+1):
        cand = start+e
        safe = jnp.minimum(cand, slots-1)
        edge = (cand == slots) | ((cand < slots) & ((clips[safe] != clips[jnp.maximum(safe-1,0)]) | (clips[safe] < 0)))
        end = jnp.where(edge, cand, end)
    return end

def fill_bias(clips, w0, start, end, bias):
    def keys(shape, dim):
        row = lax.broadcasted_iota(jnp.int32, shape, dim) + w0
        slot = (row*1338) >> 16
        key = -1-row
        for ahead in range(LIVE_MAX):
            s = start+ahead
            clip = clips[jnp.minimum(s, clips.shape[0]-1)]
            key = jnp.where((slot == s) & (s < end) & (clip >= 0), clip, key)
        return key
    bias[...] = jnp.where(keys((WIN,1),0) == keys((1,WIN),1), 0.0, NEG)

def clear_tail(ref, slots):
    tail = slots*SLOT//16*16
    ref[pl.ds(tail, ref.shape[0]-tail), :] = jnp.zeros((ref.shape[0]-tail, ref.shape[1]), BF)

def fwd_kernel(clips, t_ref, g_ref, o_ref, dy_ref, log_ref, bias):
    slots = clips.shape[0]
    rows = t_ref.shape[0]; D = o_ref.shape[1]
    clear_tail(o_ref, slots)
    clear_tail(dy_ref, slots)
    log_ref[...] = jnp.zeros_like(log_ref)
    live = lax.fori_loop(0, slots, lambda s, n: n + jnp.where(clips[s] >= 0, SLOT, 0), 0)
    row = lax.broadcasted_iota(jnp.int32,(slots*SLOT,1),0)
    dy_ref[pl.ds(0,slots*SLOT), :] = jnp.where(row < live, g_ref[...].astype(F32), 0.0).astype(BF)
    def group(g, start):
        @pl.when(start < slots)
        def _():
            end = group_end(clips, start, slots)
            r0 = start*SLOT; r1 = end*SLOT
            w0 = pl.multiple_of(jnp.minimum((r0>>4)<<4, rows-WIN), 16)
            fill_bias(clips, w0, start, end, bias)
            rowi = lax.broadcasted_iota(jnp.int32,(WIN,128),0)+w0
            mine = (rowi >= r0) & (rowi < r1)
            lane = lax.broadcasted_iota(jnp.int32,(1,128),1)
            win = pl.ds(w0, WIN)
            logs = log_ref[win, :]
            for p in range(D//128):
                q = t_ref[win, pl.ds(p*128,128)]
                k = t_ref[win, pl.ds(D+p*128,128)]
                v = t_ref[win, pl.ds(2*D+p*128,128)]
                s = dg(both(q, lane), k, 1, 1)
                es, tops = [], []
                for h in range(2):
                    part = s[h*WIN:(h+1)*WIN] + bias[...]
                    top = jnp.max(part, axis=1, keepdims=True)
                    es.append(jnp.exp(part-top).astype(BF))
                    tops.append(top)
                ones = jnp.concatenate([v, jnp.ones_like(v)], axis=1)
                mixed = jnp.dot(jnp.concatenate(es, axis=0), ones, preferred_element_type=F32)
                outs = []
                for h in range(2):
                    total = mixed[h*WIN:(h+1)*WIN, 128:]
                    outs.append(mixed[h*WIN:(h+1)*WIN, :128] / total)
                    logs = jnp.where(mine & (lane == 2*p+h), tops[h] + jnp.log(total), logs)
                o = jnp.where(lane < 64, outs[0], outs[1])
                old = o_ref[win, pl.ds(p*128,128)]
                o_ref[win, pl.ds(p*128,128)] = jnp.where(mine, o, old.astype(F32)).astype(BF)
            log_ref[win, :] = logs
        return jnp.where(start < slots, group_end(clips, start, slots), start)
    lax.fori_loop(0, (2*slots)//(LIVE_MAX+1)+1, group, 0)

def bwd_kernel(clips, t_ref, do_ref, log_ref, inner_ref, dt_ref, bias):
    slots = clips.shape[0]
    rows = t_ref.shape[0]; D = do_ref.shape[1]
    clear_tail(dt_ref, slots)
    def group(g, start):
        @pl.when(start < slots)
        def _():
            end = group_end(clips, start, slots)
            r0 = start*SLOT; r1 = end*SLOT
            w0 = pl.multiple_of(jnp.minimum((r0>>4)<<4, rows-WIN), 16)
            fill_bias(clips, w0, start, end, bias)
            rowi = lax.broadcasted_iota(jnp.int32,(WIN,128),0)+w0
            mine = (rowi >= r0) & (rowi < r1)
            lane = lax.broadcasted_iota(jnp.int32,(1,128),1)
            win = pl.ds(w0, WIN)
            logs = log_ref[win, :].T
            inners = inner_ref[win, :].T
            for p in range(D//128):
                q = t_ref[win, pl.ds(p*128,128)]
                k = t_ref[win, pl.ds(D+p*128,128)]
                v = t_ref[win, pl.ds(2*D+p*128,128)]
                do = do_ref[win, pl.ds(p*128,128)]
                s = dg(both(k, lane), q, 1, 1)
                dp = dg(both(v, lane), do, 1, 1)
                pts, dss = [], []
                for h in range(2):
                    n = 2*p+h
                    rows_h = slice(h*WIN, (h+1)*WIN)
                    pt = jnp.exp((s[rows_h] + bias[...]) - logs[n:n+1, :])
                    dss.append((pt*(dp[rows_h]-inners[n:n+1, :])).astype(BF))
                    pts.append(pt.astype(BF))
                dv = jnp.dot(jnp.concatenate(pts, axis=0), do, preferred_element_type=F32)
                dk = jnp.dot(jnp.concatenate(dss, axis=0), q, preferred_element_type=F32)
                dq = jnp.dot(jnp.concatenate([d.T for d in dss], axis=0), k, preferred_element_type=F32)
                dqs, dks, dvs = ([x[:WIN], x[WIN:]] for x in (dq, dk, dv))
                for i,x in enumerate((dqs,dks,dvs)):
                    new = jnp.where(lane < 64, x[0], x[1]).astype(BF).astype(F32)
                    if i==0: new = new*(64**-0.5)
                    c = pl.ds(i*D+p*128,128)
                    old = dt_ref[win, c].astype(F32)
                    dt_ref[win, c] = jnp.where(mine, new, old).astype(BF)
        return jnp.where(start < slots, group_end(clips, start, slots), start)
    lax.fori_loop(0, (2*slots)//(LIVE_MAX+1)+1, group, 0)

def attend(clips, t, g):
    D=t.shape[1]//3
    return pl.pallas_call(fwd_kernel, out_shape=[jax.ShapeDtypeStruct((t.shape[0],D),BF)]*2+[jax.ShapeDtypeStruct((t.shape[0],128),F32)],
      in_specs=[pl.BlockSpec(memory_space=pltpu.SMEM)]+[pl.BlockSpec(memory_space=pltpu.VMEM)]*2,
      out_specs=[pl.BlockSpec(memory_space=pltpu.VMEM)]*3,
      scratch_shapes=[pltpu.VMEM((WIN,WIN),F32)],
      compiler_params=pltpu.CompilerParams(vmem_limit_bytes=62*2**20),name="attention_forward")(clips,t,g)
def attend_back(clips, t, do, logs, inners):
    return pl.pallas_call(bwd_kernel, out_shape=jax.ShapeDtypeStruct(t.shape,BF),
      in_specs=[pl.BlockSpec(memory_space=pltpu.SMEM)]+[pl.BlockSpec(memory_space=pltpu.VMEM)]*4,
      out_specs=pl.BlockSpec(memory_space=pltpu.VMEM),
      scratch_shapes=[pltpu.VMEM((WIN,WIN),F32)],
      compiler_params=pltpu.CompilerParams(vmem_limit_bytes=62*2**20),name="attention_backward")(clips,t,do,logs,inners)


RT = 400


def dot_nt(left, right):
    return lax.dot_general(left, right, (((1,), (1,)), ((), ())), preferred_element_type=F32)


def dot_tn(left, right):
    return lax.dot_general(left, right, (((0,), (0,)), ((), ())), preferred_element_type=F32)


def dot_nn(left, right):
    return jnp.dot(left, right, preferred_element_type=F32)


def norm_parts(values):
    centred = values - jnp.mean(values, axis=-1, keepdims=True)
    scale = lax.rsqrt(jnp.mean(centred * centred, axis=-1, keepdims=True) + EPSILON)
    return centred * scale, scale


def norm_back(grad, gain, unit, scale):
    inner = grad * gain
    return scale * (
        inner
        - jnp.mean(inner, axis=-1, keepdims=True)
        - unit * jnp.mean(inner * unit, axis=-1, keepdims=True)
    )


def gelu_pair(u):
    bell = jnp.exp(-0.5 * u * u)
    t = 1.0 / (1.0 + (0.3275911 * 0.5**0.5) * jnp.abs(u))
    poly = t * (
        0.5 * 0.254829592
        + t * (-0.5 * 0.284496736 + t * (0.5 * 1.421413741 + t * (-0.5 * 1.453152027 + t * (0.5 * 1.061405429))))
    )
    tail = poly * bell
    phi = jnp.where(u < 0, tail, 1.0 - tail)
    return u * phi, phi + u * (bell * (2.0 * math.pi) ** -0.5)


def column_sum(values):
    return jnp.sum(values, axis=0, keepdims=True)


def tiles(rows, body):
    @pl.loop(0, rows // RT)
    def _(i):
        body(pl.ds(pl.multiple_of(i * RT, 16), RT))


def qkv_norm(x_ref, vec, a1_ref):
    def one(win):
        unit, _ = norm_parts(x_ref[win, :].astype(F32))
        a1_ref[win, :] = (unit * vec[0:1, :] + vec[1:2, :]).astype(BF)

    tiles(x_ref.shape[0], one)


def qkv_block(a1_ref, w_ref, t_ref, part):
    width = a1_ref.shape[1]
    weight = w_ref[part].reshape(width, width)

    def one(win):
        out = dot_nn(a1_ref[win, :], weight)
        if part == 0:
            out = out * HEAD_DIM**-0.5
        t_ref[win, pl.ds(part * width, width)] = out.astype(BF)

    tiles(a1_ref.shape[0], one)


def qkv_kernel(x_ref, vec, w_ref, t_ref, a1_ref):
    qkv_norm(x_ref, vec, a1_ref)
    for part in range(3):
        qkv_block(a1_ref, w_ref, t_ref, part)


def middle_step(x_ref, o_ref, vec, wo_ref, m_ref, a2_ref):
    def one(win):
        middle = x_ref[win, :].astype(F32) + (dot_nn(o_ref[win, :], wo_ref[...]) + vec[2:3, :])
        m_ref[win, :] = middle
        unit, _ = norm_parts(middle)
        a2_ref[win, :] = (unit * vec[3:4, :] + vec[4:5, :]).astype(BF)

    tiles(x_ref.shape[0], one)


def chunk_step(first, bias, a2_ref, dy_ref, we_ref, wc_ref, h_ref, du_ref, y_ref, da2_ref, be_ref):
    be_ref[...] = jnp.zeros_like(be_ref)

    def one(win):
        hidden, slope = gelu_pair(dot_nn(a2_ref[win, :], we_ref[...]) + bias)
        hidden = hidden.astype(BF)
        h_ref[win, :] = hidden
        du = (dot_nt(dy_ref[win, :], wc_ref[...]) * slope).astype(BF)
        du_ref[win, :] = du
        be_ref[...] += column_sum(du.astype(F32))
        y = dot_nn(hidden, wc_ref[...])
        da2 = dot_nt(du, we_ref[...])
        if first is True:
            y_ref[win, :] = y
            da2_ref[win, :] = da2
        else:
            y_ref[win, :] += y
            da2_ref[win, :] += da2

    tiles(a2_ref.shape[0], one)


def middle_back(live_rows, m_ref, y_ref, dy_ref, da2_ref, vec, wo_ref, out_ref, dm_ref, dz_ref, do_ref, sums):
    sums[...] = jnp.zeros_like(sums)

    def one(win):
        middle = m_ref[win, :]
        out_ref[win, :] = (middle + (y_ref[win, :] + vec[5:6, :])).astype(BF)
        unit, scale = norm_parts(middle)
        da2 = da2_ref[win, :]
        dy = dy_ref[win, :].astype(F32)
        dm = dy + norm_back(da2, vec[3:4, :], unit, scale)
        dm_ref[win, :] = dm
        dz = dm.astype(BF)
        dz_ref[win, :] = dz
        do_ref[win, :] = dot_nt(dz, wo_ref[...]).astype(BF)
        sums[0:1, :] += column_sum(da2 * unit)
        sums[1:2, :] += column_sum(da2)
        sums[2:3, :] += column_sum(dz.astype(F32))
        sums[3:4, :] += column_sum(dy)

    tiles(m_ref.shape[0], one)


def feed_kernel(
    x_ref, o_ref, dy_ref, vec, wo_ref, we_ref, wc_ref,
    out_ref, dm_ref, do_ref, gwo_ref, gwe_ref, gwc_ref, sums, be_ref,
    m_ref, a2_ref, h_ref, du_ref, y_ref, da2_ref, dz_ref,
):
    middle_step(x_ref, o_ref, vec, wo_ref, m_ref, a2_ref)
    for j in range(4):
        chunk_step(
            j == 0, vec[6 + j : 7 + j, :], a2_ref, dy_ref, we_ref.at[j], wc_ref.at[j],
            h_ref, du_ref, y_ref, da2_ref, be_ref.at[pl.ds(8 * j, 1)],
        )
        gwc_ref[j] = dot_tn(h_ref[...], dy_ref[...]).astype(BF)
        gwe_ref[j] = dot_tn(a2_ref[...], du_ref[...]).astype(BF)
    middle_back(None, m_ref, y_ref, dy_ref, da2_ref, vec, wo_ref, out_ref, dm_ref, dz_ref, do_ref, sums)
    gwo_ref[...] = dot_tn(o_ref[...], dz_ref[...]).astype(BF)


def first_back(x_ref, dt_ref, dm_ref, vec, w_refs, pg_ref, sums):
    sums[...] = jnp.zeros_like(sums)
    width = x_ref.shape[1]

    def one(win):
        da1 = dot_nt(dt_ref[win, pl.ds(0, width)], w_refs[0][...])
        da1 += dot_nt(dt_ref[win, pl.ds(width, width)], w_refs[1][...])
        da1 += dot_nt(dt_ref[win, pl.ds(2 * width, width)], w_refs[2][...])
        unit, scale = norm_parts(x_ref[win, :].astype(F32))
        pg_ref[win, :] = dm_ref[win, :] + norm_back(da1, vec[0:1, :], unit, scale)
        sums[0:1, :] += column_sum(da1 * unit)
        sums[1:2, :] += column_sum(da1)

    tiles(x_ref.shape[0], one)


def first_kernel(x_ref, a1_ref, dt_ref, dm_ref, vec, w_ref, pg_ref, gwi_ref, sums):
    width = x_ref.shape[1]
    for part in range(3):
        gwi_ref[part] = dot_tn(a1_ref[...], dt_ref[:, pl.ds(part * width, width)]).astype(BF)
    first_back(x_ref, dt_ref, dm_ref, vec, [w_ref.at[p] for p in range(3)], pg_ref, sums)


VM = pl.BlockSpec(memory_space=pltpu.VMEM)
SM = pl.BlockSpec(memory_space=pltpu.SMEM)


def vmem_call(kernel, name, ins, outs, scratch=(), smem=0):
    return pl.pallas_call(
        kernel,
        out_shape=[jax.ShapeDtypeStruct(s, d) for s, d in outs],
        in_specs=[SM] * smem + [VM] * (len(ins) - smem),
        out_specs=[VM] * len(outs),
        scratch_shapes=[pltpu.VMEM(s, d) for s, d in scratch],
        compiler_params=pltpu.CompilerParams(vmem_limit_bytes=60 * 2**20),
        name=name,
    )(*ins)


MESH = pl.DeviceIdType.MESH


class Place:
    def __init__(self, parts, sh, width):
        mine, copy = lax.axis_index("fsdp"), lax.axis_index("rep")
        self.outer_count = parts // 2
        self.outer, self.inner = mine // 2, mine % 2
        self.plane, self.core = copy // 2, copy % 2
        self.third = sh // 3
        self.half = width // 2

    def device(self, outer=None, inner=None, plane=None, core=None):
        outer = self.outer if outer is None else outer
        inner = self.inner if inner is None else inner
        plane = self.plane if plane is None else plane
        core = self.core if core is None else core
        return (outer * 2 + inner, plane * 2 + core)

    def far(self, k):
        return (self.outer + k) % self.outer_count

    def ranks(self):
        return range(1, self.outer_count)

    def columns(self, core=None):
        core = self.core if core is None else core
        return pl.ds(pl.multiple_of(core * self.half, 128), self.half)

    def held(self):
        return pl.ds(pl.multiple_of(self.plane * self.third, 16), 2 * self.third)

    def own(self, plane=None):
        plane = self.plane if plane is None else plane
        return pl.ds(pl.multiple_of(plane * (2 * self.third), 16), self.third)

    def peers(self):
        return [self.device(outer=self.far(k)) for k in self.ranks()] + [
            self.device(inner=1 - self.inner),
            self.device(plane=1 - self.plane),
            self.device(core=1 - self.core),
        ]

    def greet(self):
        barrier = pltpu.get_barrier_semaphore()
        peers = self.peers()
        for peer in peers:
            pl.semaphore_signal(barrier, inc=1, device_id=peer, device_id_type=MESH)
        pl.semaphore_wait(barrier, len(peers))


def remote(src, dst, sems, index, device):
    return pltpu.make_async_remote_copy(
        src_ref=src, dst_ref=dst, send_sem=sems[0].at[index], recv_sem=sems[1].at[index],
        device_id=device, device_id_type=MESH,
    )


def start(copies):
    for copy in copies:
        copy.start()


def landed(copies):
    for copy in copies:
        copy.wait_recv()


def sent(copies):
    for copy in copies:
        copy.wait_send()


class Gather:
    def __init__(self, place, shard, full, sems):
        self.p, self.shard, self.full, self.sems = place, shard, full, sems

    def far(self, b):
        p = self.p
        return [
            remote(
                self.shard.at[b, p.held(), p.columns()],
                self.full.at[b, p.outer, p.inner, p.held(), p.columns()],
                self.sems, (b, k - 1), p.device(outer=p.far(k)),
            )
            for k in p.ranks()
        ]

    def pair(self, b, which):
        p = self.p
        if which == 0:
            ref = self.full.at[b, :, p.inner, p.held(), p.columns()]
            device = p.device(inner=1 - p.inner)
        elif which == 1:
            ref = self.full.at[b, :, :, p.own(), p.columns()]
            device = p.device(plane=1 - p.plane)
        else:
            ref = self.full.at[b, :, :, :, p.columns()]
            device = p.device(core=1 - p.core)
        return [remote(ref, ref, self.sems, (b, p.outer_count - 1 + which), device)]

    def put_own(self, b):
        p = self.p
        self.full[b, p.outer, p.inner, p.held(), p.columns()] = self.shard[b, p.held(), p.columns()]

    def step(self, s, count, lag):
        for stage in range(5):
            @pl.when((s >= stage * lag) & (s < count + stage * lag))
            def _():
                self.stage(s - stage * lag, stage)

    def stage(self, b, stage):
        if stage == 0:
            start(self.far(b))
            self.put_own(b)
        else:
            landed(self.far(b) if stage == 1 else self.pair(b, stage - 2))
            if stage < 4:
                start(self.pair(b, stage - 1))

    def finish(self, count):
        @pl.loop(0, count)
        def _(b):
            sent(self.far(b))
            for which in range(3):
                sent(self.pair(b, which))


def gather_sems(blocks, parts):
    shape = (blocks, parts // 2 - 1 + 3)
    return [pltpu.SemaphoreType.DMA(shape), pltpu.SemaphoreType.DMA(shape)]


class Reduce:
    def __init__(self, place, grad, out, bufs, sems):
        self.p, self.grad, self.out, self.sems = place, grad, out, sems
        self.from_core, self.from_plane, self.from_inner, self.from_far, self.part, self.from_part = bufs

    @staticmethod
    def scratch(blocks, parts, sh, width):
        outer, third, half = parts // 2, sh // 3, width // 2
        shape = (blocks, outer - 1 + 5)
        return [
            pltpu.VMEM((blocks, outer, 2, sh, half), BF),
            pltpu.VMEM((blocks, outer, 2, third, half), BF),
            pltpu.VMEM((blocks, outer, 2 * third, half), BF),
            pltpu.VMEM((blocks, outer - 1, 2 * third, half), BF),
            pltpu.VMEM((blocks, 2 * third, half), BF),
            pltpu.VMEM((blocks, 2 * third, half), BF),
            pltpu.SemaphoreType.DMA(shape),
            pltpu.SemaphoreType.DMA(shape),
        ]

    def copies(self, b, stage):
        p = self.p
        base = p.outer_count - 1
        if stage == 0:
            src, dst = self.grad.at[b, :, :, :, p.columns(1 - p.core)], self.from_core.at[b]
            device = p.device(core=1 - p.core)
        elif stage == 1:
            src, dst = self.grad.at[b, :, :, p.own(1 - p.plane), p.columns()], self.from_plane.at[b]
            device = p.device(plane=1 - p.plane)
        elif stage == 2:
            src, dst = self.grad.at[b, :, 1 - p.inner, p.held(), p.columns()], self.from_inner.at[b]
            device = p.device(inner=1 - p.inner)
        elif stage == 3:
            return [
                remote(
                    self.grad.at[b, p.far(k), p.inner, p.held(), p.columns()],
                    self.from_far.at[b, k - 1], self.sems, (b, k - 1), p.device(outer=p.far(k)),
                )
                for k in p.ranks()
            ]
        elif stage == 4:
            src, dst = self.part.at[b], self.from_part.at[b]
            device = p.device(plane=1 - p.plane)
        else:
            src = dst = self.out.at[b, :, p.columns()]
            device = p.device(core=1 - p.core)
        return [remote(src, dst, self.sems, (b, base + (stage if stage < 3 else stage - 1)), device)]

    def add(self, b, stage):
        p = self.p
        if stage == 0:
            @pl.loop(0, p.outer_count)
            def _(o):
                for i in range(2):
                    index = (b, o, i, slice(None), p.columns())
                    self.grad[index] = (self.grad[index].astype(F32) + self.from_core[b, o, i].astype(F32)).astype(BF)
        elif stage == 1:
            for i in range(2):
                @pl.loop(0, p.outer_count)
                def _(o):
                    index = (b, o, i, p.own(), p.columns())
                    self.grad[index] = (self.grad[index].astype(F32) + self.from_plane[b, o, i].astype(F32)).astype(BF)
        elif stage == 2:
            @pl.loop(0, p.outer_count)
            def _(o):
                index = (b, o, p.inner, p.held(), p.columns())
                self.grad[index] = (self.grad[index].astype(F32) + self.from_inner[b, o].astype(F32)).astype(BF)
        elif stage == 3:
            total = self.grad[b, p.outer, p.inner, p.held(), p.columns()].astype(F32)
            for k in p.ranks():
                total += self.from_far[b, k - 1].astype(F32)
            self.part[b] = total.astype(BF)
        elif stage == 4:
            third = p.third
            for plane in range(2):
                @pl.when(p.plane == plane)
                def _():
                    mine, other = self.part, self.from_part
                    first, last = (mine, other) if plane == 0 else (other, mine)
                    self.out[b, pl.ds(0, third), p.columns()] = first[b, pl.ds(0, third), :]
                    middle = first[b, pl.ds(third, third), :].astype(F32) + last[b, pl.ds(0, third), :].astype(F32)
                    self.out[b, pl.ds(third, third), p.columns()] = middle.astype(BF)
                    self.out[b, pl.ds(2 * third, third), p.columns()] = last[b, pl.ds(third, third), :]

    def stage(self, b, stage):
        if stage > 0:
            landed(self.copies(b, stage - 1))
            self.add(b, stage - 1)
        if stage < 6:
            start(self.copies(b, stage))

    def step(self, s, count, lag):
        for stage in range(7):
            @pl.when((s >= stage * lag) & (s < count + stage * lag))
            def _():
                self.stage(s - stage * lag, stage)

    def finish(self, count):
        @pl.loop(0, count)
        def _(b):
            for stage in range(6):
                sent(self.copies(b, stage))


class Vector:
    def __init__(self, place, total, bufs, sems, everywhere):
        self.p, self.total, self.sems = place, total, sems
        self.pairs, self.fars = bufs
        self.order = (0, 1, 2) if everywhere else (2,)

    @staticmethod
    def scratch(parts, shape, dtype):
        sems = (parts // 2 - 1 + 3,)
        return [
            pltpu.VMEM((6,) + shape, dtype), pltpu.VMEM((parts // 2,) + shape, dtype),
            pltpu.SemaphoreType.DMA(sems), pltpu.SemaphoreType.DMA(sems),
        ]

    def pair(self, which):
        p = self.p
        device = (
            p.device(core=1 - p.core), p.device(plane=1 - p.plane), p.device(inner=1 - p.inner)
        )[which]
        return [remote(self.pairs.at[2 * which], self.pairs.at[2 * which + 1], self.sems, p.outer_count - 1 + which, device)]

    def far(self):
        p = self.p
        mine = self.fars.at[p.outer]
        return [remote(mine, mine, self.sems, k - 1, p.device(outer=p.far(k))) for k in p.ranks()]

    def far_landed(self):
        p = self.p
        for k in p.ranks():
            theirs = self.fars.at[(p.outer + p.outer_count - k) % p.outer_count]
            remote(theirs, theirs, self.sems, k - 1, p.device(outer=p.far(k))).wait_recv()

    def stage(self, number):
        order = self.order
        if number > 0 and number <= len(order):
            which = order[number - 1]
            landed(self.pair(which))
            self.total[...] = self.total[...] + self.pairs[2 * which + 1]
        if number < len(order):
            which = order[number]
            self.pairs[2 * which] = self.total[...]
            start(self.pair(which))
        elif number == len(order):
            self.fars[self.p.outer] = self.total[...]
            start(self.far())
        else:
            self.far_landed()
            total = self.fars[0]
            for o in range(1, self.p.outer_count):
                total = total + self.fars[o]
            self.total[...] = total

    def stages(self):
        return len(self.order) + 2

    def finish(self):
        for which in self.order:
            sent(self.pair(which))
        sent(self.far())


FIRST_BLOCKS = 10


TILES = 3


def flat(ref, b):
    block = ref[b]
    return block.reshape(block.shape[0] * block.shape[1] * block.shape[2], block.shape[3])


def one_hot(shape, shift, along):
    row = lax.broadcasted_iota(jnp.int32, shape, 0)
    column = lax.broadcasted_iota(jnp.int32, shape, 1)
    return jnp.where((column - row if along else row - column) == shift, 1.0, 0.0)


def place_vectors(parts, vector, vec):
    sh, width = vector.shape[1], vec.shape[1]
    mine, apart = lax.axis_index("fsdp"), parts // 4
    low = vector[...].astype(BF)
    vec[...] = jnp.zeros_like(vec)
    vec[0:6, :] = dot_nn(low, one_hot((sh, width), mine * sh, True).astype(BF))[0:6, :]
    row = lax.broadcasted_iota(jnp.int32, (4, width), 0)
    for i in range(4):
        spot = one_hot((sh, width), (apart * i + mine // 4) * sh, True).astype(BF)
        vec[6:10, :] += jnp.where(row == mine % 4, dot_nn(low, spot)[6 + i : 7 + i, :], 0.0)


def gather_kernel(
    parts, x_ref, vector, wi_ref, wo_ref, we_ref, wc_ref,
    t_out, a1_ref, xp_ref, wi_out, wo_out, ff_out, rest_out, vec, t_ref, full, shard, local, *scratch
):
    count, width = x_ref.shape
    rows = xp_ref.shape[0]
    sh = wo_ref.shape[0]
    place = Place(parts, sh, width)
    weights = Gather(place, shard, full, scratch[0:2])
    vectors = Vector(place, vec, scratch[2:4], scratch[4:6], False)

    def pack_chunk(j, we_to, wc_to):
        for p in range(parts):
            we_to[:, pl.ds(p * sh, sh)] = we_ref[:, pl.ds((4 * p + j) * sh, sh)].astype(BF)
        wc_to[...] = wc_ref[pl.ds(j * sh, sh), :].astype(BF)

    shard[0] = wi_ref[:, pl.ds(0, width)].astype(BF)
    place.greet()
    weights.step(0, FIRST_BLOCKS, 1)
    place_vectors(parts, vector, vec)
    vectors.stage(0)
    for part in range(1, 3):
        shard[part] = wi_ref[:, pl.ds(part * width, width)].astype(BF)
    shard[3] = wo_ref[...].astype(BF)
    weights.step(1, FIRST_BLOCKS, 1)
    vectors.stage(1)
    tail = count // 16 * 16
    xp_ref[pl.ds(tail, rows - tail), :] = jnp.zeros((rows - tail, width), BF)
    xp_ref[pl.ds(0, count), :] = x_ref[...]
    weights.step(2, FIRST_BLOCKS, 1)
    vectors.stage(2)
    pack_chunk(0, shard.at[4], shard.at[5])
    weights.step(3, FIRST_BLOCKS, 1)
    qkv_norm(xp_ref, vec, a1_ref)
    leaving = []
    for s in range(4, FIRST_BLOCKS + 4):
        b = s - 4
        weights.step(s, FIRST_BLOCKS, 1)
        out = wi_out.at[b] if b < 3 else wo_out.at[0] if b == 3 else ff_out.at[b - 4]
        leaving.append(pltpu.make_async_copy(full.at[b], out, local.at[b]))
        leaving[-1].start()
        if b < 2:
            pack_chunk(b + 1, shard.at[2 * b + 6], shard.at[2 * b + 7])
        if b == 3:
            pack_chunk(3, rest_out.at[0], rest_out.at[1])
        if b < 3:
            qkv_block(a1_ref, full, t_ref, b)
            part = pl.ds(b * width, width)
            leaving.append(pltpu.make_async_copy(t_ref.at[:, part], t_out.at[:, part], local.at[FIRST_BLOCKS + b]))
            leaving[-1].start()
    for copy in leaving:
        copy.wait()
    weights.finish(FIRST_BLOCKS)
    vectors.finish()


def feed_comm_kernel(
    parts, x_ref, o_ref, dy_ref, vec, wo_ref, early, shard,
    out_ref, dm_ref, do_ref, dz_ref, grad_out, grad_rest, sums, be_ref, inner_ref,
    a2_ref, y_ref, da2_ref, full, grad, local, *scratch,
):
    rows, width = x_ref.shape
    sh = shard.shape[1]
    place = Place(parts, sh, width)
    later, have = shard.shape[0], early.shape[0]
    weights = Gather(place, shard, full.at[pl.ds(have, later)], scratch[0:2])
    grads = Reduce(place, grad.at[pl.ds(0, 4)], grad_out, scratch[2:8], scratch[8:10])
    du_ref, h_ref = do_ref, dz_ref
    ready = [pltpu.make_async_copy(early, full.at[pl.ds(0, have)], local.at[0])]
    start(ready)
    place.greet()

    def win(i):
        return pl.ds(i * RT, RT)

    def slot(number):
        for b in range(2):
            for stage, at in enumerate((0, 4, 8, 12, 16)):
                due = at + 2 * b
                if isinstance(number, int):
                    if due == number:
                        weights.stage(b, stage)
                elif due >= 4:
                    @pl.when(number == due)
                    def _():
                        weights.stage(b, stage)

    wo = flat(wo_ref, 0)
    slot(0)
    for i in range(TILES):
        middle = x_ref[win(i), :].astype(F32) + (dot_nn(o_ref[win(i), :], wo) + vec[2:3, :])
        dm_ref[win(i), :] = middle
        unit, _ = norm_parts(middle)
        a2_ref[win(i), :] = (unit * vec[3:4, :] + vec[4:5, :]).astype(BF)
        y_ref[win(i), :] = jnp.zeros((RT, width), F32)
        da2_ref[win(i), :] = jnp.zeros((RT, width), F32)
        slot(i + 1)
    for copy in ready:
        copy.wait()

    def leave(b):
        return pltpu.make_async_copy(grad.at[b], grad_rest.at[b - 4], local.at[b - 3])

    def due(position, back, parity):
        steps = position - 3 - parity + 5 * back
        return steps // 2 if steps % 2 == 0 and 0 <= steps <= 12 else None

    def passing(j, position):
        for back in range(3, -1, -1):
            for parity in range(2):
                stage = due(position, back, parity)
                if stage is None:
                    continue

                @pl.when((j >= back) & (j < back + 2))
                def _():
                    grads.stage(2 * (j - back) + parity, stage)

    @pl.loop(0, 4)
    def _(j):
        bias = vec[pl.ds(6 + j, 1), :]
        be_sum = jnp.zeros((1, width), F32)
        for i in range(TILES):
            hidden, slope = gelu_pair(dot_nn(a2_ref[win(i), :], flat(full, 2 * j)) + bias)
            hidden = hidden.astype(BF)
            h_ref[win(i), :] = hidden
            du = (dot_nt(dy_ref[win(i), :], flat(full, 2 * j + 1)) * slope).astype(BF)
            du_ref[win(i), :] = du
            be_sum += column_sum(du.astype(F32))
            y_ref[win(i), :] += dot_nn(hidden, flat(full, 2 * j + 1))
            da2_ref[win(i), :] += dot_nt(du, flat(full, 2 * j))
            slot(4 + 5 * j + i)
            passing(j, i)
        be_ref[pl.ds(j, 1), :] = be_sum
        grad[2 * j] = dot_tn(h_ref[...], dy_ref[...]).astype(BF).reshape(grad.shape[1:])
        slot(4 + 5 * j + 3)
        passing(j, 3)
        grad[2 * j + 1] = dot_tn(a2_ref[...], du_ref[...]).astype(BF).reshape(grad.shape[1:])
        slot(4 + 5 * j + 4)
        passing(j, 4)

        @pl.when(j >= 2)
        def _():
            for parity in range(2):
                leave(2 * j + parity).start()

    sums[...] = jnp.zeros_like(sums)
    feature = lax.broadcasted_iota(jnp.int32, (width, 128), 0)
    heads = (feature // HEAD_DIM == lax.broadcasted_iota(jnp.int32, (width, 128), 1)).astype(BF)
    for position in range(5, 8):
        i = position - 5
        if i < TILES:
            middle = dm_ref[win(i), :]
            out_ref[win(i), :] = (middle + (y_ref[win(i), :] + vec[5:6, :])).astype(BF)
            unit, scale = norm_parts(middle)
            da2 = da2_ref[win(i), :]
            dy = dy_ref[win(i), :].astype(F32)
            dm = dy + norm_back(da2, vec[3:4, :], unit, scale)
            dm_ref[win(i), :] = dm
            dz = dm.astype(BF)
            dz_ref[win(i), :] = dz
            do = dot_nt(dz, wo).astype(BF)
            do_ref[win(i), :] = do
            product = do.astype(F32) * o_ref[win(i), :].astype(F32)
            high = product.astype(BF)
            inner_ref[win(i), :] = dot_nn(high, heads) + dot_nn((product - high.astype(F32)).astype(BF), heads)
            sums[0:1, :] += column_sum(da2 * unit)
            sums[1:2, :] += column_sum(da2)
            sums[2:3, :] += column_sum(dz.astype(F32))
            sums[3:4, :] += column_sum(dy)
        for j in range(0, 2):
            for parity in range(2):
                stage = due(position + 5 * (3 - j), 0, parity)
                if stage is not None:
                    grads.stage(2 * j + parity, stage)
    weights.finish(later)
    grads.finish(4)
    for b in range(4, 8):
        leave(b).wait()


LAST_BLOCKS = 8


def first_comm_kernel(
    parts, x_in, a1_in, o_in, dz_in, dt_in, dm_in, vec, wi_in, sums_two, be_ref, rest_in,
    pg_ref, grad_out, total, grad, x_ref, a1_ref, o_ref, dz_ref, dt_ref, dm_ref, wi_ref, local, *scratch,
):
    rows, width = x_ref.shape
    place = Place(parts, width // parts, width)
    grads = Reduce(place, grad, grad_out, scratch[0:6], scratch[6:8])
    vectors = Vector(place, total, scratch[8:10], scratch[10:12], True)
    arriving = [
        pltpu.make_async_copy(rest_in.at[pl.ds(0, 2)], grad.at[pl.ds(0, 2)], local.at[0]),
        pltpu.make_async_copy(rest_in.at[pl.ds(2, 2)], grad.at[pl.ds(2, 2)], local.at[1]),
    ] + [
        pltpu.make_async_copy(source, ref, local.at[2 + i])
        for i, (source, ref) in enumerate(
            ((o_in, o_ref), (dz_in, dz_ref), (a1_in, a1_ref), (dt_in, dt_ref), (wi_in, wi_ref), (x_in, x_ref), (dm_in, dm_ref))
        )
    ]
    start(arriving)
    place.greet()
    total[...] = jnp.zeros_like(total)
    total[2:3, :] = sums_two[2:3, :]
    total[3:5, :] = sums_two[0:2, :]
    total[5:6, :] = sums_two[3:4, :]
    total[6:10, :] = be_ref[0:4, :]

    def step(s):
        grads.step(s, LAST_BLOCKS, 1)

    arriving[0].wait()
    step(0)
    arriving[1].wait()
    for i in (2, 3):
        arriving[i].wait()
    grad[4] = dot_tn(o_ref[...], dz_ref[...]).astype(BF).reshape(grad.shape[1:])
    step(1)
    for i in (4, 5):
        arriving[i].wait()
    for part in range(3):
        block = dot_tn(a1_ref[...], dt_ref[:, pl.ds(part * width, width)]).astype(BF)
        grad[part + 5] = block.reshape(grad.shape[1:])
        step(part + 2)
    for i in (6, 7, 8):
        arriving[i].wait()
    for i in range(TILES):
        win = pl.ds(i * RT, RT)
        da1 = dot_nt(dt_ref[win, pl.ds(0, width)], flat(wi_ref, 0))
        da1 += dot_nt(dt_ref[win, pl.ds(width, width)], flat(wi_ref, 1))
        da1 += dot_nt(dt_ref[win, pl.ds(2 * width, width)], flat(wi_ref, 2))
        unit, scale = norm_parts(x_ref[win, :].astype(F32))
        pg_ref[win, :] = dm_ref[win, :] + norm_back(da1, vec[0:1, :], unit, scale)
        total[0:1, :] += column_sum(da1 * unit)
        total[1:2, :] += column_sum(da1)
        step(5 + i)
    for s in range(8, LAST_BLOCKS + 6):
        if s - 8 < vectors.stages():
            vectors.stage(s - 8)
        step(s)
    grads.finish(LAST_BLOCKS)
    vectors.finish()


def comm_call(kernel, name, which, ins, outs, scratch, far=(), far_out=()):
    return pl.pallas_call(
        kernel,
        out_shape=[jax.ShapeDtypeStruct(s, d) for s, d in outs],
        in_specs=[pl.BlockSpec(memory_space=pl.ANY) if i in far else VM for i in range(len(ins))],
        out_specs=[pl.BlockSpec(memory_space=pl.ANY) if i in far_out else VM for i in range(len(outs))],
        scratch_shapes=scratch,
        compiler_params=pltpu.CompilerParams(
            vmem_limit_bytes=62 * 2**20, collective_id=which, has_side_effects=True
        ),
        name=name,
    )(*ins)


STEPS = 6


def extract_vectors(parts, total, picked):
    sh, width = picked.shape[1], total.shape[1]
    mine, apart = lax.axis_index("fsdp"), parts // 4

    def pick(rows, shift):
        return jnp.dot(
            rows, one_hot((width, sh), shift, False), precision=lax.Precision.HIGHEST, preferred_element_type=F32
        )

    picked[0:8, :] = pick(total[0:8, :], mine * sh)
    held = total[6:10, :]
    row = lax.broadcasted_iota(jnp.int32, held.shape, 0)
    held = jnp.sum(jnp.where(row == mine % 4, held, 0.0), axis=0, keepdims=True)
    held = jnp.broadcast_to(held, (8, width))
    for i in range(4):
        picked[6 + i : 7 + i, :] = pick(held, (apart * i + mine // 4) * sh)[0:1, :]


def update_kernel(rates, g_two, g_one, total, out_in, pg_in, *refs):
    state, outs, picked, flat_we = refs[:15], refs[15:42], refs[42], refs[43]
    i = pl.program_id(0)
    sh, width = g_one.shape[1:]
    parts = width // sh

    @pl.when(i == 0)
    def _():
        extract_vectors(parts, total, picked)
        for j in range(4):
            for p in range(parts):
                block = g_two[2 * j + 1] if j < 2 else g_one[2 * j - 3]
                flat_we[:, pl.ds((4 * p + j) * sh, sh)] = block[:, p * sh : (p + 1) * sh].astype(F32)

    outs[0][...] = out_in[...]
    outs[1][...] = pg_in[...]
    half, sixth = width // 2, width // STEPS
    odd = pl.ds(pl.multiple_of(i % 2 * half, 128), half)
    third = sh // 3

    def contract_rows(k):
        rows = pl.ds(pl.multiple_of(k % 3 * third, 16), third)
        j = k // 3
        low, high = g_two[2 * jnp.minimum(j, 1), rows, :], g_one[2 * jnp.maximum(j, 2) - 4, rows, :]
        return jnp.where(j < 2, low.astype(F32), high.astype(F32))

    sums = (
        g_one[5 + i // 2, :, odd].astype(F32),
        g_one[4, :, pl.ds(pl.multiple_of(i * sixth, 128), sixth)].astype(F32),
        flat_we[:, pl.ds(pl.multiple_of(i * 4 * sixth, 128), 4 * sixth)],
        jnp.concatenate([contract_rows(2 * i), contract_rows(2 * i + 1)], axis=0),
        picked[0:10, :],
    )
    for member in range(5):
        weight, moment, average = (ref[...] for ref in state[3 * member : 3 * member + 3])
        for ref, value in zip(
            outs[2 + 5 * member : 7 + 5 * member], step(sums[member], rates[member], weight, moment, average)
        ):
            ref[...] = value


def update(rates, count, g_two, g_one, total, out, pg, masters, moments, averages):
    sh, width = g_one.shape[1:]
    across = [
        pl.BlockSpec((sh, width // 2), lambda i: (0, i)),
        pl.BlockSpec((sh, width // STEPS), lambda i: (0, i)),
        pl.BlockSpec((sh, 4 * width // STEPS), lambda i: (0, i)),
        pl.BlockSpec((4 * sh // STEPS, width), lambda i: (i, 0)),
        pl.BlockSpec(masters[4].shape, lambda i: (0, 0)),
    ]
    rows = (count + STEPS - 1) // STEPS
    by_row = pl.BlockSpec(((rows + 15) // 16 * 16, width), lambda i: (i, 0))
    ins, specs = [], []
    outs = [jax.ShapeDtypeStruct((count, width), BF), jax.ShapeDtypeStruct((count, width), F32)]
    out_specs = [by_row] * 2
    for member in range(5):
        ins += [masters[member], moments[member], averages[member]]
        specs += [across[member]] * 3
        shape = masters[member].shape
        outs += [jax.ShapeDtypeStruct(shape, F32)] * 4 + [jax.ShapeDtypeStruct(shape, BF)]
        out_specs += [across[member]] * 5
    return pl.pallas_call(
        functools.partial(update_kernel, rates),
        grid=(STEPS,),
        out_shape=outs,
        in_specs=[pl.BlockSpec(g.shape, lambda i: (0, 0, 0)) for g in (g_two, g_one)]
        + [pl.BlockSpec(total.shape, lambda i: (0, 0))] + [by_row] * 2 + specs,
        out_specs=out_specs,
        scratch_shapes=[pltpu.VMEM((16, sh), F32), pltpu.VMEM((sh, 4 * width), F32)],
        compiler_params=pltpu.CompilerParams(vmem_limit_bytes=62 * 2**20),
        name="momentum_step",
    )(g_two, g_one, total, out, pg, *ins)


def run_qkv(x, vec, wi):
    rows, width = x.shape
    return vmem_call(
        qkv_kernel, "project_in", (x, vec, wi), [((rows, 3 * width), BF), ((rows, width), BF)]
    )


def run_feed(x, o, dy, vec, wo, we, wc):
    rows, width = x.shape
    wide, low = ((rows, width), F32), ((rows, width), BF)
    return vmem_call(
        feed_kernel, "feed_forward", (x, o, dy, vec, wo, we, wc),
        [low, wide, low, ((width, width), BF), ((4, width, width), BF), ((4, width, width), BF),
         ((8, width), F32), ((32, width), F32)],
        [wide, low, low, low, wide, wide, low],
    )


def run_first(x, a1, dt, dm, vec, wi):
    rows, width = x.shape
    return vmem_call(
        first_kernel, "project_in_back", (x, a1, dt, dm, vec, wi),
        [((rows, width), F32), ((3, width, width), BF), ((8, width), F32)],
    )


def pack_shards(wi, wo, we, wc, parts):
    rows, width = wo.shape
    wi = wi.reshape(rows, 3, width).swapaxes(0, 1)
    we = we.reshape(rows, parts, 4, rows).transpose(2, 0, 1, 3).reshape(4, rows, width)
    wc = wc.reshape(4, rows, width)
    return jnp.concatenate([wi, wo[None], we, wc], axis=0)


def unpack_shards(blocks, parts):
    rows, width = blocks.shape[1:]
    wi = blocks[0:3].swapaxes(0, 1).reshape(rows, 3 * width)
    we = blocks[4:8].reshape(4, rows, parts, rows).transpose(1, 2, 0, 3).reshape(rows, 4 * width)
    return wi, blocks[3], we, blocks[8:12].reshape(4 * rows, width)


def step(grad_sum, rate, weight, moment, average):
    moment_new = MOMENTUM * moment + grad_sum
    weight_new = weight - rate * (grad_sum + MOMENTUM * moment_new)
    average_new = AVERAGE * average + (1.0 - AVERAGE) * weight_new
    return [grad_sum, moment_new, weight_new, average_new, weight_new.astype(BF)]


def plain_path(patches, slot_clip, out_grad, masters, moments, averages, rates):
    parts, copies = lax.axis_size("fsdp"), lax.axis_size("rep")
    mine, copy = lax.axis_index("fsdp"), lax.axis_index("rep")
    count, width = patches.shape
    rows = (count + RT - 1) // RT * RT
    sh = width // parts
    packed = pack_shards(*(m.astype(BF) for m in masters[:4]), parts).reshape(12 * sh, width)
    piece = 12 * sh // copies
    quarter = lax.dynamic_slice_in_dim(packed, copy * piece, piece, 0)
    full = lax.all_gather(quarter, ("fsdp", "rep"), axis=0, tiled=True)
    full = full.reshape(parts, 12, sh, width).swapaxes(0, 1).reshape(12, width, width)
    vec = lax.all_gather(masters[4].astype(BF), "fsdp", axis=1, tiled=True).astype(F32)
    be = vec[6:].reshape(parts, 4, sh).swapaxes(0, 1).reshape(4, width)
    vec = jnp.concatenate([vec[:6], be, jnp.zeros((6, width), F32)], axis=0)

    pad = ((0, rows - count), (0, 0))
    x = jnp.pad(patches, pad)
    t, a1 = run_qkv(x, vec, full[0:3])
    o, dy, logs = attend(slot_clip, t, out_grad)
    out, dm, do, gwo, gwe, gwc, sums_two, sums_be = run_feed(x, o, dy, vec, full[3], full[4:8], full[8:12])
    inner = jnp.sum((o.astype(F32) * do.astype(F32)).reshape(rows, -1, HEAD_DIM), axis=2)
    inner = jnp.pad(inner, ((0, 0), (0, 128 - inner.shape[1])))
    dt = attend_back(slot_clip, t, do, logs, inner)
    pg, gwi, sums_one = run_first(x, a1, dt, dm, vec, full[0:3])

    grads = jnp.concatenate([gwi, gwo[None], gwe, gwc], axis=0)
    grads = grads.reshape(12, parts, sh, width).swapaxes(0, 1).reshape(parts * 12 * sh, width)
    grads = lax.psum_scatter(grads, ("fsdp", "rep"), scatter_dimension=0, tiled=True)
    grads = lax.all_gather(grads, "rep", axis=0, tiled=True).reshape(12, sh, width)
    be_grad = sums_be[::8].reshape(4, parts, sh).swapaxes(0, 1).reshape(4, width)
    vector = jnp.concatenate(
        [sums_one[0:2], sums_two[2:3], sums_two[0:2], sums_two[3:4], be_grad], axis=0
    )
    vector = lax.dynamic_slice_in_dim(lax.psum(vector, ("fsdp", "rep")), mine * sh, sh, 1)
    outputs = []
    for member, grad in enumerate((*unpack_shards(grads, parts), vector)):
        outputs += step(grad.astype(F32), rates[member], masters[member], moments[member], averages[member])
    return (out[:count], pg[:count], *outputs)


def direct_path(patches, slot_clip, out_grad, masters, moments, averages, rates):
    parts = lax.axis_size("fsdp")
    count, width = patches.shape
    rows = (count + RT - 1) // RT * RT
    sh = width // parts
    block = (parts // 2, 2, sh, width)
    wide, low = ((rows, width), F32), ((rows, width), BF)
    t, a1, x, wi, wo, early, later, vec = comm_call(
        functools.partial(gather_kernel, parts), "gather_project_in", 0, (patches, masters[4], *masters[:4]),
        [((rows, 3 * width), BF), low, low, ((3,) + block, BF), ((1,) + block, BF),
         ((FIRST_BLOCKS - 4,) + block, BF), ((2, sh, width), BF), ((16, width), F32)],
        [pltpu.VMEM((rows, 3 * width), BF), pltpu.VMEM((FIRST_BLOCKS,) + block, BF),
         pltpu.VMEM((FIRST_BLOCKS, sh, width), BF), pltpu.SemaphoreType.DMA((FIRST_BLOCKS + 3,))]
        + gather_sems(FIRST_BLOCKS, parts) + Vector.scratch(parts, (16, width), F32),
        far_out=(0, 3, 4, 5),
    )
    o, dy, logs = attend(slot_clip, t, out_grad)
    out, dm, do, dz, grads_two, rest, sums_two, sums_be, inner = comm_call(
        functools.partial(feed_comm_kernel, parts), "feed_forward_reduce", 1,
        (x, o, dy, vec, wo, early, later),
        [low, wide, low, low, ((4, sh, width), BF), ((4,) + block, BF), ((8, width), F32), ((8, width), F32),
         ((rows, 128), F32)],
        [pltpu.VMEM(*low), pltpu.VMEM(*wide), pltpu.VMEM(*wide),
         pltpu.VMEM((8,) + block, BF), pltpu.VMEM((8,) + block, BF), pltpu.SemaphoreType.DMA((5,))]
        + gather_sems(2, parts) + Reduce.scratch(4, parts, sh, width), far=(5,), far_out=(5,),
    )
    dt = attend_back(slot_clip, t, do, logs, inner)
    pg, grads_one, total = comm_call(
        functools.partial(first_comm_kernel, parts), "project_in_back_reduce", 2,
        (x, a1, o, dz, dt, dm, vec, wi, sums_two, sums_be, rest),
        [wide, ((LAST_BLOCKS, sh, width), BF), ((16, width), F32)],
        [pltpu.VMEM((LAST_BLOCKS,) + block, BF), pltpu.VMEM(*low), pltpu.VMEM(*low), pltpu.VMEM(*low),
         pltpu.VMEM(*low), pltpu.VMEM((rows, 3 * width), BF), pltpu.VMEM(*wide), pltpu.VMEM((3,) + block, BF),
         pltpu.SemaphoreType.DMA((9,))]
        + Reduce.scratch(LAST_BLOCKS, parts, sh, width) + Vector.scratch(parts, (16, width), F32),
        far=(0, 1, 2, 3, 4, 5, 7, 10),
    )
    return update(rates, count, grads_two, grads_one, total, out, pg, masters, moments, averages)


def on_device(
    patches, slot_clip, out_grad,
    project_in_weight, project_in_moment, project_in_average,
    project_out_weight, project_out_moment, project_out_average,
    expand_weight, expand_moment, expand_average,
    contract_weight, contract_moment, contract_average,
    vector_weight, vector_moment, vector_average,
):
    masters = (project_in_weight, project_out_weight, expand_weight, contract_weight, vector_weight)
    moments = (project_in_moment, project_out_moment, expand_moment, contract_moment, vector_moment)
    averages = (project_in_average, project_out_average, expand_average, contract_average, vector_average)
    parts, copies = lax.axis_size("fsdp"), lax.axis_size("rep")
    count, width = patches.shape
    direct = copies == 4 and parts % 4 == 0 and width // parts % 48 == 0
    path = direct_path if direct else plain_path
    tokens_all = count * parts * copies
    rates = [rate / tokens_all**0.5 for rate in RATES]
    return tuple(path(patches, slot_clip, out_grad, masters, moments, averages, rates))


def solution(mesh):
    tokens = P(("fsdp", "rep"), None)
    split, split_vector = P("fsdp", None), P(None, "fsdp")
    in_specs = (tokens, P(("fsdp", "rep")), tokens) + (split,) * 12 + (split_vector,) * 3
    out_specs = (tokens,) * 2 + (split,) * 20 + (split_vector,) * 5
    return jax.shard_map(on_device, mesh=mesh, in_specs=in_specs, out_specs=out_specs, check_vma=False)
```

```python
import functools
import math

import jax
import jax.numpy as jnp
from jax import lax
from jax.sharding import PartitionSpec as P
import jax.experimental.pallas as pl
import jax.experimental.pallas.tpu as pltpu

BF, F32 = jnp.bfloat16, jnp.float32
HEAD_DIM = 64
SLOT = 49
LIVE_MAX = 8
WIN = 416
EPSILON = 1e-06
MOMENTUM = 0.5
AVERAGE = 0.5
RATES = (0.3, 0.3, 0.1, 0.03, 0.5)
NEG = -1e30

def dg(a,b,ca,cb):
    return lax.dot_general(a,b,(((ca,),(cb,)),((),())),preferred_element_type=F32)

def both(x, lane):
    keep = (lane < 64).astype(BF)
    return jnp.concatenate([x*keep, x*(1-keep)], axis=0)

def group_end(clips, start, slots):
    end = start+1
    for e in range(2, LIVE_MAX+1):
        cand = start+e
        safe = jnp.minimum(cand, slots-1)
        edge = (cand == slots) | ((cand < slots) & ((clips[safe] != clips[jnp.maximum(safe-1,0)]) | (clips[safe] < 0)))
        end = jnp.where(edge, cand, end)
    return end

def fill_bias(clips, w0, start, end, bias):
    def keys(shape, dim):
        row = lax.broadcasted_iota(jnp.int32, shape, dim) + w0
        slot = (row*1338) >> 16
        key = -1-row
        for ahead in range(LIVE_MAX):
            s = start+ahead
            clip = clips[jnp.minimum(s, clips.shape[0]-1)]
            key = jnp.where((slot == s) & (s < end) & (clip >= 0), clip, key)
        return key
    bias[...] = jnp.where(keys((WIN,1),0) == keys((1,WIN),1), 0.0, NEG)

def clear_tail(ref, slots):
    tail = slots*SLOT//16*16
    ref[pl.ds(tail, ref.shape[0]-tail), :] = jnp.zeros((ref.shape[0]-tail, ref.shape[1]), BF)

def fwd_kernel(clips, t_ref, g_ref, o_ref, dy_ref, log_ref, bias):
    slots = clips.shape[0]
    rows = t_ref.shape[0]; D = o_ref.shape[1]
    clear_tail(o_ref, slots)
    clear_tail(dy_ref, slots)
    log_ref[...] = jnp.zeros_like(log_ref)
    live = lax.fori_loop(0, slots, lambda s, n: n + jnp.where(clips[s] >= 0, SLOT, 0), 0)
    row = lax.broadcasted_iota(jnp.int32,(slots*SLOT,1),0)
    dy_ref[pl.ds(0,slots*SLOT), :] = jnp.where(row < live, g_ref[...].astype(F32), 0.0).astype(BF)
    def group(g, start):
        @pl.when(start < slots)
        def _():
            end = group_end(clips, start, slots)
            r0 = start*SLOT; r1 = end*SLOT
            w0 = pl.multiple_of(jnp.minimum((r0>>4)<<4, rows-WIN), 16)
            fill_bias(clips, w0, start, end, bias)
            rowi = lax.broadcasted_iota(jnp.int32,(WIN,128),0)+w0
            mine = (rowi >= r0) & (rowi < r1)
            lane = lax.broadcasted_iota(jnp.int32,(1,128),1)
            win = pl.ds(w0, WIN)
            logs = log_ref[win, :]
            for p in range(D//128):
                q = t_ref[win, pl.ds(p*128,128)]
                k = t_ref[win, pl.ds(D+p*128,128)]
                v = t_ref[win, pl.ds(2*D+p*128,128)]
                s = dg(both(q, lane), k, 1, 1)
                es, tops = [], []
                for h in range(2):
                    part = s[h*WIN:(h+1)*WIN] + bias[...]
                    top = jnp.max(part, axis=1, keepdims=True)
                    es.append(jnp.exp(part-top).astype(BF))
                    tops.append(top)
                ones = jnp.concatenate([v, jnp.ones_like(v)], axis=1)
                mixed = jnp.dot(jnp.concatenate(es, axis=0), ones, preferred_element_type=F32)
                outs = []
                for h in range(2):
                    total = mixed[h*WIN:(h+1)*WIN, 128:]
                    outs.append(mixed[h*WIN:(h+1)*WIN, :128] / total)
                    logs = jnp.where(mine & (lane == 2*p+h), tops[h] + jnp.log(total), logs)
                o = jnp.where(lane < 64, outs[0], outs[1])
                old = o_ref[win, pl.ds(p*128,128)]
                o_ref[win, pl.ds(p*128,128)] = jnp.where(mine, o, old.astype(F32)).astype(BF)
            log_ref[win, :] = logs
        return jnp.where(start < slots, group_end(clips, start, slots), start)
    lax.fori_loop(0, (2*slots)//(LIVE_MAX+1)+1, group, 0)

def bwd_kernel(clips, t_ref, do_ref, log_ref, inner_ref, dt_ref, bias):
    slots = clips.shape[0]
    rows = t_ref.shape[0]; D = do_ref.shape[1]
    clear_tail(dt_ref, slots)
    def group(g, start):
        @pl.when(start < slots)
        def _():
            end = group_end(clips, start, slots)
            r0 = start*SLOT; r1 = end*SLOT
            w0 = pl.multiple_of(jnp.minimum((r0>>4)<<4, rows-WIN), 16)
            fill_bias(clips, w0, start, end, bias)
            rowi = lax.broadcasted_iota(jnp.int32,(WIN,128),0)+w0
            mine = (rowi >= r0) & (rowi < r1)
            lane = lax.broadcasted_iota(jnp.int32,(1,128),1)
            win = pl.ds(w0, WIN)
            logs = log_ref[win, :].T
            inners = inner_ref[win, :].T
            for p in range(D//128):
                q = t_ref[win, pl.ds(p*128,128)]
                k = t_ref[win, pl.ds(D+p*128,128)]
                v = t_ref[win, pl.ds(2*D+p*128,128)]
                do = do_ref[win, pl.ds(p*128,128)]
                s = dg(both(k, lane), q, 1, 1)
                dp = dg(both(v, lane), do, 1, 1)
                pts, dss = [], []
                for h in range(2):
                    n = 2*p+h
                    rows_h = slice(h*WIN, (h+1)*WIN)
                    pt = jnp.exp((s[rows_h] + bias[...]) - logs[n:n+1, :])
                    dss.append((pt*(dp[rows_h]-inners[n:n+1, :])).astype(BF))
                    pts.append(pt.astype(BF))
                dv = jnp.dot(jnp.concatenate(pts, axis=0), do, preferred_element_type=F32)
                dk = jnp.dot(jnp.concatenate(dss, axis=0), q, preferred_element_type=F32)
                dq = jnp.dot(jnp.concatenate([d.T for d in dss], axis=0), k, preferred_element_type=F32)
                dqs, dks, dvs = ([x[:WIN], x[WIN:]] for x in (dq, dk, dv))
                for i,x in enumerate((dqs,dks,dvs)):
                    new = jnp.where(lane < 64, x[0], x[1]).astype(BF).astype(F32)
                    if i==0: new = new*(64**-0.5)
                    c = pl.ds(i*D+p*128,128)
                    old = dt_ref[win, c].astype(F32)
                    dt_ref[win, c] = jnp.where(mine, new, old).astype(BF)
        return jnp.where(start < slots, group_end(clips, start, slots), start)
    lax.fori_loop(0, (2*slots)//(LIVE_MAX+1)+1, group, 0)

def attend(clips, t, g):
    D=t.shape[1]//3
    return pl.pallas_call(fwd_kernel, out_shape=[jax.ShapeDtypeStruct((t.shape[0],D),BF)]*2+[jax.ShapeDtypeStruct((t.shape[0],128),F32)],
      in_specs=[pl.BlockSpec(memory_space=pltpu.SMEM)]+[pl.BlockSpec(memory_space=pltpu.VMEM)]*2,
      out_specs=[pl.BlockSpec(memory_space=pltpu.VMEM)]*3,
      scratch_shapes=[pltpu.VMEM((WIN,WIN),F32)],
      compiler_params=pltpu.CompilerParams(vmem_limit_bytes=62*2**20),name="attention_forward")(clips,t,g)
def attend_back(clips, t, do, logs, inners):
    return pl.pallas_call(bwd_kernel, out_shape=jax.ShapeDtypeStruct(t.shape,BF),
      in_specs=[pl.BlockSpec(memory_space=pltpu.SMEM)]+[pl.BlockSpec(memory_space=pltpu.VMEM)]*4,
      out_specs=pl.BlockSpec(memory_space=pltpu.VMEM),
      scratch_shapes=[pltpu.VMEM((WIN,WIN),F32)],
      compiler_params=pltpu.CompilerParams(vmem_limit_bytes=62*2**20),name="attention_backward")(clips,t,do,logs,inners)


RT = 400


def dot_nt(left, right):
    return lax.dot_general(left, right, (((1,), (1,)), ((), ())), preferred_element_type=F32)


def dot_tn(left, right):
    return lax.dot_general(left, right, (((0,), (0,)), ((), ())), preferred_element_type=F32)


def dot_nn(left, right):
    return jnp.dot(left, right, preferred_element_type=F32)


def norm_parts(values):
    centred = values - jnp.mean(values, axis=-1, keepdims=True)
    scale = lax.rsqrt(jnp.mean(centred * centred, axis=-1, keepdims=True) + EPSILON)
    return centred * scale, scale


def norm_back(grad, gain, unit, scale):
    inner = grad * gain
    return scale * (
        inner
        - jnp.mean(inner, axis=-1, keepdims=True)
        - unit * jnp.mean(inner * unit, axis=-1, keepdims=True)
    )


def gelu_pair(u):
    bell = jnp.exp(-0.5 * u * u)
    t = 1.0 / (1.0 + (0.3275911 * 0.5**0.5) * jnp.abs(u))
    poly = t * (
        0.5 * 0.254829592
        + t * (-0.5 * 0.284496736 + t * (0.5 * 1.421413741 + t * (-0.5 * 1.453152027 + t * (0.5 * 1.061405429))))
    )
    tail = poly * bell
    phi = jnp.where(u < 0, tail, 1.0 - tail)
    return u * phi, phi + u * (bell * (2.0 * math.pi) ** -0.5)


def column_sum(values):
    return jnp.sum(values, axis=0, keepdims=True)


def tiles(rows, body):
    @pl.loop(0, rows // RT)
    def _(i):
        body(pl.ds(pl.multiple_of(i * RT, 16), RT))


def qkv_norm(x_ref, vec, a1_ref):
    def one(win):
        unit, _ = norm_parts(x_ref[win, :].astype(F32))
        a1_ref[win, :] = (unit * vec[0:1, :] + vec[1:2, :]).astype(BF)

    tiles(x_ref.shape[0], one)


def qkv_block(a1_ref, w_ref, t_ref, part):
    width = a1_ref.shape[1]
    weight = w_ref[part].reshape(width, width)

    def one(win):
        out = dot_nn(a1_ref[win, :], weight)
        if part == 0:
            out = out * HEAD_DIM**-0.5
        t_ref[win, pl.ds(part * width, width)] = out.astype(BF)

    tiles(a1_ref.shape[0], one)


def qkv_kernel(x_ref, vec, w_ref, t_ref, a1_ref):
    qkv_norm(x_ref, vec, a1_ref)
    for part in range(3):
        qkv_block(a1_ref, w_ref, t_ref, part)


def middle_step(x_ref, o_ref, vec, wo_ref, m_ref, a2_ref):
    def one(win):
        middle = x_ref[win, :].astype(F32) + (dot_nn(o_ref[win, :], wo_ref[...]) + vec[2:3, :])
        m_ref[win, :] = middle
        unit, _ = norm_parts(middle)
        a2_ref[win, :] = (unit * vec[3:4, :] + vec[4:5, :]).astype(BF)

    tiles(x_ref.shape[0], one)


def chunk_step(first, bias, a2_ref, dy_ref, we_ref, wc_ref, h_ref, du_ref, y_ref, da2_ref, be_ref):
    be_ref[...] = jnp.zeros_like(be_ref)

    def one(win):
        hidden, slope = gelu_pair(dot_nn(a2_ref[win, :], we_ref[...]) + bias)
        hidden = hidden.astype(BF)
        h_ref[win, :] = hidden
        du = (dot_nt(dy_ref[win, :], wc_ref[...]) * slope).astype(BF)
        du_ref[win, :] = du
        be_ref[...] += column_sum(du.astype(F32))
        y = dot_nn(hidden, wc_ref[...])
        da2 = dot_nt(du, we_ref[...])
        if first is True:
            y_ref[win, :] = y
            da2_ref[win, :] = da2
        else:
            y_ref[win, :] += y
            da2_ref[win, :] += da2

    tiles(a2_ref.shape[0], one)


def middle_back(live_rows, m_ref, y_ref, dy_ref, da2_ref, vec, wo_ref, out_ref, dm_ref, dz_ref, do_ref, sums):
    sums[...] = jnp.zeros_like(sums)

    def one(win):
        middle = m_ref[win, :]
        out_ref[win, :] = (middle + (y_ref[win, :] + vec[5:6, :])).astype(BF)
        unit, scale = norm_parts(middle)
        da2 = da2_ref[win, :]
        dy = dy_ref[win, :].astype(F32)
        dm = dy + norm_back(da2, vec[3:4, :], unit, scale)
        dm_ref[win, :] = dm
        dz = dm.astype(BF)
        dz_ref[win, :] = dz
        do_ref[win, :] = dot_nt(dz, wo_ref[...]).astype(BF)
        sums[0:1, :] += column_sum(da2 * unit)
        sums[1:2, :] += column_sum(da2)
        sums[2:3, :] += column_sum(dz.astype(F32))
        sums[3:4, :] += column_sum(dy)

    tiles(m_ref.shape[0], one)


def feed_kernel(
    x_ref, o_ref, dy_ref, vec, wo_ref, we_ref, wc_ref,
    out_ref, dm_ref, do_ref, gwo_ref, gwe_ref, gwc_ref, sums, be_ref,
    m_ref, a2_ref, h_ref, du_ref, y_ref, da2_ref, dz_ref,
):
    middle_step(x_ref, o_ref, vec, wo_ref, m_ref, a2_ref)
    for j in range(4):
        chunk_step(
            j == 0, vec[6 + j : 7 + j, :], a2_ref, dy_ref, we_ref.at[j], wc_ref.at[j],
            h_ref, du_ref, y_ref, da2_ref, be_ref.at[pl.ds(8 * j, 1)],
        )
        gwc_ref[j] = dot_tn(h_ref[...], dy_ref[...]).astype(BF)
        gwe_ref[j] = dot_tn(a2_ref[...], du_ref[...]).astype(BF)
    middle_back(None, m_ref, y_ref, dy_ref, da2_ref, vec, wo_ref, out_ref, dm_ref, dz_ref, do_ref, sums)
    gwo_ref[...] = dot_tn(o_ref[...], dz_ref[...]).astype(BF)


def first_back(x_ref, dt_ref, dm_ref, vec, w_refs, pg_ref, sums):
    sums[...] = jnp.zeros_like(sums)
    width = x_ref.shape[1]

    def one(win):
        da1 = dot_nt(dt_ref[win, pl.ds(0, width)], w_refs[0][...])
        da1 += dot_nt(dt_ref[win, pl.ds(width, width)], w_refs[1][...])
        da1 += dot_nt(dt_ref[win, pl.ds(2 * width, width)], w_refs[2][...])
        unit, scale = norm_parts(x_ref[win, :].astype(F32))
        pg_ref[win, :] = dm_ref[win, :] + norm_back(da1, vec[0:1, :], unit, scale)
        sums[0:1, :] += column_sum(da1 * unit)
        sums[1:2, :] += column_sum(da1)

    tiles(x_ref.shape[0], one)


def first_kernel(x_ref, a1_ref, dt_ref, dm_ref, vec, w_ref, pg_ref, gwi_ref, sums):
    width = x_ref.shape[1]
    for part in range(3):
        gwi_ref[part] = dot_tn(a1_ref[...], dt_ref[:, pl.ds(part * width, width)]).astype(BF)
    first_back(x_ref, dt_ref, dm_ref, vec, [w_ref.at[p] for p in range(3)], pg_ref, sums)


VM = pl.BlockSpec(memory_space=pltpu.VMEM)
SM = pl.BlockSpec(memory_space=pltpu.SMEM)


def vmem_call(kernel, name, ins, outs, scratch=(), smem=0):
    return pl.pallas_call(
        kernel,
        out_shape=[jax.ShapeDtypeStruct(s, d) for s, d in outs],
        in_specs=[SM] * smem + [VM] * (len(ins) - smem),
        out_specs=[VM] * len(outs),
        scratch_shapes=[pltpu.VMEM(s, d) for s, d in scratch],
        compiler_params=pltpu.CompilerParams(vmem_limit_bytes=60 * 2**20),
        name=name,
    )(*ins)


MESH = pl.DeviceIdType.MESH


class Place:
    def __init__(self, parts, sh, width):
        mine, copy = lax.axis_index("fsdp"), lax.axis_index("rep")
        self.outer_count = parts // 2
        self.outer, self.inner = mine // 2, mine % 2
        self.plane, self.core = copy // 2, copy % 2
        self.third = sh // 3
        self.half = width // 2

    def device(self, outer=None, inner=None, plane=None, core=None):
        outer = self.outer if outer is None else outer
        inner = self.inner if inner is None else inner
        plane = self.plane if plane is None else plane
        core = self.core if core is None else core
        return (outer * 2 + inner, plane * 2 + core)

    def far(self, k):
        return (self.outer + k) % self.outer_count

    def ranks(self):
        return range(1, self.outer_count)

    def columns(self, core=None):
        core = self.core if core is None else core
        return pl.ds(pl.multiple_of(core * self.half, 128), self.half)

    def held(self):
        return pl.ds(pl.multiple_of(self.plane * self.third, 16), 2 * self.third)

    def own(self, plane=None):
        plane = self.plane if plane is None else plane
        return pl.ds(pl.multiple_of(plane * (2 * self.third), 16), self.third)

    def peers(self):
        return [self.device(outer=self.far(k)) for k in self.ranks()] + [
            self.device(inner=1 - self.inner),
            self.device(plane=1 - self.plane),
            self.device(core=1 - self.core),
        ]

    def greet(self):
        barrier = pltpu.get_barrier_semaphore()
        peers = self.peers()
        for peer in peers:
            pl.semaphore_signal(barrier, inc=1, device_id=peer, device_id_type=MESH)
        pl.semaphore_wait(barrier, len(peers))


def remote(src, dst, sems, index, device):
    return pltpu.make_async_remote_copy(
        src_ref=src, dst_ref=dst, send_sem=sems[0].at[index], recv_sem=sems[1].at[index],
        device_id=device, device_id_type=MESH,
    )


def start(copies):
    for copy in copies:
        copy.start()


def landed(copies):
    for copy in copies:
        copy.wait_recv()


def sent(copies):
    for copy in copies:
        copy.wait_send()


class Gather:
    def __init__(self, place, shard, full, sems):
        self.p, self.shard, self.full, self.sems = place, shard, full, sems

    def far(self, b):
        p = self.p
        return [
            remote(
                self.shard.at[b, p.held(), p.columns()],
                self.full.at[b, p.outer, p.inner, p.held(), p.columns()],
                self.sems, (b, k - 1), p.device(outer=p.far(k)),
            )
            for k in p.ranks()
        ]

    def pair(self, b, which):
        p = self.p
        if which == 0:
            ref = self.full.at[b, :, p.inner, p.held(), p.columns()]
            device = p.device(inner=1 - p.inner)
        elif which == 1:
            ref = self.full.at[b, :, :, p.own(), p.columns()]
            device = p.device(plane=1 - p.plane)
        else:
            ref = self.full.at[b, :, :, :, p.columns()]
            device = p.device(core=1 - p.core)
        return [remote(ref, ref, self.sems, (b, p.outer_count - 1 + which), device)]

    def put_own(self, b):
        p = self.p
        self.full[b, p.outer, p.inner, p.held(), p.columns()] = self.shard[b, p.held(), p.columns()]

    def step(self, s, count, lag):
        for stage in range(5):
            @pl.when((s >= stage * lag) & (s < count + stage * lag))
            def _():
                self.stage(s - stage * lag, stage)

    def stage(self, b, stage):
        if stage == 0:
            start(self.far(b))
            self.put_own(b)
        else:
            landed(self.far(b) if stage == 1 else self.pair(b, stage - 2))
            if stage < 4:
                start(self.pair(b, stage - 1))

    def finish(self, count):
        @pl.loop(0, count)
        def _(b):
            sent(self.far(b))
            for which in range(3):
                sent(self.pair(b, which))


def gather_sems(blocks, parts):
    shape = (blocks, parts // 2 - 1 + 3)
    return [pltpu.SemaphoreType.DMA(shape), pltpu.SemaphoreType.DMA(shape)]


class Reduce:
    def __init__(self, place, grad, out, bufs, sems):
        self.p, self.grad, self.out, self.sems = place, grad, out, sems
        self.from_core, self.from_plane, self.from_inner, self.from_far, self.part, self.from_part = bufs

    @staticmethod
    def scratch(blocks, parts, sh, width):
        outer, third, half = parts // 2, sh // 3, width // 2
        shape = (blocks, outer - 1 + 5)
        return [
            pltpu.VMEM((blocks, outer, 2, sh, half), BF),
            pltpu.VMEM((blocks, outer, 2, third, half), BF),
            pltpu.VMEM((blocks, outer, 2 * third, half), BF),
            pltpu.VMEM((blocks, outer - 1, 2 * third, half), BF),
            pltpu.VMEM((blocks, 2 * third, half), BF),
            pltpu.VMEM((blocks, 2 * third, half), BF),
            pltpu.SemaphoreType.DMA(shape),
            pltpu.SemaphoreType.DMA(shape),
        ]

    def copies(self, b, stage):
        p = self.p
        base = p.outer_count - 1
        if stage == 0:
            src, dst = self.grad.at[b, :, :, :, p.columns(1 - p.core)], self.from_core.at[b]
            device = p.device(core=1 - p.core)
        elif stage == 1:
            src, dst = self.grad.at[b, :, :, p.own(1 - p.plane), p.columns()], self.from_plane.at[b]
            device = p.device(plane=1 - p.plane)
        elif stage == 2:
            src, dst = self.grad.at[b, :, 1 - p.inner, p.held(), p.columns()], self.from_inner.at[b]
            device = p.device(inner=1 - p.inner)
        elif stage == 3:
            return [
                remote(
                    self.grad.at[b, p.far(k), p.inner, p.held(), p.columns()],
                    self.from_far.at[b, k - 1], self.sems, (b, k - 1), p.device(outer=p.far(k)),
                )
                for k in p.ranks()
            ]
        elif stage == 4:
            src, dst = self.part.at[b], self.from_part.at[b]
            device = p.device(plane=1 - p.plane)
        else:
            src = dst = self.out.at[b, :, p.columns()]
            device = p.device(core=1 - p.core)
        return [remote(src, dst, self.sems, (b, base + (stage if stage < 3 else stage - 1)), device)]

    def add(self, b, stage):
        p = self.p
        if stage == 0:
            @pl.loop(0, p.outer_count)
            def _(o):
                for i in range(2):
                    index = (b, o, i, slice(None), p.columns())
                    self.grad[index] = (self.grad[index].astype(F32) + self.from_core[b, o, i].astype(F32)).astype(BF)
        elif stage == 1:
            for i in range(2):
                @pl.loop(0, p.outer_count)
                def _(o):
                    index = (b, o, i, p.own(), p.columns())
                    self.grad[index] = (self.grad[index].astype(F32) + self.from_plane[b, o, i].astype(F32)).astype(BF)
        elif stage == 2:
            @pl.loop(0, p.outer_count)
            def _(o):
                index = (b, o, p.inner, p.held(), p.columns())
                self.grad[index] = (self.grad[index].astype(F32) + self.from_inner[b, o].astype(F32)).astype(BF)
        elif stage == 3:
            total = self.grad[b, p.outer, p.inner, p.held(), p.columns()].astype(F32)
            for k in p.ranks():
                total += self.from_far[b, k - 1].astype(F32)
            self.part[b] = total.astype(BF)
        elif stage == 4:
            third = p.third
            for plane in range(2):
                @pl.when(p.plane == plane)
                def _():
                    mine, other = self.part, self.from_part
                    first, last = (mine, other) if plane == 0 else (other, mine)
                    self.out[b, pl.ds(0, third), p.columns()] = first[b, pl.ds(0, third), :]
                    middle = first[b, pl.ds(third, third), :].astype(F32) + last[b, pl.ds(0, third), :].astype(F32)
                    self.out[b, pl.ds(third, third), p.columns()] = middle.astype(BF)
                    self.out[b, pl.ds(2 * third, third), p.columns()] = last[b, pl.ds(third, third), :]

    def stage(self, b, stage):
        if stage > 0:
            landed(self.copies(b, stage - 1))
            self.add(b, stage - 1)
        if stage < 6:
            start(self.copies(b, stage))

    def step(self, s, count, lag):
        for stage in range(7):
            @pl.when((s >= stage * lag) & (s < count + stage * lag))
            def _():
                self.stage(s - stage * lag, stage)

    def finish(self, count):
        @pl.loop(0, count)
        def _(b):
            for stage in range(6):
                sent(self.copies(b, stage))


class Vector:
    def __init__(self, place, total, bufs, sems, everywhere):
        self.p, self.total, self.sems = place, total, sems
        self.pairs, self.fars = bufs
        self.order = (0, 1, 2) if everywhere else (2,)

    @staticmethod
    def scratch(parts, shape, dtype):
        sems = (parts // 2 - 1 + 3,)
        return [
            pltpu.VMEM((6,) + shape, dtype), pltpu.VMEM((parts // 2,) + shape, dtype),
            pltpu.SemaphoreType.DMA(sems), pltpu.SemaphoreType.DMA(sems),
        ]

    def pair(self, which):
        p = self.p
        device = (
            p.device(core=1 - p.core), p.device(plane=1 - p.plane), p.device(inner=1 - p.inner)
        )[which]
        return [remote(self.pairs.at[2 * which], self.pairs.at[2 * which + 1], self.sems, p.outer_count - 1 + which, device)]

    def far(self):
        p = self.p
        mine = self.fars.at[p.outer]
        return [remote(mine, mine, self.sems, k - 1, p.device(outer=p.far(k))) for k in p.ranks()]

    def far_landed(self):
        p = self.p
        for k in p.ranks():
            theirs = self.fars.at[(p.outer + p.outer_count - k) % p.outer_count]
            remote(theirs, theirs, self.sems, k - 1, p.device(outer=p.far(k))).wait_recv()

    def stage(self, number):
        order = self.order
        if number > 0 and number <= len(order):
            which = order[number - 1]
            landed(self.pair(which))
            self.total[...] = self.total[...] + self.pairs[2 * which + 1]
        if number < len(order):
            which = order[number]
            self.pairs[2 * which] = self.total[...]
            start(self.pair(which))
        elif number == len(order):
            self.fars[self.p.outer] = self.total[...]
            start(self.far())
        else:
            self.far_landed()
            total = self.fars[0]
            for o in range(1, self.p.outer_count):
                total = total + self.fars[o]
            self.total[...] = total

    def stages(self):
        return len(self.order) + 2

    def finish(self):
        for which in self.order:
            sent(self.pair(which))
        sent(self.far())


FIRST_BLOCKS = 10


TILES = 3


def flat(ref, b):
    block = ref[b]
    return block.reshape(block.shape[0] * block.shape[1] * block.shape[2], block.shape[3])


def one_hot(shape, shift, along):
    row = lax.broadcasted_iota(jnp.int32, shape, 0)
    column = lax.broadcasted_iota(jnp.int32, shape, 1)
    return jnp.where((column - row if along else row - column) == shift, 1.0, 0.0)


def place_vectors(parts, vector, vec):
    sh, width = vector.shape[1], vec.shape[1]
    mine, apart = lax.axis_index("fsdp"), parts // 4
    low = vector[...].astype(BF)
    vec[...] = jnp.zeros_like(vec)
    vec[0:6, :] = dot_nn(low, one_hot((sh, width), mine * sh, True).astype(BF))[0:6, :]
    row = lax.broadcasted_iota(jnp.int32, (4, width), 0)
    for i in range(4):
        spot = one_hot((sh, width), (apart * i + mine // 4) * sh, True).astype(BF)
        vec[6:10, :] += jnp.where(row == mine % 4, dot_nn(low, spot)[6 + i : 7 + i, :], 0.0)


def gather_kernel(
    parts, x_ref, vector, wi_ref, wo_ref, we_ref, wc_ref,
    t_out, a1_ref, xp_ref, wi_out, wo_out, ff_out, rest_out, vec, t_ref, full, shard, local, *scratch
):
    count, width = x_ref.shape
    rows = xp_ref.shape[0]
    sh = wo_ref.shape[0]
    place = Place(parts, sh, width)
    weights = Gather(place, shard, full, scratch[0:2])
    vectors = Vector(place, vec, scratch[2:4], scratch[4:6], False)

    def pack_chunk(j, we_to, wc_to):
        for p in range(parts):
            we_to[:, pl.ds(p * sh, sh)] = we_ref[:, pl.ds((4 * p + j) * sh, sh)].astype(BF)
        wc_to[...] = wc_ref[pl.ds(j * sh, sh), :].astype(BF)

    shard[0] = wi_ref[:, pl.ds(0, width)].astype(BF)
    place.greet()
    weights.step(0, FIRST_BLOCKS, 1)
    place_vectors(parts, vector, vec)
    vectors.stage(0)
    for part in range(1, 3):
        shard[part] = wi_ref[:, pl.ds(part * width, width)].astype(BF)
    shard[3] = wo_ref[...].astype(BF)
    weights.step(1, FIRST_BLOCKS, 1)
    vectors.stage(1)
    tail = count // 16 * 16
    xp_ref[pl.ds(tail, rows - tail), :] = jnp.zeros((rows - tail, width), BF)
    xp_ref[pl.ds(0, count), :] = x_ref[...]
    weights.step(2, FIRST_BLOCKS, 1)
    vectors.stage(2)
    pack_chunk(0, shard.at[4], shard.at[5])
    weights.step(3, FIRST_BLOCKS, 1)
    qkv_norm(xp_ref, vec, a1_ref)
    leaving = []
    for s in range(4, FIRST_BLOCKS + 4):
        b = s - 4
        weights.step(s, FIRST_BLOCKS, 1)
        out = wi_out.at[b] if b < 3 else wo_out.at[0] if b == 3 else ff_out.at[b - 4]
        leaving.append(pltpu.make_async_copy(full.at[b], out, local.at[b]))
        leaving[-1].start()
        if b < 2:
            pack_chunk(b + 1, shard.at[2 * b + 6], shard.at[2 * b + 7])
        if b == 3:
            pack_chunk(3, rest_out.at[0], rest_out.at[1])
        if b < 3:
            qkv_block(a1_ref, full, t_ref, b)
            part = pl.ds(b * width, width)
            leaving.append(pltpu.make_async_copy(t_ref.at[:, part], t_out.at[:, part], local.at[FIRST_BLOCKS + b]))
            leaving[-1].start()
    for copy in leaving:
        copy.wait()
    weights.finish(FIRST_BLOCKS)
    vectors.finish()


def feed_comm_kernel(
    parts, x_in, o_in, dy_in, vec, wo_in, early, shard,
    out_out, dm_out, do_out, dz_out, grad_out, grad_rest, sums, be_ref, inner_ref,
    x_ref, o_ref, dy_ref, wo_ref, out_ref, dm_ref, do_ref, dz_ref,
    a2_ref, y_ref, da2_ref, full, grad, local, leaving, *scratch,
):
    rows, width = x_ref.shape
    sh = shard.shape[1]
    place = Place(parts, sh, width)
    later, have = shard.shape[0], early.shape[0]
    weights = Gather(place, shard, full.at[pl.ds(have, later)], scratch[0:2])
    grads = Reduce(place, grad.at[pl.ds(0, 4)], grad_out, scratch[2:8], scratch[8:10])
    du_ref, h_ref = do_ref, dz_ref
    moves = ((x_in, x_ref), (o_in, o_ref), (wo_in, wo_ref), (dy_in, dy_ref), (early, full.at[pl.ds(0, have)]))
    ready = [pltpu.make_async_copy(source, target, local.at[4 + i]) for i, (source, target) in enumerate(moves)]
    start(ready)
    place.greet()

    def win(i):
        return pl.ds(i * RT, RT)

    def slot(number):
        for b in range(2):
            for stage, at in enumerate((0, 4, 8, 12, 16)):
                if at + 2 * b == number:
                    weights.stage(b, stage)

    slot(0)
    for copy in ready[:3]:
        copy.wait()
    wo = flat(wo_ref, 0)
    for i in range(TILES):
        middle = x_ref[win(i), :].astype(F32) + (dot_nn(o_ref[win(i), :], wo) + vec[2:3, :])
        dm_ref[win(i), :] = middle
        unit, _ = norm_parts(middle)
        a2_ref[win(i), :] = (unit * vec[3:4, :] + vec[4:5, :]).astype(BF)
        y_ref[win(i), :] = jnp.zeros((RT, width), F32)
        da2_ref[win(i), :] = jnp.zeros((RT, width), F32)
        slot(i + 1)
    for copy in ready[3:]:
        copy.wait()

    def results(i):
        pairs = ((out_ref, out_out), (dm_ref, dm_out), (do_ref, do_out), (dz_ref, dz_out))
        return [
            pltpu.make_async_copy(source.at[win(i)], target.at[win(i)], leaving.at[i, n])
            for n, (source, target) in enumerate(pairs)
        ]

    def leave(b):
        return pltpu.make_async_copy(grad.at[b], grad_rest.at[b - 4], local.at[b - 4])

    def due(position, back, parity):
        steps = position - 3 - parity + 5 * back
        return steps // 2 if steps % 2 == 0 and 0 <= steps <= 12 else None

    def passing(j, position):
        for back in range(3, -1, -1):
            for parity in range(2):
                stage = due(position, back, parity)
                if stage is not None and back <= j < back + 2:
                    grads.stage(2 * (j - back) + parity, stage)

    for j in range(4):
        bias = vec[pl.ds(6 + j, 1), :]
        be_sum = jnp.zeros((1, width), F32)
        for i in range(TILES):
            hidden, slope = gelu_pair(dot_nn(a2_ref[win(i), :], flat(full, 2 * j)) + bias)
            hidden = hidden.astype(BF)
            h_ref[win(i), :] = hidden
            du = (dot_nt(dy_ref[win(i), :], flat(full, 2 * j + 1)) * slope).astype(BF)
            du_ref[win(i), :] = du
            be_sum += column_sum(du.astype(F32))
            y_ref[win(i), :] += dot_nn(hidden, flat(full, 2 * j + 1))
            da2_ref[win(i), :] += dot_nt(du, flat(full, 2 * j))
            slot(4 + 5 * j + i)
            passing(j, i)
        be_ref[pl.ds(j, 1), :] = be_sum
        grad[2 * j] = dot_tn(h_ref[...], dy_ref[...]).astype(BF).reshape(grad.shape[1:])
        slot(4 + 5 * j + 3)
        passing(j, 3)
        grad[2 * j + 1] = dot_tn(a2_ref[...], du_ref[...]).astype(BF).reshape(grad.shape[1:])
        slot(4 + 5 * j + 4)
        passing(j, 4)

        if j >= 2:
            for parity in range(2):
                leave(2 * j + parity).start()

    sums[...] = jnp.zeros_like(sums)
    feature = lax.broadcasted_iota(jnp.int32, (width, 128), 0)
    heads = (feature // HEAD_DIM == lax.broadcasted_iota(jnp.int32, (width, 128), 1)).astype(BF)
    for position in range(5, 8):
        i = position - 5
        if i < TILES:
            middle = dm_ref[win(i), :]
            out_ref[win(i), :] = (middle + (y_ref[win(i), :] + vec[5:6, :])).astype(BF)
            unit, scale = norm_parts(middle)
            da2 = da2_ref[win(i), :]
            dy = dy_ref[win(i), :].astype(F32)
            dm = dy + norm_back(da2, vec[3:4, :], unit, scale)
            dm_ref[win(i), :] = dm
            dz = dm.astype(BF)
            dz_ref[win(i), :] = dz
            do = dot_nt(dz, wo).astype(BF)
            do_ref[win(i), :] = do
            product = do.astype(F32) * o_ref[win(i), :].astype(F32)
            high = product.astype(BF)
            inner_ref[win(i), :] = dot_nn(high, heads) + dot_nn((product - high.astype(F32)).astype(BF), heads)
            sums[0:1, :] += column_sum(da2 * unit)
            sums[1:2, :] += column_sum(da2)
            sums[2:3, :] += column_sum(dz.astype(F32))
            sums[3:4, :] += column_sum(dy)
            start(results(i))
        for j in range(0, 2):
            for parity in range(2):
                stage = due(position + 5 * (3 - j), 0, parity)
                if stage is not None:
                    grads.stage(2 * j + parity, stage)
    weights.finish(later)
    grads.finish(4)
    for b in range(4, 8):
        leave(b).wait()
    for i in range(TILES):
        for copy in results(i):
            copy.wait()


LAST_BLOCKS = 8


def first_comm_kernel(
    parts, x_in, a1_in, o_in, dz_in, dt_in, dm_in, vec, wi_in, sums_two, be_ref, rest_in,
    pg_ref, grad_out, total, grad, x_ref, a1_ref, o_ref, dz_ref, dt_ref, dm_ref, wi_ref, local, *scratch,
):
    rows, width = x_ref.shape
    place = Place(parts, width // parts, width)
    grads = Reduce(place, grad, grad_out, scratch[0:6], scratch[6:8])
    vectors = Vector(place, total, scratch[8:10], scratch[10:12], True)
    arriving = [
        pltpu.make_async_copy(rest_in.at[pl.ds(0, 2)], grad.at[pl.ds(0, 2)], local.at[0]),
        pltpu.make_async_copy(rest_in.at[pl.ds(2, 2)], grad.at[pl.ds(2, 2)], local.at[1]),
    ] + [
        pltpu.make_async_copy(source, ref, local.at[2 + i])
        for i, (source, ref) in enumerate(
            ((o_in, o_ref), (dz_in, dz_ref), (a1_in, a1_ref), (dt_in, dt_ref), (wi_in, wi_ref), (x_in, x_ref), (dm_in, dm_ref))
        )
    ]
    start(arriving)
    place.greet()
    total[...] = jnp.zeros_like(total)
    total[2:3, :] = sums_two[2:3, :]
    total[3:5, :] = sums_two[0:2, :]
    total[5:6, :] = sums_two[3:4, :]
    total[6:10, :] = be_ref[0:4, :]

    def step(s):
        grads.step(s, LAST_BLOCKS, 1)

    arriving[0].wait()
    step(0)
    arriving[1].wait()
    for i in (2, 3):
        arriving[i].wait()
    grad[4] = dot_tn(o_ref[...], dz_ref[...]).astype(BF).reshape(grad.shape[1:])
    step(1)
    for i in (4, 5):
        arriving[i].wait()
    for part in range(3):
        block = dot_tn(a1_ref[...], dt_ref[:, pl.ds(part * width, width)]).astype(BF)
        grad[part + 5] = block.reshape(grad.shape[1:])
        step(part + 2)
    for i in (6, 7, 8):
        arriving[i].wait()
    for i in range(TILES):
        win = pl.ds(i * RT, RT)
        da1 = dot_nt(dt_ref[win, pl.ds(0, width)], flat(wi_ref, 0))
        da1 += dot_nt(dt_ref[win, pl.ds(width, width)], flat(wi_ref, 1))
        da1 += dot_nt(dt_ref[win, pl.ds(2 * width, width)], flat(wi_ref, 2))
        unit, scale = norm_parts(x_ref[win, :].astype(F32))
        pg_ref[win, :] = dm_ref[win, :] + norm_back(da1, vec[0:1, :], unit, scale)
        total[0:1, :] += column_sum(da1 * unit)
        total[1:2, :] += column_sum(da1)
        step(5 + i)
    for s in range(8, LAST_BLOCKS + 6):
        if s - 8 < vectors.stages():
            vectors.stage(s - 8)
        step(s)
    grads.finish(LAST_BLOCKS)
    vectors.finish()


def comm_call(kernel, name, which, ins, outs, scratch, far=(), far_out=()):
    return pl.pallas_call(
        kernel,
        out_shape=[jax.ShapeDtypeStruct(s, d) for s, d in outs],
        in_specs=[pl.BlockSpec(memory_space=pl.ANY) if i in far else VM for i in range(len(ins))],
        out_specs=[pl.BlockSpec(memory_space=pl.ANY) if i in far_out else VM for i in range(len(outs))],
        scratch_shapes=scratch,
        compiler_params=pltpu.CompilerParams(
            vmem_limit_bytes=62 * 2**20, collective_id=which, has_side_effects=True
        ),
        name=name,
    )(*ins)


STEPS = 6


def extract_vectors(parts, total, picked):
    sh, width = picked.shape[1], total.shape[1]
    mine, apart = lax.axis_index("fsdp"), parts // 4

    def pick(rows, shift):
        return jnp.dot(
            rows, one_hot((width, sh), shift, False), precision=lax.Precision.HIGHEST, preferred_element_type=F32
        )

    picked[0:8, :] = pick(total[0:8, :], mine * sh)
    held = total[6:10, :]
    row = lax.broadcasted_iota(jnp.int32, held.shape, 0)
    held = jnp.sum(jnp.where(row == mine % 4, held, 0.0), axis=0, keepdims=True)
    held = jnp.broadcast_to(held, (8, width))
    for i in range(4):
        picked[6 + i : 7 + i, :] = pick(held, (apart * i + mine // 4) * sh)[0:1, :]


def update_kernel(rates, g_two, g_one, total, out_in, pg_in, *refs):
    state, outs, picked, flat_we = refs[:15], refs[15:42], refs[42], refs[43]
    i = pl.program_id(0)
    sh, width = g_one.shape[1:]
    parts = width // sh

    @pl.when(i == 0)
    def _():
        extract_vectors(parts, total, picked)
        for j in range(4):
            for p in range(parts):
                block = g_two[2 * j + 1] if j < 2 else g_one[2 * j - 3]
                flat_we[:, pl.ds((4 * p + j) * sh, sh)] = block[:, p * sh : (p + 1) * sh].astype(F32)

    outs[0][...] = out_in[...]
    outs[1][...] = pg_in[...]
    half, sixth = width // 2, width // STEPS
    odd = pl.ds(pl.multiple_of(i % 2 * half, 128), half)
    third = sh // 3

    def contract_rows(k):
        rows = pl.ds(pl.multiple_of(k % 3 * third, 16), third)
        j = k // 3
        low, high = g_two[2 * jnp.minimum(j, 1), rows, :], g_one[2 * jnp.maximum(j, 2) - 4, rows, :]
        return jnp.where(j < 2, low.astype(F32), high.astype(F32))

    sums = (
        g_one[5 + i // 2, :, odd].astype(F32),
        g_one[4, :, pl.ds(pl.multiple_of(i * sixth, 128), sixth)].astype(F32),
        flat_we[:, pl.ds(pl.multiple_of(i * 4 * sixth, 128), 4 * sixth)],
        jnp.concatenate([contract_rows(2 * i), contract_rows(2 * i + 1)], axis=0),
        picked[0:10, :],
    )
    for member in range(5):
        weight, moment, average = (ref[...] for ref in state[3 * member : 3 * member + 3])
        for ref, value in zip(
            outs[2 + 5 * member : 7 + 5 * member], step(sums[member], rates[member], weight, moment, average)
        ):
            ref[...] = value


def update(rates, count, g_two, g_one, total, out, pg, masters, moments, averages):
    sh, width = g_one.shape[1:]
    across = [
        pl.BlockSpec((sh, width // 2), lambda i: (0, i)),
        pl.BlockSpec((sh, width // STEPS), lambda i: (0, i)),
        pl.BlockSpec((sh, 4 * width // STEPS), lambda i: (0, i)),
        pl.BlockSpec((4 * sh // STEPS, width), lambda i: (i, 0)),
        pl.BlockSpec(masters[4].shape, lambda i: (0, 0)),
    ]
    rows = (count + STEPS - 1) // STEPS
    by_row = pl.BlockSpec(((rows + 15) // 16 * 16, width), lambda i: (i, 0))
    ins, specs = [], []
    outs = [jax.ShapeDtypeStruct((count, width), BF), jax.ShapeDtypeStruct((count, width), F32)]
    out_specs = [by_row] * 2
    for member in range(5):
        ins += [masters[member], moments[member], averages[member]]
        specs += [across[member]] * 3
        shape = masters[member].shape
        outs += [jax.ShapeDtypeStruct(shape, F32)] * 4 + [jax.ShapeDtypeStruct(shape, BF)]
        out_specs += [across[member]] * 5
    return pl.pallas_call(
        functools.partial(update_kernel, rates),
        grid=(STEPS,),
        out_shape=outs,
        in_specs=[pl.BlockSpec(g.shape, lambda i: (0, 0, 0)) for g in (g_two, g_one)]
        + [pl.BlockSpec(total.shape, lambda i: (0, 0))] + [by_row] * 2 + specs,
        out_specs=out_specs,
        scratch_shapes=[pltpu.VMEM((16, sh), F32), pltpu.VMEM((sh, 4 * width), F32)],
        compiler_params=pltpu.CompilerParams(vmem_limit_bytes=62 * 2**20),
        name="momentum_step",
    )(g_two, g_one, total, out, pg, *ins)


def run_qkv(x, vec, wi):
    rows, width = x.shape
    return vmem_call(
        qkv_kernel, "project_in", (x, vec, wi), [((rows, 3 * width), BF), ((rows, width), BF)]
    )


def run_feed(x, o, dy, vec, wo, we, wc):
    rows, width = x.shape
    wide, low = ((rows, width), F32), ((rows, width), BF)
    return vmem_call(
        feed_kernel, "feed_forward", (x, o, dy, vec, wo, we, wc),
        [low, wide, low, ((width, width), BF), ((4, width, width), BF), ((4, width, width), BF),
         ((8, width), F32), ((32, width), F32)],
        [wide, low, low, low, wide, wide, low],
    )


def run_first(x, a1, dt, dm, vec, wi):
    rows, width = x.shape
    return vmem_call(
        first_kernel, "project_in_back", (x, a1, dt, dm, vec, wi),
        [((rows, width), F32), ((3, width, width), BF), ((8, width), F32)],
    )


def pack_shards(wi, wo, we, wc, parts):
    rows, width = wo.shape
    wi = wi.reshape(rows, 3, width).swapaxes(0, 1)
    we = we.reshape(rows, parts, 4, rows).transpose(2, 0, 1, 3).reshape(4, rows, width)
    wc = wc.reshape(4, rows, width)
    return jnp.concatenate([wi, wo[None], we, wc], axis=0)


def unpack_shards(blocks, parts):
    rows, width = blocks.shape[1:]
    wi = blocks[0:3].swapaxes(0, 1).reshape(rows, 3 * width)
    we = blocks[4:8].reshape(4, rows, parts, rows).transpose(1, 2, 0, 3).reshape(rows, 4 * width)
    return wi, blocks[3], we, blocks[8:12].reshape(4 * rows, width)


def step(grad_sum, rate, weight, moment, average):
    moment_new = MOMENTUM * moment + grad_sum
    weight_new = weight - rate * (grad_sum + MOMENTUM * moment_new)
    average_new = AVERAGE * average + (1.0 - AVERAGE) * weight_new
    return [grad_sum, moment_new, weight_new, average_new, weight_new.astype(BF)]


def plain_path(patches, slot_clip, out_grad, masters, moments, averages, rates):
    parts, copies = lax.axis_size("fsdp"), lax.axis_size("rep")
    mine, copy = lax.axis_index("fsdp"), lax.axis_index("rep")
    count, width = patches.shape
    rows = (count + RT - 1) // RT * RT
    sh = width // parts
    packed = pack_shards(*(m.astype(BF) for m in masters[:4]), parts).reshape(12 * sh, width)
    piece = 12 * sh // copies
    quarter = lax.dynamic_slice_in_dim(packed, copy * piece, piece, 0)
    full = lax.all_gather(quarter, ("fsdp", "rep"), axis=0, tiled=True)
    full = full.reshape(parts, 12, sh, width).swapaxes(0, 1).reshape(12, width, width)
    vec = lax.all_gather(masters[4].astype(BF), "fsdp", axis=1, tiled=True).astype(F32)
    be = vec[6:].reshape(parts, 4, sh).swapaxes(0, 1).reshape(4, width)
    vec = jnp.concatenate([vec[:6], be, jnp.zeros((6, width), F32)], axis=0)

    pad = ((0, rows - count), (0, 0))
    x = jnp.pad(patches, pad)
    t, a1 = run_qkv(x, vec, full[0:3])
    o, dy, logs = attend(slot_clip, t, out_grad)
    out, dm, do, gwo, gwe, gwc, sums_two, sums_be = run_feed(x, o, dy, vec, full[3], full[4:8], full[8:12])
    inner = jnp.sum((o.astype(F32) * do.astype(F32)).reshape(rows, -1, HEAD_DIM), axis=2)
    inner = jnp.pad(inner, ((0, 0), (0, 128 - inner.shape[1])))
    dt = attend_back(slot_clip, t, do, logs, inner)
    pg, gwi, sums_one = run_first(x, a1, dt, dm, vec, full[0:3])

    grads = jnp.concatenate([gwi, gwo[None], gwe, gwc], axis=0)
    grads = grads.reshape(12, parts, sh, width).swapaxes(0, 1).reshape(parts * 12 * sh, width)
    grads = lax.psum_scatter(grads, ("fsdp", "rep"), scatter_dimension=0, tiled=True)
    grads = lax.all_gather(grads, "rep", axis=0, tiled=True).reshape(12, sh, width)
    be_grad = sums_be[::8].reshape(4, parts, sh).swapaxes(0, 1).reshape(4, width)
    vector = jnp.concatenate(
        [sums_one[0:2], sums_two[2:3], sums_two[0:2], sums_two[3:4], be_grad], axis=0
    )
    vector = lax.dynamic_slice_in_dim(lax.psum(vector, ("fsdp", "rep")), mine * sh, sh, 1)
    outputs = []
    for member, grad in enumerate((*unpack_shards(grads, parts), vector)):
        outputs += step(grad.astype(F32), rates[member], masters[member], moments[member], averages[member])
    return (out[:count], pg[:count], *outputs)


def direct_path(patches, slot_clip, out_grad, masters, moments, averages, rates):
    parts = lax.axis_size("fsdp")
    count, width = patches.shape
    rows = (count + RT - 1) // RT * RT
    sh = width // parts
    block = (parts // 2, 2, sh, width)
    wide, low = ((rows, width), F32), ((rows, width), BF)
    t, a1, x, wi, wo, early, later, vec = comm_call(
        functools.partial(gather_kernel, parts), "gather_project_in", 0, (patches, masters[4], *masters[:4]),
        [((rows, 3 * width), BF), low, low, ((3,) + block, BF), ((1,) + block, BF),
         ((FIRST_BLOCKS - 4,) + block, BF), ((2, sh, width), BF), ((16, width), F32)],
        [pltpu.VMEM((rows, 3 * width), BF), pltpu.VMEM((FIRST_BLOCKS,) + block, BF),
         pltpu.VMEM((FIRST_BLOCKS, sh, width), BF), pltpu.SemaphoreType.DMA((FIRST_BLOCKS + 3,))]
        + gather_sems(FIRST_BLOCKS, parts) + Vector.scratch(parts, (16, width), F32),
        far_out=(0, 3, 4, 5),
    )
    o, dy, logs = attend(slot_clip, t, out_grad)
    out, dm, do, dz, grads_two, rest, sums_two, sums_be, inner = comm_call(
        functools.partial(feed_comm_kernel, parts), "feed_forward_reduce", 1,
        (x, o, dy, vec, wo, early, later),
        [low, wide, low, low, ((4, sh, width), BF), ((4,) + block, BF), ((8, width), F32), ((8, width), F32),
         ((rows, 128), F32)],
        [pltpu.VMEM(*low), pltpu.VMEM(*low), pltpu.VMEM(*low), pltpu.VMEM((1,) + block, BF),
         pltpu.VMEM(*low), pltpu.VMEM(*wide), pltpu.VMEM(*low), pltpu.VMEM(*low),
         pltpu.VMEM(*low), pltpu.VMEM(*wide), pltpu.VMEM(*wide), pltpu.VMEM((8,) + block, BF),
         pltpu.VMEM((8,) + block, BF), pltpu.SemaphoreType.DMA((9,)), pltpu.SemaphoreType.DMA((TILES, 4))]
        + gather_sems(2, parts) + Reduce.scratch(4, parts, sh, width),
        far=(0, 1, 2, 4, 5), far_out=(0, 1, 2, 3, 5),
    )
    dt = attend_back(slot_clip, t, do, logs, inner)
    pg, grads_one, total = comm_call(
        functools.partial(first_comm_kernel, parts), "project_in_back_reduce", 2,
        (x, a1, o, dz, dt, dm, vec, wi, sums_two, sums_be, rest),
        [wide, ((LAST_BLOCKS, sh, width), BF), ((16, width), F32)],
        [pltpu.VMEM((LAST_BLOCKS,) + block, BF), pltpu.VMEM(*low), pltpu.VMEM(*low), pltpu.VMEM(*low),
         pltpu.VMEM(*low), pltpu.VMEM((rows, 3 * width), BF), pltpu.VMEM(*wide), pltpu.VMEM((3,) + block, BF),
         pltpu.SemaphoreType.DMA((9,))]
        + Reduce.scratch(LAST_BLOCKS, parts, sh, width) + Vector.scratch(parts, (16, width), F32),
        far=(0, 1, 2, 3, 4, 5, 7, 10),
    )
    return update(rates, count, grads_two, grads_one, total, out, pg, masters, moments, averages)


def on_device(
    patches, slot_clip, out_grad,
    project_in_weight, project_in_moment, project_in_average,
    project_out_weight, project_out_moment, project_out_average,
    expand_weight, expand_moment, expand_average,
    contract_weight, contract_moment, contract_average,
    vector_weight, vector_moment, vector_average,
):
    masters = (project_in_weight, project_out_weight, expand_weight, contract_weight, vector_weight)
    moments = (project_in_moment, project_out_moment, expand_moment, contract_moment, vector_moment)
    averages = (project_in_average, project_out_average, expand_average, contract_average, vector_average)
    parts, copies = lax.axis_size("fsdp"), lax.axis_size("rep")
    count, width = patches.shape
    direct = copies == 4 and parts % 4 == 0 and width // parts % 48 == 0
    path = direct_path if direct else plain_path
    tokens_all = count * parts * copies
    rates = [rate / tokens_all**0.5 for rate in RATES]
    return tuple(path(patches, slot_clip, out_grad, masters, moments, averages, rates))


def solution(mesh):
    tokens = P(("fsdp", "rep"), None)
    split, split_vector = P("fsdp", None), P(None, "fsdp")
    in_specs = (tokens, P(("fsdp", "rep")), tokens) + (split,) * 12 + (split_vector,) * 3
    out_specs = (tokens,) * 2 + (split,) * 20 + (split_vector,) * 5
    return jax.shard_map(on_device, mesh=mesh, in_specs=in_specs, out_specs=out_specs, check_vma=False)
```

```python
import functools
import math

import jax
import jax.numpy as jnp
from jax import lax
from jax.sharding import PartitionSpec as P
import jax.experimental.pallas as pl
import jax.experimental.pallas.tpu as pltpu

BF, F32 = jnp.bfloat16, jnp.float32
HEAD_DIM = 64
SLOT = 49
LIVE_MAX = 8
WIN = 416
EPSILON = 1e-06
MOMENTUM = 0.5
AVERAGE = 0.5
RATES = (0.3, 0.3, 0.1, 0.03, 0.5)
NEG = -1e30

def dg(a,b,ca,cb):
    return lax.dot_general(a,b,(((ca,),(cb,)),((),())),preferred_element_type=F32)

def both(x, lane):
    keep = (lane < 64).astype(BF)
    return jnp.concatenate([x*keep, x*(1-keep)], axis=0)

def group_end(clips, start, slots):
    end = start+1
    for e in range(2, LIVE_MAX+1):
        cand = start+e
        safe = jnp.minimum(cand, slots-1)
        edge = (cand == slots) | ((cand < slots) & ((clips[safe] != clips[jnp.maximum(safe-1,0)]) | (clips[safe] < 0)))
        end = jnp.where(edge, cand, end)
    return end

def fill_bias(clips, w0, start, end, bias):
    def keys(shape, dim):
        row = lax.broadcasted_iota(jnp.int32, shape, dim) + w0
        slot = (row*1338) >> 16
        key = -1-row
        for ahead in range(LIVE_MAX):
            s = start+ahead
            clip = clips[jnp.minimum(s, clips.shape[0]-1)]
            key = jnp.where((slot == s) & (s < end) & (clip >= 0), clip, key)
        return key
    bias[...] = jnp.where(keys((WIN,1),0) == keys((1,WIN),1), 0.0, NEG)

def clear_tail(ref, slots):
    tail = slots*SLOT//16*16
    ref[pl.ds(tail, ref.shape[0]-tail), :] = jnp.zeros((ref.shape[0]-tail, ref.shape[1]), BF)

def fwd_kernel(clips, t_ref, g_ref, o_ref, dy_ref, log_ref, bias):
    slots = clips.shape[0]
    rows = t_ref.shape[0]; D = o_ref.shape[1]
    clear_tail(o_ref, slots)
    clear_tail(dy_ref, slots)
    log_ref[...] = jnp.zeros_like(log_ref)
    live = lax.fori_loop(0, slots, lambda s, n: n + jnp.where(clips[s] >= 0, SLOT, 0), 0)
    row = lax.broadcasted_iota(jnp.int32,(slots*SLOT,1),0)
    dy_ref[pl.ds(0,slots*SLOT), :] = jnp.where(row < live, g_ref[...].astype(F32), 0.0).astype(BF)
    def group(g, start):
        @pl.when(start < slots)
        def _():
            end = group_end(clips, start, slots)
            r0 = start*SLOT; r1 = end*SLOT
            w0 = pl.multiple_of(jnp.minimum((r0>>4)<<4, rows-WIN), 16)
            fill_bias(clips, w0, start, end, bias)
            rowi = lax.broadcasted_iota(jnp.int32,(WIN,128),0)+w0
            mine = (rowi >= r0) & (rowi < r1)
            lane = lax.broadcasted_iota(jnp.int32,(1,128),1)
            win = pl.ds(w0, WIN)
            logs = log_ref[win, :]
            for p in range(D//128):
                q = t_ref[win, pl.ds(p*128,128)]
                k = t_ref[win, pl.ds(D+p*128,128)]
                v = t_ref[win, pl.ds(2*D+p*128,128)]
                s = dg(both(q, lane), k, 1, 1)
                es, tops = [], []
                for h in range(2):
                    part = s[h*WIN:(h+1)*WIN] + bias[...]
                    top = jnp.max(part, axis=1, keepdims=True)
                    es.append(jnp.exp(part-top).astype(BF))
                    tops.append(top)
                ones = jnp.concatenate([v, jnp.ones_like(v)], axis=1)
                mixed = jnp.dot(jnp.concatenate(es, axis=0), ones, preferred_element_type=F32)
                outs = []
                for h in range(2):
                    total = mixed[h*WIN:(h+1)*WIN, 128:]
                    outs.append(mixed[h*WIN:(h+1)*WIN, :128] / total)
                    logs = jnp.where(mine & (lane == 2*p+h), tops[h] + jnp.log(total), logs)
                o = jnp.where(lane < 64, outs[0], outs[1])
                old = o_ref[win, pl.ds(p*128,128)]
                o_ref[win, pl.ds(p*128,128)] = jnp.where(mine, o, old.astype(F32)).astype(BF)
            log_ref[win, :] = logs
        return jnp.where(start < slots, group_end(clips, start, slots), start)
    lax.fori_loop(0, (2*slots)//(LIVE_MAX+1)+1, group, 0)

def bwd_kernel(clips, t_ref, do_ref, log_ref, inner_ref, dt_ref, bias):
    slots = clips.shape[0]
    rows = t_ref.shape[0]; D = do_ref.shape[1]
    clear_tail(dt_ref, slots)
    def group(g, start):
        @pl.when(start < slots)
        def _():
            end = group_end(clips, start, slots)
            r0 = start*SLOT; r1 = end*SLOT
            w0 = pl.multiple_of(jnp.minimum((r0>>4)<<4, rows-WIN), 16)
            fill_bias(clips, w0, start, end, bias)
            rowi = lax.broadcasted_iota(jnp.int32,(WIN,128),0)+w0
            mine = (rowi >= r0) & (rowi < r1)
            lane = lax.broadcasted_iota(jnp.int32,(1,128),1)
            win = pl.ds(w0, WIN)
            logs = log_ref[win, :].T
            inners = inner_ref[win, :].T
            for p in range(D//128):
                q = t_ref[win, pl.ds(p*128,128)]
                k = t_ref[win, pl.ds(D+p*128,128)]
                v = t_ref[win, pl.ds(2*D+p*128,128)]
                do = do_ref[win, pl.ds(p*128,128)]
                s = dg(both(k, lane), q, 1, 1)
                dp = dg(both(v, lane), do, 1, 1)
                pts, dss = [], []
                for h in range(2):
                    n = 2*p+h
                    rows_h = slice(h*WIN, (h+1)*WIN)
                    pt = jnp.exp((s[rows_h] + bias[...]) - logs[n:n+1, :])
                    dss.append((pt*(dp[rows_h]-inners[n:n+1, :])).astype(BF))
                    pts.append(pt.astype(BF))
                dv = jnp.dot(jnp.concatenate(pts, axis=0), do, preferred_element_type=F32)
                dk = jnp.dot(jnp.concatenate(dss, axis=0), q, preferred_element_type=F32)
                dq = jnp.dot(jnp.concatenate([d.T for d in dss], axis=0), k, preferred_element_type=F32)
                dqs, dks, dvs = ([x[:WIN], x[WIN:]] for x in (dq, dk, dv))
                for i,x in enumerate((dqs,dks,dvs)):
                    new = jnp.where(lane < 64, x[0], x[1]).astype(BF).astype(F32)
                    if i==0: new = new*(64**-0.5)
                    c = pl.ds(i*D+p*128,128)
                    old = dt_ref[win, c].astype(F32)
                    dt_ref[win, c] = jnp.where(mine, new, old).astype(BF)
        return jnp.where(start < slots, group_end(clips, start, slots), start)
    lax.fori_loop(0, (2*slots)//(LIVE_MAX+1)+1, group, 0)

def attend(clips, t, g):
    D=t.shape[1]//3
    return pl.pallas_call(fwd_kernel, out_shape=[jax.ShapeDtypeStruct((t.shape[0],D),BF)]*2+[jax.ShapeDtypeStruct((t.shape[0],128),F32)],
      in_specs=[pl.BlockSpec(memory_space=pltpu.SMEM)]+[pl.BlockSpec(memory_space=pltpu.VMEM)]*2,
      out_specs=[pl.BlockSpec(memory_space=pltpu.VMEM)]*3,
      scratch_shapes=[pltpu.VMEM((WIN,WIN),F32)],
      compiler_params=pltpu.CompilerParams(vmem_limit_bytes=62*2**20),name="attention_forward")(clips,t,g)
def attend_back(clips, t, do, logs, inners):
    return pl.pallas_call(bwd_kernel, out_shape=jax.ShapeDtypeStruct(t.shape,BF),
      in_specs=[pl.BlockSpec(memory_space=pltpu.SMEM)]+[pl.BlockSpec(memory_space=pltpu.VMEM)]*4,
      out_specs=pl.BlockSpec(memory_space=pltpu.VMEM),
      scratch_shapes=[pltpu.VMEM((WIN,WIN),F32)],
      compiler_params=pltpu.CompilerParams(vmem_limit_bytes=62*2**20),name="attention_backward")(clips,t,do,logs,inners)


RT = 400


def dot_nt(left, right):
    return lax.dot_general(left, right, (((1,), (1,)), ((), ())), preferred_element_type=F32)


def dot_tn(left, right):
    return lax.dot_general(left, right, (((0,), (0,)), ((), ())), preferred_element_type=F32)


def dot_nn(left, right):
    return jnp.dot(left, right, preferred_element_type=F32)


def norm_parts(values):
    centred = values - jnp.mean(values, axis=-1, keepdims=True)
    scale = lax.rsqrt(jnp.mean(centred * centred, axis=-1, keepdims=True) + EPSILON)
    return centred * scale, scale


def norm_back(grad, gain, unit, scale):
    inner = grad * gain
    return scale * (
        inner
        - jnp.mean(inner, axis=-1, keepdims=True)
        - unit * jnp.mean(inner * unit, axis=-1, keepdims=True)
    )


def gelu_pair(u):
    bell = jnp.exp(-0.5 * u * u)
    t = 1.0 / (1.0 + (0.3275911 * 0.5**0.5) * jnp.abs(u))
    poly = t * (
        0.5 * 0.254829592
        + t * (-0.5 * 0.284496736 + t * (0.5 * 1.421413741 + t * (-0.5 * 1.453152027 + t * (0.5 * 1.061405429))))
    )
    tail = poly * bell
    phi = jnp.where(u < 0, tail, 1.0 - tail)
    return u * phi, phi + u * (bell * (2.0 * math.pi) ** -0.5)


def column_sum(values):
    return jnp.sum(values, axis=0, keepdims=True)


def tiles(rows, body):
    @pl.loop(0, rows // RT)
    def _(i):
        body(pl.ds(pl.multiple_of(i * RT, 16), RT))


def qkv_norm(x_ref, vec, a1_ref):
    def one(win):
        unit, _ = norm_parts(x_ref[win, :].astype(F32))
        a1_ref[win, :] = (unit * vec[0:1, :] + vec[1:2, :]).astype(BF)

    tiles(x_ref.shape[0], one)


def qkv_block(a1_ref, w_ref, t_ref, part):
    width = a1_ref.shape[1]
    weight = w_ref[part].reshape(width, width)

    def one(win):
        out = dot_nn(a1_ref[win, :], weight)
        if part == 0:
            out = out * HEAD_DIM**-0.5
        t_ref[win, pl.ds(part * width, width)] = out.astype(BF)

    tiles(a1_ref.shape[0], one)


def qkv_kernel(x_ref, vec, w_ref, t_ref, a1_ref):
    qkv_norm(x_ref, vec, a1_ref)
    for part in range(3):
        qkv_block(a1_ref, w_ref, t_ref, part)


def middle_step(x_ref, o_ref, vec, wo_ref, m_ref, a2_ref):
    def one(win):
        middle = x_ref[win, :].astype(F32) + (dot_nn(o_ref[win, :], wo_ref[...]) + vec[2:3, :])
        m_ref[win, :] = middle
        unit, _ = norm_parts(middle)
        a2_ref[win, :] = (unit * vec[3:4, :] + vec[4:5, :]).astype(BF)

    tiles(x_ref.shape[0], one)


def chunk_step(first, bias, a2_ref, dy_ref, we_ref, wc_ref, h_ref, du_ref, y_ref, da2_ref, be_ref):
    be_ref[...] = jnp.zeros_like(be_ref)

    def one(win):
        hidden, slope = gelu_pair(dot_nn(a2_ref[win, :], we_ref[...]) + bias)
        hidden = hidden.astype(BF)
        h_ref[win, :] = hidden
        du = (dot_nt(dy_ref[win, :], wc_ref[...]) * slope).astype(BF)
        du_ref[win, :] = du
        be_ref[...] += column_sum(du.astype(F32))
        y = dot_nn(hidden, wc_ref[...])
        da2 = dot_nt(du, we_ref[...])
        if first is True:
            y_ref[win, :] = y
            da2_ref[win, :] = da2
        else:
            y_ref[win, :] += y
            da2_ref[win, :] += da2

    tiles(a2_ref.shape[0], one)


def middle_back(live_rows, m_ref, y_ref, dy_ref, da2_ref, vec, wo_ref, out_ref, dm_ref, dz_ref, do_ref, sums):
    sums[...] = jnp.zeros_like(sums)

    def one(win):
        middle = m_ref[win, :]
        out_ref[win, :] = (middle + (y_ref[win, :] + vec[5:6, :])).astype(BF)
        unit, scale = norm_parts(middle)
        da2 = da2_ref[win, :]
        dy = dy_ref[win, :].astype(F32)
        dm = dy + norm_back(da2, vec[3:4, :], unit, scale)
        dm_ref[win, :] = dm
        dz = dm.astype(BF)
        dz_ref[win, :] = dz
        do_ref[win, :] = dot_nt(dz, wo_ref[...]).astype(BF)
        sums[0:1, :] += column_sum(da2 * unit)
        sums[1:2, :] += column_sum(da2)
        sums[2:3, :] += column_sum(dz.astype(F32))
        sums[3:4, :] += column_sum(dy)

    tiles(m_ref.shape[0], one)


def feed_kernel(
    x_ref, o_ref, dy_ref, vec, wo_ref, we_ref, wc_ref,
    out_ref, dm_ref, do_ref, gwo_ref, gwe_ref, gwc_ref, sums, be_ref,
    m_ref, a2_ref, h_ref, du_ref, y_ref, da2_ref, dz_ref,
):
    middle_step(x_ref, o_ref, vec, wo_ref, m_ref, a2_ref)
    for j in range(4):
        chunk_step(
            j == 0, vec[6 + j : 7 + j, :], a2_ref, dy_ref, we_ref.at[j], wc_ref.at[j],
            h_ref, du_ref, y_ref, da2_ref, be_ref.at[pl.ds(8 * j, 1)],
        )
        gwc_ref[j] = dot_tn(h_ref[...], dy_ref[...]).astype(BF)
        gwe_ref[j] = dot_tn(a2_ref[...], du_ref[...]).astype(BF)
    middle_back(None, m_ref, y_ref, dy_ref, da2_ref, vec, wo_ref, out_ref, dm_ref, dz_ref, do_ref, sums)
    gwo_ref[...] = dot_tn(o_ref[...], dz_ref[...]).astype(BF)


def first_back(x_ref, dt_ref, dm_ref, vec, w_refs, pg_ref, sums):
    sums[...] = jnp.zeros_like(sums)
    width = x_ref.shape[1]

    def one(win):
        da1 = dot_nt(dt_ref[win, pl.ds(0, width)], w_refs[0][...])
        da1 += dot_nt(dt_ref[win, pl.ds(width, width)], w_refs[1][...])
        da1 += dot_nt(dt_ref[win, pl.ds(2 * width, width)], w_refs[2][...])
        unit, scale = norm_parts(x_ref[win, :].astype(F32))
        pg_ref[win, :] = dm_ref[win, :] + norm_back(da1, vec[0:1, :], unit, scale)
        sums[0:1, :] += column_sum(da1 * unit)
        sums[1:2, :] += column_sum(da1)

    tiles(x_ref.shape[0], one)


def first_kernel(x_ref, a1_ref, dt_ref, dm_ref, vec, w_ref, pg_ref, gwi_ref, sums):
    width = x_ref.shape[1]
    for part in range(3):
        gwi_ref[part] = dot_tn(a1_ref[...], dt_ref[:, pl.ds(part * width, width)]).astype(BF)
    first_back(x_ref, dt_ref, dm_ref, vec, [w_ref.at[p] for p in range(3)], pg_ref, sums)


VM = pl.BlockSpec(memory_space=pltpu.VMEM)
SM = pl.BlockSpec(memory_space=pltpu.SMEM)


def vmem_call(kernel, name, ins, outs, scratch=(), smem=0):
    return pl.pallas_call(
        kernel,
        out_shape=[jax.ShapeDtypeStruct(s, d) for s, d in outs],
        in_specs=[SM] * smem + [VM] * (len(ins) - smem),
        out_specs=[VM] * len(outs),
        scratch_shapes=[pltpu.VMEM(s, d) for s, d in scratch],
        compiler_params=pltpu.CompilerParams(vmem_limit_bytes=60 * 2**20),
        name=name,
    )(*ins)


MESH = pl.DeviceIdType.MESH


class Place:
    def __init__(self, parts, sh, width):
        mine, copy = lax.axis_index("fsdp"), lax.axis_index("rep")
        self.outer_count = parts // 2
        self.outer, self.inner = mine // 2, mine % 2
        self.plane, self.core = copy // 2, copy % 2
        self.third = sh // 3
        self.half = width // 2

    def device(self, outer=None, inner=None, plane=None, core=None):
        outer = self.outer if outer is None else outer
        inner = self.inner if inner is None else inner
        plane = self.plane if plane is None else plane
        core = self.core if core is None else core
        return (outer * 2 + inner, plane * 2 + core)

    def far(self, k):
        return (self.outer + k) % self.outer_count

    def ranks(self):
        return range(1, self.outer_count)

    def columns(self, core=None):
        core = self.core if core is None else core
        return pl.ds(pl.multiple_of(core * self.half, 128), self.half)

    def held(self):
        return pl.ds(pl.multiple_of(self.plane * self.third, 16), 2 * self.third)

    def own(self, plane=None):
        plane = self.plane if plane is None else plane
        return pl.ds(pl.multiple_of(plane * (2 * self.third), 16), self.third)

    def peers(self):
        return [self.device(outer=self.far(k)) for k in self.ranks()] + [
            self.device(inner=1 - self.inner),
            self.device(plane=1 - self.plane),
            self.device(core=1 - self.core),
            self.device(plane=1 - self.plane, core=1 - self.core),
        ]

    def greet(self):
        barrier = pltpu.get_barrier_semaphore()
        peers = self.peers()
        for peer in peers:
            pl.semaphore_signal(barrier, inc=1, device_id=peer, device_id_type=MESH)
        pl.semaphore_wait(barrier, len(peers))


def remote(src, dst, sems, index, device):
    return pltpu.make_async_remote_copy(
        src_ref=src, dst_ref=dst, send_sem=sems[0].at[index], recv_sem=sems[1].at[index],
        device_id=device, device_id_type=MESH,
    )


def start(copies):
    for copy in copies:
        copy.start()


def landed(copies):
    for copy in copies:
        copy.wait_recv()


def sent(copies):
    for copy in copies:
        copy.wait_send()


class Gather:
    def __init__(self, place, shard, full, sems):
        self.p, self.shard, self.full, self.sems = place, shard, full, sems

    def far(self, b):
        p = self.p
        return [
            remote(
                self.shard.at[b, p.held(), p.columns()],
                self.full.at[b, p.outer, p.inner, p.held(), p.columns()],
                self.sems, (b, k - 1), p.device(outer=p.far(k)),
            )
            for k in p.ranks()
        ]

    def pair(self, b, which):
        p = self.p
        if which == 0:
            ref = self.full.at[b, :, p.inner, p.held(), p.columns()]
            device = p.device(inner=1 - p.inner)
        elif which == 1:
            ref = self.full.at[b, :, :, p.own(), p.columns()]
            device = p.device(plane=1 - p.plane)
        else:
            ref = self.full.at[b, :, :, :, p.columns()]
            device = p.device(core=1 - p.core)
        return [remote(ref, ref, self.sems, (b, p.outer_count - 1 + which), device)]

    def put_own(self, b):
        p = self.p
        self.full[b, p.outer, p.inner, p.held(), p.columns()] = self.shard[b, p.held(), p.columns()]

    def step(self, s, count, lag):
        for stage in range(5):
            @pl.when((s >= stage * lag) & (s < count + stage * lag))
            def _():
                self.stage(s - stage * lag, stage)

    def stage(self, b, stage):
        if stage == 0:
            start(self.far(b))
            self.put_own(b)
        else:
            landed(self.far(b) if stage == 1 else self.pair(b, stage - 2))
            if stage < 4:
                start(self.pair(b, stage - 1))

    def finish(self, count):
        @pl.loop(0, count)
        def _(b):
            sent(self.far(b))
            for which in range(3):
                sent(self.pair(b, which))


def gather_sems(blocks, parts):
    shape = (blocks, parts // 2 - 1 + 3)
    return [pltpu.SemaphoreType.DMA(shape), pltpu.SemaphoreType.DMA(shape)]


class Reduce:
    def __init__(self, place, grad, out, bufs, sems):
        self.p, self.grad, self.out, self.sems = place, grad, out, sems
        self.from_core, self.from_plane, self.from_inner, self.from_far, self.part, self.from_part = bufs

    @staticmethod
    def scratch(blocks, parts, sh, width):
        outer, third, half = parts // 2, sh // 3, width // 2
        shape = (blocks, outer - 1 + 6)
        return [
            pltpu.VMEM((blocks, outer, 2, sh, half), BF),
            pltpu.VMEM((blocks, outer, 2, third, half), BF),
            pltpu.VMEM((blocks, outer, 2 * third, half), BF),
            pltpu.VMEM((blocks, outer - 1, 2 * third, half), BF),
            pltpu.VMEM((blocks, 2 * third, half), BF),
            pltpu.VMEM((blocks, 3, 2 * third, half), BF),
            pltpu.SemaphoreType.DMA(shape),
            pltpu.SemaphoreType.DMA(shape),
        ]

    def copies(self, b, stage):
        p = self.p
        base = p.outer_count - 1
        if stage == 0:
            src, dst = self.grad.at[b, :, :, :, p.columns(1 - p.core)], self.from_core.at[b]
            device = p.device(core=1 - p.core)
        elif stage == 1:
            src, dst = self.grad.at[b, :, :, p.own(1 - p.plane), p.columns()], self.from_plane.at[b]
            device = p.device(plane=1 - p.plane)
        elif stage == 2:
            src, dst = self.grad.at[b, :, 1 - p.inner, p.held(), p.columns()], self.from_inner.at[b]
            device = p.device(inner=1 - p.inner)
        elif stage == 3:
            return [
                remote(
                    self.grad.at[b, p.far(k), p.inner, p.held(), p.columns()],
                    self.from_far.at[b, k - 1], self.sems, (b, k - 1), p.device(outer=p.far(k)),
                )
                for k in p.ranks()
            ]
        else:
            others = (
                p.device(plane=1 - p.plane), p.device(core=1 - p.core),
                p.device(plane=1 - p.plane, core=1 - p.core),
            )
            return [
                remote(self.part.at[b], self.from_part.at[b, n], self.sems, (b, base + 3 + n), other)
                for n, other in enumerate(others)
            ]
        return [remote(src, dst, self.sems, (b, base + stage), device)]

    def add(self, b, stage):
        p = self.p
        if stage == 0:
            @pl.loop(0, p.outer_count)
            def _(o):
                for i in range(2):
                    index = (b, o, i, slice(None), p.columns())
                    self.grad[index] = (self.grad[index].astype(F32) + self.from_core[b, o, i].astype(F32)).astype(BF)
        elif stage == 1:
            for i in range(2):
                @pl.loop(0, p.outer_count)
                def _(o):
                    index = (b, o, i, p.own(), p.columns())
                    self.grad[index] = (self.grad[index].astype(F32) + self.from_plane[b, o, i].astype(F32)).astype(BF)
        elif stage == 2:
            @pl.loop(0, p.outer_count)
            def _(o):
                index = (b, o, p.inner, p.held(), p.columns())
                self.grad[index] = (self.grad[index].astype(F32) + self.from_inner[b, o].astype(F32)).astype(BF)
        elif stage == 3:
            total = self.grad[b, p.outer, p.inner, p.held(), p.columns()].astype(F32)
            for k in p.ranks():
                total += self.from_far[b, k - 1].astype(F32)
            self.part[b] = total.astype(BF)
        elif stage == 4:
            third = p.third
            for core in range(2):
                for plane in range(2):
                    @pl.when((p.core == core) & (p.plane == plane))
                    def _():
                        pieces = self.part.at[b], *(self.from_part.at[b, n] for n in range(3))
                        for other in range(2):
                            mine, theirs = pieces[2 * other], pieces[2 * other + 1]
                            first, last = (mine, theirs) if plane == 0 else (theirs, mine)
                            half = core if other == 0 else 1 - core
                            columns = pl.ds(half * p.half, p.half)
                            middle = first[pl.ds(third, third), :].astype(F32) + last[pl.ds(0, third), :].astype(F32)
                            self.out[b, pl.ds(0, third), columns] = first[pl.ds(0, third), :]
                            self.out[b, pl.ds(third, third), columns] = middle.astype(BF)
                            self.out[b, pl.ds(2 * third, third), columns] = last[pl.ds(third, third), :]

    def stage(self, b, stage):
        if stage > 0:
            landed(self.copies(b, stage - 1))
            self.add(b, stage - 1)
        if stage < 5:
            start(self.copies(b, stage))

    def step(self, s, count, lag):
        for stage in range(6):
            @pl.when((s >= stage * lag) & (s < count + stage * lag))
            def _():
                self.stage(s - stage * lag, stage)

    def finish(self, count):
        @pl.loop(0, count)
        def _(b):
            for stage in range(5):
                sent(self.copies(b, stage))


class Vector:
    def __init__(self, place, total, bufs, sems, everywhere):
        self.p, self.total, self.sems = place, total, sems
        self.pairs, self.fars = bufs
        self.order = (0, 1, 2) if everywhere else (2,)

    @staticmethod
    def scratch(parts, shape, dtype):
        sems = (parts // 2 - 1 + 3,)
        return [
            pltpu.VMEM((6,) + shape, dtype), pltpu.VMEM((parts // 2,) + shape, dtype),
            pltpu.SemaphoreType.DMA(sems), pltpu.SemaphoreType.DMA(sems),
        ]

    def pair(self, which):
        p = self.p
        device = (
            p.device(core=1 - p.core), p.device(plane=1 - p.plane), p.device(inner=1 - p.inner)
        )[which]
        return [remote(self.pairs.at[2 * which], self.pairs.at[2 * which + 1], self.sems, p.outer_count - 1 + which, device)]

    def far(self):
        p = self.p
        mine = self.fars.at[p.outer]
        return [remote(mine, mine, self.sems, k - 1, p.device(outer=p.far(k))) for k in p.ranks()]

    def far_landed(self):
        p = self.p
        for k in p.ranks():
            theirs = self.fars.at[(p.outer + p.outer_count - k) % p.outer_count]
            remote(theirs, theirs, self.sems, k - 1, p.device(outer=p.far(k))).wait_recv()

    def stage(self, number):
        order = self.order
        if number > 0 and number <= len(order):
            which = order[number - 1]
            landed(self.pair(which))
            self.total[...] = self.total[...] + self.pairs[2 * which + 1]
        if number < len(order):
            which = order[number]
            self.pairs[2 * which] = self.total[...]
            start(self.pair(which))
        elif number == len(order):
            self.fars[self.p.outer] = self.total[...]
            start(self.far())
        else:
            self.far_landed()
            total = self.fars[0]
            for o in range(1, self.p.outer_count):
                total = total + self.fars[o]
            self.total[...] = total

    def stages(self):
        return len(self.order) + 2

    def finish(self):
        for which in self.order:
            sent(self.pair(which))
        sent(self.far())


FIRST_BLOCKS = 8


TILES = 3


def flat(ref, b):
    block = ref[b]
    return block.reshape(block.shape[0] * block.shape[1] * block.shape[2], block.shape[3])


def one_hot(shape, shift, along):
    row = lax.broadcasted_iota(jnp.int32, shape, 0)
    column = lax.broadcasted_iota(jnp.int32, shape, 1)
    return jnp.where((column - row if along else row - column) == shift, 1.0, 0.0)


def place_vectors(parts, vector, vec):
    sh, width = vector.shape[1], vec.shape[1]
    mine, apart = lax.axis_index("fsdp"), parts // 4
    low = vector[...].astype(BF)
    vec[...] = jnp.zeros_like(vec)
    vec[0:6, :] = dot_nn(low, one_hot((sh, width), mine * sh, True).astype(BF))[0:6, :]
    row = lax.broadcasted_iota(jnp.int32, (4, width), 0)
    for i in range(4):
        spot = one_hot((sh, width), (apart * i + mine // 4) * sh, True).astype(BF)
        vec[6:10, :] += jnp.where(row == mine % 4, dot_nn(low, spot)[6 + i : 7 + i, :], 0.0)


def gather_kernel(
    parts, x_ref, vector, wi_ref, wo_ref, we_ref, wc_ref,
    t_out, a1_ref, xp_ref, wi_out, wo_out, ff_out, rest_out, vec, t_ref, full, shard, local, *scratch
):
    count, width = x_ref.shape
    rows = xp_ref.shape[0]
    sh = wo_ref.shape[0]
    place = Place(parts, sh, width)
    weights = Gather(place, shard, full, scratch[0:2])
    vectors = Vector(place, vec, scratch[2:4], scratch[4:6], False)

    def pack_chunk(j, we_to, wc_to):
        for p in range(parts):
            we_to[:, pl.ds(p * sh, sh)] = we_ref[:, pl.ds((4 * p + j) * sh, sh)].astype(BF)
        wc_to[...] = wc_ref[pl.ds(j * sh, sh), :].astype(BF)

    shard[0] = wi_ref[:, pl.ds(0, width)].astype(BF)
    place.greet()
    weights.step(0, FIRST_BLOCKS, 1)
    place_vectors(parts, vector, vec)
    vectors.stage(0)
    for part in range(1, 3):
        shard[part] = wi_ref[:, pl.ds(part * width, width)].astype(BF)
    shard[3] = wo_ref[...].astype(BF)
    weights.step(1, FIRST_BLOCKS, 1)
    vectors.stage(1)
    tail = count // 16 * 16
    xp_ref[pl.ds(tail, rows - tail), :] = jnp.zeros((rows - tail, width), BF)
    xp_ref[pl.ds(0, count), :] = x_ref[...]
    weights.step(2, FIRST_BLOCKS, 1)
    vectors.stage(2)
    pack_chunk(0, shard.at[4], shard.at[5])
    weights.step(3, FIRST_BLOCKS, 1)
    qkv_norm(xp_ref, vec, a1_ref)
    leaving = []
    for s in range(4, FIRST_BLOCKS + 4):
        b = s - 4
        weights.step(s, FIRST_BLOCKS, 1)
        out = wi_out.at[b] if b < 3 else wo_out.at[0] if b == 3 else ff_out.at[b - 4]
        leaving.append(pltpu.make_async_copy(full.at[b], out, local.at[b]))
        leaving[-1].start()
        if b == 0:
            pack_chunk(1, shard.at[6], shard.at[7])
        if b in (3, 4):
            pack_chunk(b - 1, rest_out.at[2 * b - 6], rest_out.at[2 * b - 5])
        if b < 3:
            qkv_block(a1_ref, full, t_ref, b)
            part = pl.ds(b * width, width)
            leaving.append(pltpu.make_async_copy(t_ref.at[:, part], t_out.at[:, part], local.at[FIRST_BLOCKS + b]))
            leaving[-1].start()
    for copy in leaving:
        copy.wait()
    weights.finish(FIRST_BLOCKS)
    vectors.finish()


def feed_comm_kernel(
    parts, x_in, o_in, dy_in, vec, wo_in, early, shard,
    out_out, dm_out, do_out, dz_out, grad_out, grad_rest, sums, be_ref, inner_ref,
    x_ref, o_ref, dy_ref, wo_ref, out_ref, dm_ref, do_ref, dz_ref,
    a2_ref, y_ref, da2_ref, full, grad, local, leaving, *scratch,
):
    rows, width = x_ref.shape
    sh = shard.shape[1]
    place = Place(parts, sh, width)
    later, have = shard.shape[0], early.shape[0]
    weights = Gather(place, shard, full.at[pl.ds(have, later)], scratch[0:2])
    grads = Reduce(place, grad.at[pl.ds(0, 4)], grad_out, scratch[2:8], scratch[8:10])
    du_ref, h_ref = do_ref, dz_ref
    moves = ((x_in, x_ref), (o_in, o_ref), (wo_in, wo_ref), (dy_in, dy_ref), (early, full.at[pl.ds(0, have)]))
    ready = [pltpu.make_async_copy(source, target, local.at[4 + i]) for i, (source, target) in enumerate(moves)]
    start(ready)
    place.greet()

    def win(i):
        return pl.ds(i * RT, RT)

    def slot(number):
        for b in range(2):
            for stage in range(5):
                if (0, 3, 6, 9, 12)[stage] + b == number:
                    weights.stage(b, stage)
                if (4, 8, 12, 15, 17)[stage] + b == number:
                    weights.stage(b + 2, stage)

    slot(0)
    for copy in ready[:3]:
        copy.wait()
    wo = flat(wo_ref, 0)
    for i in range(TILES):
        middle = x_ref[win(i), :].astype(F32) + (dot_nn(o_ref[win(i), :], wo) + vec[2:3, :])
        dm_ref[win(i), :] = middle
        unit, _ = norm_parts(middle)
        a2_ref[win(i), :] = (unit * vec[3:4, :] + vec[4:5, :]).astype(BF)
        y_ref[win(i), :] = jnp.zeros((RT, width), F32)
        da2_ref[win(i), :] = jnp.zeros((RT, width), F32)
        slot(i + 1)
    for copy in ready[3:]:
        copy.wait()

    def results(i):
        pairs = ((out_ref, out_out), (dm_ref, dm_out), (do_ref, do_out), (dz_ref, dz_out))
        return [
            pltpu.make_async_copy(source.at[win(i)], target.at[win(i)], leaving.at[i, n])
            for n, (source, target) in enumerate(pairs)
        ]

    def leave(b):
        return pltpu.make_async_copy(grad.at[b], grad_rest.at[b - 4], local.at[b - 4])

    def due(position, back, parity):
        steps = position - 3 - parity + 5 * back
        return steps // 2 if steps % 2 == 0 and 0 <= steps <= 10 else None

    def passing(j, position):
        for back in range(3, -1, -1):
            for parity in range(2):
                stage = due(position, back, parity)
                if stage is not None and back <= j < back + 2:
                    grads.stage(2 * (j - back) + parity, stage)

    for j in range(4):
        bias = vec[pl.ds(6 + j, 1), :]
        be_sum = jnp.zeros((1, width), F32)
        for i in range(TILES):
            hidden, slope = gelu_pair(dot_nn(a2_ref[win(i), :], flat(full, 2 * j)) + bias)
            hidden = hidden.astype(BF)
            h_ref[win(i), :] = hidden
            du = (dot_nt(dy_ref[win(i), :], flat(full, 2 * j + 1)) * slope).astype(BF)
            du_ref[win(i), :] = du
            be_sum += column_sum(du.astype(F32))
            y_ref[win(i), :] += dot_nn(hidden, flat(full, 2 * j + 1))
            da2_ref[win(i), :] += dot_nt(du, flat(full, 2 * j))
            slot(4 + 5 * j + i)
            passing(j, i)
        be_ref[pl.ds(j, 1), :] = be_sum
        grad[2 * j] = dot_tn(h_ref[...], dy_ref[...]).astype(BF).reshape(grad.shape[1:])
        slot(4 + 5 * j + 3)
        passing(j, 3)
        grad[2 * j + 1] = dot_tn(a2_ref[...], du_ref[...]).astype(BF).reshape(grad.shape[1:])
        slot(4 + 5 * j + 4)
        passing(j, 4)

        if j >= 2:
            for parity in range(2):
                leave(2 * j + parity).start()

    sums[...] = jnp.zeros_like(sums)
    feature = lax.broadcasted_iota(jnp.int32, (width, 128), 0)
    heads = (feature // HEAD_DIM == lax.broadcasted_iota(jnp.int32, (width, 128), 1)).astype(BF)
    for position in range(5, 8):
        i = position - 5
        if i < TILES:
            middle = dm_ref[win(i), :]
            out_ref[win(i), :] = (middle + (y_ref[win(i), :] + vec[5:6, :])).astype(BF)
            unit, scale = norm_parts(middle)
            da2 = da2_ref[win(i), :]
            dy = dy_ref[win(i), :].astype(F32)
            dm = dy + norm_back(da2, vec[3:4, :], unit, scale)
            dm_ref[win(i), :] = dm
            dz = dm.astype(BF)
            dz_ref[win(i), :] = dz
            do = dot_nt(dz, wo).astype(BF)
            do_ref[win(i), :] = do
            product = do.astype(F32) * o_ref[win(i), :].astype(F32)
            high = product.astype(BF)
            inner_ref[win(i), :] = dot_nn(high, heads) + dot_nn((product - high.astype(F32)).astype(BF), heads)
            sums[0:1, :] += column_sum(da2 * unit)
            sums[1:2, :] += column_sum(da2)
            sums[2:3, :] += column_sum(dz.astype(F32))
            sums[3:4, :] += column_sum(dy)
            start(results(i))
        for j in range(0, 2):
            for parity in range(2):
                stage = due(position + 5 * (3 - j), 0, parity)
                if stage is not None:
                    grads.stage(2 * j + parity, stage)
    weights.finish(later)
    grads.finish(4)
    for b in range(4, 8):
        leave(b).wait()
    for i in range(TILES):
        for copy in results(i):
            copy.wait()


LAST_BLOCKS = 8


def first_comm_kernel(
    parts, x_in, a1_in, o_in, dz_in, dt_in, dm_in, vec, wi_in, sums_two, be_ref, rest_in,
    pg_ref, grad_out, total, grad, x_ref, a1_ref, o_ref, dz_ref, dt_ref, dm_ref, wi_ref, local, *scratch,
):
    rows, width = x_ref.shape
    place = Place(parts, width // parts, width)
    grads = Reduce(place, grad, grad_out, scratch[0:6], scratch[6:8])
    vectors = Vector(place, total, scratch[8:10], scratch[10:12], True)
    arriving = [
        pltpu.make_async_copy(rest_in.at[pl.ds(0, 2)], grad.at[pl.ds(0, 2)], local.at[0]),
        pltpu.make_async_copy(rest_in.at[pl.ds(2, 2)], grad.at[pl.ds(2, 2)], local.at[1]),
    ] + [
        pltpu.make_async_copy(source, ref, local.at[2 + i])
        for i, (source, ref) in enumerate(
            ((o_in, o_ref), (dz_in, dz_ref), (a1_in, a1_ref), (dt_in, dt_ref), (wi_in, wi_ref), (x_in, x_ref), (dm_in, dm_ref))
        )
    ]
    start(arriving)
    place.greet()
    total[...] = jnp.zeros_like(total)
    total[2:3, :] = sums_two[2:3, :]
    total[3:5, :] = sums_two[0:2, :]
    total[5:6, :] = sums_two[3:4, :]
    total[6:10, :] = be_ref[0:4, :]

    def step(s):
        grads.step(s, LAST_BLOCKS, 1)

    arriving[0].wait()
    step(0)
    arriving[1].wait()
    for i in (2, 3):
        arriving[i].wait()
    grad[4] = dot_tn(o_ref[...], dz_ref[...]).astype(BF).reshape(grad.shape[1:])
    step(1)
    for i in (4, 5):
        arriving[i].wait()
    for part in range(3):
        block = dot_tn(a1_ref[...], dt_ref[:, pl.ds(part * width, width)]).astype(BF)
        grad[part + 5] = block.reshape(grad.shape[1:])
        step(part + 2)
    for i in (6, 7, 8):
        arriving[i].wait()
    for i in range(TILES):
        win = pl.ds(i * RT, RT)
        da1 = dot_nt(dt_ref[win, pl.ds(0, width)], flat(wi_ref, 0))
        da1 += dot_nt(dt_ref[win, pl.ds(width, width)], flat(wi_ref, 1))
        da1 += dot_nt(dt_ref[win, pl.ds(2 * width, width)], flat(wi_ref, 2))
        unit, scale = norm_parts(x_ref[win, :].astype(F32))
        pg_ref[win, :] = dm_ref[win, :] + norm_back(da1, vec[0:1, :], unit, scale)
        total[0:1, :] += column_sum(da1 * unit)
        total[1:2, :] += column_sum(da1)
        step(5 + i)
    for s in range(8, LAST_BLOCKS + 5):
        if s - 8 < vectors.stages():
            vectors.stage(s - 8)
        step(s)
    grads.finish(LAST_BLOCKS)
    vectors.finish()


def comm_call(kernel, name, which, ins, outs, scratch, far=(), far_out=()):
    return pl.pallas_call(
        kernel,
        out_shape=[jax.ShapeDtypeStruct(s, d) for s, d in outs],
        in_specs=[pl.BlockSpec(memory_space=pl.ANY) if i in far else VM for i in range(len(ins))],
        out_specs=[pl.BlockSpec(memory_space=pl.ANY) if i in far_out else VM for i in range(len(outs))],
        scratch_shapes=scratch,
        compiler_params=pltpu.CompilerParams(
            vmem_limit_bytes=62 * 2**20, collective_id=which, has_side_effects=True
        ),
        name=name,
    )(*ins)


STEPS = 6


def extract_vectors(parts, total, picked):
    sh, width = picked.shape[1], total.shape[1]
    mine, apart = lax.axis_index("fsdp"), parts // 4

    def pick(rows, shift):
        return jnp.dot(
            rows, one_hot((width, sh), shift, False), precision=lax.Precision.HIGHEST, preferred_element_type=F32
        )

    picked[0:8, :] = pick(total[0:8, :], mine * sh)
    held = total[6:10, :]
    row = lax.broadcasted_iota(jnp.int32, held.shape, 0)
    held = jnp.sum(jnp.where(row == mine % 4, held, 0.0), axis=0, keepdims=True)
    held = jnp.broadcast_to(held, (8, width))
    for i in range(4):
        picked[6 + i : 7 + i, :] = pick(held, (apart * i + mine // 4) * sh)[0:1, :]


def update_kernel(rates, g_two, g_one, total, out_in, pg_in, *refs):
    state, outs, picked, flat_we = refs[:15], refs[15:42], refs[42], refs[43]
    i = pl.program_id(0)
    sh, width = g_one.shape[1:]
    parts = width // sh

    @pl.when(i == 0)
    def _():
        extract_vectors(parts, total, picked)
        for j in range(4):
            for p in range(parts):
                block = g_two[2 * j + 1] if j < 2 else g_one[2 * j - 3]
                flat_we[:, pl.ds((4 * p + j) * sh, sh)] = block[:, p * sh : (p + 1) * sh].astype(F32)

    outs[0][...] = out_in[...]
    outs[1][...] = pg_in[...]
    half, sixth = width // 2, width // STEPS
    odd = pl.ds(pl.multiple_of(i % 2 * half, 128), half)
    third = sh // 3

    def contract_rows(k):
        rows = pl.ds(pl.multiple_of(k % 3 * third, 16), third)
        j = k // 3
        low, high = g_two[2 * jnp.minimum(j, 1), rows, :], g_one[2 * jnp.maximum(j, 2) - 4, rows, :]
        return jnp.where(j < 2, low.astype(F32), high.astype(F32))

    sums = (
        g_one[5 + i // 2, :, odd].astype(F32),
        g_one[4, :, pl.ds(pl.multiple_of(i * sixth, 128), sixth)].astype(F32),
        flat_we[:, pl.ds(pl.multiple_of(i * 4 * sixth, 128), 4 * sixth)],
        jnp.concatenate([contract_rows(2 * i), contract_rows(2 * i + 1)], axis=0),
        picked[0:10, :],
    )
    for member in range(5):
        weight, moment, average = (ref[...] for ref in state[3 * member : 3 * member + 3])
        for ref, value in zip(
            outs[2 + 5 * member : 7 + 5 * member], step(sums[member], rates[member], weight, moment, average)
        ):
            ref[...] = value


def update(rates, count, g_two, g_one, total, out, pg, masters, moments, averages):
    sh, width = g_one.shape[1:]
    across = [
        pl.BlockSpec((sh, width // 2), lambda i: (0, i)),
        pl.BlockSpec((sh, width // STEPS), lambda i: (0, i)),
        pl.BlockSpec((sh, 4 * width // STEPS), lambda i: (0, i)),
        pl.BlockSpec((4 * sh // STEPS, width), lambda i: (i, 0)),
        pl.BlockSpec(masters[4].shape, lambda i: (0, 0)),
    ]
    rows = (count + STEPS - 1) // STEPS
    by_row = pl.BlockSpec(((rows + 15) // 16 * 16, width), lambda i: (i, 0))
    ins, specs = [], []
    outs = [jax.ShapeDtypeStruct((count, width), BF), jax.ShapeDtypeStruct((count, width), F32)]
    out_specs = [by_row] * 2
    for member in range(5):
        ins += [masters[member], moments[member], averages[member]]
        specs += [across[member]] * 3
        shape = masters[member].shape
        outs += [jax.ShapeDtypeStruct(shape, F32)] * 4 + [jax.ShapeDtypeStruct(shape, BF)]
        out_specs += [across[member]] * 5
    return pl.pallas_call(
        functools.partial(update_kernel, rates),
        grid=(STEPS,),
        out_shape=outs,
        in_specs=[pl.BlockSpec(g.shape, lambda i: (0, 0, 0)) for g in (g_two, g_one)]
        + [pl.BlockSpec(total.shape, lambda i: (0, 0))] + [by_row] * 2 + specs,
        out_specs=out_specs,
        scratch_shapes=[pltpu.VMEM((16, sh), F32), pltpu.VMEM((sh, 4 * width), F32)],
        compiler_params=pltpu.CompilerParams(vmem_limit_bytes=62 * 2**20),
        name="momentum_step",
    )(g_two, g_one, total, out, pg, *ins)


def run_qkv(x, vec, wi):
    rows, width = x.shape
    return vmem_call(
        qkv_kernel, "project_in", (x, vec, wi), [((rows, 3 * width), BF), ((rows, width), BF)]
    )


def run_feed(x, o, dy, vec, wo, we, wc):
    rows, width = x.shape
    wide, low = ((rows, width), F32), ((rows, width), BF)
    return vmem_call(
        feed_kernel, "feed_forward", (x, o, dy, vec, wo, we, wc),
        [low, wide, low, ((width, width), BF), ((4, width, width), BF), ((4, width, width), BF),
         ((8, width), F32), ((32, width), F32)],
        [wide, low, low, low, wide, wide, low],
    )


def run_first(x, a1, dt, dm, vec, wi):
    rows, width = x.shape
    return vmem_call(
        first_kernel, "project_in_back", (x, a1, dt, dm, vec, wi),
        [((rows, width), F32), ((3, width, width), BF), ((8, width), F32)],
    )


def pack_shards(wi, wo, we, wc, parts):
    rows, width = wo.shape
    wi = wi.reshape(rows, 3, width).swapaxes(0, 1)
    we = we.reshape(rows, parts, 4, rows).transpose(2, 0, 1, 3).reshape(4, rows, width)
    wc = wc.reshape(4, rows, width)
    return jnp.concatenate([wi, wo[None], we, wc], axis=0)


def unpack_shards(blocks, parts):
    rows, width = blocks.shape[1:]
    wi = blocks[0:3].swapaxes(0, 1).reshape(rows, 3 * width)
    we = blocks[4:8].reshape(4, rows, parts, rows).transpose(1, 2, 0, 3).reshape(rows, 4 * width)
    return wi, blocks[3], we, blocks[8:12].reshape(4 * rows, width)


def step(grad_sum, rate, weight, moment, average):
    moment_new = MOMENTUM * moment + grad_sum
    weight_new = weight - rate * (grad_sum + MOMENTUM * moment_new)
    average_new = AVERAGE * average + (1.0 - AVERAGE) * weight_new
    return [grad_sum, moment_new, weight_new, average_new, weight_new.astype(BF)]


def plain_path(patches, slot_clip, out_grad, masters, moments, averages, rates):
    parts, copies = lax.axis_size("fsdp"), lax.axis_size("rep")
    mine, copy = lax.axis_index("fsdp"), lax.axis_index("rep")
    count, width = patches.shape
    rows = (count + RT - 1) // RT * RT
    sh = width // parts
    packed = pack_shards(*(m.astype(BF) for m in masters[:4]), parts).reshape(12 * sh, width)
    piece = 12 * sh // copies
    quarter = lax.dynamic_slice_in_dim(packed, copy * piece, piece, 0)
    full = lax.all_gather(quarter, ("fsdp", "rep"), axis=0, tiled=True)
    full = full.reshape(parts, 12, sh, width).swapaxes(0, 1).reshape(12, width, width)
    vec = lax.all_gather(masters[4].astype(BF), "fsdp", axis=1, tiled=True).astype(F32)
    be = vec[6:].reshape(parts, 4, sh).swapaxes(0, 1).reshape(4, width)
    vec = jnp.concatenate([vec[:6], be, jnp.zeros((6, width), F32)], axis=0)

    pad = ((0, rows - count), (0, 0))
    x = jnp.pad(patches, pad)
    t, a1 = run_qkv(x, vec, full[0:3])
    o, dy, logs = attend(slot_clip, t, out_grad)
    out, dm, do, gwo, gwe, gwc, sums_two, sums_be = run_feed(x, o, dy, vec, full[3], full[4:8], full[8:12])
    inner = jnp.sum((o.astype(F32) * do.astype(F32)).reshape(rows, -1, HEAD_DIM), axis=2)
    inner = jnp.pad(inner, ((0, 0), (0, 128 - inner.shape[1])))
    dt = attend_back(slot_clip, t, do, logs, inner)
    pg, gwi, sums_one = run_first(x, a1, dt, dm, vec, full[0:3])

    grads = jnp.concatenate([gwi, gwo[None], gwe, gwc], axis=0)
    grads = grads.reshape(12, parts, sh, width).swapaxes(0, 1).reshape(parts * 12 * sh, width)
    grads = lax.psum_scatter(grads, ("fsdp", "rep"), scatter_dimension=0, tiled=True)
    grads = lax.all_gather(grads, "rep", axis=0, tiled=True).reshape(12, sh, width)
    be_grad = sums_be[::8].reshape(4, parts, sh).swapaxes(0, 1).reshape(4, width)
    vector = jnp.concatenate(
        [sums_one[0:2], sums_two[2:3], sums_two[0:2], sums_two[3:4], be_grad], axis=0
    )
    vector = lax.dynamic_slice_in_dim(lax.psum(vector, ("fsdp", "rep")), mine * sh, sh, 1)
    outputs = []
    for member, grad in enumerate((*unpack_shards(grads, parts), vector)):
        outputs += step(grad.astype(F32), rates[member], masters[member], moments[member], averages[member])
    return (out[:count], pg[:count], *outputs)


def direct_path(patches, slot_clip, out_grad, masters, moments, averages, rates):
    parts = lax.axis_size("fsdp")
    count, width = patches.shape
    rows = (count + RT - 1) // RT * RT
    sh = width // parts
    block = (parts // 2, 2, sh, width)
    wide, low = ((rows, width), F32), ((rows, width), BF)
    t, a1, x, wi, wo, early, later, vec = comm_call(
        functools.partial(gather_kernel, parts), "gather_project_in", 0, (patches, masters[4], *masters[:4]),
        [((rows, 3 * width), BF), low, low, ((3,) + block, BF), ((1,) + block, BF),
         ((FIRST_BLOCKS - 4,) + block, BF), ((4, sh, width), BF), ((16, width), F32)],
        [pltpu.VMEM((rows, 3 * width), BF), pltpu.VMEM((FIRST_BLOCKS,) + block, BF),
         pltpu.VMEM((FIRST_BLOCKS, sh, width), BF), pltpu.SemaphoreType.DMA((FIRST_BLOCKS + 3,))]
        + gather_sems(FIRST_BLOCKS, parts) + Vector.scratch(parts, (16, width), F32),
        far_out=(0, 3, 4, 5),
    )
    o, dy, logs = attend(slot_clip, t, out_grad)
    out, dm, do, dz, grads_two, rest, sums_two, sums_be, inner = comm_call(
        functools.partial(feed_comm_kernel, parts), "feed_forward_reduce", 1,
        (x, o, dy, vec, wo, early, later),
        [low, wide, low, low, ((4, sh, width), BF), ((4,) + block, BF), ((8, width), F32), ((8, width), F32),
         ((rows, 128), F32)],
        [pltpu.VMEM(*low), pltpu.VMEM(*low), pltpu.VMEM(*low), pltpu.VMEM((1,) + block, BF),
         pltpu.VMEM(*low), pltpu.VMEM(*wide), pltpu.VMEM(*low), pltpu.VMEM(*low),
         pltpu.VMEM(*low), pltpu.VMEM(*wide), pltpu.VMEM(*wide), pltpu.VMEM((8,) + block, BF),
         pltpu.VMEM((8,) + block, BF), pltpu.SemaphoreType.DMA((9,)), pltpu.SemaphoreType.DMA((TILES, 4))]
        + gather_sems(4, parts) + Reduce.scratch(4, parts, sh, width),
        far=(0, 1, 2, 4, 5), far_out=(0, 1, 2, 3, 5),
    )
    dt = attend_back(slot_clip, t, do, logs, inner)
    pg, grads_one, total = comm_call(
        functools.partial(first_comm_kernel, parts), "project_in_back_reduce", 2,
        (x, a1, o, dz, dt, dm, vec, wi, sums_two, sums_be, rest),
        [wide, ((LAST_BLOCKS, sh, width), BF), ((16, width), F32)],
        [pltpu.VMEM((LAST_BLOCKS,) + block, BF), pltpu.VMEM(*low), pltpu.VMEM(*low), pltpu.VMEM(*low),
         pltpu.VMEM(*low), pltpu.VMEM((rows, 3 * width), BF), pltpu.VMEM(*wide), pltpu.VMEM((3,) + block, BF),
         pltpu.SemaphoreType.DMA((9,))]
        + Reduce.scratch(LAST_BLOCKS, parts, sh, width) + Vector.scratch(parts, (16, width), F32),
        far=(0, 1, 2, 3, 4, 5, 7, 10),
    )
    return update(rates, count, grads_two, grads_one, total, out, pg, masters, moments, averages)


def on_device(
    patches, slot_clip, out_grad,
    project_in_weight, project_in_moment, project_in_average,
    project_out_weight, project_out_moment, project_out_average,
    expand_weight, expand_moment, expand_average,
    contract_weight, contract_moment, contract_average,
    vector_weight, vector_moment, vector_average,
):
    masters = (project_in_weight, project_out_weight, expand_weight, contract_weight, vector_weight)
    moments = (project_in_moment, project_out_moment, expand_moment, contract_moment, vector_moment)
    averages = (project_in_average, project_out_average, expand_average, contract_average, vector_average)
    parts, copies = lax.axis_size("fsdp"), lax.axis_size("rep")
    count, width = patches.shape
    direct = copies == 4 and parts % 4 == 0 and width // parts % 48 == 0
    path = direct_path if direct else plain_path
    tokens_all = count * parts * copies
    rates = [rate / tokens_all**0.5 for rate in RATES]
    return tuple(path(patches, slot_clip, out_grad, masters, moments, averages, rates))


def solution(mesh):
    tokens = P(("fsdp", "rep"), None)
    split, split_vector = P("fsdp", None), P(None, "fsdp")
    in_specs = (tokens, P(("fsdp", "rep")), tokens) + (split,) * 12 + (split_vector,) * 3
    out_specs = (tokens,) * 2 + (split,) * 20 + (split_vector,) * 5
    return jax.shard_map(on_device, mesh=mesh, in_specs=in_specs, out_specs=out_specs, check_vma=False)
```

```python
import functools
import math

import jax
import jax.numpy as jnp
from jax import lax
from jax.sharding import PartitionSpec as P
import jax.experimental.pallas as pl
import jax.experimental.pallas.tpu as pltpu

BF, F32 = jnp.bfloat16, jnp.float32
HEAD_DIM = 64
SLOT = 49
LIVE_MAX = 8
WIN = 416
EPSILON = 1e-06
MOMENTUM = 0.5
AVERAGE = 0.5
RATES = (0.3, 0.3, 0.1, 0.03, 0.5)
NEG = -1e30

def dg(a,b,ca,cb):
    return lax.dot_general(a,b,(((ca,),(cb,)),((),())),preferred_element_type=F32)

def both(x, lane):
    keep = (lane < 64).astype(BF)
    return jnp.concatenate([x*keep, x*(1-keep)], axis=0)

def group_end(clips, start, slots):
    end = start+1
    for e in range(2, LIVE_MAX+1):
        cand = start+e
        safe = jnp.minimum(cand, slots-1)
        edge = (cand == slots) | ((cand < slots) & ((clips[safe] != clips[jnp.maximum(safe-1,0)]) | (clips[safe] < 0)))
        end = jnp.where(edge, cand, end)
    return end

def fill_bias(clips, w0, start, end, bias):
    def keys(shape, dim):
        row = lax.broadcasted_iota(jnp.int32, shape, dim) + w0
        slot = (row*1338) >> 16
        key = -1-row
        for ahead in range(LIVE_MAX):
            s = start+ahead
            clip = clips[jnp.minimum(s, clips.shape[0]-1)]
            key = jnp.where((slot == s) & (s < end) & (clip >= 0), clip, key)
        return key
    bias[...] = jnp.where(keys((WIN,1),0) == keys((1,WIN),1), 0.0, NEG)

def clear_tail(ref, slots):
    tail = slots*SLOT//16*16
    ref[pl.ds(tail, ref.shape[0]-tail), :] = jnp.zeros((ref.shape[0]-tail, ref.shape[1]), BF)

def fwd_kernel(clips, t_ref, g_ref, o_ref, dy_ref, log_ref, bias):
    slots = clips.shape[0]
    rows = t_ref.shape[0]; D = o_ref.shape[1]
    clear_tail(o_ref, slots)
    clear_tail(dy_ref, slots)
    log_ref[...] = jnp.zeros_like(log_ref)
    live = lax.fori_loop(0, slots, lambda s, n: n + jnp.where(clips[s] >= 0, SLOT, 0), 0)
    row = lax.broadcasted_iota(jnp.int32,(slots*SLOT,1),0)
    dy_ref[pl.ds(0,slots*SLOT), :] = jnp.where(row < live, g_ref[...].astype(F32), 0.0).astype(BF)
    def group(g, start):
        @pl.when(start < slots)
        def _():
            end = group_end(clips, start, slots)
            r0 = start*SLOT; r1 = end*SLOT
            w0 = pl.multiple_of(jnp.minimum((r0>>4)<<4, rows-WIN), 16)
            fill_bias(clips, w0, start, end, bias)
            rowi = lax.broadcasted_iota(jnp.int32,(WIN,128),0)+w0
            mine = (rowi >= r0) & (rowi < r1)
            lane = lax.broadcasted_iota(jnp.int32,(1,128),1)
            win = pl.ds(w0, WIN)
            logs = log_ref[win, :]
            for p in range(D//128):
                q = t_ref[win, pl.ds(p*128,128)]
                k = t_ref[win, pl.ds(D+p*128,128)]
                v = t_ref[win, pl.ds(2*D+p*128,128)]
                s = dg(both(q, lane), k, 1, 1)
                es, tops = [], []
                for h in range(2):
                    part = s[h*WIN:(h+1)*WIN] + bias[...]
                    top = jnp.max(part, axis=1, keepdims=True)
                    es.append(jnp.exp(part-top).astype(BF))
                    tops.append(top)
                ones = jnp.concatenate([v, jnp.ones_like(v)], axis=1)
                mixed = jnp.dot(jnp.concatenate(es, axis=0), ones, preferred_element_type=F32)
                outs = []
                for h in range(2):
                    total = mixed[h*WIN:(h+1)*WIN, 128:]
                    outs.append(mixed[h*WIN:(h+1)*WIN, :128] / total)
                    logs = jnp.where(mine & (lane == 2*p+h), tops[h] + jnp.log(total), logs)
                o = jnp.where(lane < 64, outs[0], outs[1])
                old = o_ref[win, pl.ds(p*128,128)]
                o_ref[win, pl.ds(p*128,128)] = jnp.where(mine, o, old.astype(F32)).astype(BF)
            log_ref[win, :] = logs
        return jnp.where(start < slots, group_end(clips, start, slots), start)
    lax.fori_loop(0, (2*slots)//(LIVE_MAX+1)+1, group, 0)

def bwd_kernel(clips, t_ref, do_ref, log_ref, inner_ref, dt_ref, bias):
    slots = clips.shape[0]
    rows = t_ref.shape[0]; D = do_ref.shape[1]
    clear_tail(dt_ref, slots)
    def group(g, start):
        @pl.when(start < slots)
        def _():
            end = group_end(clips, start, slots)
            r0 = start*SLOT; r1 = end*SLOT
            w0 = pl.multiple_of(jnp.minimum((r0>>4)<<4, rows-WIN), 16)
            fill_bias(clips, w0, start, end, bias)
            rowi = lax.broadcasted_iota(jnp.int32,(WIN,128),0)+w0
            mine = (rowi >= r0) & (rowi < r1)
            lane = lax.broadcasted_iota(jnp.int32,(1,128),1)
            win = pl.ds(w0, WIN)
            logs = log_ref[win, :].T
            inners = inner_ref[win, :].T
            for p in range(D//128):
                q = t_ref[win, pl.ds(p*128,128)]
                k = t_ref[win, pl.ds(D+p*128,128)]
                v = t_ref[win, pl.ds(2*D+p*128,128)]
                do = do_ref[win, pl.ds(p*128,128)]
                s = dg(both(k, lane), q, 1, 1)
                dp = dg(both(v, lane), do, 1, 1)
                pts, dss = [], []
                for h in range(2):
                    n = 2*p+h
                    rows_h = slice(h*WIN, (h+1)*WIN)
                    pt = jnp.exp((s[rows_h] + bias[...]) - logs[n:n+1, :])
                    dss.append((pt*(dp[rows_h]-inners[n:n+1, :])).astype(BF))
                    pts.append(pt.astype(BF))
                dv = jnp.dot(jnp.concatenate(pts, axis=0), do, preferred_element_type=F32)
                dk = jnp.dot(jnp.concatenate(dss, axis=0), q, preferred_element_type=F32)
                dq = jnp.dot(jnp.concatenate([d.T for d in dss], axis=0), k, preferred_element_type=F32)
                dqs, dks, dvs = ([x[:WIN], x[WIN:]] for x in (dq, dk, dv))
                for i,x in enumerate((dqs,dks,dvs)):
                    new = jnp.where(lane < 64, x[0], x[1]).astype(BF).astype(F32)
                    if i==0: new = new*(64**-0.5)
                    c = pl.ds(i*D+p*128,128)
                    old = dt_ref[win, c].astype(F32)
                    dt_ref[win, c] = jnp.where(mine, new, old).astype(BF)
        return jnp.where(start < slots, group_end(clips, start, slots), start)
    lax.fori_loop(0, (2*slots)//(LIVE_MAX+1)+1, group, 0)

def attend(clips, t, g):
    D=t.shape[1]//3
    return pl.pallas_call(fwd_kernel, out_shape=[jax.ShapeDtypeStruct((t.shape[0],D),BF)]*2+[jax.ShapeDtypeStruct((t.shape[0],128),F32)],
      in_specs=[pl.BlockSpec(memory_space=pltpu.SMEM)]+[pl.BlockSpec(memory_space=pltpu.VMEM)]*2,
      out_specs=[pl.BlockSpec(memory_space=pltpu.VMEM)]*3,
      scratch_shapes=[pltpu.VMEM((WIN,WIN),F32)],
      compiler_params=pltpu.CompilerParams(vmem_limit_bytes=62*2**20),name="attention_forward")(clips,t,g)
def attend_back(clips, t, do, logs, inners):
    return pl.pallas_call(bwd_kernel, out_shape=jax.ShapeDtypeStruct(t.shape,BF),
      in_specs=[pl.BlockSpec(memory_space=pltpu.SMEM)]+[pl.BlockSpec(memory_space=pltpu.VMEM)]*4,
      out_specs=pl.BlockSpec(memory_space=pltpu.VMEM),
      scratch_shapes=[pltpu.VMEM((WIN,WIN),F32)],
      compiler_params=pltpu.CompilerParams(vmem_limit_bytes=62*2**20),name="attention_backward")(clips,t,do,logs,inners)


RT = 400


def dot_nt(left, right):
    return lax.dot_general(left, right, (((1,), (1,)), ((), ())), preferred_element_type=F32)


def dot_tn(left, right):
    return lax.dot_general(left, right, (((0,), (0,)), ((), ())), preferred_element_type=F32)


def dot_nn(left, right):
    return jnp.dot(left, right, preferred_element_type=F32)


def norm_parts(values):
    centred = values - jnp.mean(values, axis=-1, keepdims=True)
    scale = lax.rsqrt(jnp.mean(centred * centred, axis=-1, keepdims=True) + EPSILON)
    return centred * scale, scale


def norm_back(grad, gain, unit, scale):
    inner = grad * gain
    return scale * (
        inner
        - jnp.mean(inner, axis=-1, keepdims=True)
        - unit * jnp.mean(inner * unit, axis=-1, keepdims=True)
    )


def gelu_pair(u):
    bell = jnp.exp(-0.5 * u * u)
    t = 1.0 / (1.0 + (0.3275911 * 0.5**0.5) * jnp.abs(u))
    poly = t * (
        0.5 * 0.254829592
        + t * (-0.5 * 0.284496736 + t * (0.5 * 1.421413741 + t * (-0.5 * 1.453152027 + t * (0.5 * 1.061405429))))
    )
    tail = poly * bell
    phi = jnp.where(u < 0, tail, 1.0 - tail)
    return u * phi, phi + u * (bell * (2.0 * math.pi) ** -0.5)


def column_sum(values):
    return jnp.sum(values, axis=0, keepdims=True)


def tiles(rows, body):
    @pl.loop(0, rows // RT)
    def _(i):
        body(pl.ds(pl.multiple_of(i * RT, 16), RT))


def qkv_norm(x_ref, vec, a1_ref):
    def one(win):
        unit, _ = norm_parts(x_ref[win, :].astype(F32))
        a1_ref[win, :] = (unit * vec[0:1, :] + vec[1:2, :]).astype(BF)

    tiles(x_ref.shape[0], one)


def qkv_block(a1_ref, w_ref, t_ref, part):
    width = a1_ref.shape[1]
    weight = w_ref[part].reshape(width, width)

    def one(win):
        out = dot_nn(a1_ref[win, :], weight)
        if part == 0:
            out = out * HEAD_DIM**-0.5
        t_ref[win, pl.ds(part * width, width)] = out.astype(BF)

    tiles(a1_ref.shape[0], one)


def qkv_kernel(x_ref, vec, w_ref, t_ref, a1_ref):
    qkv_norm(x_ref, vec, a1_ref)
    for part in range(3):
        qkv_block(a1_ref, w_ref, t_ref, part)


def middle_step(x_ref, o_ref, vec, wo_ref, m_ref, a2_ref):
    def one(win):
        middle = x_ref[win, :].astype(F32) + (dot_nn(o_ref[win, :], wo_ref[...]) + vec[2:3, :])
        m_ref[win, :] = middle
        unit, _ = norm_parts(middle)
        a2_ref[win, :] = (unit * vec[3:4, :] + vec[4:5, :]).astype(BF)

    tiles(x_ref.shape[0], one)


def chunk_step(first, bias, a2_ref, dy_ref, we_ref, wc_ref, h_ref, du_ref, y_ref, da2_ref, be_ref):
    be_ref[...] = jnp.zeros_like(be_ref)

    def one(win):
        hidden, slope = gelu_pair(dot_nn(a2_ref[win, :], we_ref[...]) + bias)
        hidden = hidden.astype(BF)
        h_ref[win, :] = hidden
        du = (dot_nt(dy_ref[win, :], wc_ref[...]) * slope).astype(BF)
        du_ref[win, :] = du
        be_ref[...] += column_sum(du.astype(F32))
        y = dot_nn(hidden, wc_ref[...])
        da2 = dot_nt(du, we_ref[...])
        if first is True:
            y_ref[win, :] = y
            da2_ref[win, :] = da2
        else:
            y_ref[win, :] += y
            da2_ref[win, :] += da2

    tiles(a2_ref.shape[0], one)


def middle_back(live_rows, m_ref, y_ref, dy_ref, da2_ref, vec, wo_ref, out_ref, dm_ref, dz_ref, do_ref, sums):
    sums[...] = jnp.zeros_like(sums)

    def one(win):
        middle = m_ref[win, :]
        out_ref[win, :] = (middle + (y_ref[win, :] + vec[5:6, :])).astype(BF)
        unit, scale = norm_parts(middle)
        da2 = da2_ref[win, :]
        dy = dy_ref[win, :].astype(F32)
        dm = dy + norm_back(da2, vec[3:4, :], unit, scale)
        dm_ref[win, :] = dm
        dz = dm.astype(BF)
        dz_ref[win, :] = dz
        do_ref[win, :] = dot_nt(dz, wo_ref[...]).astype(BF)
        sums[0:1, :] += column_sum(da2 * unit)
        sums[1:2, :] += column_sum(da2)
        sums[2:3, :] += column_sum(dz.astype(F32))
        sums[3:4, :] += column_sum(dy)

    tiles(m_ref.shape[0], one)


def feed_kernel(
    x_ref, o_ref, dy_ref, vec, wo_ref, we_ref, wc_ref,
    out_ref, dm_ref, do_ref, gwo_ref, gwe_ref, gwc_ref, sums, be_ref,
    m_ref, a2_ref, h_ref, du_ref, y_ref, da2_ref, dz_ref,
):
    middle_step(x_ref, o_ref, vec, wo_ref, m_ref, a2_ref)
    for j in range(4):
        chunk_step(
            j == 0, vec[6 + j : 7 + j, :], a2_ref, dy_ref, we_ref.at[j], wc_ref.at[j],
            h_ref, du_ref, y_ref, da2_ref, be_ref.at[pl.ds(8 * j, 1)],
        )
        gwc_ref[j] = dot_tn(h_ref[...], dy_ref[...]).astype(BF)
        gwe_ref[j] = dot_tn(a2_ref[...], du_ref[...]).astype(BF)
    middle_back(None, m_ref, y_ref, dy_ref, da2_ref, vec, wo_ref, out_ref, dm_ref, dz_ref, do_ref, sums)
    gwo_ref[...] = dot_tn(o_ref[...], dz_ref[...]).astype(BF)


def first_back(x_ref, dt_ref, dm_ref, vec, w_refs, pg_ref, sums):
    sums[...] = jnp.zeros_like(sums)
    width = x_ref.shape[1]

    def one(win):
        da1 = dot_nt(dt_ref[win, pl.ds(0, width)], w_refs[0][...])
        da1 += dot_nt(dt_ref[win, pl.ds(width, width)], w_refs[1][...])
        da1 += dot_nt(dt_ref[win, pl.ds(2 * width, width)], w_refs[2][...])
        unit, scale = norm_parts(x_ref[win, :].astype(F32))
        pg_ref[win, :] = dm_ref[win, :] + norm_back(da1, vec[0:1, :], unit, scale)
        sums[0:1, :] += column_sum(da1 * unit)
        sums[1:2, :] += column_sum(da1)

    tiles(x_ref.shape[0], one)


def first_kernel(x_ref, a1_ref, dt_ref, dm_ref, vec, w_ref, pg_ref, gwi_ref, sums):
    width = x_ref.shape[1]
    for part in range(3):
        gwi_ref[part] = dot_tn(a1_ref[...], dt_ref[:, pl.ds(part * width, width)]).astype(BF)
    first_back(x_ref, dt_ref, dm_ref, vec, [w_ref.at[p] for p in range(3)], pg_ref, sums)


VM = pl.BlockSpec(memory_space=pltpu.VMEM)
SM = pl.BlockSpec(memory_space=pltpu.SMEM)


def vmem_call(kernel, name, ins, outs, scratch=(), smem=0):
    return pl.pallas_call(
        kernel,
        out_shape=[jax.ShapeDtypeStruct(s, d) for s, d in outs],
        in_specs=[SM] * smem + [VM] * (len(ins) - smem),
        out_specs=[VM] * len(outs),
        scratch_shapes=[pltpu.VMEM(s, d) for s, d in scratch],
        compiler_params=pltpu.CompilerParams(vmem_limit_bytes=60 * 2**20),
        name=name,
    )(*ins)


MESH = pl.DeviceIdType.MESH


class Place:
    def __init__(self, parts, sh, width):
        mine, copy = lax.axis_index("fsdp"), lax.axis_index("rep")
        self.outer_count = parts // 2
        self.outer, self.inner = mine // 2, mine % 2
        self.plane, self.core = copy // 2, copy % 2
        self.third = sh // 3
        self.half = width // 2

    def device(self, outer=None, inner=None, plane=None, core=None):
        outer = self.outer if outer is None else outer
        inner = self.inner if inner is None else inner
        plane = self.plane if plane is None else plane
        core = self.core if core is None else core
        return (outer * 2 + inner, plane * 2 + core)

    def far(self, k):
        return (self.outer + k) % self.outer_count

    def ranks(self):
        return range(1, self.outer_count)

    def columns(self, core=None):
        core = self.core if core is None else core
        return pl.ds(pl.multiple_of(core * self.half, 128), self.half)

    def held(self):
        return pl.ds(pl.multiple_of(self.plane * self.third, 16), 2 * self.third)

    def own(self, plane=None):
        plane = self.plane if plane is None else plane
        return pl.ds(pl.multiple_of(plane * (2 * self.third), 16), self.third)

    def peers(self):
        return [self.device(outer=self.far(k)) for k in self.ranks()] + [
            self.device(inner=1 - self.inner),
            self.device(plane=1 - self.plane),
            self.device(core=1 - self.core),
        ]

    def greet(self):
        barrier = pltpu.get_barrier_semaphore()
        peers = self.peers()
        for peer in peers:
            pl.semaphore_signal(barrier, inc=1, device_id=peer, device_id_type=MESH)
        pl.semaphore_wait(barrier, len(peers))


def remote(src, dst, sems, index, device):
    return pltpu.make_async_remote_copy(
        src_ref=src, dst_ref=dst, send_sem=sems[0].at[index], recv_sem=sems[1].at[index],
        device_id=device, device_id_type=MESH,
    )


def start(copies):
    for copy in copies:
        copy.start()


def landed(copies):
    for copy in copies:
        copy.wait_recv()


def sent(copies):
    for copy in copies:
        copy.wait_send()


class Gather:
    def __init__(self, place, shard, full, sems):
        self.p, self.shard, self.full, self.sems = place, shard, full, sems

    def far(self, b):
        p = self.p
        return [
            remote(
                self.shard.at[b, p.held(), p.columns()],
                self.full.at[b, p.outer, p.inner, p.held(), p.columns()],
                self.sems, (b, k - 1), p.device(outer=p.far(k)),
            )
            for k in p.ranks()
        ]

    def pair(self, b, which):
        p = self.p
        if which == 0:
            ref = self.full.at[b, :, p.inner, p.held(), p.columns()]
            device = p.device(inner=1 - p.inner)
        elif which == 1:
            ref = self.full.at[b, :, :, p.own(), p.columns()]
            device = p.device(plane=1 - p.plane)
        else:
            ref = self.full.at[b, :, :, :, p.columns()]
            device = p.device(core=1 - p.core)
        return [remote(ref, ref, self.sems, (b, p.outer_count - 1 + which), device)]

    def put_own(self, b):
        p = self.p
        self.full[b, p.outer, p.inner, p.held(), p.columns()] = self.shard[b, p.held(), p.columns()]

    def step(self, s, count, lag):
        for stage in range(5):
            @pl.when((s >= stage * lag) & (s < count + stage * lag))
            def _():
                self.stage(s - stage * lag, stage)

    def stage(self, b, stage):
        if stage == 0:
            start(self.far(b))
            self.put_own(b)
        else:
            landed(self.far(b) if stage == 1 else self.pair(b, stage - 2))
            if stage < 4:
                start(self.pair(b, stage - 1))

    def finish(self, count):
        @pl.loop(0, count)
        def _(b):
            sent(self.far(b))
            for which in range(3):
                sent(self.pair(b, which))


def gather_sems(blocks, parts):
    shape = (blocks, parts // 2 - 1 + 3)
    return [pltpu.SemaphoreType.DMA(shape), pltpu.SemaphoreType.DMA(shape)]


class Reduce:
    def __init__(self, place, grad, out, bufs, sems):
        self.p, self.grad, self.out, self.sems = place, grad, out, sems
        self.from_core, self.from_plane, self.from_inner, self.from_far, self.part, self.from_part = bufs

    @staticmethod
    def scratch(blocks, parts, sh, width):
        outer, third, half = parts // 2, sh // 3, width // 2
        shape = (blocks, outer - 1 + 5)
        return [
            pltpu.VMEM((blocks, outer, 2, sh, half), BF),
            pltpu.VMEM((blocks, outer, 2, third, half), BF),
            pltpu.VMEM((blocks, outer, 2 * third, half), BF),
            pltpu.VMEM((blocks, outer - 1, 2 * third, half), BF),
            pltpu.VMEM((blocks, 2 * third, half), BF),
            pltpu.VMEM((blocks, 2 * third, half), BF),
            pltpu.SemaphoreType.DMA(shape),
            pltpu.SemaphoreType.DMA(shape),
        ]

    def copies(self, b, stage):
        p = self.p
        base = p.outer_count - 1
        if stage == 0:
            src, dst = self.grad.at[b, :, :, :, p.columns(1 - p.core)], self.from_core.at[b]
            device = p.device(core=1 - p.core)
        elif stage == 1:
            src, dst = self.grad.at[b, :, :, p.own(1 - p.plane), p.columns()], self.from_plane.at[b]
            device = p.device(plane=1 - p.plane)
        elif stage == 2:
            src, dst = self.grad.at[b, :, 1 - p.inner, p.held(), p.columns()], self.from_inner.at[b]
            device = p.device(inner=1 - p.inner)
        elif stage == 3:
            return [
                remote(
                    self.grad.at[b, p.far(k), p.inner, p.held(), p.columns()],
                    self.from_far.at[b, k - 1], self.sems, (b, k - 1), p.device(outer=p.far(k)),
                )
                for k in p.ranks()
            ]
        elif stage == 4:
            src, dst = self.part.at[b], self.from_part.at[b]
            device = p.device(plane=1 - p.plane)
        else:
            src = dst = self.out.at[b, :, p.columns()]
            device = p.device(core=1 - p.core)
        return [remote(src, dst, self.sems, (b, base + (stage if stage < 3 else stage - 1)), device)]

    def add(self, b, stage):
        p = self.p
        if stage == 0:
            @pl.loop(0, p.outer_count)
            def _(o):
                for i in range(2):
                    index = (b, o, i, slice(None), p.columns())
                    self.grad[index] = (self.grad[index].astype(F32) + self.from_core[b, o, i].astype(F32)).astype(BF)
        elif stage == 1:
            for i in range(2):
                @pl.loop(0, p.outer_count)
                def _(o):
                    index = (b, o, i, p.own(), p.columns())
                    self.grad[index] = (self.grad[index].astype(F32) + self.from_plane[b, o, i].astype(F32)).astype(BF)
        elif stage == 2:
            @pl.loop(0, p.outer_count)
            def _(o):
                index = (b, o, p.inner, p.held(), p.columns())
                self.grad[index] = (self.grad[index].astype(F32) + self.from_inner[b, o].astype(F32)).astype(BF)
        elif stage == 3:
            total = self.grad[b, p.outer, p.inner, p.held(), p.columns()].astype(F32)
            for k in p.ranks():
                total += self.from_far[b, k - 1].astype(F32)
            self.part[b] = total.astype(BF)
        elif stage == 4:
            third = p.third
            for plane in range(2):
                @pl.when(p.plane == plane)
                def _():
                    mine, other = self.part, self.from_part
                    first, last = (mine, other) if plane == 0 else (other, mine)
                    self.out[b, pl.ds(0, third), p.columns()] = first[b, pl.ds(0, third), :]
                    middle = first[b, pl.ds(third, third), :].astype(F32) + last[b, pl.ds(0, third), :].astype(F32)
                    self.out[b, pl.ds(third, third), p.columns()] = middle.astype(BF)
                    self.out[b, pl.ds(2 * third, third), p.columns()] = last[b, pl.ds(third, third), :]

    def stage(self, b, stage):
        if stage > 0:
            landed(self.copies(b, stage - 1))
            self.add(b, stage - 1)
        if stage < 6:
            start(self.copies(b, stage))

    def step(self, s, count, lag):
        for stage in range(7):
            @pl.when((s >= stage * lag) & (s < count + stage * lag))
            def _():
                self.stage(s - stage * lag, stage)

    def finish(self, count):
        @pl.loop(0, count)
        def _(b):
            for stage in range(6):
                sent(self.copies(b, stage))


class Vector:
    def __init__(self, place, total, bufs, sems, everywhere):
        self.p, self.total, self.sems = place, total, sems
        self.pairs, self.fars = bufs
        self.order = (0, 1, 2) if everywhere else (2,)

    @staticmethod
    def scratch(parts, shape, dtype):
        sems = (parts // 2 - 1 + 3,)
        return [
            pltpu.VMEM((6,) + shape, dtype), pltpu.VMEM((parts // 2,) + shape, dtype),
            pltpu.SemaphoreType.DMA(sems), pltpu.SemaphoreType.DMA(sems),
        ]

    def pair(self, which):
        p = self.p
        device = (
            p.device(core=1 - p.core), p.device(plane=1 - p.plane), p.device(inner=1 - p.inner)
        )[which]
        return [remote(self.pairs.at[2 * which], self.pairs.at[2 * which + 1], self.sems, p.outer_count - 1 + which, device)]

    def far(self):
        p = self.p
        mine = self.fars.at[p.outer]
        return [remote(mine, mine, self.sems, k - 1, p.device(outer=p.far(k))) for k in p.ranks()]

    def far_landed(self):
        p = self.p
        for k in p.ranks():
            theirs = self.fars.at[(p.outer + p.outer_count - k) % p.outer_count]
            remote(theirs, theirs, self.sems, k - 1, p.device(outer=p.far(k))).wait_recv()

    def stage(self, number):
        order = self.order
        if number > 0 and number <= len(order):
            which = order[number - 1]
            landed(self.pair(which))
            self.total[...] = self.total[...] + self.pairs[2 * which + 1]
        if number < len(order):
            which = order[number]
            self.pairs[2 * which] = self.total[...]
            start(self.pair(which))
        elif number == len(order):
            self.fars[self.p.outer] = self.total[...]
            start(self.far())
        else:
            self.far_landed()
            total = self.fars[0]
            for o in range(1, self.p.outer_count):
                total = total + self.fars[o]
            self.total[...] = total

    def stages(self):
        return len(self.order) + 2

    def finish(self):
        for which in self.order:
            sent(self.pair(which))
        sent(self.far())


FIRST_BLOCKS = 6


TILES = 3


def flat(ref, b):
    block = ref[b]
    return block.reshape(block.shape[0] * block.shape[1] * block.shape[2], block.shape[3])


def one_hot(shape, shift, along):
    row = lax.broadcasted_iota(jnp.int32, shape, 0)
    column = lax.broadcasted_iota(jnp.int32, shape, 1)
    return jnp.where((column - row if along else row - column) == shift, 1.0, 0.0)


def place_vectors(parts, vector, vec):
    sh, width = vector.shape[1], vec.shape[1]
    mine, apart = lax.axis_index("fsdp"), parts // 4
    low = vector[...].astype(BF)
    vec[...] = jnp.zeros_like(vec)
    vec[0:6, :] = dot_nn(low, one_hot((sh, width), mine * sh, True).astype(BF))[0:6, :]
    row = lax.broadcasted_iota(jnp.int32, (4, width), 0)
    for i in range(4):
        spot = one_hot((sh, width), (apart * i + mine // 4) * sh, True).astype(BF)
        vec[6:10, :] += jnp.where(row == mine % 4, dot_nn(low, spot)[6 + i : 7 + i, :], 0.0)


def gather_kernel(
    parts, x_ref, vector, wi_ref, wo_ref, we_ref, wc_ref,
    t_out, a1_ref, xp_ref, wi_out, wo_out, ff_out, rest_out, vec, t_ref, full, shard, local, *scratch
):
    count, width = x_ref.shape
    rows = xp_ref.shape[0]
    sh = wo_ref.shape[0]
    place = Place(parts, sh, width)
    weights = Gather(place, shard, full, scratch[0:2])
    vectors = Vector(place, vec, scratch[2:4], scratch[4:6], False)

    def pack_chunk(j, we_to, wc_to):
        for p in range(parts):
            we_to[:, pl.ds(p * sh, sh)] = we_ref[:, pl.ds((4 * p + j) * sh, sh)].astype(BF)
        wc_to[...] = wc_ref[pl.ds(j * sh, sh), :].astype(BF)

    shard[0] = wi_ref[:, pl.ds(0, width)].astype(BF)
    place.greet()
    weights.step(0, FIRST_BLOCKS, 1)
    place_vectors(parts, vector, vec)
    vectors.stage(0)
    for part in range(1, 3):
        shard[part] = wi_ref[:, pl.ds(part * width, width)].astype(BF)
    shard[3] = wo_ref[...].astype(BF)
    weights.step(1, FIRST_BLOCKS, 1)
    vectors.stage(1)
    tail = count // 16 * 16
    xp_ref[pl.ds(tail, rows - tail), :] = jnp.zeros((rows - tail, width), BF)
    xp_ref[pl.ds(0, count), :] = x_ref[...]
    weights.step(2, FIRST_BLOCKS, 1)
    vectors.stage(2)
    pack_chunk(0, shard.at[4], shard.at[5])
    weights.step(3, FIRST_BLOCKS, 1)
    qkv_norm(xp_ref, vec, a1_ref)
    leaving = []
    for s in range(4, FIRST_BLOCKS + 4):
        b = s - 4
        weights.step(s, FIRST_BLOCKS, 1)
        out = wi_out.at[b] if b < 3 else wo_out.at[0] if b == 3 else ff_out.at[b - 4]
        leaving.append(pltpu.make_async_copy(full.at[b], out, local.at[b]))
        leaving[-1].start()
        if b > 2:
            pack_chunk(b - 2, rest_out.at[2 * b - 6], rest_out.at[2 * b - 5])
        if b < 3:
            qkv_block(a1_ref, full, t_ref, b)
            part = pl.ds(b * width, width)
            leaving.append(pltpu.make_async_copy(t_ref.at[:, part], t_out.at[:, part], local.at[FIRST_BLOCKS + b]))
            leaving[-1].start()
    for copy in leaving:
        copy.wait()
    weights.finish(FIRST_BLOCKS)
    vectors.finish()


def feed_comm_kernel(
    parts, x_in, o_in, dy_in, vec, wo_in, early, shard,
    out_out, dm_out, do_out, dz_out, grad_out, grad_rest, sums, be_ref, inner_ref,
    x_ref, o_ref, dy_ref, wo_ref, out_ref, dm_ref, do_ref, dz_ref,
    a2_ref, y_ref, da2_ref, full, grad, local, leaving, *scratch,
):
    rows, width = x_ref.shape
    sh = shard.shape[1]
    place = Place(parts, sh, width)
    later, have = shard.shape[0], early.shape[0]
    weights = Gather(place, shard, full.at[pl.ds(have, later)], scratch[0:2])
    grads = Reduce(place, grad.at[pl.ds(0, 4)], grad_out, scratch[2:8], scratch[8:10])
    du_ref, h_ref = do_ref, dz_ref
    moves = ((x_in, x_ref), (o_in, o_ref), (wo_in, wo_ref), (dy_in, dy_ref), (early, full.at[pl.ds(0, have)]))
    ready = [pltpu.make_async_copy(source, target, local.at[4 + i]) for i, (source, target) in enumerate(moves)]
    start(ready)
    place.greet()

    def win(i):
        return pl.ds(i * RT, RT)

    def slot(number):
        for b in range(2):
            for stage in range(5):
                if (0, 2, 4, 6, 7)[stage] + b == number:
                    weights.stage(b, stage)
                if (3, 6, 8, 10, 12)[stage] + b == number:
                    weights.stage(b + 2, stage)
                if (8, 11, 13, 15, 17)[stage] + b == number:
                    weights.stage(b + 4, stage)

    slot(0)
    for copy in ready[:3]:
        copy.wait()
    wo = flat(wo_ref, 0)
    for i in range(TILES):
        middle = x_ref[win(i), :].astype(F32) + (dot_nn(o_ref[win(i), :], wo) + vec[2:3, :])
        dm_ref[win(i), :] = middle
        unit, _ = norm_parts(middle)
        a2_ref[win(i), :] = (unit * vec[3:4, :] + vec[4:5, :]).astype(BF)
        y_ref[win(i), :] = jnp.zeros((RT, width), F32)
        da2_ref[win(i), :] = jnp.zeros((RT, width), F32)
        slot(i + 1)
    for copy in ready[3:]:
        copy.wait()

    def results(i):
        pairs = ((out_ref, out_out), (dm_ref, dm_out), (do_ref, do_out), (dz_ref, dz_out))
        return [
            pltpu.make_async_copy(source.at[win(i)], target.at[win(i)], leaving.at[i, n])
            for n, (source, target) in enumerate(pairs)
        ]

    def leave(b):
        return pltpu.make_async_copy(grad.at[b], grad_rest.at[b - 4], local.at[b - 4])

    def due(position, back, parity):
        steps = position - 3 - parity + 5 * back
        return steps // 2 if steps % 2 == 0 and 0 <= steps <= 12 else None

    def passing(j, position):
        for back in range(3, -1, -1):
            for parity in range(2):
                stage = due(position, back, parity)
                if stage is not None and back <= j < back + 2:
                    grads.stage(2 * (j - back) + parity, stage)

    for j in range(4):
        bias = vec[pl.ds(6 + j, 1), :]
        be_sum = jnp.zeros((1, width), F32)
        for i in range(TILES):
            hidden, slope = gelu_pair(dot_nn(a2_ref[win(i), :], flat(full, 2 * j)) + bias)
            hidden = hidden.astype(BF)
            h_ref[win(i), :] = hidden
            du = (dot_nt(dy_ref[win(i), :], flat(full, 2 * j + 1)) * slope).astype(BF)
            du_ref[win(i), :] = du
            be_sum += column_sum(du.astype(F32))
            y_ref[win(i), :] += dot_nn(hidden, flat(full, 2 * j + 1))
            da2_ref[win(i), :] += dot_nt(du, flat(full, 2 * j))
            slot(4 + 5 * j + i)
            passing(j, i)
        be_ref[pl.ds(j, 1), :] = be_sum
        grad[2 * j] = dot_tn(h_ref[...], dy_ref[...]).astype(BF).reshape(grad.shape[1:])
        slot(4 + 5 * j + 3)
        passing(j, 3)
        grad[2 * j + 1] = dot_tn(a2_ref[...], du_ref[...]).astype(BF).reshape(grad.shape[1:])
        slot(4 + 5 * j + 4)
        passing(j, 4)

        if j >= 2:
            for parity in range(2):
                leave(2 * j + parity).start()

    sums[...] = jnp.zeros_like(sums)
    feature = lax.broadcasted_iota(jnp.int32, (width, 128), 0)
    heads = (feature // HEAD_DIM == lax.broadcasted_iota(jnp.int32, (width, 128), 1)).astype(BF)
    for position in range(5, 8):
        i = position - 5
        if i < TILES:
            middle = dm_ref[win(i), :]
            out_ref[win(i), :] = (middle + (y_ref[win(i), :] + vec[5:6, :])).astype(BF)
            unit, scale = norm_parts(middle)
            da2 = da2_ref[win(i), :]
            dy = dy_ref[win(i), :].astype(F32)
            dm = dy + norm_back(da2, vec[3:4, :], unit, scale)
            dm_ref[win(i), :] = dm
            dz = dm.astype(BF)
            dz_ref[win(i), :] = dz
            do = dot_nt(dz, wo).astype(BF)
            do_ref[win(i), :] = do
            product = do.astype(F32) * o_ref[win(i), :].astype(F32)
            high = product.astype(BF)
            inner_ref[win(i), :] = dot_nn(high, heads) + dot_nn((product - high.astype(F32)).astype(BF), heads)
            sums[0:1, :] += column_sum(da2 * unit)
            sums[1:2, :] += column_sum(da2)
            sums[2:3, :] += column_sum(dz.astype(F32))
            sums[3:4, :] += column_sum(dy)
            start(results(i))
        for j in range(0, 2):
            for parity in range(2):
                stage = due(position + 5 * (3 - j), 0, parity)
                if stage is not None:
                    grads.stage(2 * j + parity, stage)
    weights.finish(later)
    grads.finish(4)
    for b in range(4, 8):
        leave(b).wait()
    for i in range(TILES):
        for copy in results(i):
            copy.wait()


LAST_BLOCKS = 8


def first_comm_kernel(
    parts, x_in, a1_in, o_in, dz_in, dt_in, dm_in, vec, wi_in, sums_two, be_ref, rest_in,
    pg_ref, grad_out, total, grad, x_ref, a1_ref, o_ref, dz_ref, dt_ref, dm_ref, wi_ref, local, *scratch,
):
    rows, width = x_ref.shape
    place = Place(parts, width // parts, width)
    grads = Reduce(place, grad, grad_out, scratch[0:6], scratch[6:8])
    vectors = Vector(place, total, scratch[8:10], scratch[10:12], True)
    arriving = [
        pltpu.make_async_copy(rest_in.at[pl.ds(0, 2)], grad.at[pl.ds(0, 2)], local.at[0]),
        pltpu.make_async_copy(rest_in.at[pl.ds(2, 2)], grad.at[pl.ds(2, 2)], local.at[1]),
    ] + [
        pltpu.make_async_copy(source, ref, local.at[2 + i])
        for i, (source, ref) in enumerate(
            ((o_in, o_ref), (dz_in, dz_ref), (a1_in, a1_ref), (dt_in, dt_ref), (wi_in, wi_ref), (x_in, x_ref), (dm_in, dm_ref))
        )
    ]
    start(arriving)
    place.greet()
    total[...] = jnp.zeros_like(total)
    total[2:3, :] = sums_two[2:3, :]
    total[3:5, :] = sums_two[0:2, :]
    total[5:6, :] = sums_two[3:4, :]
    total[6:10, :] = be_ref[0:4, :]

    def step(s):
        grads.step(s, LAST_BLOCKS, 1)

    arriving[0].wait()
    step(0)
    arriving[1].wait()
    for i in (2, 3):
        arriving[i].wait()
    grad[4] = dot_tn(o_ref[...], dz_ref[...]).astype(BF).reshape(grad.shape[1:])
    step(1)
    for i in (4, 5):
        arriving[i].wait()
    for part in range(3):
        block = dot_tn(a1_ref[...], dt_ref[:, pl.ds(part * width, width)]).astype(BF)
        grad[part + 5] = block.reshape(grad.shape[1:])
        step(part + 2)
    for i in (6, 7, 8):
        arriving[i].wait()
    for i in range(TILES):
        win = pl.ds(i * RT, RT)
        da1 = dot_nt(dt_ref[win, pl.ds(0, width)], flat(wi_ref, 0))
        da1 += dot_nt(dt_ref[win, pl.ds(width, width)], flat(wi_ref, 1))
        da1 += dot_nt(dt_ref[win, pl.ds(2 * width, width)], flat(wi_ref, 2))
        unit, scale = norm_parts(x_ref[win, :].astype(F32))
        pg_ref[win, :] = dm_ref[win, :] + norm_back(da1, vec[0:1, :], unit, scale)
        total[0:1, :] += column_sum(da1 * unit)
        total[1:2, :] += column_sum(da1)
        step(5 + i)
    for s in range(8, LAST_BLOCKS + 6):
        if s - 8 < vectors.stages():
            vectors.stage(s - 8)
        step(s)
    grads.finish(LAST_BLOCKS)
    vectors.finish()


def comm_call(kernel, name, which, ins, outs, scratch, far=(), far_out=()):
    return pl.pallas_call(
        kernel,
        out_shape=[jax.ShapeDtypeStruct(s, d) for s, d in outs],
        in_specs=[pl.BlockSpec(memory_space=pl.ANY) if i in far else VM for i in range(len(ins))],
        out_specs=[pl.BlockSpec(memory_space=pl.ANY) if i in far_out else VM for i in range(len(outs))],
        scratch_shapes=scratch,
        compiler_params=pltpu.CompilerParams(
            vmem_limit_bytes=62 * 2**20, collective_id=which, has_side_effects=True
        ),
        name=name,
    )(*ins)


STEPS = 6


def extract_vectors(parts, total, picked):
    sh, width = picked.shape[1], total.shape[1]
    mine, apart = lax.axis_index("fsdp"), parts // 4

    def pick(rows, shift):
        return jnp.dot(
            rows, one_hot((width, sh), shift, False), precision=lax.Precision.HIGHEST, preferred_element_type=F32
        )

    picked[0:8, :] = pick(total[0:8, :], mine * sh)
    held = total[6:10, :]
    row = lax.broadcasted_iota(jnp.int32, held.shape, 0)
    held = jnp.sum(jnp.where(row == mine % 4, held, 0.0), axis=0, keepdims=True)
    held = jnp.broadcast_to(held, (8, width))
    for i in range(4):
        picked[6 + i : 7 + i, :] = pick(held, (apart * i + mine // 4) * sh)[0:1, :]


def update_kernel(rates, g_two, g_one, total, out_in, pg_in, *refs):
    state, outs, picked, flat_we = refs[:15], refs[15:42], refs[42], refs[43]
    i = pl.program_id(0)
    sh, width = g_one.shape[1:]
    parts = width // sh

    @pl.when(i == 0)
    def _():
        extract_vectors(parts, total, picked)
        for j in range(4):
            for p in range(parts):
                block = g_two[2 * j + 1] if j < 2 else g_one[2 * j - 3]
                flat_we[:, pl.ds((4 * p + j) * sh, sh)] = block[:, p * sh : (p + 1) * sh].astype(F32)

    outs[0][...] = out_in[...]
    outs[1][...] = pg_in[...]
    half, sixth = width // 2, width // STEPS
    odd = pl.ds(pl.multiple_of(i % 2 * half, 128), half)
    third = sh // 3

    def contract_rows(k):
        rows = pl.ds(pl.multiple_of(k % 3 * third, 16), third)
        j = k // 3
        low, high = g_two[2 * jnp.minimum(j, 1), rows, :], g_one[2 * jnp.maximum(j, 2) - 4, rows, :]
        return jnp.where(j < 2, low.astype(F32), high.astype(F32))

    sums = (
        g_one[5 + i // 2, :, odd].astype(F32),
        g_one[4, :, pl.ds(pl.multiple_of(i * sixth, 128), sixth)].astype(F32),
        flat_we[:, pl.ds(pl.multiple_of(i * 4 * sixth, 128), 4 * sixth)],
        jnp.concatenate([contract_rows(2 * i), contract_rows(2 * i + 1)], axis=0),
        picked[0:10, :],
    )
    for member in range(5):
        weight, moment, average = (ref[...] for ref in state[3 * member : 3 * member + 3])
        for ref, value in zip(
            outs[2 + 5 * member : 7 + 5 * member], step(sums[member], rates[member], weight, moment, average)
        ):
            ref[...] = value


def update(rates, count, g_two, g_one, total, out, pg, masters, moments, averages):
    sh, width = g_one.shape[1:]
    across = [
        pl.BlockSpec((sh, width // 2), lambda i: (0, i)),
        pl.BlockSpec((sh, width // STEPS), lambda i: (0, i)),
        pl.BlockSpec((sh, 4 * width // STEPS), lambda i: (0, i)),
        pl.BlockSpec((4 * sh // STEPS, width), lambda i: (i, 0)),
        pl.BlockSpec(masters[4].shape, lambda i: (0, 0)),
    ]
    rows = (count + STEPS - 1) // STEPS
    by_row = pl.BlockSpec(((rows + 15) // 16 * 16, width), lambda i: (i, 0))
    ins, specs = [], []
    outs = [jax.ShapeDtypeStruct((count, width), BF), jax.ShapeDtypeStruct((count, width), F32)]
    out_specs = [by_row] * 2
    for member in range(5):
        ins += [masters[member], moments[member], averages[member]]
        specs += [across[member]] * 3
        shape = masters[member].shape
        outs += [jax.ShapeDtypeStruct(shape, F32)] * 4 + [jax.ShapeDtypeStruct(shape, BF)]
        out_specs += [across[member]] * 5
    return pl.pallas_call(
        functools.partial(update_kernel, rates),
        grid=(STEPS,),
        out_shape=outs,
        in_specs=[pl.BlockSpec(g.shape, lambda i: (0, 0, 0)) for g in (g_two, g_one)]
        + [pl.BlockSpec(total.shape, lambda i: (0, 0))] + [by_row] * 2 + specs,
        out_specs=out_specs,
        scratch_shapes=[pltpu.VMEM((16, sh), F32), pltpu.VMEM((sh, 4 * width), F32)],
        compiler_params=pltpu.CompilerParams(vmem_limit_bytes=62 * 2**20),
        name="momentum_step",
    )(g_two, g_one, total, out, pg, *ins)


def run_qkv(x, vec, wi):
    rows, width = x.shape
    return vmem_call(
        qkv_kernel, "project_in", (x, vec, wi), [((rows, 3 * width), BF), ((rows, width), BF)]
    )


def run_feed(x, o, dy, vec, wo, we, wc):
    rows, width = x.shape
    wide, low = ((rows, width), F32), ((rows, width), BF)
    return vmem_call(
        feed_kernel, "feed_forward", (x, o, dy, vec, wo, we, wc),
        [low, wide, low, ((width, width), BF), ((4, width, width), BF), ((4, width, width), BF),
         ((8, width), F32), ((32, width), F32)],
        [wide, low, low, low, wide, wide, low],
    )


def run_first(x, a1, dt, dm, vec, wi):
    rows, width = x.shape
    return vmem_call(
        first_kernel, "project_in_back", (x, a1, dt, dm, vec, wi),
        [((rows, width), F32), ((3, width, width), BF), ((8, width), F32)],
    )


def pack_shards(wi, wo, we, wc, parts):
    rows, width = wo.shape
    wi = wi.reshape(rows, 3, width).swapaxes(0, 1)
    we = we.reshape(rows, parts, 4, rows).transpose(2, 0, 1, 3).reshape(4, rows, width)
    wc = wc.reshape(4, rows, width)
    return jnp.concatenate([wi, wo[None], we, wc], axis=0)


def unpack_shards(blocks, parts):
    rows, width = blocks.shape[1:]
    wi = blocks[0:3].swapaxes(0, 1).reshape(rows, 3 * width)
    we = blocks[4:8].reshape(4, rows, parts, rows).transpose(1, 2, 0, 3).reshape(rows, 4 * width)
    return wi, blocks[3], we, blocks[8:12].reshape(4 * rows, width)


def step(grad_sum, rate, weight, moment, average):
    moment_new = MOMENTUM * moment + grad_sum
    weight_new = weight - rate * (grad_sum + MOMENTUM * moment_new)
    average_new = AVERAGE * average + (1.0 - AVERAGE) * weight_new
    return [grad_sum, moment_new, weight_new, average_new, weight_new.astype(BF)]


def plain_path(patches, slot_clip, out_grad, masters, moments, averages, rates):
    parts, copies = lax.axis_size("fsdp"), lax.axis_size("rep")
    mine, copy = lax.axis_index("fsdp"), lax.axis_index("rep")
    count, width = patches.shape
    rows = (count + RT - 1) // RT * RT
    sh = width // parts
    packed = pack_shards(*(m.astype(BF) for m in masters[:4]), parts).reshape(12 * sh, width)
    piece = 12 * sh // copies
    quarter = lax.dynamic_slice_in_dim(packed, copy * piece, piece, 0)
    full = lax.all_gather(quarter, ("fsdp", "rep"), axis=0, tiled=True)
    full = full.reshape(parts, 12, sh, width).swapaxes(0, 1).reshape(12, width, width)
    vec = lax.all_gather(masters[4].astype(BF), "fsdp", axis=1, tiled=True).astype(F32)
    be = vec[6:].reshape(parts, 4, sh).swapaxes(0, 1).reshape(4, width)
    vec = jnp.concatenate([vec[:6], be, jnp.zeros((6, width), F32)], axis=0)

    pad = ((0, rows - count), (0, 0))
    x = jnp.pad(patches, pad)
    t, a1 = run_qkv(x, vec, full[0:3])
    o, dy, logs = attend(slot_clip, t, out_grad)
    out, dm, do, gwo, gwe, gwc, sums_two, sums_be = run_feed(x, o, dy, vec, full[3], full[4:8], full[8:12])
    inner = jnp.sum((o.astype(F32) * do.astype(F32)).reshape(rows, -1, HEAD_DIM), axis=2)
    inner = jnp.pad(inner, ((0, 0), (0, 128 - inner.shape[1])))
    dt = attend_back(slot_clip, t, do, logs, inner)
    pg, gwi, sums_one = run_first(x, a1, dt, dm, vec, full[0:3])

    grads = jnp.concatenate([gwi, gwo[None], gwe, gwc], axis=0)
    grads = grads.reshape(12, parts, sh, width).swapaxes(0, 1).reshape(parts * 12 * sh, width)
    grads = lax.psum_scatter(grads, ("fsdp", "rep"), scatter_dimension=0, tiled=True)
    grads = lax.all_gather(grads, "rep", axis=0, tiled=True).reshape(12, sh, width)
    be_grad = sums_be[::8].reshape(4, parts, sh).swapaxes(0, 1).reshape(4, width)
    vector = jnp.concatenate(
        [sums_one[0:2], sums_two[2:3], sums_two[0:2], sums_two[3:4], be_grad], axis=0
    )
    vector = lax.dynamic_slice_in_dim(lax.psum(vector, ("fsdp", "rep")), mine * sh, sh, 1)
    outputs = []
    for member, grad in enumerate((*unpack_shards(grads, parts), vector)):
        outputs += step(grad.astype(F32), rates[member], masters[member], moments[member], averages[member])
    return (out[:count], pg[:count], *outputs)


def direct_path(patches, slot_clip, out_grad, masters, moments, averages, rates):
    parts = lax.axis_size("fsdp")
    count, width = patches.shape
    rows = (count + RT - 1) // RT * RT
    sh = width // parts
    block = (parts // 2, 2, sh, width)
    wide, low = ((rows, width), F32), ((rows, width), BF)
    t, a1, x, wi, wo, early, later, vec = comm_call(
        functools.partial(gather_kernel, parts), "gather_project_in", 0, (patches, masters[4], *masters[:4]),
        [((rows, 3 * width), BF), low, low, ((3,) + block, BF), ((1,) + block, BF),
         ((FIRST_BLOCKS - 4,) + block, BF), ((6, sh, width), BF), ((16, width), F32)],
        [pltpu.VMEM((rows, 3 * width), BF), pltpu.VMEM((FIRST_BLOCKS,) + block, BF),
         pltpu.VMEM((FIRST_BLOCKS, sh, width), BF), pltpu.SemaphoreType.DMA((FIRST_BLOCKS + 3,))]
        + gather_sems(FIRST_BLOCKS, parts) + Vector.scratch(parts, (16, width), F32),
        far_out=(0, 3, 4, 5),
    )
    o, dy, logs = attend(slot_clip, t, out_grad)
    out, dm, do, dz, grads_two, rest, sums_two, sums_be, inner = comm_call(
        functools.partial(feed_comm_kernel, parts), "feed_forward_reduce", 1,
        (x, o, dy, vec, wo, early, later),
        [low, wide, low, low, ((4, sh, width), BF), ((4,) + block, BF), ((8, width), F32), ((8, width), F32),
         ((rows, 128), F32)],
        [pltpu.VMEM(*low), pltpu.VMEM(*low), pltpu.VMEM(*low), pltpu.VMEM((1,) + block, BF),
         pltpu.VMEM(*low), pltpu.VMEM(*wide), pltpu.VMEM(*low), pltpu.VMEM(*low),
         pltpu.VMEM(*low), pltpu.VMEM(*wide), pltpu.VMEM(*wide), pltpu.VMEM((8,) + block, BF),
         pltpu.VMEM((8,) + block, BF), pltpu.SemaphoreType.DMA((9,)), pltpu.SemaphoreType.DMA((TILES, 4))]
        + gather_sems(6, parts) + Reduce.scratch(4, parts, sh, width),
        far=(0, 1, 2, 4, 5), far_out=(0, 1, 2, 3, 5),
    )
    dt = attend_back(slot_clip, t, do, logs, inner)
    pg, grads_one, total = comm_call(
        functools.partial(first_comm_kernel, parts), "project_in_back_reduce", 2,
        (x, a1, o, dz, dt, dm, vec, wi, sums_two, sums_be, rest),
        [wide, ((LAST_BLOCKS, sh, width), BF), ((16, width), F32)],
        [pltpu.VMEM((LAST_BLOCKS,) + block, BF), pltpu.VMEM(*low), pltpu.VMEM(*low), pltpu.VMEM(*low),
         pltpu.VMEM(*low), pltpu.VMEM((rows, 3 * width), BF), pltpu.VMEM(*wide), pltpu.VMEM((3,) + block, BF),
         pltpu.SemaphoreType.DMA((9,))]
        + Reduce.scratch(LAST_BLOCKS, parts, sh, width) + Vector.scratch(parts, (16, width), F32),
        far=(0, 1, 2, 3, 4, 5, 7, 10),
    )
    return update(rates, count, grads_two, grads_one, total, out, pg, masters, moments, averages)


def on_device(
    patches, slot_clip, out_grad,
    project_in_weight, project_in_moment, project_in_average,
    project_out_weight, project_out_moment, project_out_average,
    expand_weight, expand_moment, expand_average,
    contract_weight, contract_moment, contract_average,
    vector_weight, vector_moment, vector_average,
):
    masters = (project_in_weight, project_out_weight, expand_weight, contract_weight, vector_weight)
    moments = (project_in_moment, project_out_moment, expand_moment, contract_moment, vector_moment)
    averages = (project_in_average, project_out_average, expand_average, contract_average, vector_average)
    parts, copies = lax.axis_size("fsdp"), lax.axis_size("rep")
    count, width = patches.shape
    direct = copies == 4 and parts % 4 == 0 and width // parts % 48 == 0
    path = direct_path if direct else plain_path
    tokens_all = count * parts * copies
    rates = [rate / tokens_all**0.5 for rate in RATES]
    return tuple(path(patches, slot_clip, out_grad, masters, moments, averages, rates))


def solution(mesh):
    tokens = P(("fsdp", "rep"), None)
    split, split_vector = P("fsdp", None), P(None, "fsdp")
    in_specs = (tokens, P(("fsdp", "rep")), tokens) + (split,) * 12 + (split_vector,) * 3
    out_specs = (tokens,) * 2 + (split,) * 20 + (split_vector,) * 5
    return jax.shard_map(on_device, mesh=mesh, in_specs=in_specs, out_specs=out_specs, check_vma=False)
```
